128 devices in a mesh: tm: 4 (over z_lo, core), strip: 32 (over y, z_hi, x).
Axes of the slice: x: 4, y: 4, z: 4 (z_hi: 2, z_lo: 2; z = z_hi * 2 + z_lo), core: 2. Of those that a mesh axis runs over, the one named last changes fastest.
Arguments:
- screen_vec: float32 [4, 4096, 4096], P('tm', 'strip'), may hold values from -8 to 8
- prior_scale: float32 [4], P('tm'), may hold values from 0.5 to 2
- flow_weight: float32 [4], P('tm'), may hold values from 0.5 to 2
- wind: int32 [4, 2], P('tm'), may hold values from -32 to 32, as said below
- pierce_point_strip: int32 [4, 4096, 64, 1], P('tm', 'strip'), may hold values from 0 to 31; in each aligned block of 8192 rows (0 to 8191, 8192 to 16383, ..., all dimensions but the last counted through in order) at most 512 rows name the same one
- pierce_block: int32 [4, 4096, 64], P('tm', 'strip'), may hold values from 0 to 4095
- pierce_weights: bfloat16 [4, 4096, 64, 128], P('tm', 'strip'), may hold values from -1.5 to 1.5
- noise_prec: float32 [4, 4096, 64], P('tm', 'strip'), may hold values from 1 to 16
Outputs:
- hessian_vec: float32 [4, 4096, 4096], P('tm', 'strip')
The draws below stay inside these ranges and needn't reach their ends.
Inputs may be any that keep to these rules, and one draw needn't show every extreme that they name: `pierce_point_strip`: among the pierce points of one slot and one group of 128 antennas (the rows of one device), at most 512 lie in one strip. `wind`: row shifts are never zero.
All inputs are finite; a program needn't handle non-finite values.
Results may differ from the reference program's by a relative error of at most 0.0015.
Values may be sent and summed in bfloat16 or wider, within the bound.
A program may use at most 192 MiB of HBM per device.

```python
import math
import jax
import jax.numpy as jnp
import numpy as np

M = 4096
DIRECTION_COUNT = 64
BLOCK = 128
WIND = 32
GROUP_ANTENNAS = 128
ANTENNA_COUNT = 4096
TIME_SLOT_COUNT = 4
POINT_LIMIT = 512
N_STRIP = 32


def draw_wind(key, part):
    key = jax.random.fold_in(key, 7)
    key_mag, key_sign, key_col = jax.random.split(key, 3)
    magnitude = jax.random.randint(key_mag, (TIME_SLOT_COUNT,), 1, WIND + 1)
    signs = jax.random.randint(key_sign, (TIME_SLOT_COUNT,), 0, 2) * 2 - 1
    row_shift = (magnitude * signs).at[0].set(WIND).at[1].set(-WIND)
    col_shift = jax.random.randint(key_col, (TIME_SLOT_COUNT,), -WIND, WIND + 1)
    return jnp.stack([row_shift, col_shift], axis=1).astype(jnp.int32)


def radius_count(side_pixels, limit):
    digits = np.arange(side_pixels, dtype=np.int64)
    folded = np.minimum(digits, side_pixels - digits)
    squares = folded * folded
    sorted_sq = np.sort(squares)
    return int(np.searchsorted(sorted_sq, limit * limit - squares, side='left').sum())


def band_filter(noise_field, shelf_level):
    side_pixels = noise_field.shape[-1]
    low_cut = max(side_pixels // 64, 1)
    high_cut = max(side_pixels // 16, 2)
    lower_count = radius_count(side_pixels, low_cut)
    upper_count = radius_count(side_pixels, high_cut)
    total_count = side_pixels * side_pixels
    mean_square = (upper_count - lower_count + shelf_level * shelf_level * (total_count - upper_count)) / total_count
    row_index = jnp.arange(side_pixels, dtype=jnp.int32)
    rows_fold = jnp.minimum(row_index, side_pixels - row_index)
    cols_fold = jnp.arange(side_pixels // 2 + 1, dtype=jnp.int32)
    squared = rows_fold[:, None] * rows_fold[:, None] + cols_fold[None, :] * cols_fold[None, :]
    mode_gain = jnp.where(squared < low_cut * low_cut, 0.0, jnp.where(squared < high_cut * high_cut, 1.0, shelf_level)).astype(jnp.float32)
    spectrum = jnp.fft.rfft2(noise_field) * mode_gain
    filtered = jnp.fft.irfft2(spectrum, s=(side_pixels, side_pixels))
    return (filtered / math.sqrt(mean_square)).astype(jnp.float32)


def draw_screen_vec(key, part):
    key = jax.random.fold_in(key, 11)
    noise_field = jax.random.normal(key, (TIME_SLOT_COUNT, M, M), jnp.float32)
    shelf_level = 0.1
    return band_filter(noise_field, shelf_level)


def set_ends(entries, stream_key, least, high):
    longest = entries.shape.index(max(entries.shape))
    spots = []
    for shift in (0, 1):
        where = [jax.random.randint(jax.random.fold_in(stream_key, axis), (), 0, length) for axis, length in enumerate(entries.shape)]
        where[longest] = (where[longest] + shift) % entries.shape[longest]
        spots.append(tuple(where))
    return entries.at[spots[0]].set(least).at[spots[1]].set(high)


def shard_levels(key, shape, cuts, smallest, top_value):
    gain, own = 1.0, jax.random.fold_in(key, 6)
    for axis_at, parts in cuts:
        heights = jnp.exp(jax.random.uniform(jax.random.fold_in(own, axis_at), (parts,), jnp.float32, smallest / len(cuts), top_value / len(cuts)))
        gain = gain * jnp.repeat(heights, shape[axis_at] // parts).reshape([-1 if axis == axis_at else 1 for axis in range(len(shape))])
    return gain


def assign_block(rng, own, number, rows, count, top, most, lean):
    ranking = jax.random.permutation(rng, count)
    packed, ordinary = portions_of(count, rows * top, most, lean, True), portions_of(count, rows * top, most, lean, False)
    places = jnp.arange(count)

    def named(tallies, rotation):
        used = int((tallies > 0).sum())
        fixed = max(1, used // 4)
        moved = fixed + (places - fixed + rotation * (used - fixed)) % max(1, count - fixed)
        return jnp.zeros((count,), jnp.int32).at[ranking[jnp.where(places < fixed, places, moved)]].set(jnp.asarray(tallies, jnp.int32))

    tallies = jnp.where(number % 4 == 0, named(packed, number // 4), named(ordinary, number - number // 4 - 1))
    mixed = jax.random.permutation(jax.random.fold_in(own, 3), count)
    giver, sink = mixed[0:count // 2 * 2:2], mixed[1:count // 2 * 2:2]
    slack = jnp.minimum(tallies[giver] - 1, most - tallies[sink]) // 2
    slack = jnp.where((giver == ranking[0]) | (sink == ranking[0]) | (tallies[sink] == 0), 0, jnp.maximum(slack, 0))
    moved = jax.random.randint(jax.random.fold_in(own, 4), (count // 2,), 0, 1 << 20) % (slack + 1)
    tallies = tallies.at[giver].add(-moved).at[sink].add(moved)
    members = jnp.searchsorted(jnp.cumsum(tallies), jnp.arange(rows * top), side="right").astype(jnp.int32)
    table = members.reshape(top, rows).T
    table = table[jax.random.permutation(jax.random.fold_in(own, 1), rows)]
    rotation = jax.random.randint(jax.random.fold_in(own, 2), (rows, 1), 0, top)
    return jnp.take_along_axis(table, (jnp.arange(top)[None, :] + rotation) % top, axis=1)


def portions_of(count, total, bound, slope, full):
    loads = [(1 << 20) // math.isqrt(rank ** slope) + 1 for rank in range(1, count + 1)]
    largest = bound if full else min(bound, max(-(-total // count), total * loads[0] // sum(loads)))
    least = 1 if total - largest >= count - 1 else 0
    given, surplus = [largest] + [least] * (count - 1), total - largest - least * (count - 1)
    while surplus > 0:
        candidates = [i for i in range(1, count) if given[i] < largest] or [i for i in range(1, count) if given[i] < bound]
        mass, left = sum([loads[i] for i in candidates]), surplus
        for i in candidates:
            addition = min(bound - given[i], max(1, left * loads[i] // mass), surplus)
            given[i] = given[i] + addition
            surplus = surplus - addition
    return np.array(given)


def noise(stream_key, extent, scale, most, pieces=(), held_as=jnp.bfloat16):
    factor_of = shard_levels(stream_key, extent, pieces, -0.22, 0.18) if pieces else 1.0
    array = jax.random.normal(stream_key, extent, jnp.float32) * scale * factor_of
    return jnp.minimum(jnp.maximum(array, -most), most).astype(held_as)


def setup_inputs(seed: int = 0) -> dict:
    splits = jax.random.split(jax.random.key(seed), 9)
    screen_vec = draw_screen_vec(jax.random.fold_in(splits[8], 71), 0)
    prior_scale = jnp.clip(jnp.exp(math.log(2.0) - 1.3862944 * jax.random.uniform(splits[1], (TIME_SLOT_COUNT,), jnp.float32) ** shard_levels(splits[1], (TIME_SLOT_COUNT,), ((0, 4),), -0.2, 0.2)), 0.5, 2.0)
    flow_weight = jnp.clip(jnp.exp(math.log(2.0) - 1.3862944 * jax.random.uniform(splits[2], (TIME_SLOT_COUNT,), jnp.float32) ** shard_levels(splits[2], (TIME_SLOT_COUNT,), ((0, 4),), -0.2, 0.2)), 0.5, 2.0)
    wind = draw_wind(jax.random.fold_in(splits[8], 71), 0)
    pierce_point_strip_keys = jax.random.split(jax.random.fold_in(splits[4], 1), TIME_SLOT_COUNT * ANTENNA_COUNT * DIRECTION_COUNT // (GROUP_ANTENNAS * DIRECTION_COUNT))
    pierce_point_strip_turns = jax.random.permutation(jax.random.fold_in(splits[4], 3), TIME_SLOT_COUNT * ANTENNA_COUNT * DIRECTION_COUNT // (GROUP_ANTENNAS * DIRECTION_COUNT))
    pierce_point_strip = jax.vmap(lambda own, number: assign_block(jax.random.fold_in(splits[4], 2), own, number, GROUP_ANTENNAS * DIRECTION_COUNT, N_STRIP, 1, POINT_LIMIT, 1))(pierce_point_strip_keys, pierce_point_strip_turns).reshape((TIME_SLOT_COUNT, ANTENNA_COUNT, DIRECTION_COUNT, 1))
    pierce_block = set_ends(jax.random.randint(splits[5], (TIME_SLOT_COUNT, ANTENNA_COUNT, DIRECTION_COUNT), 0, (M // N_STRIP) * (M // BLOCK)), jax.random.fold_in(splits[5], 1), 0, ((M // N_STRIP) * (M // BLOCK)) - 1).astype(jnp.int32)
    pierce_weights = noise(splits[6], (TIME_SLOT_COUNT, ANTENNA_COUNT, DIRECTION_COUNT, BLOCK), 16 ** -0.5, 1.5, ((0, 4), (1, 32)))
    noise_prec = jnp.clip(jnp.exp(math.log(16.0) - 2.7725887 * jax.random.uniform(splits[7], (TIME_SLOT_COUNT, ANTENNA_COUNT, DIRECTION_COUNT), jnp.float32) ** shard_levels(splits[7], (TIME_SLOT_COUNT, ANTENNA_COUNT, DIRECTION_COUNT), ((0, 4), (1, 32)), -0.2, 0.2)), 1.0, 16.0)
    return dict(screen_vec=screen_vec, prior_scale=prior_scale, flow_weight=flow_weight, wind=wind, pierce_point_strip=pierce_point_strip, pierce_block=pierce_block, pierce_weights=pierce_weights, noise_prec=noise_prec)


KZERO = 2.0


def amplitude(freq_rows, freq_cols, side):
    fold_rows = jnp.minimum(freq_rows, side - freq_rows).astype(jnp.float32)
    fold_cols = jnp.minimum(freq_cols, side - freq_cols).astype(jnp.float32)
    radius = (fold_rows * fold_rows + fold_cols * fold_cols) / (KZERO * KZERO)
    return (side / (2.0 * KZERO)) * jnp.power(1.0 + radius, -11.0 / 12.0)


def whiten(screen_in, slot_scale):
    side = screen_in.shape[0]
    freqs = jnp.arange(side, dtype=jnp.int32)
    spectrum = amplitude(freqs[:, None], freqs[None, :], side) * slot_scale
    return jnp.real(jnp.fft.ifft2(jnp.fft.fft2(screen_in) * spectrum)).astype(screen_in.dtype)


def data_term(screen, strip_of, block_of, weights, precision_of):
    per_strip = (M // N_STRIP) * (M // BLOCK)
    global_ids = (strip_of[..., 0] * per_strip + block_of).reshape(-1).astype(jnp.int32)
    tiles = screen.reshape(-1, BLOCK)
    flat_w = weights.reshape(-1, BLOCK).astype(jnp.float32)
    phase = jnp.sum(tiles[global_ids] * flat_w, axis=1).reshape(ANTENNA_COUNT, DIRECTION_COUNT)
    centre = jnp.sum(precision_of * phase, axis=1, keepdims=True) / jnp.sum(precision_of, axis=1, keepdims=True)
    weighted = precision_of * (phase - centre)
    update = jnp.zeros_like(tiles).at[global_ids].add(flat_w * weighted.reshape(-1, 1))
    return update.reshape(screen.shape)


def reference(screen_vec, prior_scale, flow_weight, wind, pierce_point_strip, pierce_block, pierce_weights, noise_prec):
    screens = [whiten(screen_vec[slot], prior_scale[slot]) for slot in range(TIME_SLOT_COUNT)]
    grads = [data_term(screens[slot], pierce_point_strip[slot], pierce_block[slot], pierce_weights[slot], noise_prec[slot]) for slot in range(TIME_SLOT_COUNT)]
    for slot in range(TIME_SLOT_COUNT - 1):
        shifted = jnp.roll(screens[slot], (wind[slot, 0], wind[slot, 1]), (0, 1))
        diff = flow_weight[slot] * (screens[slot + 1] - shifted)
        grads[slot + 1] = grads[slot + 1] + diff
        grads[slot] = grads[slot] - jnp.roll(diff, (-wind[slot, 0], -wind[slot, 1]), (0, 1))
    outputs = [screen_vec[slot] + whiten(grads[slot], prior_scale[slot]) for slot in range(TIME_SLOT_COUNT)]
    return jnp.stack(outputs)
```

```python
import math

import jax
import jax.numpy as jnp
import ml_dtypes
import numpy as np
from jax import lax
from jax.experimental import pallas as pl
from jax.experimental.pallas import tpu as pltpu
from jax.sharding import PartitionSpec as P

KZERO = 2.0
SIDE = 4096
OUTER = 32
INNER = 128
HALF = 64
PEERS = 32
SLOTS = 512
POINT_ROWS = 64
VMEM_BYTES = 56 * 1024 * 1024
F32 = jnp.float32
BF16 = jnp.bfloat16


def pieces(table, count):
    rest = np.asarray(table, np.float64)
    out = []
    for _ in range(count):
        out.append(rest.astype(np.float32).astype(ml_dtypes.bfloat16))
        rest = rest - out[-1].astype(np.float64)
    return np.stack(out)


def row_tables():
    b = np.arange(INNER)[:, None]
    j = np.arange(HALF)[None, :]
    theta = [2 * np.pi * ((b * j) % INNER) / INNER, 2 * np.pi * ((b * (INNER - 1 - j)) % INNER) / INNER]
    forward = []
    backward = []
    for t in theta:
        forward.append(np.concatenate([np.cos(t), -np.sin(t)], axis=1))
        forward.append(np.concatenate([np.sin(t), np.cos(t)], axis=1))
        backward.append(np.concatenate([np.cos(t).T, np.sin(t).T], axis=1))
        backward.append(np.concatenate([-np.sin(t).T, np.cos(t).T], axis=1))
    fwd = np.concatenate(
        [np.concatenate([forward[0], forward[1]], axis=0), np.concatenate([forward[2], forward[3]], axis=0)], axis=1
    )
    inv = np.concatenate(backward, axis=0)
    sign = np.where(np.arange(INNER) % 2 == 0, 1.0, -1.0)
    t0 = theta[0]
    first = np.concatenate([np.cos(t0), -np.sin(t0)], axis=1)
    first[:, HALF] = sign
    first_inv = np.concatenate([2 * np.cos(t0).T, -2 * np.sin(t0).T], axis=0)
    first_inv[0, :] = 1.0
    first_inv[HALF, :] = sign
    t16 = 2 * np.pi * ((b * (16 + 32 * j)) % SIDE) / SIDE
    mid = np.concatenate([np.cos(t16), -np.sin(t16)], axis=1)
    mid_inv = np.concatenate([2 * np.cos(t16).T, -2 * np.sin(t16).T], axis=0)
    k1 = np.arange(16)[:, None]
    tw = 2 * np.pi * (k1 * np.arange(INNER)[None, :]) / SIDE
    twiddle = np.stack([np.cos(tw), np.sin(tw)]).astype(np.float32)
    return fwd, inv, first, first_inv, mid, mid_inv, twiddle


def column_tables():
    k1 = np.arange(OUTER)[:, None, None]
    k2 = np.arange(INNER)[None, :, None]
    r = np.arange(INNER)[None, None, :]
    theta = 2 * np.pi * (((k1 + OUTER * k2) * r) % SIDE) / SIDE
    fwd = np.concatenate([np.cos(theta), -np.sin(theta)], axis=1)
    theta = theta.transpose(0, 2, 1)
    inv = np.concatenate([np.cos(theta), np.sin(theta)], axis=1)
    return fwd, inv


def split(value):
    high = value.astype(BF16)
    return high, (value - high.astype(F32)).astype(BF16)


def mm(left, right):
    return lax.dot_general(left, right, (((1,), (0,)), ((), ())), preferred_element_type=F32)


def mm_nt(left, right):
    return lax.dot_general(left, right, (((1,), (1,)), ((), ())), preferred_element_type=F32)


def split_into(value, count):
    parts = []
    for i in range(count):
        parts.append(value.astype(BF16))
        if i + 1 < count:
            value = value - parts[-1].astype(F32)
    return parts


def data_by_table(value, tables):
    count = len(tables)
    parts = split_into(value, count)
    total = None
    for order in reversed(range(count)):
        for i in range(order + 1):
            term = mm(parts[i], tables[order - i])
            total = term if total is None else total + term
    return total


def table_by_data(tables, value):
    parts = split_into(value, len(tables))
    left = jnp.concatenate(tables[0:2], axis=1)
    right = jnp.concatenate(parts[0:2], axis=1)
    r = mm(left, jnp.concatenate([right, right], axis=0))
    total = r[:, INNER : 2 * INNER] + r[:, 0:INNER]
    if len(tables) == 3:
        left = jnp.concatenate([tables[0], tables[2]], axis=1)
        total = total + mm(left, jnp.concatenate([parts[2], parts[0]], axis=0))
    return total


def every(ref):
    return [ref[i] for i in range(ref.shape[0])]


def c_mul(value, factor):
    re, im = value
    c, s = factor.real, factor.imag
    if im is None:
        return (re * c, re * s)
    return (re * c - im * s, re * s + im * c)


def real_forward(xs):
    n = len(xs)
    if n == 2:
        return [(xs[0] + xs[1], None), (xs[0] - xs[1], None)]
    even, odd = real_forward(xs[0::2]), real_forward(xs[1::2])
    m = n // 2
    out = [None] * (m + 1)
    for k in range(m // 2 + 1):
        if k == 0:
            out[0] = (even[0][0] + odd[0][0], None)
            out[m] = (even[0][0] - odd[0][0], None)
        elif 2 * k == m:
            out[k] = (even[k][0], -odd[k][0])
        else:
            tr, ti = c_mul(odd[k], complex(math.cos(2 * math.pi * k / n), -math.sin(2 * math.pi * k / n)))
            er, ei = even[k]
            out[k] = (er + tr, ei + ti)
            out[m - k] = (er - tr, ti - ei)
    return out


def real_backward(spec):
    n = 2 * (len(spec) - 1)
    if n == 2:
        return [spec[0][0] + spec[1][0], spec[0][0] - spec[1][0]]
    m = n // 2
    even, odd = [], []
    for k in range(m // 2 + 1):
        if k == 0:
            even.append((spec[0][0] + spec[m][0], None))
            odd.append((spec[0][0] - spec[m][0], None))
        elif 2 * k == m:
            even.append((2.0 * spec[k][0], None))
            odd.append((-2.0 * spec[k][1], None))
        else:
            ar, ai = spec[k]
            br, bi = spec[m - k]
            even.append((ar + br, ai - bi))
            odd.append(c_mul((ar - br, ai + bi), complex(math.cos(2 * math.pi * k / n), math.sin(2 * math.pi * k / n))))
    xe, xo = real_backward(even), real_backward(odd)
    out = [None] * n
    out[0::2] = xe
    out[1::2] = xo
    return out


def packed_fft(xs, sign, flip):
    n = len(xs)
    if n == 1:
        return xs
    even, odd = packed_fft(xs[0::2], sign, flip), packed_fft(xs[1::2], sign, flip)
    out = [None] * n
    for k in range(n // 2):
        t = odd[k]
        if k:
            turned = pltpu.roll(t, HALF, 1) * flip
            c, s = math.cos(2 * math.pi * k / n), sign * math.sin(2 * math.pi * k / n)
            t = (-s) * turned if 4 * k == n else c * t - s * turned
        out[k] = even[k] + t
        out[k + n // 2] = even[k] - t
    return out


def flip_lanes(rows):
    lane = lax.broadcasted_iota(jnp.int32, (rows, INNER), 1)
    return jnp.where(lane < HALF, 1.0, -1.0).astype(F32)


def row_forward_kernel(tiled, x_ref, tw_ref, f_ref, a_ref, m_ref, out_ref, y_scr, e_scr):
    def slab(g, carry):
        if tiled:
            xs = [x_ref[pl.ds(pl.multiple_of(g * 256 + a * 8, 8), 8), :] for a in range(OUTER)]
        else:
            xs = [x_ref[pl.ds(pl.multiple_of(g * 8, 8), 8), a * INNER : (a + 1) * INNER] for a in range(OUTER)]
        ys = real_forward(xs)
        rows = pl.ds(pl.multiple_of(g * 8, 8), 8)
        e_scr[0, rows, :] = ys[0][0]
        e_scr[1, rows, :] = ys[16][0]
        for k in range(1, 16):
            c = tw_ref[0, k : k + 1, :]
            s = tw_ref[1, k : k + 1, :]
            re, im = ys[k]
            base = pl.ds(pl.multiple_of((k - 1) * INNER + g * 8, 8), 8)
            y_scr[base, 0:INNER] = re * c + im * s
            y_scr[base, INNER : 2 * INNER] = im * c - re * s
        return carry

    lax.fori_loop(0, 16, slab, 0)
    out_ref[0] = data_by_table(e_scr[0], every(a_ref))
    out_ref[1] = data_by_table(e_scr[1], every(m_ref))

    def group(q, carry):
        v = data_by_table(y_scr[pl.ds(pl.multiple_of(q * 384, 8), 384), :], every(f_ref))
        for i in range(3):
            out_ref[2 + 2 * (3 * q + i)] = v[i * INNER : (i + 1) * INNER, 0:INNER]
            out_ref[3 + 2 * (3 * q + i)] = v[i * INNER : (i + 1) * INNER, INNER : 2 * INNER]
        return carry

    lax.fori_loop(0, 5, group, 0)


def row_backward_kernel(final, *refs):
    if final:
        in_ref, base_ref, tw_ref, f_ref, a_ref, m_ref, out_ref, z_scr, e_scr = refs
    else:
        in_ref, tw_ref, f_ref, a_ref, m_ref, out_ref, z_scr, e_scr = refs
    e_scr[0] = data_by_table(in_ref[0], every(a_ref))
    e_scr[1] = data_by_table(in_ref[1], every(m_ref))

    def group(q, carry):
        parts = []
        for i in range(3):
            k = 3 * q + i
            parts.append(jnp.concatenate([in_ref[2 + 2 * k], in_ref[3 + 2 * k]], axis=1))
        v = jnp.concatenate(parts, axis=0)
        z_scr[pl.ds(pl.multiple_of(q * 384, 8), 384), :] = data_by_table(v, every(f_ref))
        return carry

    lax.fori_loop(0, 5, group, 0)

    def slab(g, carry):
        rows = pl.ds(pl.multiple_of(g * 8, 8), 8)
        spec = [(e_scr[0, rows, :], None)]
        for k in range(1, 16):
            c = tw_ref[0, k : k + 1, :]
            s = tw_ref[1, k : k + 1, :]
            base = pl.ds(pl.multiple_of((k - 1) * INNER + g * 8, 8), 8)
            re = z_scr[base, 0:INNER]
            im = z_scr[base, INNER : 2 * INNER]
            spec.append((re * c - im * s, im * c + re * s))
        spec.append((e_scr[1, rows, :], None))
        xs = real_backward(spec)
        for a in range(OUTER):
            if final:
                cols = slice(a * INNER, (a + 1) * INNER)
                out_ref[rows, cols] = base_ref[rows, cols] + xs[a]
            else:
                out_ref[pl.ds(pl.multiple_of(g * 256 + a * 8, 8), 8), :] = xs[a]
        return carry

    lax.fori_loop(0, 16, slab, 0)


def column_first_step(in_ref, y_scr, sign):
    flip = flip_lanes(8)

    def slab(g, carry):
        rows = pl.ds(pl.multiple_of(g * 8, 8), 8)
        ys = packed_fft([in_ref[s, rows, :] for s in range(OUTER)], sign, flip)
        for k in range(OUTER):
            y_scr[k, rows, :] = ys[k]
        return carry

    lax.fori_loop(0, 16, slab, 0)


def apply_packed(e_ref, k1, value, flip):
    r = table_by_data([e_ref[i, k1] for i in range(e_ref.shape[0])], value)
    return r[0:INNER] - pltpu.roll(r[INNER : 2 * INNER], HALF, 1) * flip


def edge_lanes():
    lane = lax.broadcasted_iota(jnp.int32, (INNER, INNER), 1)
    return jnp.logical_or(lane == 0, lane == HALF), lane < HALF


def edge_gather(ref):
    mask, _ = edge_lanes()

    def step(k1, acc):
        return acc + pltpu.roll(jnp.where(mask, ref[k1], 0.0), k1, 1)

    return lax.fori_loop(0, OUTER, step, jnp.zeros((INNER, INNER), F32), unroll=4)


def edge_split(spec, amp):
    i = lax.broadcasted_iota(jnp.int32, (INNER, INNER), 0)
    j = lax.broadcasted_iota(jnp.int32, (INNER, INNER), 1)
    one = jnp.ones((INNER, INNER), F32)
    none = jnp.zeros((INNER, INNER), F32)
    rows = jnp.where(i + j == INNER - 1, one, none).astype(BF16)
    rows0 = jnp.where(((i + j) & (INNER - 1)) == 0, one, none).astype(BF16)
    sign = jnp.where(j < HALF, one, -one)
    col = j & (HALF - 1)
    same = (i < HALF) == (j < HALF)
    lanes = jnp.where(
        jnp.logical_and(same, jnp.logical_and(col > 0, col + (i & (HALF - 1)) == OUTER)), sign, none
    ).astype(BF16)
    lanes0 = jnp.where(jnp.logical_and(i == j, col == 0), sign, none).astype(BF16)

    def move(left, value, right):
        value = sum(mm(left, p) for p in reversed(split_into(value, 3)))
        return sum(mm(p, right) for p in reversed(split_into(value, 3)))

    rev = move(rows, spec, lanes) + move(rows0, spec, lanes0)
    swapped = pltpu.roll(amp, HALF, 1)
    _, left = edge_lanes()
    a0 = jnp.where(left, amp, swapped)
    a2 = jnp.where(left, swapped, amp)
    return 0.5 * (spec + rev), 0.5 * (spec - rev), a0, a2


def turn(c, s, value, flip):
    return c * value + s * (pltpu.roll(value, HALF, 1) * flip)


def column_first_kernel(
    scal, in_ref, amp_ref, ph_ref, edge_ref, ef, ei, out_ref, own_ref, up_ref, down_ref, y_scr, z_scr
):
    column_first_step(in_ref, y_scr, -1.0)
    flip = flip_lanes(INNER)

    def step(k1, carry):
        value = apply_packed(ef, k1, y_scr[k1], flip)
        amp = amp_ref[k1]
        once = value * amp
        twice = once * amp
        y_scr[k1] = value
        z_scr[k1] = scal[0] * once
        own_ref[k1] = scal[3] * twice
        for n, ref, gain in ((0, up_ref, scal[1]), (1, down_ref, scal[2])):
            cb = ph_ref[2 * n]
            sb = ph_ref[2 * n + 1]
            ca = scal[8 + 64 * n + k1] * gain
            sa = scal[8 + 64 * n + 32 + k1] * gain
            ref[k1] = turn(cb * ca - sb * sa, sb * ca + cb * sa, twice, flip).astype(BF16)
        return carry

    lax.fori_loop(0, OUTER, step, 0, unroll=4)

    @pl.when(scal[6] > 0.5)
    def _():
        u0, u2, a0, a2 = edge_split(edge_gather(y_scr), edge_gather(amp_ref))
        mask, _ = edge_lanes()
        e0 = a0 * u0
        e2 = a2 * u2
        fixed = [scal[0] * (e0 + e2)]
        e0 = a0 * e0
        e2 = a2 * e2
        fixed.append(scal[3] * (e0 + e2))
        fixed.append(scal[1] * turn(edge_ref[0], edge_ref[1], e0 + scal[4] * e2, flip))
        fixed.append(scal[2] * turn(edge_ref[2], edge_ref[3], e0 + scal[5] * e2, flip))

        def put(k1, carry):
            back = lax.rem(INNER - k1, INNER)
            for ref, value in zip((z_scr, own_ref, up_ref, down_ref), fixed):
                value = jnp.where(mask, pltpu.roll(value, back, 1), ref[k1].astype(F32))
                ref[k1] = value.astype(ref.dtype)
            return carry

        lax.fori_loop(0, OUTER, put, 0)

    def inverse(k1, carry):
        z_scr[k1] = apply_packed(ei, k1, z_scr[k1], flip)
        return carry

    lax.fori_loop(0, OUTER, inverse, 0, unroll=4)
    column_first_step(z_scr, out_ref, 1.0)


def column_second_kernel(scal, in_ref, amp_ref, own_ref, prev_ref, next_ref, ef, ei, out_ref, y_scr, z_scr):
    column_first_step(in_ref, y_scr, -1.0)
    flip = flip_lanes(INNER)

    def step(k1, carry):
        value = apply_packed(ef, k1, y_scr[k1], flip)
        moved = prev_ref[k1].astype(F32) + next_ref[k1].astype(F32)
        y_scr[k1] = value
        z_scr[k1] = scal[0] * (value * amp_ref[k1] - moved) + own_ref[k1]
        return carry

    lax.fori_loop(0, OUTER, step, 0, unroll=4)

    @pl.when(scal[6] > 0.5)
    def _():
        spec = edge_gather(y_scr)
        amp = edge_gather(amp_ref)
        u0, u2, a0, a2 = edge_split(spec, amp)
        mask, _ = edge_lanes()
        change = scal[0] * (a0 * u0 + a2 * u2 - amp * spec)

        def put(k1, carry):
            back = lax.rem(INNER - k1, INNER)
            z_scr[k1] = z_scr[k1] + jnp.where(mask, pltpu.roll(change, back, 1), 0.0)
            return carry

        lax.fori_loop(0, OUTER, put, 0)

    def inverse(k1, carry):
        z_scr[k1] = apply_packed(ei, k1, z_scr[k1], flip)
        return carry

    lax.fori_loop(0, OUTER, inverse, 0, unroll=4)
    column_first_step(z_scr, out_ref, 1.0)


def route_kernel(t_ref, id_ref, slot_ref, idp_ref, cnt_ref):
    row = lax.broadcasted_iota(jnp.int32, (INNER, 2 * INNER), 0)
    col = lax.broadcasted_iota(jnp.int32, (INNER, 2 * INNER), 1)
    tri = jnp.where(jnp.logical_or(row < col, col >= INNER), 1.0, 0.0).astype(BF16)
    peer = lax.broadcasted_iota(jnp.int32, (PEERS, INNER), 0)
    base = jnp.zeros((PEERS, INNER), F32)
    for i in range(0, POINT_ROWS, 8):
        hots = [jnp.where(peer == t_ref[i + j : i + j + 1, :], 1.0, 0.0) for j in range(8)]
        cum = mm(jnp.concatenate(hots, axis=0).astype(BF16), tri)
        for j in range(8):
            part = cum[j * PEERS : (j + 1) * PEERS]
            pos = jnp.sum(hots[j] * (part[:, 0:INNER] + base), axis=0, keepdims=True)
            base = base + part[:, INNER : 2 * INNER]
            slot_ref[i + j : i + j + 1, :] = t_ref[i + j : i + j + 1, :] * SLOTS + pos.astype(jnp.int32)
    cnt_ref[...] = base.astype(jnp.int32)
    ids = id_ref[...]
    r = lax.shift_right_logical(ids, 5)
    idp_ref[...] = lax.shift_right_logical(r, 3) * 256 + (ids & 31) * 8 + (r & 7)


def pack_kernel(slot_ref, idp_ref, cnt_ref, w_ref, out_ref, sid_ref, w_scr, buf):
    def clear(i, carry):
        rows = pl.ds(pl.multiple_of(i * 64, 64), 64)
        buf[rows, :] = jnp.zeros((64, INNER), F32)
        buf[pl.ds(pl.multiple_of(i * 64 + PEERS * SLOTS // 2, 64), 64), :] = jnp.zeros((64, INNER), F32)
        w_scr[rows, :] = w_ref[rows, :].astype(F32)
        return carry

    lax.fori_loop(0, PEERS * SLOTS // INNER, clear, 0)

    def some(q, carry):
        first = q * 16
        slots = [slot_ref[first + j] for j in range(16)]
        ids = [idp_ref[first + j] for j in range(16)]
        rows = [w_scr[pl.ds(first + j, 1), :] for j in range(16)]
        for j in range(16):
            buf[pl.ds(slots[j], 1), :] = rows[j]
        for j in range(16):
            sid_ref[slots[j]] = ids[j]
        return carry

    lax.fori_loop(0, POINT_ROWS * INNER // 16, some, 0)

    def tag(d, carry):
        sid_ref[d * SLOTS] = (sid_ref[d * SLOTS] & 4095) | (cnt_ref[d, 0] * 4096)
        return carry

    lax.fori_loop(0, PEERS, tag, 0)

    def narrow(i, carry):
        rows = pl.ds(pl.multiple_of(i * INNER, INNER), INNER)
        out_ref[rows, :] = buf[rows, :].astype(BF16)
        return carry

    lax.fori_loop(0, PEERS * SLOTS // INNER, narrow, 0)


def gather_kernel(sid_ref, cnt_ref, tiles_ref, w_ref, out_ref, g_scr):
    g_scr[...] = jnp.zeros_like(g_scr)
    ones = jnp.ones((8, INNER), BF16)

    def source(s, carry):
        def some(q, inner):
            first = s * SLOTS + q * 16
            ids = [sid_ref[first + j] for j in range(16)]
            rows = [tiles_ref[pl.ds(ids[j], 1), :] for j in range(16)]
            for j in range(16):
                g_scr[pl.ds(q * 16 + j, 1), :] = rows[j]
            return inner

        lax.fori_loop(0, lax.shift_right_logical(cnt_ref[s] + 15, 4), some, 0)
        w = w_ref[pl.ds(pl.multiple_of(s * SLOTS, SLOTS), SLOTS), :].astype(F32)
        high, low = split(g_scr[...] * w)
        phase = mm_nt(ones, high) + mm_nt(ones, low)
        for q in range(4):
            out_ref[pl.ds(s * 4 + q, 1), :] = phase[0:1, q * INNER : (q + 1) * INNER]
        return carry

    lax.fori_loop(0, PEERS, source, 0)


def residual_kernel(slot_ref, prec_ref, phase_ref, out_ref, p_scr):
    high, low = split(phase_ref[...])
    table = jnp.concatenate([high, low], axis=0)
    batch = 4
    index = lax.broadcasted_iota(jnp.int32, (INNER, batch * INNER), 0)

    def wide(ref, i):
        return jnp.concatenate([ref[pl.ds(i * batch + j, 1), :] for j in range(batch)], axis=1)

    def pick(i, carry):
        slot = wide(slot_ref, i)
        hot = jnp.where(index == (slot & 127), 1.0, 0.0).astype(BF16)
        v = mm(table, hot)
        v = v[0:INNER] + v[INNER : 2 * INNER]
        got = jnp.sum(jnp.where(index == lax.shift_right_logical(slot, 7), v, 0.0), axis=0, keepdims=True)
        for j in range(batch):
            p_scr[pl.ds(i * batch + j, 1), :] = got[:, j * INNER : (j + 1) * INNER]
        return carry

    lax.fori_loop(0, POINT_ROWS // batch, pick, 0, unroll=2)
    row = lax.broadcasted_iota(jnp.int32, (INNER, INNER), 0)
    lane = lax.broadcasted_iota(jnp.int32, (INNER, INNER), 1)
    same = jnp.where((row < HALF) == (lane < HALF), 1.0, 0.0).astype(BF16)
    prec = prec_ref[...]
    phase = p_scr[...]

    def total(value):
        return sum(mm(p, same) for p in reversed(split_into(value, 3)))

    p_scr[...] = prec * (phase - total(prec * phase) / total(prec))

    def put(i, acc):
        slot = wide(slot_ref, i)
        hot = jnp.where(index == (slot & 127), 1.0, 0.0).astype(BF16)
        v = jnp.where(index == lax.shift_right_logical(slot, 7), wide(p_scr, i), 0.0)
        vh, vl = split(v)
        return acc + mm_nt(jnp.concatenate([vh, vl], axis=0), hot)

    acc = lax.fori_loop(0, POINT_ROWS // batch, put, jnp.zeros((2 * INNER, INNER), F32), unroll=2)
    out_ref[...] = acc[0:INNER] + acc[INNER : 2 * INNER]


COPIES = 8


def scatter_kernel(sid_ref, cnt_ref, r_ref, w_ref, out_ref, rt_scr, u_scr, *accs):
    def clear(i, carry):
        rows = pl.ds(pl.multiple_of(i * 64, 64), 64)
        for acc in accs:
            acc[rows, :] = jnp.zeros((64, INNER), F32)
        return carry

    lax.fori_loop(0, SIDE // 64, clear, 0)
    rt_scr[...] = r_ref[...].T
    lane = lax.broadcasted_iota(jnp.int32, (INNER, INNER), 1)

    def source(s, carry):
        for q in range(4):
            col = jnp.sum(jnp.where(lane == s * 4 + q, rt_scr[...], 0.0), axis=1, keepdims=True)
            base = pl.multiple_of(s * SLOTS + q * INNER, INNER)
            u_scr[q * INNER : (q + 1) * INNER, :] = w_ref[pl.ds(base, INNER), :].astype(F32) * col

        def some(q, inner):
            first = s * SLOTS + q * 16
            ids = [sid_ref[first + j] for j in range(16)]
            us = [u_scr[pl.ds(q * 16 + j, 1), :] for j in range(16)]
            for h in range(0, 16, COPIES):
                sums = [accs[j][pl.ds(ids[h + j], 1), :] + us[h + j] for j in range(COPIES)]
                for j in range(COPIES):
                    accs[j][pl.ds(ids[h + j], 1), :] = sums[j]
            return inner

        lax.fori_loop(0, lax.shift_right_logical(cnt_ref[s] + 15, 4), some, 0)
        return carry

    lax.fori_loop(0, PEERS, source, 0)

    def add(i, carry):
        rows = pl.ds(pl.multiple_of(i * 64, 64), 64)
        total = accs[0][rows, :]
        for acc in accs[1:]:
            total = total + acc[rows, :]
        out_ref[rows, :] = total
        return carry

    lax.fori_loop(0, SIDE // 64, add, 0)


def call(kernel, name, out_shapes, args, smem=0, smem_outs=(), scratch=()):
    vmem = pl.BlockSpec(memory_space=pltpu.VMEM)
    small = pl.BlockSpec(memory_space=pltpu.SMEM)
    outs = [small if i in smem_outs else vmem for i in range(len(out_shapes))]
    result = pl.pallas_call(
        kernel,
        out_shape=out_shapes,
        in_specs=[small] * smem + [vmem] * (len(args) - smem),
        out_specs=outs,
        scratch_shapes=list(scratch),
        compiler_params=pltpu.CompilerParams(vmem_limit_bytes=VMEM_BYTES),
        cost_estimate=pl.CostEstimate(flops=1024, bytes_accessed=1024, transcendentals=0),
        name=name,
    )(*args)
    return result


def shape(dims, dtype=F32):
    return jax.ShapeDtypeStruct(dims, dtype)


PENCILS = (PEERS, INNER, INNER)


def row_forward(x, tables, tiled):
    args = [x] + tables
    return call(
        lambda *refs: row_forward_kernel(tiled, *refs),
        "row_forward",
        [shape(PENCILS)],
        args,
        scratch=[pltpu.VMEM((15 * INNER, 2 * INNER), F32), pltpu.VMEM((2, INNER, INNER), F32)],
    )[0]


def row_backward(pencils, base, tables):
    final = base is not None
    args = [pencils] + ([base] if final else []) + tables
    return call(
        lambda *refs: row_backward_kernel(final, *refs),
        "row_backward",
        [shape((INNER, SIDE) if final else (SIDE, INNER))],
        args,
        scratch=[pltpu.VMEM((15 * INNER, 2 * INNER), F32), pltpu.VMEM((2, INNER, INNER), F32)],
    )[0]


def exchange(value):
    return lax.all_to_all(value, "strip", split_axis=0, concat_axis=0, tiled=True)


def amplitude_table(strip):
    j = jnp.arange(HALF, dtype=jnp.int32)
    k1 = strip // 2
    fold = jnp.where(strip % 2 == 0, k1 + OUTER * j, OUTER - k1 + OUTER * j)
    fold = jnp.where(strip == 1, 16 + OUTER * j, fold)
    edge = jnp.where((strip == 0) & (j == 0), SIDE // 2, fold)
    cols = jnp.concatenate([fold, edge]).astype(F32)[None, None, :]
    kr = jnp.arange(OUTER, dtype=jnp.int32)[:, None] + OUTER * jnp.arange(INNER, dtype=jnp.int32)[None, :]
    rows = jnp.minimum(kr, SIDE - kr).astype(F32)[:, :, None]
    radius = (rows * rows + cols * cols) / (KZERO * KZERO)
    return SIDE / (2.0 * KZERO) * jnp.power(1.0 + radius, -11.0 / 12.0)


def signed_columns(strip):
    j = jnp.arange(HALF, dtype=jnp.int32)
    k1 = strip // 2
    cols = jnp.where(strip % 2 == 0, k1 + OUTER * j, k1 + OUTER * (INNER - 1 - j))
    cols = jnp.where(strip == 1, 16 + OUTER * j, cols)
    return jnp.concatenate([cols, cols])


def phase_tables(wind_row, wind_col, strip, sign):
    unit = 2.0 * math.pi / SIDE
    k2 = jnp.arange(INNER, dtype=jnp.int32)[:, None]
    turn = (OUTER * k2 * wind_row + signed_columns(strip)[None, :] * wind_col) % SIDE
    angle = turn.astype(F32) * unit
    small = ((jnp.arange(OUTER, dtype=jnp.int32) * wind_row) % SIDE).astype(F32) * unit
    return jnp.cos(angle), sign * jnp.sin(angle), jnp.cos(small), sign * jnp.sin(small)


def edge_tables(wind_row, sign):
    k1 = jnp.arange(INNER, dtype=jnp.int32)[None, :] % HALF
    kr = k1 + OUTER * jnp.arange(INNER, dtype=jnp.int32)[:, None]
    angle = ((kr * wind_row) % SIDE).astype(F32) * (2.0 * math.pi / SIDE)
    return [jnp.cos(angle), sign * jnp.sin(angle)]


def const(*tables):
    return [jnp.asarray(t) for t in tables]


def local(
    screen_vec,
    prior_scale,
    flow_weight,
    wind,
    pierce_point_strip,
    pierce_block,
    pierce_weights,
    noise_prec,
):
    strip = lax.axis_index("strip")
    slot = lax.axis_index("tm")
    fwd, inv, first, first_inv, mid, mid_inv, twiddle = row_tables()
    row_fwd_tables = const(twiddle, pieces(fwd, 2), pieces(first, 2), pieces(mid, 2))
    row_fine_tables = const(twiddle, pieces(fwd, 3), pieces(first, 3), pieces(mid, 3))
    row_inv_tables = const(twiddle, pieces(inv, 2), pieces(first_inv, 2), pieces(mid_inv, 2))
    col_fwd, col_inv = column_tables()
    col_fine_tables = const(pieces(col_fwd, 3), pieces(col_inv, 2))
    col_tables = const(pieces(col_fwd, 2), pieces(col_inv, 2))

    x = screen_vec[0]
    scale = prior_scale[0]
    weights = pierce_weights[0].reshape(POINT_ROWS * INNER, INNER)
    target = pierce_point_strip.reshape(POINT_ROWS, INNER)
    block = pierce_block.reshape(POINT_ROWS, INNER)
    prec = noise_prec.reshape(POINT_ROWS, INNER)

    last = lax.axis_size("tm") - 1
    rate = flow_weight[0] * (slot < last).astype(F32)
    mine = jnp.stack([rate, wind[0, 0].astype(F32), wind[0, 1].astype(F32)])
    up_pairs = [(i, i + 1) for i in range(last)]
    down_pairs = [(i + 1, i) for i in range(last)]
    prior = lax.ppermute(mine, "tm", up_pairs)
    back_row, back_col = prior[1].astype(jnp.int32), prior[2].astype(jnp.int32)
    cu, su, cua, sua = phase_tables(wind[0, 0], wind[0, 1], strip, 1.0)
    cd, sd, cda, sda = phase_tables(back_row, back_col, strip, -1.0)
    phases = jnp.stack([cu, su, cd, sd])
    edge_phases = jnp.stack(edge_tables(wind[0, 0], 1.0) + edge_tables(back_row, -1.0))
    norm = scale / (SIDE * SIDE)
    parity_up = jnp.where(wind[0, 1] % 2 == 0, 1.0, -1.0)
    parity_down = jnp.where(back_col % 2 == 0, 1.0, -1.0)
    head = jnp.stack(
        [
            norm,
            rate * scale,
            prior[0] * scale,
            (rate + prior[0]) * scale * norm,
            parity_up,
            parity_down,
            (strip == 0).astype(F32),
            jnp.zeros((), F32),
        ]
    )
    scal = jnp.concatenate([head, cua, sua, cda, sda])
    amp = amplitude_table(strip)

    slots, ids, counts = call(
        route_kernel,
        "route",
        [shape((POINT_ROWS, INNER), jnp.int32)] * 2 + [shape((PEERS, INNER), jnp.int32)],
        [target, block],
    )
    sent, sent_ids = call(
        pack_kernel,
        "pack",
        [shape((PEERS * SLOTS, INNER), BF16), shape((PEERS * SLOTS,), jnp.int32)],
        [slots.reshape(-1), ids.reshape(-1), counts, weights],
        smem=3,
        smem_outs=(1,),
        scratch=[pltpu.VMEM((POINT_ROWS * INNER, INNER), F32), pltpu.VMEM((PEERS * SLOTS, INNER), F32)],
    )
    pencils = exchange(row_forward(x, row_fine_tables, False))
    here = exchange(sent.reshape(PEERS, SLOTS, INNER)).reshape(PEERS * SLOTS, INNER)
    tagged = exchange(sent_ids.reshape(PEERS, 4, INNER))
    here_counts = lax.shift_right_logical(tagged[:, 0, 0], 12)
    here_ids = (tagged & 4095).reshape(PEERS * SLOTS)

    spectral = [pltpu.VMEM(PENCILS, F32), pltpu.VMEM(PENCILS, F32)]
    screen_pencils, own, up, down = call(
        column_first_kernel,
        "column_first",
        [shape(PENCILS), shape(PENCILS), shape(PENCILS, BF16), shape(PENCILS, BF16)],
        [scal, pencils, amp, phases, edge_phases] + col_fine_tables,
        smem=1,
        scratch=spectral,
    )
    from_prev = lax.ppermute(up, "tm", up_pairs)
    from_next = lax.ppermute(down, "tm", down_pairs)
    tiles = row_backward(exchange(screen_pencils), None, row_inv_tables)

    phase = call(
        gather_kernel,
        "gather",
        [shape((INNER, INNER))],
        [here_ids, here_counts, tiles, here],
        smem=2,
        scratch=[pltpu.VMEM((SLOTS, INNER), F32)],
    )[0]
    returned = exchange(phase.reshape(PEERS, 4, INNER)).reshape(INNER, INNER)
    resid = call(
        residual_kernel,
        "residual",
        [shape((INNER, INNER))],
        [slots, prec, returned],
        scratch=[pltpu.VMEM((POINT_ROWS, INNER), F32)],
    )[0]
    resid_here = exchange(resid.reshape(PEERS, 4, INNER)).reshape(INNER, INNER)
    gradient = call(
        scatter_kernel,
        "scatter",
        [shape((SIDE, INNER))],
        [here_ids, here_counts, resid_here, here],
        smem=2,
        scratch=[pltpu.VMEM((INNER, INNER), F32), pltpu.VMEM((SLOTS, INNER), F32)]
        + [pltpu.VMEM((SIDE, INNER), F32)] * COPIES,
    )[0]
    pencils = exchange(row_forward(gradient, row_fwd_tables, True))
    out_pencils = call(
        column_second_kernel,
        "column_second",
        [shape(PENCILS)],
        [scal, pencils, amp, own, from_prev, from_next] + col_tables,
        smem=1,
        scratch=spectral,
    )[0]
    return row_backward(exchange(out_pencils), x, row_inv_tables)[None]


def solution(mesh):
    in_specs = (
        P("tm", "strip", None),
        P("tm"),
        P("tm"),
        P("tm", None),
        P("tm", "strip", None, None),
        P("tm", "strip", None),
        P("tm", "strip", None, None),
        P("tm", "strip", None),
    )
    out_specs = P("tm", "strip", None)
    return jax.shard_map(local, mesh=mesh, in_specs=in_specs, out_specs=out_specs, check_vma=False)
```

```python
import math

import jax
import jax.numpy as jnp
import ml_dtypes
import numpy as np
from jax import lax
from jax.experimental import pallas as pl
from jax.experimental.pallas import tpu as pltpu
from jax.sharding import PartitionSpec as P

KZERO = 2.0
SIDE = 4096
OUTER = 32
INNER = 128
HALF = 64
PEERS = 32
SLOTS = 512
POINT_ROWS = 64
TAIL = 16
GROUP = SLOTS + TAIL
VMEM_BYTES = 56 * 1024 * 1024
F32 = jnp.float32
BF16 = jnp.bfloat16


def pieces(table, count):
    rest = np.asarray(table, np.float64)
    out = []
    for _ in range(count):
        out.append(rest.astype(np.float32).astype(ml_dtypes.bfloat16))
        rest = rest - out[-1].astype(np.float64)
    return np.stack(out)


def row_tables():
    b = np.arange(INNER)[:, None]
    j = np.arange(HALF)[None, :]
    theta = [2 * np.pi * ((b * j) % INNER) / INNER, 2 * np.pi * ((b * (INNER - 1 - j)) % INNER) / INNER]
    forward = []
    backward = []
    for t in theta:
        forward.append(np.concatenate([np.cos(t), -np.sin(t)], axis=1))
        forward.append(np.concatenate([np.sin(t), np.cos(t)], axis=1))
        backward.append(np.concatenate([np.cos(t).T, np.sin(t).T], axis=1))
        backward.append(np.concatenate([-np.sin(t).T, np.cos(t).T], axis=1))
    fwd = np.concatenate(
        [np.concatenate([forward[0], forward[1]], axis=0), np.concatenate([forward[2], forward[3]], axis=0)], axis=1
    )
    inv = np.concatenate(backward, axis=0)
    sign = np.where(np.arange(INNER) % 2 == 0, 1.0, -1.0)
    t0 = theta[0]
    first = np.concatenate([np.cos(t0), -np.sin(t0)], axis=1)
    first[:, HALF] = sign
    first_inv = np.concatenate([2 * np.cos(t0).T, -2 * np.sin(t0).T], axis=0)
    first_inv[0, :] = 1.0
    first_inv[HALF, :] = sign
    t16 = 2 * np.pi * ((b * (16 + 32 * j)) % SIDE) / SIDE
    mid = np.concatenate([np.cos(t16), -np.sin(t16)], axis=1)
    mid_inv = np.concatenate([2 * np.cos(t16).T, -2 * np.sin(t16).T], axis=0)
    k1 = np.arange(16)[:, None]
    tw = 2 * np.pi * (k1 * np.arange(INNER)[None, :]) / SIDE
    twiddle = np.stack([np.cos(tw), np.sin(tw)]).astype(np.float32)
    return fwd, inv, first, first_inv, mid, mid_inv, twiddle


def column_tables():
    k1 = np.arange(OUTER)[:, None, None]
    k2 = np.arange(INNER)[None, :, None]
    r = np.arange(INNER)[None, None, :]
    theta = 2 * np.pi * (((k1 + OUTER * k2) * r) % SIDE) / SIDE
    fwd = np.concatenate([np.cos(theta), -np.sin(theta)], axis=1)
    theta = theta.transpose(0, 2, 1)
    inv = np.concatenate([np.cos(theta), np.sin(theta)], axis=1)
    return fwd, inv


def split(value):
    high = value.astype(BF16)
    return high, (value - high.astype(F32)).astype(BF16)


def mm(left, right):
    return lax.dot_general(left, right, (((1,), (0,)), ((), ())), preferred_element_type=F32)


def mm_nt(left, right):
    return lax.dot_general(left, right, (((1,), (1,)), ((), ())), preferred_element_type=F32)


def split_into(value, count):
    parts = []
    for i in range(count):
        parts.append(value.astype(BF16))
        if i + 1 < count:
            value = value - parts[-1].astype(F32)
    return parts


def data_by_table(value, tables):
    count = len(tables)
    parts = split_into(value, count)
    total = None
    for order in reversed(range(count)):
        for i in range(order + 1):
            term = mm(parts[i], tables[order - i])
            total = term if total is None else total + term
    return total


def table_by_data(tables, value):
    parts = split_into(value, len(tables))
    left = jnp.concatenate(tables[0:2], axis=1)
    right = jnp.concatenate(parts[0:2], axis=1)
    r = mm(left, jnp.concatenate([right, right], axis=0))
    total = r[:, INNER : 2 * INNER] + r[:, 0:INNER]
    if len(tables) == 3:
        left = jnp.concatenate([tables[0], tables[2]], axis=1)
        total = total + mm(left, jnp.concatenate([parts[2], parts[0]], axis=0))
    return total


def every(ref):
    return [ref[i] for i in range(ref.shape[0])]


def c_mul(value, factor):
    re, im = value
    c, s = factor.real, factor.imag
    if im is None:
        return (re * c, re * s)
    return (re * c - im * s, re * s + im * c)


def real_forward(xs):
    n = len(xs)
    if n == 2:
        return [(xs[0] + xs[1], None), (xs[0] - xs[1], None)]
    even, odd = real_forward(xs[0::2]), real_forward(xs[1::2])
    m = n // 2
    out = [None] * (m + 1)
    for k in range(m // 2 + 1):
        if k == 0:
            out[0] = (even[0][0] + odd[0][0], None)
            out[m] = (even[0][0] - odd[0][0], None)
        elif 2 * k == m:
            out[k] = (even[k][0], -odd[k][0])
        else:
            tr, ti = c_mul(odd[k], complex(math.cos(2 * math.pi * k / n), -math.sin(2 * math.pi * k / n)))
            er, ei = even[k]
            out[k] = (er + tr, ei + ti)
            out[m - k] = (er - tr, ti - ei)
    return out


def real_backward(spec):
    n = 2 * (len(spec) - 1)
    if n == 2:
        return [spec[0][0] + spec[1][0], spec[0][0] - spec[1][0]]
    m = n // 2
    even, odd = [], []
    for k in range(m // 2 + 1):
        if k == 0:
            even.append((spec[0][0] + spec[m][0], None))
            odd.append((spec[0][0] - spec[m][0], None))
        elif 2 * k == m:
            even.append((2.0 * spec[k][0], None))
            odd.append((-2.0 * spec[k][1], None))
        else:
            ar, ai = spec[k]
            br, bi = spec[m - k]
            even.append((ar + br, ai - bi))
            odd.append(c_mul((ar - br, ai + bi), complex(math.cos(2 * math.pi * k / n), math.sin(2 * math.pi * k / n))))
    xe, xo = real_backward(even), real_backward(odd)
    out = [None] * n
    out[0::2] = xe
    out[1::2] = xo
    return out


def packed_fft(xs, sign, flip):
    n = len(xs)
    if n == 1:
        return xs
    even, odd = packed_fft(xs[0::2], sign, flip), packed_fft(xs[1::2], sign, flip)
    out = [None] * n
    for k in range(n // 2):
        t = odd[k]
        if k:
            turned = pltpu.roll(t, HALF, 1) * flip
            c, s = math.cos(2 * math.pi * k / n), sign * math.sin(2 * math.pi * k / n)
            t = (-s) * turned if 4 * k == n else c * t - s * turned
        out[k] = even[k] + t
        out[k + n // 2] = even[k] - t
    return out


def flip_lanes(rows):
    lane = lax.broadcasted_iota(jnp.int32, (rows, INNER), 1)
    return jnp.where(lane < HALF, 1.0, -1.0).astype(F32)


def put_message(ref, d, value, fine):
    lane = lax.broadcasted_iota(jnp.int32, (INNER, INNER), 1)
    high = value.astype(BF16)
    ref[d, 0:INNER, :] = high
    rest = value - high.astype(F32)
    if fine:
        third = rest - rest.astype(BF16).astype(F32)
        rest = jnp.where((lane & (HALF - 1)) == 7, pltpu.roll(third, 7, 1), rest)
    rest = jnp.where(lane < 8, rest, pltpu.roll(rest, 72, 1))
    rest = jnp.where(lane < 16, rest, 0.0)
    total = rest[0:16]
    for g in range(1, 8):
        total = total + pltpu.roll(rest[16 * g : 16 * g + 16], 16 * g, 1)
    ref[d, INNER : INNER + TAIL, :] = total.astype(BF16)


def get_message(ref, d, fine):
    lane = lax.broadcasted_iota(jnp.int32, (INNER, INNER), 1)
    packed = ref[d, INNER : INNER + TAIL, :].astype(F32)
    rest = jnp.concatenate([packed] + [pltpu.roll(packed, INNER - 16 * g, 1) for g in range(1, 8)], axis=0)
    rest = jnp.where(lane < 8, rest, pltpu.roll(rest, 56, 1))
    column = lane & (HALF - 1)
    if fine:
        third = jnp.where(column == 0, pltpu.roll(rest, INNER - 7, 1), 0.0)
        rest = jnp.where(column < 7, rest, 0.0) + third
    else:
        rest = jnp.where(column < 8, rest, 0.0)
    return ref[d, 0:INNER, :].astype(F32) + rest


def row_forward_kernel(tiled, fine, x_ref, tw_ref, f_ref, a_ref, m_ref, out_ref, y_scr, e_scr):
    def slab(g, carry):
        if tiled:
            xs = [x_ref[pl.ds(pl.multiple_of(g * 256 + a * 8, 8), 8), :] for a in range(OUTER)]
        else:
            xs = [x_ref[pl.ds(pl.multiple_of(g * 8, 8), 8), a * INNER : (a + 1) * INNER] for a in range(OUTER)]
        ys = real_forward(xs)
        rows = pl.ds(pl.multiple_of(g * 8, 8), 8)
        e_scr[0, rows, :] = ys[0][0]
        e_scr[1, rows, :] = ys[16][0]
        for k in range(1, 16):
            c = tw_ref[0, k : k + 1, :]
            s = tw_ref[1, k : k + 1, :]
            re, im = ys[k]
            base = pl.ds(pl.multiple_of((k - 1) * INNER + g * 8, 8), 8)
            y_scr[base, 0:INNER] = re * c + im * s
            y_scr[base, INNER : 2 * INNER] = im * c - re * s
        return carry

    lax.fori_loop(0, 16, slab, 0, unroll=2)
    put_message(out_ref, 0, data_by_table(e_scr[0], every(a_ref)), fine)
    put_message(out_ref, 1, data_by_table(e_scr[1], every(m_ref)), fine)

    def group(q, carry):
        v = data_by_table(y_scr[pl.ds(pl.multiple_of(q * 384, 8), 384), :], every(f_ref))
        for i in range(3):
            rows = v[i * INNER : (i + 1) * INNER]
            put_message(out_ref, 2 + 2 * (3 * q + i), rows[:, 0:INNER], fine)
            put_message(out_ref, 3 + 2 * (3 * q + i), rows[:, INNER : 2 * INNER], fine)
        return carry

    lax.fori_loop(0, 5, group, 0)


def row_backward_kernel(final, *refs):
    if final:
        in_ref, base_ref, tw_ref, f_ref, a_ref, m_ref, out_ref, z_scr, e_scr = refs
    else:
        in_ref, tw_ref, f_ref, a_ref, m_ref, out_ref, z_scr, e_scr = refs
    e_scr[0] = data_by_table(get_message(in_ref, 0, False), every(a_ref))
    e_scr[1] = data_by_table(get_message(in_ref, 1, False), every(m_ref))

    def group(q, carry):
        parts = []
        for i in range(3):
            k = 3 * q + i
            parts.append(jnp.concatenate([get_message(in_ref, 2 + 2 * k + h, False) for h in range(2)], axis=1))
        v = jnp.concatenate(parts, axis=0)
        z_scr[pl.ds(pl.multiple_of(q * 384, 8), 384), :] = data_by_table(v, every(f_ref))
        return carry

    lax.fori_loop(0, 5, group, 0)

    def slab(g, carry):
        rows = pl.ds(pl.multiple_of(g * 8, 8), 8)
        spec = [(e_scr[0, rows, :], None)]
        for k in range(1, 16):
            c = tw_ref[0, k : k + 1, :]
            s = tw_ref[1, k : k + 1, :]
            base = pl.ds(pl.multiple_of((k - 1) * INNER + g * 8, 8), 8)
            re = z_scr[base, 0:INNER]
            im = z_scr[base, INNER : 2 * INNER]
            spec.append((re * c - im * s, im * c + re * s))
        spec.append((e_scr[1, rows, :], None))
        xs = real_backward(spec)
        for a in range(OUTER):
            if final:
                cols = slice(a * INNER, (a + 1) * INNER)
                out_ref[rows, cols] = base_ref[rows, cols] + xs[a]
            else:
                out_ref[pl.ds(pl.multiple_of(g * 256 + a * 8, 8), 8), :] = xs[a]
        return carry

    lax.fori_loop(0, 16, slab, 0, unroll=2)


def take_all(in_ref, scr, fine):
    def step(s, carry):
        scr[s] = get_message(in_ref, s, fine)
        return carry

    lax.fori_loop(0, OUTER, step, 0, unroll=4)


def give_all(scr, out_ref):
    def step(s, carry):
        put_message(out_ref, s, scr[s], False)
        return carry

    lax.fori_loop(0, OUTER, step, 0, unroll=4)


def column_first_step(in_ref, y_scr, sign):
    flip = flip_lanes(8)

    def slab(g, carry):
        rows = pl.ds(pl.multiple_of(g * 8, 8), 8)
        ys = packed_fft([in_ref[s, rows, :] for s in range(OUTER)], sign, flip)
        for k in range(OUTER):
            y_scr[k, rows, :] = ys[k]
        return carry

    lax.fori_loop(0, 16, slab, 0, unroll=2)


def apply_packed(e_ref, k1, value, flip):
    r = table_by_data([e_ref[i, k1] for i in range(e_ref.shape[0])], value)
    return r[0:INNER] - pltpu.roll(r[INNER : 2 * INNER], HALF, 1) * flip


def edge_lanes():
    lane = lax.broadcasted_iota(jnp.int32, (INNER, INNER), 1)
    return jnp.logical_or(lane == 0, lane == HALF), lane < HALF


def edge_gather(ref):
    mask, _ = edge_lanes()

    def step(k1, acc):
        return acc + pltpu.roll(jnp.where(mask, ref[k1], 0.0), k1, 1)

    return lax.fori_loop(0, OUTER, step, jnp.zeros((INNER, INNER), F32), unroll=4)


def edge_split(spec, amp):
    i = lax.broadcasted_iota(jnp.int32, (INNER, INNER), 0)
    j = lax.broadcasted_iota(jnp.int32, (INNER, INNER), 1)
    one = jnp.ones((INNER, INNER), F32)
    none = jnp.zeros((INNER, INNER), F32)
    rows = jnp.where(i + j == INNER - 1, one, none).astype(BF16)
    rows0 = jnp.where(((i + j) & (INNER - 1)) == 0, one, none).astype(BF16)
    sign = jnp.where(j < HALF, one, -one)
    col = j & (HALF - 1)
    same = (i < HALF) == (j < HALF)
    lanes = jnp.where(
        jnp.logical_and(same, jnp.logical_and(col > 0, col + (i & (HALF - 1)) == OUTER)), sign, none
    ).astype(BF16)
    lanes0 = jnp.where(jnp.logical_and(i == j, col == 0), sign, none).astype(BF16)

    def move(left, value, right):
        value = sum(mm(left, p) for p in reversed(split_into(value, 3)))
        return sum(mm(p, right) for p in reversed(split_into(value, 3)))

    rev = move(rows, spec, lanes) + move(rows0, spec, lanes0)
    swapped = pltpu.roll(amp, HALF, 1)
    _, left = edge_lanes()
    a0 = jnp.where(left, amp, swapped)
    a2 = jnp.where(left, swapped, amp)
    return 0.5 * (spec + rev), 0.5 * (spec - rev), a0, a2


def turn(c, s, value, flip):
    return c * value + s * (pltpu.roll(value, HALF, 1) * flip)


def column_first_kernel(
    scal, in_ref, amp_ref, ph_ref, edge_ref, ef, ei, out_ref, own_ref, up_ref, down_ref, y_scr, z_scr
):
    take_all(in_ref, z_scr, True)
    column_first_step(z_scr, y_scr, -1.0)
    flip = flip_lanes(INNER)

    def step(k1, carry):
        value = apply_packed(ef, k1, y_scr[k1], flip)
        amp = amp_ref[k1]
        once = value * amp
        twice = once * amp
        y_scr[k1] = value
        z_scr[k1] = scal[0] * once
        own_ref[k1] = scal[3] * twice
        for n, ref, gain in ((0, up_ref, scal[1]), (1, down_ref, scal[2])):
            cb = ph_ref[2 * n]
            sb = ph_ref[2 * n + 1]
            ca = scal[8 + 64 * n + k1] * gain
            sa = scal[8 + 64 * n + 32 + k1] * gain
            ref[k1] = turn(cb * ca - sb * sa, sb * ca + cb * sa, twice, flip).astype(BF16)
        return carry

    lax.fori_loop(0, OUTER, step, 0, unroll=8)

    @pl.when(scal[6] > 0.5)
    def _():
        u0, u2, a0, a2 = edge_split(edge_gather(y_scr), edge_gather(amp_ref))
        mask, _ = edge_lanes()
        e0 = a0 * u0
        e2 = a2 * u2
        fixed = [scal[0] * (e0 + e2)]
        e0 = a0 * e0
        e2 = a2 * e2
        fixed.append(scal[3] * (e0 + e2))
        fixed.append(scal[1] * turn(edge_ref[0], edge_ref[1], e0 + scal[4] * e2, flip))
        fixed.append(scal[2] * turn(edge_ref[2], edge_ref[3], e0 + scal[5] * e2, flip))

        def put(k1, carry):
            back = lax.rem(INNER - k1, INNER)
            for ref, value in zip((z_scr, own_ref, up_ref, down_ref), fixed):
                value = jnp.where(mask, pltpu.roll(value, back, 1), ref[k1].astype(F32))
                ref[k1] = value.astype(ref.dtype)
            return carry

        lax.fori_loop(0, OUTER, put, 0, unroll=4)

    def inverse(k1, carry):
        z_scr[k1] = apply_packed(ei, k1, z_scr[k1], flip)
        return carry

    lax.fori_loop(0, OUTER, inverse, 0, unroll=8)
    column_first_step(z_scr, y_scr, 1.0)
    give_all(y_scr, out_ref)


def column_second_kernel(scal, in_ref, amp_ref, own_ref, prev_ref, next_ref, ef, ei, out_ref, y_scr, z_scr):
    take_all(in_ref, z_scr, False)
    column_first_step(z_scr, y_scr, -1.0)
    flip = flip_lanes(INNER)

    def step(k1, carry):
        value = apply_packed(ef, k1, y_scr[k1], flip)
        moved = prev_ref[k1].astype(F32) + next_ref[k1].astype(F32)
        y_scr[k1] = value
        z_scr[k1] = scal[0] * (value * amp_ref[k1] - moved) + own_ref[k1]
        return carry

    lax.fori_loop(0, OUTER, step, 0, unroll=8)

    @pl.when(scal[6] > 0.5)
    def _():
        spec = edge_gather(y_scr)
        amp = edge_gather(amp_ref)
        u0, u2, a0, a2 = edge_split(spec, amp)
        mask, _ = edge_lanes()
        change = scal[0] * (a0 * u0 + a2 * u2 - amp * spec)

        def put(k1, carry):
            back = lax.rem(INNER - k1, INNER)
            z_scr[k1] = z_scr[k1] + jnp.where(mask, pltpu.roll(change, back, 1), 0.0)
            return carry

        lax.fori_loop(0, OUTER, put, 0, unroll=4)

    def inverse(k1, carry):
        z_scr[k1] = apply_packed(ei, k1, z_scr[k1], flip)
        return carry

    lax.fori_loop(0, OUTER, inverse, 0, unroll=8)
    column_first_step(z_scr, y_scr, 1.0)
    give_all(y_scr, out_ref)


def route_kernel(t_ref, id_ref, slot_ref, tail_ref, tail_scr):
    row = lax.broadcasted_iota(jnp.int32, (INNER, 2 * INNER), 0)
    col = lax.broadcasted_iota(jnp.int32, (INNER, 2 * INNER), 1)
    tri = jnp.where(jnp.logical_or(row < col, col >= INNER), 1.0, 0.0).astype(BF16)
    peer = lax.broadcasted_iota(jnp.int32, (PEERS, INNER), 0)
    base = jnp.zeros((PEERS, INNER), F32)
    for i in range(0, POINT_ROWS, 8):
        hots = [jnp.where(peer == t_ref[i + j : i + j + 1, :], 1.0, 0.0) for j in range(8)]
        cum = mm(jnp.concatenate(hots, axis=0).astype(BF16), tri)
        for j in range(8):
            part = cum[j * PEERS : (j + 1) * PEERS]
            pos = jnp.sum(hots[j] * (part[:, 0:INNER] + base), axis=0, keepdims=True)
            base = base + part[:, INNER : 2 * INNER]
            slot_ref[i + j : i + j + 1, :] = t_ref[i + j : i + j + 1, :] * SLOTS + pos.astype(jnp.int32)
    batch = 4
    index = lax.broadcasted_iota(jnp.int32, (INNER, batch * INNER), 0)

    def wide(ref, i):
        return jnp.concatenate([ref[pl.ds(i * batch + j, 1), :] for j in range(batch)], axis=1)

    def put(i, acc):
        slot = wide(slot_ref, i)
        ids = wide(id_ref, i)
        r = lax.shift_right_logical(ids, 5)
        ids = lax.shift_right_logical(r, 3) * 256 + (ids & 31) * 8 + (r & 7)
        hot = jnp.where(index == (slot & 127), 1.0, 0.0).astype(BF16)
        line = index == lax.shift_right_logical(slot, 7)
        v = [
            jnp.where(line, d.astype(F32), 0.0).astype(BF16) for d in (lax.shift_right_logical(ids, 6), ids & 63)
        ]
        return acc + mm_nt(jnp.concatenate(v, axis=0), hot)

    acc = lax.fori_loop(0, POINT_ROWS // batch, put, jnp.zeros((2 * INNER, INNER), F32), unroll=2)
    count = base.astype(jnp.int32)
    count_high = lax.shift_right_logical(count, 6).astype(F32)
    count_low = (count & 63).astype(F32)
    tail_scr[...] = jnp.zeros_like(tail_scr)
    for s in range(PEERS):
        tail_scr[s * TAIL : s * TAIL + 4, :] = acc[4 * s : 4 * s + 4]
        tail_scr[s * TAIL + 4 : s * TAIL + 8, :] = acc[INNER + 4 * s : INNER + 4 * s + 4]
        tail_scr[s * TAIL + 8 : s * TAIL + 9, :] = count_high[s : s + 1]
        tail_scr[s * TAIL + 9 : s * TAIL + 10, :] = count_low[s : s + 1]
    tail_ref[...] = tail_scr[...].astype(BF16)


def pack_kernel(slot_ref, w_ref, tail_ref, out_ref, w_scr, buf):
    def clear(i, carry):
        rows = pl.ds(pl.multiple_of(i * 64, 64), 64)
        buf[rows, :] = jnp.zeros((64, INNER), F32)
        buf[pl.ds(pl.multiple_of(i * 64 + PEERS * SLOTS // 2, 64), 64), :] = jnp.zeros((64, INNER), F32)
        w_scr[rows, :] = w_ref[rows, :].astype(F32)
        return carry

    lax.fori_loop(0, PEERS * SLOTS // INNER, clear, 0)

    def some(q, carry):
        first = q * 16
        slots = [slot_ref[first + j] for j in range(16)]
        rows = [w_scr[pl.ds(first + j, 1), :] for j in range(16)]
        for j in range(16):
            buf[pl.ds(slots[j], 1), :] = rows[j]
        return carry

    lax.fori_loop(0, POINT_ROWS * INNER // 16, some, 0)

    def narrow(d, carry):
        for i in range(4):
            rows = pl.ds(pl.multiple_of(d * SLOTS + i * INNER, INNER), INNER)
            out_ref[pl.ds(pl.multiple_of(d * GROUP + i * INNER, TAIL), INNER), :] = buf[rows, :].astype(BF16)
        tail = tail_ref[pl.ds(pl.multiple_of(d * TAIL, TAIL), TAIL), :]
        out_ref[pl.ds(pl.multiple_of(d * GROUP + SLOTS, TAIL), TAIL), :] = tail
        return carry

    lax.fori_loop(0, PEERS, narrow, 0)


def gather_kernel(sid_ref, cnt_ref, tiles_ref, w_ref, out_ref, g_scr):
    def source(s, carry):
        def some(q, inner):
            first = s * SLOTS + q * 16
            ids = [sid_ref[first + j] for j in range(16)]
            rows = [tiles_ref[pl.ds(ids[j], 1), :] for j in range(16)]
            for j in range(16):
                g_scr[pl.ds(first + j, 1), :] = rows[j]
            return inner

        return lax.fori_loop(0, lax.shift_right_logical(cnt_ref[s] + 15, 4), some, carry)

    lax.fori_loop(0, PEERS, source, 0)
    ones = jnp.ones((2 * INNER, INNER), BF16)
    lane = lax.broadcasted_iota(jnp.int32, (INNER, INNER), 1)
    diagonal = lane == lax.broadcasted_iota(jnp.int32, (INNER, INNER), 0)
    place = lax.broadcasted_iota(jnp.int32, (1, INNER), 1)

    def total(s, carry):
        w = w_ref[pl.ds(pl.multiple_of(s * GROUP, TAIL), SLOTS), :].astype(F32)
        g = g_scr[pl.ds(pl.multiple_of(s * SLOTS, SLOTS), SLOTS), :]
        sums = mm(jnp.concatenate(split(g * w), axis=1), ones)
        for q in range(4):
            got = jnp.where(diagonal, sums[q * INNER : (q + 1) * INNER], 0.0)
            got = jnp.sum(got, axis=0, keepdims=True)
            out_ref[s, q : q + 1, :] = jnp.where(place + q * INNER < cnt_ref[s], got, 0.0)
        return carry

    lax.fori_loop(0, PEERS, total, 0, unroll=2)


def residual_kernel(slot_ref, prec_ref, phase_ref, out_ref, p_scr):
    high, low = split(phase_ref[...])
    table = jnp.concatenate([high, low], axis=0)
    batch = 4
    index = lax.broadcasted_iota(jnp.int32, (INNER, batch * INNER), 0)

    def wide(ref, i):
        return jnp.concatenate([ref[pl.ds(i * batch + j, 1), :] for j in range(batch)], axis=1)

    def pick(i, carry):
        slot = wide(slot_ref, i)
        hot = jnp.where(index == (slot & 127), 1.0, 0.0).astype(BF16)
        v = mm(table, hot)
        v = v[0:INNER] + v[INNER : 2 * INNER]
        got = jnp.sum(jnp.where(index == lax.shift_right_logical(slot, 7), v, 0.0), axis=0, keepdims=True)
        for j in range(batch):
            p_scr[pl.ds(i * batch + j, 1), :] = got[:, j * INNER : (j + 1) * INNER]
        return carry

    lax.fori_loop(0, POINT_ROWS // batch, pick, 0, unroll=2)
    row = lax.broadcasted_iota(jnp.int32, (INNER, INNER), 0)
    lane = lax.broadcasted_iota(jnp.int32, (INNER, INNER), 1)
    same = jnp.where((row < HALF) == (lane < HALF), 1.0, 0.0).astype(BF16)
    prec = prec_ref[...]
    phase = p_scr[...]

    def total(value):
        return sum(mm(p, same) for p in reversed(split_into(value, 3)))

    p_scr[...] = prec * (phase - total(prec * phase) / total(prec))

    def put(i, acc):
        slot = wide(slot_ref, i)
        hot = jnp.where(index == (slot & 127), 1.0, 0.0).astype(BF16)
        v = jnp.where(index == lax.shift_right_logical(slot, 7), wide(p_scr, i), 0.0)
        vh, vl = split(v)
        return acc + mm_nt(jnp.concatenate([vh, vl], axis=0), hot)

    acc = lax.fori_loop(0, POINT_ROWS // batch, put, jnp.zeros((2 * INNER, INNER), F32), unroll=2)
    out_ref[...] = acc[0:INNER] + acc[INNER : 2 * INNER]


COPIES = 8


def scatter_kernel(sid_ref, cnt_ref, r_ref, w_ref, out_ref, rt_scr, u_scr, *accs):
    def clear(i, carry):
        rows = pl.ds(pl.multiple_of(i * 64, 64), 64)
        for acc in accs:
            acc[rows, :] = jnp.zeros((64, INNER), F32)
        return carry

    lax.fori_loop(0, SIDE // 64, clear, 0)
    rt_scr[...] = r_ref[...].T
    lane = lax.broadcasted_iota(jnp.int32, (INNER, INNER), 1)

    def scaled(s, carry):
        for q in range(4):
            col = jnp.sum(jnp.where(lane == s * 4 + q, rt_scr[...], 0.0), axis=1, keepdims=True)
            base = pl.multiple_of(s * GROUP + q * INNER, TAIL)
            rows = pl.ds(pl.multiple_of(s * SLOTS + q * INNER, INNER), INNER)
            u_scr[rows, :] = w_ref[pl.ds(base, INNER), :].astype(F32) * col
        return carry

    lax.fori_loop(0, PEERS, scaled, 0, unroll=2)

    def source(s, carry):
        def some(q, inner):
            first = s * SLOTS + q * 16
            ids = [sid_ref[first + j] for j in range(16)]
            us = [u_scr[pl.ds(first + j, 1), :] for j in range(16)]
            for h in range(0, 16, COPIES):
                sums = [accs[j][pl.ds(ids[h + j], 1), :] + us[h + j] for j in range(COPIES)]
                for j in range(COPIES):
                    accs[j][pl.ds(ids[h + j], 1), :] = sums[j]
            return inner

        return lax.fori_loop(0, lax.shift_right_logical(cnt_ref[s] + 15, 4), some, carry)

    lax.fori_loop(0, PEERS, source, 0)

    def add(i, carry):
        rows = pl.ds(pl.multiple_of(i * 64, 64), 64)
        total = accs[0][rows, :]
        for acc in accs[1:]:
            total = total + acc[rows, :]
        out_ref[rows, :] = total
        return carry

    lax.fori_loop(0, SIDE // 64, add, 0)


def call(kernel, name, out_shapes, args, smem=0, smem_outs=(), scratch=()):
    vmem = pl.BlockSpec(memory_space=pltpu.VMEM)
    small = pl.BlockSpec(memory_space=pltpu.SMEM)
    outs = [small if i in smem_outs else vmem for i in range(len(out_shapes))]
    result = pl.pallas_call(
        kernel,
        out_shape=out_shapes,
        in_specs=[small] * smem + [vmem] * (len(args) - smem),
        out_specs=outs,
        scratch_shapes=list(scratch),
        compiler_params=pltpu.CompilerParams(vmem_limit_bytes=VMEM_BYTES),
        cost_estimate=pl.CostEstimate(flops=1024, bytes_accessed=1024, transcendentals=0),
        name=name,
    )(*args)
    return result


def shape(dims, dtype=F32):
    return jax.ShapeDtypeStruct(dims, dtype)


PENCILS = (PEERS, INNER, INNER)
MESSAGES = (PEERS, INNER + TAIL, INNER)


def row_forward(x, tables, tiled):
    args = [x] + tables
    return call(
        lambda *refs: row_forward_kernel(tiled, not tiled, *refs),
        "row_forward",
        [shape(MESSAGES, BF16)],
        args,
        scratch=[pltpu.VMEM((15 * INNER, 2 * INNER), F32), pltpu.VMEM((2, INNER, INNER), F32)],
    )[0]


def row_backward(pencils, base, tables):
    final = base is not None
    args = [pencils] + ([base] if final else []) + tables
    return call(
        lambda *refs: row_backward_kernel(final, *refs),
        "row_backward",
        [shape((INNER, SIDE) if final else (SIDE, INNER))],
        args,
        scratch=[pltpu.VMEM((15 * INNER, 2 * INNER), F32), pltpu.VMEM((2, INNER, INNER), F32)],
    )[0]


def swap_kernel(in_ref, out_ref, send_sem, recv_sem, own_sem):
    me = lax.axis_index("strip")
    barrier = pltpu.get_barrier_semaphore()

    def greet(i, carry):
        peer = lax.rem(me + i, PEERS)
        pl.semaphore_signal(barrier, inc=1, device_id={"strip": peer}, device_id_type=pl.DeviceIdType.MESH)
        return carry

    lax.fori_loop(1, PEERS, greet, 0)
    pl.semaphore_wait(barrier, PEERS - 1)

    def remote(i, row):
        peer = lax.rem(me + i, PEERS)
        return pltpu.make_async_remote_copy(
            src_ref=in_ref.at[peer],
            dst_ref=out_ref.at[row],
            send_sem=send_sem.at[i],
            recv_sem=recv_sem.at[i],
            device_id={"strip": peer},
            device_id_type=pl.DeviceIdType.MESH,
        )

    def start(i, carry):
        remote(i, me).start()
        return carry

    lax.fori_loop(1, PEERS, start, 0)
    own = pltpu.make_async_copy(in_ref.at[me], out_ref.at[me], own_sem)
    own.start()
    own.wait()

    def finish(i, carry):
        copy = remote(i, lax.rem(me + PEERS - i, PEERS))
        copy.wait_send()
        copy.wait_recv()
        return carry

    lax.fori_loop(1, PEERS, finish, 0)


def swap(value, collective_id):
    anywhere = pl.BlockSpec(memory_space=pl.ANY)
    return pl.pallas_call(
        swap_kernel,
        out_shape=shape(value.shape, value.dtype),
        in_specs=[anywhere],
        out_specs=anywhere,
        scratch_shapes=[
            pltpu.SemaphoreType.DMA((PEERS,)),
            pltpu.SemaphoreType.DMA((PEERS,)),
            pltpu.SemaphoreType.DMA,
        ],
        compiler_params=pltpu.CompilerParams(collective_id=collective_id, has_side_effects=True),
        name="swap",
    )(value)


def exchange(value):
    return lax.all_to_all(value, "strip", split_axis=0, concat_axis=0, tiled=True)


def amplitude_table(strip):
    j = jnp.arange(HALF, dtype=jnp.int32)
    k1 = strip // 2
    fold = jnp.where(strip % 2 == 0, k1 + OUTER * j, OUTER - k1 + OUTER * j)
    fold = jnp.where(strip == 1, 16 + OUTER * j, fold)
    edge = jnp.where((strip == 0) & (j == 0), SIDE // 2, fold)
    cols = jnp.concatenate([fold, edge]).astype(F32)[None, None, :]
    kr = jnp.arange(OUTER, dtype=jnp.int32)[:, None] + OUTER * jnp.arange(INNER, dtype=jnp.int32)[None, :]
    rows = jnp.minimum(kr, SIDE - kr).astype(F32)[:, :, None]
    radius = (rows * rows + cols * cols) / (KZERO * KZERO)
    return SIDE / (2.0 * KZERO) * jnp.power(1.0 + radius, -11.0 / 12.0)


def signed_columns(strip):
    j = jnp.arange(HALF, dtype=jnp.int32)
    k1 = strip // 2
    cols = jnp.where(strip % 2 == 0, k1 + OUTER * j, k1 + OUTER * (INNER - 1 - j))
    cols = jnp.where(strip == 1, 16 + OUTER * j, cols)
    return jnp.concatenate([cols, cols])


def phase_tables(wind_row, wind_col, strip, sign):
    unit = 2.0 * math.pi / SIDE
    k2 = jnp.arange(INNER, dtype=jnp.int32)[:, None]
    turn = (OUTER * k2 * wind_row + signed_columns(strip)[None, :] * wind_col) % SIDE
    angle = turn.astype(F32) * unit
    small = ((jnp.arange(OUTER, dtype=jnp.int32) * wind_row) % SIDE).astype(F32) * unit
    return jnp.cos(angle), sign * jnp.sin(angle), jnp.cos(small), sign * jnp.sin(small)


def edge_tables(wind_row, sign):
    k1 = jnp.arange(INNER, dtype=jnp.int32)[None, :] % HALF
    kr = k1 + OUTER * jnp.arange(INNER, dtype=jnp.int32)[:, None]
    angle = ((kr * wind_row) % SIDE).astype(F32) * (2.0 * math.pi / SIDE)
    return [jnp.cos(angle), sign * jnp.sin(angle)]


def const(*tables):
    return [jnp.asarray(t) for t in tables]


def local(
    screen_vec,
    prior_scale,
    flow_weight,
    wind,
    pierce_point_strip,
    pierce_block,
    pierce_weights,
    noise_prec,
):
    strip = lax.axis_index("strip")
    slot = lax.axis_index("tm")
    fwd, inv, first, first_inv, mid, mid_inv, twiddle = row_tables()
    row_fwd_tables = const(twiddle, pieces(fwd, 2), pieces(first, 2), pieces(mid, 2))
    row_fine_tables = const(twiddle, pieces(fwd, 3), pieces(first, 3), pieces(mid, 3))
    row_inv_tables = const(twiddle, pieces(inv, 2), pieces(first_inv, 2), pieces(mid_inv, 2))
    col_fwd, col_inv = column_tables()
    col_fine_tables = const(pieces(col_fwd, 3), pieces(col_inv, 2))
    col_tables = const(pieces(col_fwd, 2), pieces(col_inv, 2))

    x = screen_vec[0]
    scale = prior_scale[0]
    weights = pierce_weights[0].reshape(POINT_ROWS * INNER, INNER)
    target = pierce_point_strip.reshape(POINT_ROWS, INNER)
    block = pierce_block.reshape(POINT_ROWS, INNER)
    prec = noise_prec.reshape(POINT_ROWS, INNER)

    last = lax.axis_size("tm") - 1
    rate = flow_weight[0] * (slot < last).astype(F32)
    mine = jnp.stack([rate, wind[0, 0].astype(F32), wind[0, 1].astype(F32)])
    up_pairs = [(i, i + 1) for i in range(last)]
    down_pairs = [(i + 1, i) for i in range(last)]
    prior = lax.ppermute(mine, "tm", up_pairs)
    back_row, back_col = prior[1].astype(jnp.int32), prior[2].astype(jnp.int32)
    cu, su, cua, sua = phase_tables(wind[0, 0], wind[0, 1], strip, 1.0)
    cd, sd, cda, sda = phase_tables(back_row, back_col, strip, -1.0)
    phases = jnp.stack([cu, su, cd, sd])
    edge_phases = jnp.stack(edge_tables(wind[0, 0], 1.0) + edge_tables(back_row, -1.0))
    norm = scale / (SIDE * SIDE)
    parity_up = jnp.where(wind[0, 1] % 2 == 0, 1.0, -1.0)
    parity_down = jnp.where(back_col % 2 == 0, 1.0, -1.0)
    head = jnp.stack(
        [
            norm,
            rate * scale,
            prior[0] * scale,
            (rate + prior[0]) * scale * norm,
            parity_up,
            parity_down,
            (strip == 0).astype(F32),
            jnp.zeros((), F32),
        ]
    )
    scal = jnp.concatenate([head, cua, sua, cda, sda])
    amp = amplitude_table(strip)

    slots, tail = call(
        route_kernel,
        "route",
        [shape((POINT_ROWS, INNER), jnp.int32), shape((PEERS * TAIL, INNER), BF16)],
        [target, block],
        scratch=[pltpu.VMEM((PEERS * TAIL, INNER), F32)],
    )
    sent = call(
        pack_kernel,
        "pack",
        [shape((PEERS * GROUP, INNER), BF16)],
        [slots.reshape(-1), weights, tail],
        smem=1,
        scratch=[pltpu.VMEM((POINT_ROWS * INNER, INNER), F32), pltpu.VMEM((PEERS * SLOTS, INNER), F32)],
    )[0]
    pencils = exchange(row_forward(x, row_fine_tables, False))
    pencils, sent = lax.optimization_barrier((pencils, sent))
    arrived = exchange(sent.reshape(PEERS, GROUP, INNER))

    spectral = [pltpu.VMEM(PENCILS, F32), pltpu.VMEM(PENCILS, F32)]
    screen_pencils, own, up, down = call(
        column_first_kernel,
        "column_first",
        [shape(MESSAGES, BF16), shape(PENCILS), shape(PENCILS, BF16), shape(PENCILS, BF16)],
        [scal, pencils, amp, phases, edge_phases] + col_fine_tables,
        smem=1,
        scratch=spectral,
    )
    from_prev = lax.ppermute(up, "tm", up_pairs)
    from_next = lax.ppermute(down, "tm", down_pairs)
    screen_pencils, arrived = lax.optimization_barrier((screen_pencils, arrived))
    tiles = row_backward(swap(screen_pencils, 1), None, row_inv_tables)
    here = arrived.reshape(PEERS * GROUP, INNER)
    digits = arrived[:, SLOTS:, :].astype(F32)
    here_ids = (digits[:, 0:4] * 64.0 + digits[:, 4:8]).astype(jnp.int32).reshape(PEERS * SLOTS)
    here_counts = (digits[:, 8, 0] * 64.0 + digits[:, 9, 0]).astype(jnp.int32)

    phase = call(
        gather_kernel,
        "gather",
        [shape((PEERS, 4, INNER))],
        [here_ids, here_counts, tiles, here],
        smem=2,
        scratch=[pltpu.VMEM((PEERS * SLOTS, INNER), F32)],
    )[0]
    returned = swap(phase, 2).reshape(INNER, INNER)
    from_prev, from_next, returned = lax.optimization_barrier((from_prev, from_next, returned))
    resid = call(
        residual_kernel,
        "residual",
        [shape((INNER, INNER))],
        [slots, prec, returned],
        scratch=[pltpu.VMEM((POINT_ROWS, INNER), F32)],
    )[0]
    resid_here = swap(resid.reshape(PEERS, 4, INNER), 2).reshape(INNER, INNER)
    gradient = call(
        scatter_kernel,
        "scatter",
        [shape((SIDE, INNER))],
        [here_ids, here_counts, resid_here, here],
        smem=2,
        scratch=[pltpu.VMEM((INNER, INNER), F32), pltpu.VMEM((PEERS * SLOTS, INNER), F32)]
        + [pltpu.VMEM((SIDE, INNER), F32)] * COPIES,
    )[0]
    pencils = swap(row_forward(gradient, row_fwd_tables, True), 1)
    out_pencils = call(
        column_second_kernel,
        "column_second",
        [shape(MESSAGES, BF16)],
        [scal, pencils, amp, own, from_prev, from_next] + col_tables,
        smem=1,
        scratch=spectral,
    )[0]
    return row_backward(swap(out_pencils, 1), x, row_inv_tables)[None]


def solution(mesh):
    in_specs = (
        P("tm", "strip", None),
        P("tm"),
        P("tm"),
        P("tm", None),
        P("tm", "strip", None, None),
        P("tm", "strip", None),
        P("tm", "strip", None, None),
        P("tm", "strip", None),
    )
    out_specs = P("tm", "strip", None)
    return jax.shard_map(local, mesh=mesh, in_specs=in_specs, out_specs=out_specs, check_vma=False)
```

```python
import math

import jax
import jax.numpy as jnp
import ml_dtypes
import numpy as np
from jax import lax
from jax.experimental import pallas as pl
from jax.experimental.pallas import tpu as pltpu
from jax.sharding import PartitionSpec as P

KZERO = 2.0
SIDE = 4096
OUTER = 32
INNER = 128
HALF = 64
PEERS = 32
SLOTS = 512
POINT_ROWS = 64
TAIL = 16
GROUP = SLOTS + TAIL
VMEM_BYTES = 56 * 1024 * 1024
F32 = jnp.float32
BF16 = jnp.bfloat16


def pieces(table, count):
    rest = np.asarray(table, np.float64)
    out = []
    for _ in range(count):
        out.append(rest.astype(np.float32).astype(ml_dtypes.bfloat16))
        rest = rest - out[-1].astype(np.float64)
    return np.stack(out)


def row_tables():
    b = np.arange(INNER)[:, None]
    j = np.arange(HALF)[None, :]
    theta = [2 * np.pi * ((b * j) % INNER) / INNER, 2 * np.pi * ((b * (INNER - 1 - j)) % INNER) / INNER]
    forward = []
    backward = []
    for t in theta:
        forward.append(np.concatenate([np.cos(t), -np.sin(t)], axis=1))
        forward.append(np.concatenate([np.sin(t), np.cos(t)], axis=1))
        backward.append(np.concatenate([np.cos(t).T, np.sin(t).T], axis=1))
        backward.append(np.concatenate([-np.sin(t).T, np.cos(t).T], axis=1))
    fwd = np.concatenate(
        [np.concatenate([forward[0], forward[1]], axis=0), np.concatenate([forward[2], forward[3]], axis=0)], axis=1
    )
    inv = np.concatenate(backward, axis=0)
    sign = np.where(np.arange(INNER) % 2 == 0, 1.0, -1.0)
    t0 = theta[0]
    first = np.concatenate([np.cos(t0), -np.sin(t0)], axis=1)
    first[:, HALF] = sign
    first_inv = np.concatenate([2 * np.cos(t0).T, -2 * np.sin(t0).T], axis=0)
    first_inv[0, :] = 1.0
    first_inv[HALF, :] = sign
    t16 = 2 * np.pi * ((b * (16 + 32 * j)) % SIDE) / SIDE
    mid = np.concatenate([np.cos(t16), -np.sin(t16)], axis=1)
    mid_inv = np.concatenate([2 * np.cos(t16).T, -2 * np.sin(t16).T], axis=0)
    k1 = np.arange(16)[:, None]
    tw = 2 * np.pi * (k1 * np.arange(INNER)[None, :]) / SIDE
    twiddle = np.stack([np.cos(tw), np.sin(tw)]).astype(np.float32)
    return fwd, inv, first, first_inv, mid, mid_inv, twiddle


def column_tables():
    k1 = np.arange(OUTER)[:, None, None]
    k2 = np.arange(INNER)[None, :, None]
    r = np.arange(INNER)[None, None, :]
    theta = 2 * np.pi * (((k1 + OUTER * k2) * r) % SIDE) / SIDE
    fwd = np.concatenate([np.cos(theta), -np.sin(theta)], axis=1)
    theta = theta.transpose(0, 2, 1)
    inv = np.concatenate([np.cos(theta), np.sin(theta)], axis=1)
    return fwd, inv


def split(value):
    high = value.astype(BF16)
    return high, (value - high.astype(F32)).astype(BF16)


def mm(left, right):
    return lax.dot_general(left, right, (((1,), (0,)), ((), ())), preferred_element_type=F32)


def mm_nt(left, right):
    return lax.dot_general(left, right, (((1,), (1,)), ((), ())), preferred_element_type=F32)


def split_into(value, count):
    parts = []
    for i in range(count):
        parts.append(value.astype(BF16))
        if i + 1 < count:
            value = value - parts[-1].astype(F32)
    return parts


def data_by_table(value, tables):
    count = len(tables)
    parts = split_into(value, count)
    total = None
    for order in reversed(range(count)):
        for i in range(order + 1):
            term = mm(parts[i], tables[order - i])
            total = term if total is None else total + term
    return total


def table_by_data(tables, value):
    parts = split_into(value, len(tables))
    left = jnp.concatenate(tables[0:2], axis=1)
    right = jnp.concatenate(parts[0:2], axis=1)
    r = mm(left, jnp.concatenate([right, right], axis=0))
    total = r[:, INNER : 2 * INNER] + r[:, 0:INNER]
    if len(tables) == 3:
        left = jnp.concatenate([tables[0], tables[2]], axis=1)
        total = total + mm(left, jnp.concatenate([parts[2], parts[0]], axis=0))
    return total


def every(ref):
    return [ref[i] for i in range(ref.shape[0])]


def c_mul(value, factor):
    re, im = value
    c, s = factor.real, factor.imag
    if im is None:
        return (re * c, re * s)
    return (re * c - im * s, re * s + im * c)


def real_forward(xs):
    n = len(xs)
    if n == 2:
        return [(xs[0] + xs[1], None), (xs[0] - xs[1], None)]
    even, odd = real_forward(xs[0::2]), real_forward(xs[1::2])
    m = n // 2
    out = [None] * (m + 1)
    for k in range(m // 2 + 1):
        if k == 0:
            out[0] = (even[0][0] + odd[0][0], None)
            out[m] = (even[0][0] - odd[0][0], None)
        elif 2 * k == m:
            out[k] = (even[k][0], -odd[k][0])
        else:
            tr, ti = c_mul(odd[k], complex(math.cos(2 * math.pi * k / n), -math.sin(2 * math.pi * k / n)))
            er, ei = even[k]
            out[k] = (er + tr, ei + ti)
            out[m - k] = (er - tr, ti - ei)
    return out


def real_backward(spec):
    n = 2 * (len(spec) - 1)
    if n == 2:
        return [spec[0][0] + spec[1][0], spec[0][0] - spec[1][0]]
    m = n // 2
    even, odd = [], []
    for k in range(m // 2 + 1):
        if k == 0:
            even.append((spec[0][0] + spec[m][0], None))
            odd.append((spec[0][0] - spec[m][0], None))
        elif 2 * k == m:
            even.append((2.0 * spec[k][0], None))
            odd.append((-2.0 * spec[k][1], None))
        else:
            ar, ai = spec[k]
            br, bi = spec[m - k]
            even.append((ar + br, ai - bi))
            odd.append(c_mul((ar - br, ai + bi), complex(math.cos(2 * math.pi * k / n), math.sin(2 * math.pi * k / n))))
    xe, xo = real_backward(even), real_backward(odd)
    out = [None] * n
    out[0::2] = xe
    out[1::2] = xo
    return out


def packed_fft(xs, sign, flip):
    n = len(xs)
    if n == 1:
        return xs
    even, odd = packed_fft(xs[0::2], sign, flip), packed_fft(xs[1::2], sign, flip)
    out = [None] * n
    for k in range(n // 2):
        t = odd[k]
        if k:
            turned = pltpu.roll(t, HALF, 1) * flip
            c, s = math.cos(2 * math.pi * k / n), sign * math.sin(2 * math.pi * k / n)
            t = (-s) * turned if 4 * k == n else c * t - s * turned
        out[k] = even[k] + t
        out[k + n // 2] = even[k] - t
    return out


def flip_lanes(rows):
    lane = lax.broadcasted_iota(jnp.int32, (rows, INNER), 1)
    return jnp.where(lane < HALF, 1.0, -1.0).astype(F32)


def put_message(ref, d, value, fine):
    lane = lax.broadcasted_iota(jnp.int32, (INNER, INNER), 1)
    high = value.astype(BF16)
    ref[d, 0:INNER, :] = high
    rest = value - high.astype(F32)
    if fine:
        third = rest - rest.astype(BF16).astype(F32)
        rest = jnp.where((lane & (HALF - 1)) == 7, pltpu.roll(third, 7, 1), rest)
    rest = jnp.where(lane < 8, rest, pltpu.roll(rest, 72, 1))
    rest = jnp.where(lane < 16, rest, 0.0)
    total = rest[0:16]
    for g in range(1, 8):
        total = total + pltpu.roll(rest[16 * g : 16 * g + 16], 16 * g, 1)
    ref[d, INNER : INNER + TAIL, :] = total.astype(BF16)


def get_message(ref, d, fine):
    lane = lax.broadcasted_iota(jnp.int32, (INNER, INNER), 1)
    packed = ref[d, INNER : INNER + TAIL, :].astype(F32)
    rest = jnp.concatenate([packed] + [pltpu.roll(packed, INNER - 16 * g, 1) for g in range(1, 8)], axis=0)
    rest = jnp.where(lane < 8, rest, pltpu.roll(rest, 56, 1))
    column = lane & (HALF - 1)
    if fine:
        third = jnp.where(column == 0, pltpu.roll(rest, INNER - 7, 1), 0.0)
        rest = jnp.where(column < 7, rest, 0.0) + third
    else:
        rest = jnp.where(column < 8, rest, 0.0)
    return ref[d, 0:INNER, :].astype(F32) + rest


def row_forward_kernel(tiled, fine, x_ref, tw_ref, f_ref, a_ref, m_ref, out_ref, y_scr, e_scr):
    def slab(g, carry):
        if tiled:
            xs = [x_ref[pl.ds(pl.multiple_of(g * 256 + a * 8, 8), 8), :] for a in range(OUTER)]
        else:
            xs = [x_ref[pl.ds(pl.multiple_of(g * 8, 8), 8), a * INNER : (a + 1) * INNER] for a in range(OUTER)]
        ys = real_forward(xs)
        rows = pl.ds(pl.multiple_of(g * 8, 8), 8)
        e_scr[0, rows, :] = ys[0][0]
        e_scr[1, rows, :] = ys[16][0]
        for k in range(1, 16):
            c = tw_ref[0, k : k + 1, :]
            s = tw_ref[1, k : k + 1, :]
            re, im = ys[k]
            base = pl.ds(pl.multiple_of((k - 1) * INNER + g * 8, 8), 8)
            y_scr[base, 0:INNER] = re * c + im * s
            y_scr[base, INNER : 2 * INNER] = im * c - re * s
        return carry

    lax.fori_loop(0, 16, slab, 0, unroll=2)
    put_message(out_ref, 0, data_by_table(e_scr[0], every(a_ref)), fine)
    put_message(out_ref, 1, data_by_table(e_scr[1], every(m_ref)), fine)

    def group(q, carry):
        v = data_by_table(y_scr[pl.ds(pl.multiple_of(q * 384, 8), 384), :], every(f_ref))
        for i in range(3):
            rows = v[i * INNER : (i + 1) * INNER]
            put_message(out_ref, 2 + 2 * (3 * q + i), rows[:, 0:INNER], fine)
            put_message(out_ref, 3 + 2 * (3 * q + i), rows[:, INNER : 2 * INNER], fine)
        return carry

    lax.fori_loop(0, 5, group, 0)


def row_backward_kernel(final, *refs):
    if final:
        in_ref, base_ref, tw_ref, f_ref, a_ref, m_ref, out_ref, z_scr, e_scr = refs
    else:
        in_ref, tw_ref, f_ref, a_ref, m_ref, out_ref, z_scr, e_scr = refs
    e_scr[0] = data_by_table(get_message(in_ref, 0, False), every(a_ref))
    e_scr[1] = data_by_table(get_message(in_ref, 1, False), every(m_ref))

    def group(q, carry):
        parts = []
        for i in range(3):
            k = 3 * q + i
            parts.append(jnp.concatenate([get_message(in_ref, 2 + 2 * k + h, False) for h in range(2)], axis=1))
        v = jnp.concatenate(parts, axis=0)
        z_scr[pl.ds(pl.multiple_of(q * 384, 8), 384), :] = data_by_table(v, every(f_ref))
        return carry

    lax.fori_loop(0, 5, group, 0)

    def slab(g, carry):
        rows = pl.ds(pl.multiple_of(g * 8, 8), 8)
        spec = [(e_scr[0, rows, :], None)]
        for k in range(1, 16):
            c = tw_ref[0, k : k + 1, :]
            s = tw_ref[1, k : k + 1, :]
            base = pl.ds(pl.multiple_of((k - 1) * INNER + g * 8, 8), 8)
            re = z_scr[base, 0:INNER]
            im = z_scr[base, INNER : 2 * INNER]
            spec.append((re * c - im * s, im * c + re * s))
        spec.append((e_scr[1, rows, :], None))
        xs = real_backward(spec)
        for a in range(OUTER):
            if final:
                cols = slice(a * INNER, (a + 1) * INNER)
                out_ref[rows, cols] = base_ref[rows, cols] + xs[a]
            else:
                out_ref[pl.ds(pl.multiple_of(g * 256 + a * 8, 8), 8), :] = xs[a]
        return carry

    lax.fori_loop(0, 16, slab, 0, unroll=2)


def take_all(in_ref, scr, fine):
    def step(s, carry):
        scr[s] = get_message(in_ref, s, fine)
        return carry

    lax.fori_loop(0, OUTER, step, 0, unroll=4)


def give_all(scr, out_ref):
    def step(s, carry):
        put_message(out_ref, s, scr[s], False)
        return carry

    lax.fori_loop(0, OUTER, step, 0, unroll=4)


def column_first_step(in_ref, y_scr, sign):
    flip = flip_lanes(8)

    def slab(g, carry):
        rows = pl.ds(pl.multiple_of(g * 8, 8), 8)
        ys = packed_fft([in_ref[s, rows, :] for s in range(OUTER)], sign, flip)
        for k in range(OUTER):
            y_scr[k, rows, :] = ys[k]
        return carry

    lax.fori_loop(0, 16, slab, 0, unroll=2)


def apply_packed(e_ref, k1, value, flip):
    r = table_by_data([e_ref[i, k1] for i in range(e_ref.shape[0])], value)
    return r[0:INNER] - pltpu.roll(r[INNER : 2 * INNER], HALF, 1) * flip


MESH = pl.DeviceIdType.MESH


def greet_peers(me, barrier, extra=()):
    def greet(i, carry):
        pl.semaphore_signal(barrier, inc=1, device_id={"strip": lax.rem(me + i, PEERS)}, device_id_type=MESH)
        return carry

    lax.fori_loop(1, PEERS, greet, 0)
    for device in extra:
        pl.semaphore_signal(barrier, inc=1, device_id=device, device_id_type=MESH)
    pl.semaphore_wait(barrier, PEERS - 1 + len(extra))


class Exchange:
    def __init__(self, me, in_ref, out_ref, send_sem, recv_sem, own_sem):
        self.me, self.in_ref, self.out_ref = me, in_ref, out_ref
        self.send_sem, self.recv_sem = send_sem, recv_sem
        self.own = pltpu.make_async_copy(in_ref.at[me], out_ref.at[me], own_sem)

    def copy(self, peer, send, source):
        return pltpu.make_async_remote_copy(
            src_ref=self.in_ref.at[peer],
            dst_ref=self.out_ref.at[source],
            send_sem=self.send_sem.at[send],
            recv_sem=self.recv_sem.at[source],
            device_id={"strip": peer},
            device_id_type=MESH,
        )

    def peer(self, i):
        return lax.rem(self.me + 1 + lax.rem(i + 2 * self.me, PEERS - 1), PEERS)

    def start(self):
        def step(i, carry):
            self.copy(self.peer(i), i, self.me).start()
            return carry

        lax.fori_loop(0, PEERS - 1, step, 0)
        self.own.start()

    def wait(self):
        def step(i, carry):
            peer = self.peer(i)
            copy = self.copy(peer, i, peer)
            copy.wait_send()
            copy.wait_recv()
            return carry

        self.own.wait()
        lax.fori_loop(0, PEERS - 1, step, 0)


def exchange_sems():
    return [pltpu.SemaphoreType.DMA((PEERS,)), pltpu.SemaphoreType.DMA((PEERS,)), pltpu.SemaphoreType.DMA]


def edge_lanes():
    lane = lax.broadcasted_iota(jnp.int32, (INNER, INNER), 1)
    return jnp.logical_or(lane == 0, lane == HALF), lane < HALF


def edge_gather(ref):
    mask, _ = edge_lanes()

    def step(k1, acc):
        return acc + pltpu.roll(jnp.where(mask, ref[k1], 0.0), k1, 1)

    return lax.fori_loop(0, OUTER, step, jnp.zeros((INNER, INNER), F32), unroll=4)


def edge_split(spec, amp):
    i = lax.broadcasted_iota(jnp.int32, (INNER, INNER), 0)
    j = lax.broadcasted_iota(jnp.int32, (INNER, INNER), 1)
    one = jnp.ones((INNER, INNER), F32)
    none = jnp.zeros((INNER, INNER), F32)
    rows = jnp.where(i + j == INNER - 1, one, none).astype(BF16)
    rows0 = jnp.where(((i + j) & (INNER - 1)) == 0, one, none).astype(BF16)
    sign = jnp.where(j < HALF, one, -one)
    col = j & (HALF - 1)
    same = (i < HALF) == (j < HALF)
    lanes = jnp.where(
        jnp.logical_and(same, jnp.logical_and(col > 0, col + (i & (HALF - 1)) == OUTER)), sign, none
    ).astype(BF16)
    lanes0 = jnp.where(jnp.logical_and(i == j, col == 0), sign, none).astype(BF16)

    def move(left, value, right):
        value = sum(mm(left, p) for p in reversed(split_into(value, 3)))
        return sum(mm(p, right) for p in reversed(split_into(value, 3)))

    rev = move(rows, spec, lanes) + move(rows0, spec, lanes0)
    swapped = pltpu.roll(amp, HALF, 1)
    _, left = edge_lanes()
    a0 = jnp.where(left, amp, swapped)
    a2 = jnp.where(left, swapped, amp)
    return 0.5 * (spec + rev), 0.5 * (spec - rev), a0, a2


def turn(c, s, value, flip):
    return c * value + s * (pltpu.roll(value, HALF, 1) * flip)


def column_first_kernel(
    scale, rate, wind, prior, in_ref, ef, ei, sent_ref,
    back_ref, own_ref, up_ref, down_ref, here_ref, amp_ref, par, *scratch,
):
    y_scr, z_scr, msg_scr, tab_ref = scratch[0:4]
    me = lax.axis_index("strip")
    greet_peers(me, pltpu.get_barrier_semaphore())
    weights = Exchange(me, sent_ref, here_ref, *scratch[4:7])
    weights.start()
    tables_kernel(scale, rate, wind, prior, tab_ref, amp_ref, par)
    take_all(in_ref, z_scr, True)
    column_first_step(z_scr, y_scr, -1.0)
    flip = flip_lanes(INNER)

    def step(k1, carry):
        value = apply_packed(ef, k1, y_scr[k1], flip)
        amp = amp_ref[k1]
        once = value * amp
        twice = once * amp
        y_scr[k1] = value
        z_scr[k1] = par[0] * once
        own_ref[k1] = par[3] * twice
        for n, ref, gain in ((0, up_ref, par[1]), (1, down_ref, par[2])):
            cb = tab_ref[2 * n]
            sb = tab_ref[2 * n + 1]
            ca = tab_ref[8, pl.ds(64 * n + k1, 1), :] * gain
            sa = tab_ref[8, pl.ds(64 * n + 32 + k1, 1), :] * gain
            ref[k1] = turn(cb * ca - sb * sa, sb * ca + cb * sa, twice, flip).astype(BF16)
        return carry

    lax.fori_loop(0, OUTER, step, 0, unroll=8)

    @pl.when(me == 0)
    def _():
        u0, u2, a0, a2 = edge_split(edge_gather(y_scr), edge_gather(amp_ref))
        mask, _ = edge_lanes()
        e0 = a0 * u0
        e2 = a2 * u2
        fixed = [par[0] * (e0 + e2)]
        e0 = a0 * e0
        e2 = a2 * e2
        fixed.append(par[3] * (e0 + e2))
        fixed.append(par[1] * turn(tab_ref[4], tab_ref[5], e0 + par[4] * e2, flip))
        fixed.append(par[2] * turn(tab_ref[6], tab_ref[7], e0 + par[5] * e2, flip))

        def put(k1, carry):
            back = lax.rem(INNER - k1, INNER)
            for ref, value in zip((z_scr, own_ref, up_ref, down_ref), fixed):
                value = jnp.where(mask, pltpu.roll(value, back, 1), ref[k1].astype(F32))
                ref[k1] = value.astype(ref.dtype)
            return carry

        lax.fori_loop(0, OUTER, put, 0, unroll=4)

    def inverse(k1, carry):
        z_scr[k1] = apply_packed(ei, k1, z_scr[k1], flip)
        return carry

    lax.fori_loop(0, OUTER, inverse, 0, unroll=8)
    column_first_step(z_scr, y_scr, 1.0)
    give_all(y_scr, msg_scr)
    back = Exchange(me, msg_scr, back_ref, *scratch[7:10])
    back.start()
    back.wait()
    weights.wait()


SIDE_PARTS = 4


def column_second_kernel(par, in_ref, amp_ref, own_ref, up_ref, down_ref, ef, ei, back_ref, *scratch):
    y_scr, z_scr, msg_scr, prev_ref, next_ref, side_sems = scratch[0:6]
    me = lax.axis_index("strip")
    slot_at = lax.axis_index("tm")
    above, below = lax.rem(slot_at + 1, 4), lax.rem(slot_at + 3, 4)
    greet_peers(me, pltpu.get_barrier_semaphore(), ({"tm": above}, {"tm": below}))
    pencils = Exchange(me, in_ref, msg_scr, *scratch[6:9])
    pencils.start()
    sides = []
    for p in range(SIDE_PARTS):
        rows = pl.ds(p * (OUTER // SIDE_PARTS), OUTER // SIDE_PARTS)
        for n, (src, dst, device) in enumerate(((up_ref, prev_ref, above), (down_ref, next_ref, below))):
            sides.append(
                pltpu.make_async_remote_copy(
                    src_ref=src.at[rows],
                    dst_ref=dst.at[rows],
                    send_sem=side_sems.at[0, n, p],
                    recv_sem=side_sems.at[1, n, p],
                    device_id={"tm": device},
                    device_id_type=MESH,
                )
            )
    for side in sides:
        side.start()
    pencils.wait()
    take_all(msg_scr, z_scr, False)
    column_first_step(z_scr, y_scr, -1.0)
    flip = flip_lanes(INNER)

    def step(k1, carry):
        value = apply_packed(ef, k1, y_scr[k1], flip)
        y_scr[k1] = value
        z_scr[k1] = par[0] * (value * amp_ref[k1]) + own_ref[k1]
        return carry

    lax.fori_loop(0, OUTER, step, 0, unroll=8)

    @pl.when(me == 0)
    def _():
        spec = edge_gather(y_scr)
        amp = edge_gather(amp_ref)
        u0, u2, a0, a2 = edge_split(spec, amp)
        mask, _ = edge_lanes()
        change = par[0] * (a0 * u0 + a2 * u2 - amp * spec)

        def put(k1, carry):
            back = lax.rem(INNER - k1, INNER)
            z_scr[k1] = z_scr[k1] + jnp.where(mask, pltpu.roll(change, back, 1), 0.0)
            return carry

        lax.fori_loop(0, OUTER, put, 0, unroll=4)

    for side in sides:
        side.wait()

    def inverse(k1, carry):
        moved = prev_ref[k1].astype(F32) + next_ref[k1].astype(F32)
        z_scr[k1] = apply_packed(ei, k1, z_scr[k1] - par[0] * moved, flip)
        return carry

    lax.fori_loop(0, OUTER, inverse, 0, unroll=8)
    column_first_step(z_scr, y_scr, 1.0)
    give_all(y_scr, msg_scr)
    back = Exchange(me, msg_scr, back_ref, *scratch[9:12])
    back.start()
    back.wait()


def route_kernel(t_ref, id_ref, slot_ref, tail_ref, tail_scr):
    row = lax.broadcasted_iota(jnp.int32, (INNER, 2 * INNER), 0)
    col = lax.broadcasted_iota(jnp.int32, (INNER, 2 * INNER), 1)
    tri = jnp.where(jnp.logical_or(row < col, col >= INNER), 1.0, 0.0).astype(BF16)
    peer = lax.broadcasted_iota(jnp.int32, (PEERS, INNER), 0)
    base = jnp.zeros((PEERS, INNER), F32)
    for i in range(0, POINT_ROWS, 8):
        hots = [jnp.where(peer == t_ref[i + j : i + j + 1, :], 1.0, 0.0) for j in range(8)]
        cum = mm(jnp.concatenate(hots, axis=0).astype(BF16), tri)
        for j in range(8):
            part = cum[j * PEERS : (j + 1) * PEERS]
            pos = jnp.sum(hots[j] * (part[:, 0:INNER] + base), axis=0, keepdims=True)
            base = base + part[:, INNER : 2 * INNER]
            slot_ref[i + j : i + j + 1, :] = t_ref[i + j : i + j + 1, :] * SLOTS + pos.astype(jnp.int32)
    batch = 4
    index = lax.broadcasted_iota(jnp.int32, (INNER, batch * INNER), 0)

    def wide(ref, i):
        return jnp.concatenate([ref[pl.ds(i * batch + j, 1), :] for j in range(batch)], axis=1)

    def put(i, acc):
        slot = wide(slot_ref, i)
        ids = wide(id_ref, i)
        r = lax.shift_right_logical(ids, 5)
        ids = lax.shift_right_logical(r, 3) * 256 + (ids & 31) * 8 + (r & 7)
        hot = jnp.where(index == (slot & 127), 1.0, 0.0).astype(BF16)
        line = index == lax.shift_right_logical(slot, 7)
        v = [
            jnp.where(line, d.astype(F32), 0.0).astype(BF16) for d in (lax.shift_right_logical(ids, 6), ids & 63)
        ]
        return acc + mm_nt(jnp.concatenate(v, axis=0), hot)

    acc = lax.fori_loop(0, POINT_ROWS // batch, put, jnp.zeros((2 * INNER, INNER), F32), unroll=2)
    count = base.astype(jnp.int32)
    count_high = lax.shift_right_logical(count, 6).astype(F32)
    count_low = (count & 63).astype(F32)
    tail_scr[...] = jnp.zeros_like(tail_scr)
    for s in range(PEERS):
        tail_scr[s * TAIL : s * TAIL + 4, :] = acc[4 * s : 4 * s + 4]
        tail_scr[s * TAIL + 4 : s * TAIL + 8, :] = acc[INNER + 4 * s : INNER + 4 * s + 4]
        tail_scr[s * TAIL + 8 : s * TAIL + 9, :] = count_high[s : s + 1]
        tail_scr[s * TAIL + 9 : s * TAIL + 10, :] = count_low[s : s + 1]
    tail_ref[...] = tail_scr[...].astype(BF16)


def pack_kernel(slot_ref, w_ref, tail_ref, out_ref, w_scr, buf):
    def clear(i, carry):
        rows = pl.ds(pl.multiple_of(i * 64, 64), 64)
        buf[rows, :] = jnp.zeros((64, INNER), F32)
        buf[pl.ds(pl.multiple_of(i * 64 + PEERS * SLOTS // 2, 64), 64), :] = jnp.zeros((64, INNER), F32)
        w_scr[rows, :] = w_ref[rows, :].astype(F32)
        return carry

    lax.fori_loop(0, PEERS * SLOTS // INNER, clear, 0)

    def some(q, carry):
        first = q * 16
        slots = [slot_ref[first + j] for j in range(16)]
        rows = [w_scr[pl.ds(first + j, 1), :] for j in range(16)]
        for j in range(16):
            buf[pl.ds(slots[j], 1), :] = rows[j]
        return carry

    lax.fori_loop(0, POINT_ROWS * INNER // 16, some, 0)

    def narrow(d, carry):
        for i in range(4):
            rows = pl.ds(pl.multiple_of(d * SLOTS + i * INNER, INNER), INNER)
            out_ref[pl.ds(pl.multiple_of(d * GROUP + i * INNER, TAIL), INNER), :] = buf[rows, :].astype(BF16)
        tail = tail_ref[pl.ds(pl.multiple_of(d * TAIL, TAIL), TAIL), :]
        out_ref[pl.ds(pl.multiple_of(d * GROUP + SLOTS, TAIL), TAIL), :] = tail
        return carry

    lax.fori_loop(0, PEERS, narrow, 0)


def gather_kernel(sid_ref, cnt_ref, in_ref, w_ref, tw, f_ref, a_ref, m_ref, out_ref, g_scr, tiles_ref, z_scr, e_scr):
    row_backward_kernel(False, in_ref, tw, f_ref, a_ref, m_ref, tiles_ref, z_scr, e_scr)

    def source(s, carry):
        def some(q, inner):
            first = s * SLOTS + q * 16
            ids = [sid_ref[first + j] for j in range(16)]
            rows = [tiles_ref[pl.ds(ids[j], 1), :] for j in range(16)]
            for j in range(16):
                g_scr[pl.ds(first + j, 1), :] = rows[j]
            return inner

        return lax.fori_loop(0, lax.shift_right_logical(cnt_ref[s] + 15, 4), some, carry)

    lax.fori_loop(0, PEERS, source, 0)
    ones = jnp.ones((2 * INNER, INNER), BF16)
    lane = lax.broadcasted_iota(jnp.int32, (INNER, INNER), 1)
    diagonal = lane == lax.broadcasted_iota(jnp.int32, (INNER, INNER), 0)
    place = lax.broadcasted_iota(jnp.int32, (1, INNER), 1)

    def total(s, carry):
        w = w_ref[pl.ds(pl.multiple_of(s * GROUP, TAIL), SLOTS), :].astype(F32)
        g = g_scr[pl.ds(pl.multiple_of(s * SLOTS, SLOTS), SLOTS), :]
        sums = mm(jnp.concatenate(split(g * w), axis=1), ones)
        for q in range(4):
            got = jnp.where(diagonal, sums[q * INNER : (q + 1) * INNER], 0.0)
            got = jnp.sum(got, axis=0, keepdims=True)
            out_ref[s, q : q + 1, :] = jnp.where(place + q * INNER < cnt_ref[s], got, 0.0)
        return carry

    lax.fori_loop(0, PEERS, total, 0, unroll=2)


def residual_kernel(slot_ref, prec_ref, phase_ref, out_ref, *scratch):
    p_scr, landed, table_scr, res_scr = scratch[0:4]
    me = lax.axis_index("strip")
    greet_peers(me, pltpu.get_barrier_semaphore())
    phases = Exchange(me, phase_ref, landed, *scratch[4:7])
    phases.start()
    phases.wait()
    for s in range(PEERS):
        table_scr[4 * s : 4 * s + 4, :] = landed[s]
    high, low = split(table_scr[...])
    table = jnp.concatenate([high, low], axis=0)
    batch = 4
    index = lax.broadcasted_iota(jnp.int32, (INNER, batch * INNER), 0)

    def wide(ref, i):
        return jnp.concatenate([ref[pl.ds(i * batch + j, 1), :] for j in range(batch)], axis=1)

    def pick(i, carry):
        slot = wide(slot_ref, i)
        hot = jnp.where(index == (slot & 127), 1.0, 0.0).astype(BF16)
        v = mm(table, hot)
        v = v[0:INNER] + v[INNER : 2 * INNER]
        got = jnp.sum(jnp.where(index == lax.shift_right_logical(slot, 7), v, 0.0), axis=0, keepdims=True)
        for j in range(batch):
            p_scr[pl.ds(i * batch + j, 1), :] = got[:, j * INNER : (j + 1) * INNER]
        return carry

    lax.fori_loop(0, POINT_ROWS // batch, pick, 0, unroll=2)
    row = lax.broadcasted_iota(jnp.int32, (INNER, INNER), 0)
    lane = lax.broadcasted_iota(jnp.int32, (INNER, INNER), 1)
    same = jnp.where((row < HALF) == (lane < HALF), 1.0, 0.0).astype(BF16)
    prec = prec_ref[...]
    phase = p_scr[...]

    def total(value):
        return sum(mm(p, same) for p in reversed(split_into(value, 3)))

    p_scr[...] = prec * (phase - total(prec * phase) / total(prec))

    def put(i, acc):
        slot = wide(slot_ref, i)
        hot = jnp.where(index == (slot & 127), 1.0, 0.0).astype(BF16)
        v = jnp.where(index == lax.shift_right_logical(slot, 7), wide(p_scr, i), 0.0)
        vh, vl = split(v)
        return acc + mm_nt(jnp.concatenate([vh, vl], axis=0), hot)

    acc = lax.fori_loop(0, POINT_ROWS // batch, put, jnp.zeros((2 * INNER, INNER), F32), unroll=2)
    acc = acc[0:INNER] + acc[INNER : 2 * INNER]
    for s in range(PEERS):
        res_scr[s] = acc[4 * s : 4 * s + 4]
    residuals = Exchange(me, res_scr, out_ref, *scratch[7:10])
    residuals.start()
    residuals.wait()


COPIES = 8


def scatter_kernel(
    sid_ref, cnt_ref, r_ref, w_ref, tw, f_ref, a_ref, m_ref, out_ref, rt_scr, u_scr, y_scr, e_scr, *accs
):
    def clear(i, carry):
        rows = pl.ds(pl.multiple_of(i * 64, 64), 64)
        for acc in accs:
            acc[rows, :] = jnp.zeros((64, INNER), F32)
        return carry

    lax.fori_loop(0, SIDE // 64, clear, 0)
    rt_scr[...] = r_ref[...].T
    lane = lax.broadcasted_iota(jnp.int32, (INNER, INNER), 1)

    def scaled(s, carry):
        for q in range(4):
            col = jnp.sum(jnp.where(lane == s * 4 + q, rt_scr[...], 0.0), axis=1, keepdims=True)
            base = pl.multiple_of(s * GROUP + q * INNER, TAIL)
            rows = pl.ds(pl.multiple_of(s * SLOTS + q * INNER, INNER), INNER)
            u_scr[rows, :] = w_ref[pl.ds(base, INNER), :].astype(F32) * col
        return carry

    lax.fori_loop(0, PEERS, scaled, 0, unroll=2)

    def source(s, carry):
        def some(q, inner):
            first = s * SLOTS + q * 16
            ids = [sid_ref[first + j] for j in range(16)]
            us = [u_scr[pl.ds(first + j, 1), :] for j in range(16)]
            for h in range(0, 16, COPIES):
                sums = [accs[j][pl.ds(ids[h + j], 1), :] + us[h + j] for j in range(COPIES)]
                for j in range(COPIES):
                    accs[j][pl.ds(ids[h + j], 1), :] = sums[j]
            return inner

        return lax.fori_loop(0, lax.shift_right_logical(cnt_ref[s] + 15, 4), some, carry)

    lax.fori_loop(0, PEERS, source, 0)

    def add(i, carry):
        rows = pl.ds(pl.multiple_of(i * 64, 64), 64)
        total = accs[0][rows, :]
        for acc in accs[1:]:
            total = total + acc[rows, :]
        accs[0][rows, :] = total
        return carry

    lax.fori_loop(0, SIDE // 64, add, 0)
    row_forward_kernel(True, False, accs[0], tw, f_ref, a_ref, m_ref, out_ref, y_scr, e_scr)


def call(kernel, name, out_shapes, args, smem=0, scratch=(), any_args=(), any_outs=(), smem_outs=(), collective_id=None):
    spaces = [pltpu.SMEM if i < smem else pl.ANY if i in any_args else pltpu.VMEM for i in range(len(args))]
    outs = [pl.ANY if i in any_outs else pltpu.SMEM if i in smem_outs else pltpu.VMEM for i in range(len(out_shapes))]
    remote = dict(collective_id=collective_id, has_side_effects=True) if collective_id is not None else {}
    return pl.pallas_call(
        kernel,
        out_shape=out_shapes,
        in_specs=[pl.BlockSpec(memory_space=space) for space in spaces],
        out_specs=[pl.BlockSpec(memory_space=space) for space in outs],
        scratch_shapes=list(scratch),
        compiler_params=pltpu.CompilerParams(vmem_limit_bytes=VMEM_BYTES, **remote),
        cost_estimate=pl.CostEstimate(flops=1024, bytes_accessed=1024, transcendentals=0),
        name=name,
    )(*args)


def shape(dims, dtype=F32):
    return jax.ShapeDtypeStruct(dims, dtype)


PENCILS = (PEERS, INNER, INNER)
MESSAGES = (PEERS, INNER + TAIL, INNER)


def row_forward(x, tables, tiled):
    args = [x] + tables
    return call(
        lambda *refs: row_forward_kernel(tiled, not tiled, *refs),
        "row_forward",
        [shape(MESSAGES, BF16)],
        args,
        scratch=[pltpu.VMEM((15 * INNER, 2 * INNER), F32), pltpu.VMEM((2, INNER, INNER), F32)],
    )[0]


def row_backward(pencils, base, tables):
    final = base is not None
    args = [pencils] + ([base] if final else []) + tables
    return call(
        lambda *refs: row_backward_kernel(final, *refs),
        "row_backward",
        [shape((INNER, SIDE) if final else (SIDE, INNER))],
        args,
        scratch=[pltpu.VMEM((15 * INNER, 2 * INNER), F32), pltpu.VMEM((2, INNER, INNER), F32)],
    )[0]


def exchange(value):
    return lax.all_to_all(value, "strip", split_axis=0, concat_axis=0, tiled=True)


def tables_kernel(scale, rate, wind, prior, tab_ref, amp_ref, par_ref):
    strip = lax.axis_index("strip")
    live = (lax.axis_index("tm") < 3).astype(F32)
    k1 = (strip // 2).astype(F32)
    even = strip % 2 == 0
    row = lax.broadcasted_iota(jnp.int32, (INNER, INNER), 0)
    lane = lax.broadcasted_iota(jnp.int32, (INNER, INNER), 1)
    line = row.astype(F32)
    j = (lane & (HALF - 1)).astype(F32)
    cols = jnp.where(even, k1 + OUTER * j, k1 + OUTER * (INNER - 1.0 - j))
    cols = jnp.where(strip == 1, 16.0 + OUTER * j, cols)
    winds = ((wind[0, 0].astype(F32), wind[0, 1].astype(F32)), (prior[1], prior[2]))

    def cosine(turns):
        turns = turns - SIDE * jnp.floor(turns * (1.0 / SIDE))
        return jnp.cos(turns * (2.0 * math.pi / SIDE))

    small = jnp.zeros((INNER, INNER), F32)
    for kind in range(4):
        wind_row, wind_col = winds[kind // 2]
        quarter = (0.0, 3.0 * SIDE / 4, 0.0, SIDE / 4.0)[kind]
        base = OUTER * line * wind_row + quarter
        tab_ref[kind] = cosine(base + cols * wind_col)
        tab_ref[4 + kind] = cosine(base + j * wind_row)
        turns = (row & (OUTER - 1)).astype(F32) * wind_row + quarter
        small = jnp.where(lax.shift_right_logical(row, 5) == kind, turns, small)
    tab_ref[8] = cosine(small)

    fold = jnp.where(even, k1 + OUTER * j, OUTER - k1 + OUTER * j)
    fold = jnp.where(strip == 1, 16.0 + OUTER * j, fold)
    fold = jnp.where(jnp.logical_and(strip == 0, lane == HALF), SIDE / 2.0, fold)
    fold = fold * fold

    def step(k, carry):
        kr = line * OUTER + k.astype(F32)
        kr = jnp.minimum(kr, SIDE - kr)
        radius = (kr * kr + fold) / (KZERO * KZERO)
        amp_ref[k] = SIDE / (2.0 * KZERO) * jnp.exp((-11.0 / 12.0) * jnp.log(1.0 + radius))
        return carry

    lax.fori_loop(0, OUTER, step, 0, unroll=2)
    norm = scale[0] / (SIDE * SIDE)
    mine = rate[0] * live
    par_ref[0] = norm
    par_ref[1] = mine * scale[0]
    par_ref[2] = prior[0] * scale[0]
    par_ref[3] = (mine + prior[0]) * scale[0] * norm
    par_ref[4] = 1.0 - 2.0 * (wind[0, 1] & 1).astype(F32)
    par_ref[5] = 1.0 - 2.0 * (prior[2].astype(jnp.int32) & 1).astype(F32)
    par_ref[6] = 0.0
    par_ref[7] = 0.0


def const(*tables):
    return [jnp.asarray(t) for t in tables]


def local(
    screen_vec,
    prior_scale,
    flow_weight,
    wind,
    pierce_point_strip,
    pierce_block,
    pierce_weights,
    noise_prec,
):
    fwd, inv, first, first_inv, mid, mid_inv, twiddle = row_tables()
    row_fwd_tables = const(twiddle, pieces(fwd, 2), pieces(first, 2), pieces(mid, 2))
    row_fine_tables = const(twiddle, pieces(fwd, 3), pieces(first, 3), pieces(mid, 3))
    row_inv_tables = const(twiddle, pieces(inv, 2), pieces(first_inv, 2), pieces(mid_inv, 2))
    col_fwd, col_inv = column_tables()
    col_fine_tables = const(pieces(col_fwd, 3), pieces(col_inv, 2))
    col_tables = const(pieces(col_fwd, 2), pieces(col_inv, 2))

    x = screen_vec[0]
    weights = pierce_weights[0].reshape(POINT_ROWS * INNER, INNER)
    target = pierce_point_strip.reshape(POINT_ROWS, INNER)
    block = pierce_block.reshape(POINT_ROWS, INNER)
    prec = noise_prec.reshape(POINT_ROWS, INNER)

    mine = jnp.concatenate([flow_weight, wind[0].astype(F32)])
    prior = lax.ppermute(mine, "tm", [(i, i + 1) for i in range(lax.axis_size("tm") - 1)])
    slots, tail = call(
        route_kernel,
        "route",
        [shape((POINT_ROWS, INNER), jnp.int32), shape((PEERS * TAIL, INNER), BF16)],
        [target, block],
        scratch=[pltpu.VMEM((PEERS * TAIL, INNER), F32)],
    )
    tail, prior, prec = lax.optimization_barrier((tail, prior, prec))
    sent = call(
        pack_kernel,
        "pack",
        [shape((PEERS * GROUP, INNER), BF16)],
        [slots.reshape(-1), weights, tail],
        smem=1,
        scratch=[pltpu.VMEM((POINT_ROWS * INNER, INNER), F32), pltpu.VMEM((PEERS * SLOTS, INNER), F32)],
    )[0]
    pencils = exchange(row_forward(x, row_fine_tables, False))

    spectral = [pltpu.VMEM(PENCILS, F32), pltpu.VMEM(PENCILS, F32)]
    message = shape(MESSAGES, BF16)
    back, own, up, down, arrived, amp, par = call(
        column_first_kernel,
        "column_first",
        [
            message,
            shape(PENCILS),
            shape(PENCILS, BF16),
            shape(PENCILS, BF16),
            shape((PEERS, GROUP, INNER), BF16),
            shape(PENCILS),
            shape((8,)),
        ],
        [prior_scale, flow_weight, wind, prior, pencils] + col_fine_tables + [sent.reshape(PEERS, GROUP, INNER)],
        smem=4,
        any_args=(7,),
        any_outs=(0, 4),
        smem_outs=(6,),
        collective_id=3,
        scratch=spectral
        + [pltpu.VMEM(MESSAGES, BF16), pltpu.VMEM((9, INNER, INNER), F32)]
        + exchange_sems()
        + exchange_sems(),
    )
    here = arrived.reshape(PEERS * GROUP, INNER)
    digits = arrived[:, SLOTS:, :].astype(F32)
    here_ids = (digits[:, 0:4] * 64.0 + digits[:, 4:8]).astype(jnp.int32).reshape(PEERS * SLOTS)
    here_counts = (digits[:, 8, 0] * 64.0 + digits[:, 9, 0]).astype(jnp.int32)

    rows = [pltpu.VMEM((15 * INNER, 2 * INNER), F32), pltpu.VMEM((2, INNER, INNER), F32)]
    points = pltpu.VMEM((PEERS * SLOTS, INNER), F32)
    screen = pltpu.VMEM((SIDE, INNER), F32)
    small = (PEERS, 4, INNER)
    phase = call(
        gather_kernel,
        "gather",
        [shape(small)],
        [here_ids, here_counts, back, here] + row_inv_tables,
        smem=2,
        scratch=[points, screen] + rows,
    )[0]
    resid = call(
        residual_kernel,
        "residual",
        [shape(small)],
        [slots, prec, phase],
        collective_id=2,
        scratch=[
            pltpu.VMEM((POINT_ROWS, INNER), F32),
            pltpu.VMEM(small, F32),
            pltpu.VMEM((INNER, INNER), F32),
            pltpu.VMEM(small, F32),
        ]
        + exchange_sems()
        + exchange_sems(),
    )[0]
    pencils = call(
        scatter_kernel,
        "scatter",
        [message],
        [here_ids, here_counts, resid.reshape(INNER, INNER), here] + row_fwd_tables,
        smem=2,
        scratch=[pltpu.VMEM((INNER, INNER), F32), points] + rows + [screen] * COPIES,
    )[0]
    out_pencils = call(
        column_second_kernel,
        "column_second",
        [message],
        [par, pencils, amp, own, up, down] + col_tables,
        smem=1,
        any_args=(1, 4, 5),
        any_outs=(0,),
        collective_id=1,
        scratch=spectral
        + [pltpu.VMEM(MESSAGES, BF16), pltpu.VMEM(PENCILS, BF16), pltpu.VMEM(PENCILS, BF16)]
        + [pltpu.SemaphoreType.DMA((2, 2, SIDE_PARTS))]
        + exchange_sems()
        + exchange_sems(),
    )[0]
    return row_backward(out_pencils, x, row_inv_tables)[None]


def solution(mesh):
    in_specs = (
        P("tm", "strip", None),
        P("tm"),
        P("tm"),
        P("tm", None),
        P("tm", "strip", None, None),
        P("tm", "strip", None),
        P("tm", "strip", None, None),
        P("tm", "strip", None),
    )
    out_specs = P("tm", "strip", None)
    return jax.shard_map(local, mesh=mesh, in_specs=in_specs, out_specs=out_specs, check_vma=False)
```

```python
import math

import jax
import jax.numpy as jnp
import ml_dtypes
import numpy as np
from jax import lax
from jax.experimental import pallas as pl
from jax.experimental.pallas import tpu as pltpu
from jax.sharding import PartitionSpec as P

KZERO = 2.0
SIDE = 4096
OUTER = 32
INNER = 128
HALF = 64
PEERS = 32
SLOTS = 512
POINT_ROWS = 64
TAIL = 16
ID_ROWS = 8
ID_STRIDE = ID_ROWS * 128
VMEM_BYTES = 56 * 1024 * 1024
F32 = jnp.float32
BF16 = jnp.bfloat16


def pieces(table, count):
    rest = np.asarray(table, np.float64)
    out = []
    for _ in range(count):
        out.append(rest.astype(np.float32).astype(ml_dtypes.bfloat16))
        rest = rest - out[-1].astype(np.float64)
    return np.stack(out)


def row_tables():
    b = np.arange(INNER)[:, None]
    j = np.arange(HALF)[None, :]
    theta = [2 * np.pi * ((b * j) % INNER) / INNER, 2 * np.pi * ((b * (INNER - 1 - j)) % INNER) / INNER]
    forward = []
    backward = []
    for t in theta:
        forward.append(np.concatenate([np.cos(t), -np.sin(t)], axis=1))
        forward.append(np.concatenate([np.sin(t), np.cos(t)], axis=1))
        backward.append(np.concatenate([np.cos(t).T, np.sin(t).T], axis=1))
        backward.append(np.concatenate([-np.sin(t).T, np.cos(t).T], axis=1))
    fwd = np.concatenate(
        [np.concatenate([forward[0], forward[1]], axis=0), np.concatenate([forward[2], forward[3]], axis=0)], axis=1
    )
    inv = np.concatenate(backward, axis=0)
    sign = np.where(np.arange(INNER) % 2 == 0, 1.0, -1.0)
    t0 = theta[0]
    first = np.concatenate([np.cos(t0), -np.sin(t0)], axis=1)
    first[:, HALF] = sign
    first_inv = np.concatenate([2 * np.cos(t0).T, -2 * np.sin(t0).T], axis=0)
    first_inv[0, :] = 1.0
    first_inv[HALF, :] = sign
    t16 = 2 * np.pi * ((b * (16 + 32 * j)) % SIDE) / SIDE
    mid = np.concatenate([np.cos(t16), -np.sin(t16)], axis=1)
    mid_inv = np.concatenate([2 * np.cos(t16).T, -2 * np.sin(t16).T], axis=0)
    k1 = np.arange(16)[:, None]
    tw = 2 * np.pi * (k1 * np.arange(INNER)[None, :]) / SIDE
    twiddle = np.stack([np.cos(tw), np.sin(tw)]).astype(np.float32)
    return fwd, inv, first, first_inv, mid, mid_inv, twiddle


def column_tables():
    k1 = np.arange(OUTER)[:, None, None]
    k2 = np.arange(INNER)[None, :, None]
    r = np.arange(INNER)[None, None, :]
    theta = 2 * np.pi * (((k1 + OUTER * k2) * r) % SIDE) / SIDE
    fwd = np.concatenate([np.cos(theta), -np.sin(theta)], axis=1)
    theta = theta.transpose(0, 2, 1)
    inv = np.concatenate([np.cos(theta), np.sin(theta)], axis=1)
    return fwd, inv


def split(value):
    high = value.astype(BF16)
    return high, (value - high.astype(F32)).astype(BF16)


def mm(left, right):
    return lax.dot_general(left, right, (((1,), (0,)), ((), ())), preferred_element_type=F32)


def mm_nt(left, right):
    return lax.dot_general(left, right, (((1,), (1,)), ((), ())), preferred_element_type=F32)


def split_into(value, count):
    parts = []
    for i in range(count):
        parts.append(value.astype(BF16))
        if i + 1 < count:
            value = value - parts[-1].astype(F32)
    return parts


def data_by_table(value, tables):
    count = len(tables)
    parts = split_into(value, count)
    total = None
    for order in reversed(range(count)):
        for i in range(order + 1):
            term = mm(parts[i], tables[order - i])
            total = term if total is None else total + term
    return total


def table_by_data(tables, value):
    parts = split_into(value, len(tables))
    left = jnp.concatenate(tables[0:2], axis=1)
    right = jnp.concatenate(parts[0:2], axis=1)
    r = mm(left, jnp.concatenate([right, right], axis=0))
    total = r[:, INNER : 2 * INNER] + r[:, 0:INNER]
    if len(tables) == 3:
        left = jnp.concatenate([tables[0], tables[2]], axis=1)
        total = total + mm(left, jnp.concatenate([parts[2], parts[0]], axis=0))
    return total


def every(ref):
    return [ref[i] for i in range(ref.shape[0])]


def c_mul(value, factor):
    re, im = value
    c, s = factor.real, factor.imag
    if im is None:
        return (re * c, re * s)
    return (re * c - im * s, re * s + im * c)


def real_forward(xs):
    n = len(xs)
    if n == 2:
        return [(xs[0] + xs[1], None), (xs[0] - xs[1], None)]
    even, odd = real_forward(xs[0::2]), real_forward(xs[1::2])
    m = n // 2
    out = [None] * (m + 1)
    for k in range(m // 2 + 1):
        if k == 0:
            out[0] = (even[0][0] + odd[0][0], None)
            out[m] = (even[0][0] - odd[0][0], None)
        elif 2 * k == m:
            out[k] = (even[k][0], -odd[k][0])
        else:
            tr, ti = c_mul(odd[k], complex(math.cos(2 * math.pi * k / n), -math.sin(2 * math.pi * k / n)))
            er, ei = even[k]
            out[k] = (er + tr, ei + ti)
            out[m - k] = (er - tr, ti - ei)
    return out


def real_backward(spec):
    n = 2 * (len(spec) - 1)
    if n == 2:
        return [spec[0][0] + spec[1][0], spec[0][0] - spec[1][0]]
    m = n // 2
    even, odd = [], []
    for k in range(m // 2 + 1):
        if k == 0:
            even.append((spec[0][0] + spec[m][0], None))
            odd.append((spec[0][0] - spec[m][0], None))
        elif 2 * k == m:
            even.append((2.0 * spec[k][0], None))
            odd.append((-2.0 * spec[k][1], None))
        else:
            ar, ai = spec[k]
            br, bi = spec[m - k]
            even.append((ar + br, ai - bi))
            odd.append(c_mul((ar - br, ai + bi), complex(math.cos(2 * math.pi * k / n), math.sin(2 * math.pi * k / n))))
    xe, xo = real_backward(even), real_backward(odd)
    out = [None] * n
    out[0::2] = xe
    out[1::2] = xo
    return out


def packed_fft(xs, sign, flip):
    n = len(xs)
    if n == 1:
        return xs
    even, odd = packed_fft(xs[0::2], sign, flip), packed_fft(xs[1::2], sign, flip)
    out = [None] * n
    for k in range(n // 2):
        t = odd[k]
        if k:
            turned = pltpu.roll(t, HALF, 1) * flip
            c, s = math.cos(2 * math.pi * k / n), sign * math.sin(2 * math.pi * k / n)
            t = (-s) * turned if 4 * k == n else c * t - s * turned
        out[k] = even[k] + t
        out[k + n // 2] = even[k] - t
    return out


def flip_lanes(rows):
    lane = lax.broadcasted_iota(jnp.int32, (rows, INNER), 1)
    return jnp.where(lane < HALF, 1.0, -1.0).astype(F32)


def put_message(ref, d, value, fine):
    lane = lax.broadcasted_iota(jnp.int32, (INNER, INNER), 1)
    high = value.astype(BF16)
    ref[d, 0:INNER, :] = high
    rest = value - high.astype(F32)
    if fine:
        third = rest - rest.astype(BF16).astype(F32)
        rest = jnp.where((lane & (HALF - 1)) == 7, pltpu.roll(third, 7, 1), rest)
    rest = jnp.where(lane < 8, rest, pltpu.roll(rest, 72, 1))
    rest = jnp.where(lane < 16, rest, 0.0)
    total = rest[0:16]
    for g in range(1, 8):
        total = total + pltpu.roll(rest[16 * g : 16 * g + 16], 16 * g, 1)
    ref[d, INNER : INNER + TAIL, :] = total.astype(BF16)


def get_message(ref, d, fine):
    lane = lax.broadcasted_iota(jnp.int32, (INNER, INNER), 1)
    packed = ref[d, INNER : INNER + TAIL, :].astype(F32)
    rest = jnp.concatenate([packed] + [pltpu.roll(packed, INNER - 16 * g, 1) for g in range(1, 8)], axis=0)
    rest = jnp.where(lane < 8, rest, pltpu.roll(rest, 56, 1))
    column = lane & (HALF - 1)
    if fine:
        third = jnp.where(column == 0, pltpu.roll(rest, INNER - 7, 1), 0.0)
        rest = jnp.where(column < 7, rest, 0.0) + third
    else:
        rest = jnp.where(column < 8, rest, 0.0)
    return ref[d, 0:INNER, :].astype(F32) + rest


def row_forward_kernel(tiled, fine, x_ref, tw_ref, f_ref, a_ref, m_ref, out_ref, y_scr, e_scr):
    def slab(g, carry):
        if tiled:
            xs = [x_ref[pl.ds(pl.multiple_of(g * 256 + a * 8, 8), 8), :] for a in range(OUTER)]
        else:
            xs = [x_ref[pl.ds(pl.multiple_of(g * 8, 8), 8), a * INNER : (a + 1) * INNER] for a in range(OUTER)]
        ys = real_forward(xs)
        rows = pl.ds(pl.multiple_of(g * 8, 8), 8)
        e_scr[0, rows, :] = ys[0][0]
        e_scr[1, rows, :] = ys[16][0]
        for k in range(1, 16):
            c = tw_ref[0, k : k + 1, :]
            s = tw_ref[1, k : k + 1, :]
            re, im = ys[k]
            base = pl.ds(pl.multiple_of((k - 1) * INNER + g * 8, 8), 8)
            y_scr[base, 0:INNER] = re * c + im * s
            y_scr[base, INNER : 2 * INNER] = im * c - re * s
        return carry

    lax.fori_loop(0, 16, slab, 0, unroll=2)
    put_message(out_ref, 0, data_by_table(e_scr[0], every(a_ref)), fine)
    put_message(out_ref, 1, data_by_table(e_scr[1], every(m_ref)), fine)

    def group(q, carry):
        v = data_by_table(y_scr[pl.ds(pl.multiple_of(q * 384, 8), 384), :], every(f_ref))
        for i in range(3):
            rows = v[i * INNER : (i + 1) * INNER]
            put_message(out_ref, 2 + 2 * (3 * q + i), rows[:, 0:INNER], fine)
            put_message(out_ref, 3 + 2 * (3 * q + i), rows[:, INNER : 2 * INNER], fine)
        return carry

    lax.fori_loop(0, 5, group, 0)


def row_backward_kernel(final, *refs):
    if final:
        in_ref, base_ref, tw_ref, f_ref, a_ref, m_ref, out_ref, z_scr, e_scr = refs
    else:
        in_ref, tw_ref, f_ref, a_ref, m_ref, out_ref, z_scr, e_scr = refs
    e_scr[0] = data_by_table(get_message(in_ref, 0, False), every(a_ref))
    e_scr[1] = data_by_table(get_message(in_ref, 1, False), every(m_ref))

    def group(q, carry):
        parts = []
        for i in range(3):
            k = 3 * q + i
            parts.append(jnp.concatenate([get_message(in_ref, 2 + 2 * k + h, False) for h in range(2)], axis=1))
        v = jnp.concatenate(parts, axis=0)
        z_scr[pl.ds(pl.multiple_of(q * 384, 8), 384), :] = data_by_table(v, every(f_ref))
        return carry

    lax.fori_loop(0, 5, group, 0)

    def slab(g, carry):
        rows = pl.ds(pl.multiple_of(g * 8, 8), 8)
        spec = [(e_scr[0, rows, :], None)]
        for k in range(1, 16):
            c = tw_ref[0, k : k + 1, :]
            s = tw_ref[1, k : k + 1, :]
            base = pl.ds(pl.multiple_of((k - 1) * INNER + g * 8, 8), 8)
            re = z_scr[base, 0:INNER]
            im = z_scr[base, INNER : 2 * INNER]
            spec.append((re * c - im * s, im * c + re * s))
        spec.append((e_scr[1, rows, :], None))
        xs = real_backward(spec)
        for a in range(OUTER):
            if final:
                cols = slice(a * INNER, (a + 1) * INNER)
                out_ref[rows, cols] = base_ref[rows, cols] + xs[a]
            else:
                out_ref[pl.ds(pl.multiple_of(g * 256 + a * 8, 8), 8), :] = xs[a]
        return carry

    lax.fori_loop(0, 16, slab, 0, unroll=2)


def take_all(in_ref, scr, fine):
    def step(s, carry):
        scr[s] = get_message(in_ref, s, fine)
        return carry

    lax.fori_loop(0, OUTER, step, 0, unroll=4)


def give_all(scr, out_ref):
    def step(s, carry):
        put_message(out_ref, s, scr[s], False)
        return carry

    lax.fori_loop(0, OUTER, step, 0, unroll=4)


def column_first_step(in_ref, y_scr, sign):
    flip = flip_lanes(8)

    def slab(g, carry):
        rows = pl.ds(pl.multiple_of(g * 8, 8), 8)
        ys = packed_fft([in_ref[s, rows, :] for s in range(OUTER)], sign, flip)
        for k in range(OUTER):
            y_scr[k, rows, :] = ys[k]
        return carry

    lax.fori_loop(0, 16, slab, 0, unroll=2)


def apply_packed(e_ref, k1, value, flip):
    r = table_by_data([e_ref[i, k1] for i in range(e_ref.shape[0])], value)
    return r[0:INNER] - pltpu.roll(r[INNER : 2 * INNER], HALF, 1) * flip


MESH = pl.DeviceIdType.MESH


def greet_peers(me, barrier, extra=()):
    def greet(i, carry):
        pl.semaphore_signal(barrier, inc=1, device_id={"strip": lax.rem(me + i, PEERS)}, device_id_type=MESH)
        return carry

    lax.fori_loop(1, PEERS, greet, 0)
    for device in extra:
        pl.semaphore_signal(barrier, inc=1, device_id=device, device_id_type=MESH)
    pl.semaphore_wait(barrier, PEERS - 1 + len(extra))


class Exchange:
    def __init__(self, me, in_ref, out_ref, send_sem, recv_sem, own_sem):
        self.me, self.in_ref, self.out_ref = me, in_ref, out_ref
        self.send_sem, self.recv_sem = send_sem, recv_sem
        self.own = pltpu.make_async_copy(in_ref.at[me], out_ref.at[me], own_sem)

    def copy(self, peer, send, source):
        return pltpu.make_async_remote_copy(
            src_ref=self.in_ref.at[peer],
            dst_ref=self.out_ref.at[source],
            send_sem=self.send_sem.at[send],
            recv_sem=self.recv_sem.at[source],
            device_id={"strip": peer},
            device_id_type=MESH,
        )

    def peer(self, i):
        return lax.rem(self.me + 1 + lax.rem(i + 2 * self.me, PEERS - 1), PEERS)

    def start(self, first=0, last=PEERS - 1):
        def step(i, carry):
            self.copy(self.peer(i), i, self.me).start()
            return carry

        lax.fori_loop(first, last, step, 0)
        if first == 0:
            self.own.start()

    def wait(self):
        def step(i, carry):
            peer = self.peer(i)
            copy = self.copy(peer, i, peer)
            copy.wait_send()
            copy.wait_recv()
            return carry

        self.own.wait()
        lax.fori_loop(0, PEERS - 1, step, 0)


def exchange_sems():
    return [pltpu.SemaphoreType.DMA((PEERS,)), pltpu.SemaphoreType.DMA((PEERS,)), pltpu.SemaphoreType.DMA]


def edge_lanes():
    lane = lax.broadcasted_iota(jnp.int32, (INNER, INNER), 1)
    return jnp.logical_or(lane == 0, lane == HALF), lane < HALF


def edge_gather(ref):
    mask, _ = edge_lanes()

    def step(k1, acc):
        return acc + pltpu.roll(jnp.where(mask, ref[k1], 0.0), k1, 1)

    return lax.fori_loop(0, OUTER, step, jnp.zeros((INNER, INNER), F32), unroll=4)


def edge_split(spec, amp):
    i = lax.broadcasted_iota(jnp.int32, (INNER, INNER), 0)
    j = lax.broadcasted_iota(jnp.int32, (INNER, INNER), 1)
    one = jnp.ones((INNER, INNER), F32)
    none = jnp.zeros((INNER, INNER), F32)
    rows = jnp.where(i + j == INNER - 1, one, none).astype(BF16)
    rows0 = jnp.where(((i + j) & (INNER - 1)) == 0, one, none).astype(BF16)
    sign = jnp.where(j < HALF, one, -one)
    col = j & (HALF - 1)
    same = (i < HALF) == (j < HALF)
    lanes = jnp.where(
        jnp.logical_and(same, jnp.logical_and(col > 0, col + (i & (HALF - 1)) == OUTER)), sign, none
    ).astype(BF16)
    lanes0 = jnp.where(jnp.logical_and(i == j, col == 0), sign, none).astype(BF16)

    def move(left, value, right):
        value = sum(mm(left, p) for p in reversed(split_into(value, 3)))
        return sum(mm(p, right) for p in reversed(split_into(value, 3)))

    rev = move(rows, spec, lanes) + move(rows0, spec, lanes0)
    swapped = pltpu.roll(amp, HALF, 1)
    _, left = edge_lanes()
    a0 = jnp.where(left, amp, swapped)
    a2 = jnp.where(left, swapped, amp)
    return 0.5 * (spec + rev), 0.5 * (spec - rev), a0, a2


def turn(c, s, value, flip):
    return c * value + s * (pltpu.roll(value, HALF, 1) * flip)


EARLY = 8


def column_first_kernel(
    scale, rate, wind, prior, x_ref, tw, f_ref, a_ref, m_ref, ef, ei, sent_ref, ids_ref,
    back_ref, own_ref, up_ref, down_ref, here_ref, here_ids_ref, amp_ref, par, *scratch,
):
    y_scr, z_scr, msg_scr, land_scr, tab_ref, row_scr, row_edge = scratch[0:7]
    me = lax.axis_index("strip")
    greet_peers(me, pltpu.get_barrier_semaphore())
    ids = Exchange(me, ids_ref, here_ids_ref, *scratch[7:10])
    weights = Exchange(me, sent_ref, here_ref, *scratch[10:13])
    pencils = Exchange(me, msg_scr, land_scr, *scratch[13:16])
    ids.start()
    weights.start(0, EARLY)
    row_forward_kernel(False, True, x_ref, tw, f_ref, a_ref, m_ref, msg_scr, row_scr, row_edge)
    pencils.start()
    weights.start(EARLY)
    tables_kernel(scale, rate, wind, prior, tab_ref, amp_ref, par)
    pencils.wait()
    take_all(land_scr, z_scr, True)
    column_first_step(z_scr, y_scr, -1.0)
    flip = flip_lanes(INNER)

    def step(k1, carry):
        value = apply_packed(ef, k1, y_scr[k1], flip)
        amp = amp_ref[k1]
        once = value * amp
        twice = once * amp
        y_scr[k1] = value
        z_scr[k1] = par[0] * once
        own_ref[k1] = par[3] * twice
        for n, ref, gain in ((0, up_ref, par[1]), (1, down_ref, par[2])):
            cb = tab_ref[2 * n]
            sb = tab_ref[2 * n + 1]
            ca = tab_ref[8, pl.ds(64 * n + k1, 1), :] * gain
            sa = tab_ref[8, pl.ds(64 * n + 32 + k1, 1), :] * gain
            ref[k1] = turn(cb * ca - sb * sa, sb * ca + cb * sa, twice, flip).astype(BF16)
        return carry

    lax.fori_loop(0, OUTER, step, 0, unroll=8)

    @pl.when(me == 0)
    def _():
        u0, u2, a0, a2 = edge_split(edge_gather(y_scr), edge_gather(amp_ref))
        mask, _ = edge_lanes()
        e0 = a0 * u0
        e2 = a2 * u2
        fixed = [par[0] * (e0 + e2)]
        e0 = a0 * e0
        e2 = a2 * e2
        fixed.append(par[3] * (e0 + e2))
        fixed.append(par[1] * turn(tab_ref[4], tab_ref[5], e0 + par[4] * e2, flip))
        fixed.append(par[2] * turn(tab_ref[6], tab_ref[7], e0 + par[5] * e2, flip))

        def put(k1, carry):
            back = lax.rem(INNER - k1, INNER)
            for ref, value in zip((z_scr, own_ref, up_ref, down_ref), fixed):
                value = jnp.where(mask, pltpu.roll(value, back, 1), ref[k1].astype(F32))
                ref[k1] = value.astype(ref.dtype)
            return carry

        lax.fori_loop(0, OUTER, put, 0, unroll=4)

    def inverse(k1, carry):
        z_scr[k1] = apply_packed(ei, k1, z_scr[k1], flip)
        return carry

    lax.fori_loop(0, OUTER, inverse, 0, unroll=8)
    column_first_step(z_scr, y_scr, 1.0)
    give_all(y_scr, msg_scr)
    back = Exchange(me, msg_scr, back_ref, *scratch[16:19])
    back.start()
    ids.wait()
    back.wait()
    weights.wait()


def column_second_kernel(par, in_ref, amp_ref, own_ref, prev_ref, next_ref, ef, ei, back_ref, *scratch):
    y_scr, z_scr, msg_scr = scratch[0:3]
    me = lax.axis_index("strip")
    slot_at = lax.axis_index("tm")
    greet_peers(me, pltpu.get_barrier_semaphore())
    pencils = Exchange(me, in_ref, msg_scr, *scratch[3:6])
    pencils.start()
    pencils.wait()
    take_all(msg_scr, z_scr, False)
    column_first_step(z_scr, y_scr, -1.0)
    flip = flip_lanes(INNER)

    def step(k1, carry):
        value = apply_packed(ef, k1, y_scr[k1], flip)
        y_scr[k1] = value
        z_scr[k1] = par[0] * (value * amp_ref[k1]) + own_ref[k1]
        return carry

    lax.fori_loop(0, OUTER, step, 0, unroll=8)

    @pl.when(me == 0)
    def _():
        spec = edge_gather(y_scr)
        amp = edge_gather(amp_ref)
        u0, u2, a0, a2 = edge_split(spec, amp)
        mask, _ = edge_lanes()
        change = par[0] * (a0 * u0 + a2 * u2 - amp * spec)

        def put(k1, carry):
            back = lax.rem(INNER - k1, INNER)
            z_scr[k1] = z_scr[k1] + jnp.where(mask, pltpu.roll(change, back, 1), 0.0)
            return carry

        lax.fori_loop(0, OUTER, put, 0, unroll=4)

    def inverse(k1, carry):
        moved = jnp.where(slot_at > 0, prev_ref[k1].astype(F32), 0.0)
        moved = moved + jnp.where(slot_at < 3, next_ref[k1].astype(F32), 0.0)
        z_scr[k1] = apply_packed(ei, k1, z_scr[k1] - par[0] * moved, flip)
        return carry

    lax.fori_loop(0, OUTER, inverse, 0, unroll=8)
    column_first_step(z_scr, y_scr, 1.0)
    give_all(y_scr, msg_scr)
    back = Exchange(me, msg_scr, back_ref, *scratch[6:9])
    back.start()
    back.wait()


def route_kernel(t_ref, id_ref, slot_ref, tail_ref):
    row = lax.broadcasted_iota(jnp.int32, (INNER, 2 * INNER), 0)
    col = lax.broadcasted_iota(jnp.int32, (INNER, 2 * INNER), 1)
    tri = jnp.where(jnp.logical_or(row < col, col >= INNER), 1.0, 0.0).astype(BF16)
    peer = lax.broadcasted_iota(jnp.int32, (PEERS, INNER), 0)
    base = jnp.zeros((PEERS, INNER), F32)
    for i in range(0, POINT_ROWS, 8):
        hots = [jnp.where(peer == t_ref[i + j : i + j + 1, :], 1.0, 0.0) for j in range(8)]
        cum = mm(jnp.concatenate(hots, axis=0).astype(BF16), tri)
        for j in range(8):
            part = cum[j * PEERS : (j + 1) * PEERS]
            pos = jnp.sum(hots[j] * (part[:, 0:INNER] + base), axis=0, keepdims=True)
            base = base + part[:, INNER : 2 * INNER]
            slot_ref[i + j : i + j + 1, :] = t_ref[i + j : i + j + 1, :] * SLOTS + pos.astype(jnp.int32)
    batch = 4
    index = lax.broadcasted_iota(jnp.int32, (INNER, batch * INNER), 0)

    def wide(ref, i):
        return jnp.concatenate([ref[pl.ds(i * batch + j, 1), :] for j in range(batch)], axis=1)

    def put(i, acc):
        slot = wide(slot_ref, i)
        ids = wide(id_ref, i)
        r = lax.shift_right_logical(ids, 5)
        ids = lax.shift_right_logical(r, 3) * 256 + (ids & 31) * 8 + (r & 7)
        hot = jnp.where(index == (slot & 127), 1.0, 0.0).astype(BF16)
        line = index == lax.shift_right_logical(slot, 7)
        v = [
            jnp.where(line, d.astype(F32), 0.0).astype(BF16) for d in (lax.shift_right_logical(ids, 6), ids & 63)
        ]
        return acc + mm_nt(jnp.concatenate(v, axis=0), hot)

    acc = lax.fori_loop(0, POINT_ROWS // batch, put, jnp.zeros((2 * INNER, INNER), F32), unroll=2)
    ids = (acc[0:INNER] * 64.0 + acc[INNER : 2 * INNER]).astype(jnp.int32)
    count = base.astype(jnp.int32)
    tail_ref[...] = jnp.zeros_like(tail_ref)
    for s in range(PEERS):
        tail_ref[s, 0:4, :] = ids[4 * s : 4 * s + 4]
        tail_ref[s, 4:5, :] = count[s : s + 1]


def pack_kernel(slot_ref, w_ref, out_ref, w_scr, buf):
    def widen(i, carry):
        rows = pl.ds(pl.multiple_of(i * 64, 64), 64)
        w_scr[rows, :] = w_ref[rows, :].astype(F32)
        return carry

    lax.fori_loop(0, POINT_ROWS * INNER // 64, widen, 0, unroll=2)

    def some(q, carry):
        first = q * 32
        slots = [slot_ref[first + j] for j in range(32)]
        rows = [w_scr[pl.ds(first + j, 1), :] for j in range(32)]
        for j in range(32):
            buf[pl.ds(slots[j], 1), :] = rows[j]
        return carry

    lax.fori_loop(0, POINT_ROWS * INNER // 32, some, 0)

    def narrow(i, carry):
        rows = pl.ds(pl.multiple_of(i * INNER, INNER), INNER)
        out_ref[rows, :] = buf[rows, :].astype(BF16)
        return carry

    lax.fori_loop(0, PEERS * SLOTS // INNER, narrow, 0, unroll=2)


def gather_kernel(sid_ref, in_ref, w_ref, tw, f_ref, a_ref, m_ref, out_ref, g_scr, tiles_ref, z_scr, e_scr):
    row_backward_kernel(False, in_ref, tw, f_ref, a_ref, m_ref, tiles_ref, z_scr, e_scr)

    def source(s, carry):
        def some(q, inner):
            first = s * SLOTS + q * 16
            line = s * ID_STRIDE + q * 16
            ids = [sid_ref[line + j] for j in range(16)]
            rows = [tiles_ref[pl.ds(ids[j], 1), :] for j in range(16)]
            for j in range(16):
                g_scr[pl.ds(first + j, 1), :] = rows[j]
            return inner

        return lax.fori_loop(0, lax.shift_right_logical(sid_ref[s * ID_STRIDE + SLOTS] + 15, 4), some, carry)

    lax.fori_loop(0, PEERS, source, 0)
    ones = jnp.ones((2 * INNER, INNER), BF16)
    lane = lax.broadcasted_iota(jnp.int32, (INNER, INNER), 1)
    diagonal = lane == lax.broadcasted_iota(jnp.int32, (INNER, INNER), 0)
    place = lax.broadcasted_iota(jnp.int32, (1, INNER), 1)

    def total(s, carry):
        count = sid_ref[s * ID_STRIDE + SLOTS]
        w = w_ref[pl.ds(pl.multiple_of(s * SLOTS, SLOTS), SLOTS), :].astype(F32)
        g = g_scr[pl.ds(pl.multiple_of(s * SLOTS, SLOTS), SLOTS), :]
        sums = mm(jnp.concatenate(split(g * w), axis=1), ones)
        for q in range(4):
            got = jnp.where(diagonal, sums[q * INNER : (q + 1) * INNER], 0.0)
            got = jnp.sum(got, axis=0, keepdims=True)
            out_ref[s, q : q + 1, :] = jnp.where(place + q * INNER < count, got, 0.0)
        return carry

    lax.fori_loop(0, PEERS, total, 0, unroll=2)


SIDE_PARTS = 4


def residual_kernel(slot_ref, prec_ref, phase_ref, up_ref, down_ref, out_ref, prev_ref, next_ref, *scratch):
    p_scr, landed, table_scr, res_scr = scratch[0:4]
    me = lax.axis_index("strip")
    side_sems = scratch[10]
    slot_at = lax.axis_index("tm")
    above, below = lax.rem(slot_at + 1, 4), lax.rem(slot_at + 3, 4)
    greet_peers(me, pltpu.get_barrier_semaphore(), ({"tm": above}, {"tm": below}))

    def sides(n):
        src, dst, device = ((up_ref, prev_ref, above), (down_ref, next_ref, below))[n]
        for p in range(SIDE_PARTS):
            rows = pl.ds(p * (OUTER // SIDE_PARTS), OUTER // SIDE_PARTS)
            yield pltpu.make_async_remote_copy(
                src_ref=src.at[rows],
                dst_ref=dst.at[rows],
                send_sem=side_sems.at[0, n, p],
                recv_sem=side_sems.at[1, n, p],
                device_id={"tm": device},
                device_id_type=MESH,
            )

    phases = Exchange(me, phase_ref, landed, *scratch[4:7])
    phases.start()
    phases.wait()

    @pl.when(slot_at < 3)
    def _():
        for side in sides(0):
            side.start()

    @pl.when(slot_at > 0)
    def _():
        for side in sides(1):
            side.start()

    for s in range(PEERS):
        table_scr[4 * s : 4 * s + 4, :] = landed[s]
    high, low = split(table_scr[...])
    table = jnp.concatenate([high, low], axis=0)
    batch = 4
    index = lax.broadcasted_iota(jnp.int32, (INNER, batch * INNER), 0)

    def wide(ref, i):
        return jnp.concatenate([ref[pl.ds(i * batch + j, 1), :] for j in range(batch)], axis=1)

    def pick(i, carry):
        slot = wide(slot_ref, i)
        hot = jnp.where(index == (slot & 127), 1.0, 0.0).astype(BF16)
        v = mm(table, hot)
        v = v[0:INNER] + v[INNER : 2 * INNER]
        got = jnp.sum(jnp.where(index == lax.shift_right_logical(slot, 7), v, 0.0), axis=0, keepdims=True)
        for j in range(batch):
            p_scr[pl.ds(i * batch + j, 1), :] = got[:, j * INNER : (j + 1) * INNER]
        return carry

    lax.fori_loop(0, POINT_ROWS // batch, pick, 0, unroll=2)
    row = lax.broadcasted_iota(jnp.int32, (INNER, INNER), 0)
    lane = lax.broadcasted_iota(jnp.int32, (INNER, INNER), 1)
    same = jnp.where((row < HALF) == (lane < HALF), 1.0, 0.0).astype(BF16)
    prec = prec_ref[...]
    phase = p_scr[...]

    def total(value):
        return sum(mm(p, same) for p in reversed(split_into(value, 3)))

    p_scr[...] = prec * (phase - total(prec * phase) / total(prec))

    def put(i, acc):
        slot = wide(slot_ref, i)
        hot = jnp.where(index == (slot & 127), 1.0, 0.0).astype(BF16)
        v = jnp.where(index == lax.shift_right_logical(slot, 7), wide(p_scr, i), 0.0)
        vh, vl = split(v)
        return acc + mm_nt(jnp.concatenate([vh, vl], axis=0), hot)

    acc = lax.fori_loop(0, POINT_ROWS // batch, put, jnp.zeros((2 * INNER, INNER), F32), unroll=2)
    acc = acc[0:INNER] + acc[INNER : 2 * INNER]
    for s in range(PEERS):
        res_scr[s] = acc[4 * s : 4 * s + 4]
    residuals = Exchange(me, res_scr, out_ref, *scratch[7:10])
    residuals.start()
    residuals.wait()

    @pl.when(slot_at < 3)
    def _():
        for up, down in zip(sides(0), sides(1)):
            up.wait_send()
            down.wait_recv()

    @pl.when(slot_at > 0)
    def _():
        for up, down in zip(sides(0), sides(1)):
            up.wait_recv()
            down.wait_send()


COPIES = 8


def scatter_kernel(
    sid_ref, r_ref, w_ref, tw, f_ref, a_ref, m_ref, out_ref, rt_scr, u_scr, y_scr, e_scr, *accs
):
    def clear(i, carry):
        rows = pl.ds(pl.multiple_of(i * 64, 64), 64)
        for acc in accs:
            acc[rows, :] = jnp.zeros((64, INNER), F32)
        return carry

    lax.fori_loop(0, SIDE // 64, clear, 0)
    rt_scr[...] = r_ref[...].T
    lane = lax.broadcasted_iota(jnp.int32, (INNER, INNER), 1)
    row = lax.broadcasted_iota(jnp.int32, (INNER, INNER), 0)

    def scaled(s, carry):
        for q in range(4):
            col = jnp.sum(jnp.where(lane == s * 4 + q, rt_scr[...], 0.0), axis=1, keepdims=True)
            rows = pl.ds(pl.multiple_of(s * SLOTS + q * INNER, INNER), INNER)
            used = row + q * INNER < sid_ref[s * ID_STRIDE + SLOTS]
            u_scr[rows, :] = jnp.where(used, w_ref[rows, :].astype(F32) * col, 0.0)
        return carry

    lax.fori_loop(0, PEERS, scaled, 0, unroll=2)

    def source(s, carry):
        def some(q, inner):
            first = s * SLOTS + q * 16
            line = s * ID_STRIDE + q * 16
            ids = [sid_ref[line + j] for j in range(16)]
            us = [u_scr[pl.ds(first + j, 1), :] for j in range(16)]
            for h in range(0, 16, COPIES):
                sums = [accs[j][pl.ds(ids[h + j], 1), :] + us[h + j] for j in range(COPIES)]
                for j in range(COPIES):
                    accs[j][pl.ds(ids[h + j], 1), :] = sums[j]
            return inner

        return lax.fori_loop(0, lax.shift_right_logical(sid_ref[s * ID_STRIDE + SLOTS] + 15, 4), some, carry)

    lax.fori_loop(0, PEERS, source, 0)

    def add(i, carry):
        rows = pl.ds(pl.multiple_of(i * 64, 64), 64)
        total = accs[0][rows, :]
        for acc in accs[1:]:
            total = total + acc[rows, :]
        accs[0][rows, :] = total
        return carry

    lax.fori_loop(0, SIDE // 64, add, 0)
    row_forward_kernel(True, False, accs[0], tw, f_ref, a_ref, m_ref, out_ref, y_scr, e_scr)


def call(kernel, name, out_shapes, args, smem=0, scratch=(), any_args=(), any_outs=(), smem_outs=(), collective_id=None):
    spaces = [pltpu.SMEM if i < smem else pl.ANY if i in any_args else pltpu.VMEM for i in range(len(args))]
    outs = [pl.ANY if i in any_outs else pltpu.SMEM if i in smem_outs else pltpu.VMEM for i in range(len(out_shapes))]
    remote = dict(collective_id=collective_id, has_side_effects=True) if collective_id is not None else {}
    return pl.pallas_call(
        kernel,
        out_shape=out_shapes,
        in_specs=[pl.BlockSpec(memory_space=space) for space in spaces],
        out_specs=[pl.BlockSpec(memory_space=space) for space in outs],
        scratch_shapes=list(scratch),
        compiler_params=pltpu.CompilerParams(vmem_limit_bytes=VMEM_BYTES, **remote),
        cost_estimate=pl.CostEstimate(flops=1024, bytes_accessed=1024, transcendentals=0),
        name=name,
    )(*args)


def shape(dims, dtype=F32):
    return jax.ShapeDtypeStruct(dims, dtype)


PENCILS = (PEERS, INNER, INNER)
MESSAGES = (PEERS, INNER + TAIL, INNER)


def row_backward(pencils, base, tables):
    final = base is not None
    args = [pencils] + ([base] if final else []) + tables
    return call(
        lambda *refs: row_backward_kernel(final, *refs),
        "row_backward",
        [shape((INNER, SIDE) if final else (SIDE, INNER))],
        args,
        scratch=[pltpu.VMEM((15 * INNER, 2 * INNER), F32), pltpu.VMEM((2, INNER, INNER), F32)],
    )[0]


def tables_kernel(scale, rate, wind, prior, tab_ref, amp_ref, par_ref):
    strip = lax.axis_index("strip")
    live = (lax.axis_index("tm") < 3).astype(F32)
    k1 = (strip // 2).astype(F32)
    even = strip % 2 == 0
    row = lax.broadcasted_iota(jnp.int32, (INNER, INNER), 0)
    lane = lax.broadcasted_iota(jnp.int32, (INNER, INNER), 1)
    line = row.astype(F32)
    j = (lane & (HALF - 1)).astype(F32)
    cols = jnp.where(even, k1 + OUTER * j, k1 + OUTER * (INNER - 1.0 - j))
    cols = jnp.where(strip == 1, 16.0 + OUTER * j, cols)
    winds = ((wind[0, 0].astype(F32), wind[0, 1].astype(F32)), (prior[1], prior[2]))

    def cosine(turns):
        turns = turns - SIDE * jnp.floor(turns * (1.0 / SIDE))
        return jnp.cos(turns * (2.0 * math.pi / SIDE))

    small = jnp.zeros((INNER, INNER), F32)
    for kind in range(4):
        wind_row, wind_col = winds[kind // 2]
        quarter = (0.0, 3.0 * SIDE / 4, 0.0, SIDE / 4.0)[kind]
        base = OUTER * line * wind_row + quarter
        tab_ref[kind] = cosine(base + cols * wind_col)
        tab_ref[4 + kind] = cosine(base + j * wind_row)
        turns = (row & (OUTER - 1)).astype(F32) * wind_row + quarter
        small = jnp.where(lax.shift_right_logical(row, 5) == kind, turns, small)
    tab_ref[8] = cosine(small)

    fold = jnp.where(even, k1 + OUTER * j, OUTER - k1 + OUTER * j)
    fold = jnp.where(strip == 1, 16.0 + OUTER * j, fold)
    fold = jnp.where(jnp.logical_and(strip == 0, lane == HALF), SIDE / 2.0, fold)
    fold = fold * fold

    def step(k, carry):
        kr = line * OUTER + k.astype(F32)
        kr = jnp.minimum(kr, SIDE - kr)
        radius = (kr * kr + fold) / (KZERO * KZERO)
        amp_ref[k] = SIDE / (2.0 * KZERO) * jnp.exp((-11.0 / 12.0) * jnp.log(1.0 + radius))
        return carry

    lax.fori_loop(0, OUTER, step, 0, unroll=2)
    norm = scale[0] / (SIDE * SIDE)
    mine = rate[0] * live
    par_ref[0] = norm
    par_ref[1] = mine * scale[0]
    par_ref[2] = prior[0] * scale[0]
    par_ref[3] = (mine + prior[0]) * scale[0] * norm
    par_ref[4] = 1.0 - 2.0 * (wind[0, 1] & 1).astype(F32)
    par_ref[5] = 1.0 - 2.0 * (prior[2].astype(jnp.int32) & 1).astype(F32)
    par_ref[6] = 0.0
    par_ref[7] = 0.0


def const(*tables):
    return [jnp.asarray(t) for t in tables]


def local(
    screen_vec,
    prior_scale,
    flow_weight,
    wind,
    pierce_point_strip,
    pierce_block,
    pierce_weights,
    noise_prec,
):
    fwd, inv, first, first_inv, mid, mid_inv, twiddle = row_tables()
    row_fwd_tables = const(twiddle, pieces(fwd, 2), pieces(first, 2), pieces(mid, 2))
    row_fine_tables = const(twiddle, pieces(fwd, 3), pieces(first, 3), pieces(mid, 3))
    row_inv_tables = const(twiddle, pieces(inv, 2), pieces(first_inv, 2), pieces(mid_inv, 2))
    col_fwd, col_inv = column_tables()
    col_fine_tables = const(pieces(col_fwd, 3), pieces(col_inv, 2))
    col_tables = const(pieces(col_fwd, 2), pieces(col_inv, 2))

    x = screen_vec[0]
    weights = pierce_weights[0].reshape(POINT_ROWS * INNER, INNER)
    target = pierce_point_strip.reshape(POINT_ROWS, INNER)
    block = pierce_block.reshape(POINT_ROWS, INNER)
    prec = noise_prec.reshape(POINT_ROWS, INNER)

    mine = jnp.concatenate([flow_weight, wind[0].astype(F32)])
    prior = lax.ppermute(mine, "tm", [(i, i + 1) for i in range(lax.axis_size("tm") - 1)])
    slots, ids = call(
        route_kernel,
        "route",
        [shape((POINT_ROWS, INNER), jnp.int32), shape((PEERS, ID_ROWS, INNER), jnp.int32)],
        [target, block],
    )
    ids, prior, prec = lax.optimization_barrier((ids, prior, prec))
    sent = call(
        pack_kernel,
        "pack",
        [shape((PEERS * SLOTS, INNER), BF16)],
        [slots.reshape(-1), weights],
        smem=1,
        scratch=[pltpu.VMEM((POINT_ROWS * INNER, INNER), F32), pltpu.VMEM((PEERS * SLOTS, INNER), F32)],
    )[0]

    spectral = [pltpu.VMEM(PENCILS, F32), pltpu.VMEM(PENCILS, F32)]
    rows = [pltpu.VMEM((15 * INNER, 2 * INNER), F32), pltpu.VMEM((2, INNER, INNER), F32)]
    message = shape(MESSAGES, BF16)
    back, own, up, down, arrived, here_ids, amp, par = call(
        column_first_kernel,
        "column_first",
        [
            message,
            shape(PENCILS),
            shape(PENCILS, BF16),
            shape(PENCILS, BF16),
            shape((PEERS, SLOTS, INNER), BF16),
            shape((PEERS, ID_ROWS, INNER), jnp.int32),
            shape(PENCILS),
            shape((8,)),
        ],
        [prior_scale, flow_weight, wind, prior, x]
        + row_fine_tables
        + col_fine_tables
        + [sent.reshape(PEERS, SLOTS, INNER), ids],
        smem=4,
        any_args=(11, 12),
        any_outs=(0, 4, 5),
        smem_outs=(7,),
        collective_id=3,
        scratch=spectral
        + [pltpu.VMEM(MESSAGES, BF16), pltpu.VMEM(MESSAGES, BF16), pltpu.VMEM((9, INNER, INNER), F32)]
        + rows
        + exchange_sems() * 4,
    )
    here = arrived.reshape(PEERS * SLOTS, INNER)
    here_ids = here_ids.reshape(PEERS * ID_STRIDE)

    points = pltpu.VMEM((PEERS * SLOTS, INNER), F32)
    screen = pltpu.VMEM((SIDE, INNER), F32)
    small = (PEERS, 4, INNER)
    phase = call(
        gather_kernel,
        "gather",
        [shape(small)],
        [here_ids, back, here] + row_inv_tables,
        smem=1,
        scratch=[points, screen] + rows,
    )[0]
    resid, from_prev, from_next = call(
        residual_kernel,
        "residual",
        [shape(small), shape(PENCILS, BF16), shape(PENCILS, BF16)],
        [slots, prec, phase, up, down],
        any_args=(3, 4),
        any_outs=(1, 2),
        collective_id=2,
        scratch=[
            pltpu.VMEM((POINT_ROWS, INNER), F32),
            pltpu.VMEM(small, F32),
            pltpu.VMEM((INNER, INNER), F32),
            pltpu.VMEM(small, F32),
        ]
        + exchange_sems()
        + exchange_sems()
        + [pltpu.SemaphoreType.DMA((2, 2, SIDE_PARTS))],
    )
    pencils = call(
        scatter_kernel,
        "scatter",
        [message],
        [here_ids, resid.reshape(INNER, INNER), here] + row_fwd_tables,
        smem=1,
        scratch=[pltpu.VMEM((INNER, INNER), F32), points] + rows + [screen] * COPIES,
    )[0]
    out_pencils = call(
        column_second_kernel,
        "column_second",
        [message],
        [par, pencils, amp, own, from_prev, from_next] + col_tables,
        smem=1,
        any_args=(1,),
        any_outs=(0,),
        collective_id=1,
        scratch=spectral + [pltpu.VMEM(MESSAGES, BF16)] + exchange_sems() + exchange_sems(),
    )[0]
    return row_backward(out_pencils, x, row_inv_tables)[None]


def solution(mesh):
    in_specs = (
        P("tm", "strip", None),
        P("tm"),
        P("tm"),
        P("tm", None),
        P("tm", "strip", None, None),
        P("tm", "strip", None),
        P("tm", "strip", None, None),
        P("tm", "strip", None),
    )
    out_specs = P("tm", "strip", None)
    return jax.shard_map(local, mesh=mesh, in_specs=in_specs, out_specs=out_specs, check_vma=False)
```

```python
import math

import jax
import jax.numpy as jnp
import ml_dtypes
import numpy as np
from jax import lax
from jax.experimental import pallas as pl
from jax.experimental.pallas import tpu as pltpu
from jax.sharding import PartitionSpec as P

KZERO = 2.0
SIDE = 4096
OUTER = 32
INNER = 128
HALF = 64
PEERS = 32
SLOTS = 512
POINT_ROWS = 64
TAIL = 16
ID_ROWS = 8
ID_STRIDE = ID_ROWS * 128
VMEM_BYTES = 56 * 1024 * 1024
F32 = jnp.float32
BF16 = jnp.bfloat16


def pieces(table, count):
    rest = np.asarray(table, np.float64)
    out = []
    for _ in range(count):
        out.append(rest.astype(np.float32).astype(ml_dtypes.bfloat16))
        rest = rest - out[-1].astype(np.float64)
    return np.stack(out)


def row_tables():
    b = np.arange(INNER)[:, None]
    j = np.arange(HALF)[None, :]
    theta = [2 * np.pi * ((b * j) % INNER) / INNER, 2 * np.pi * ((b * (INNER - 1 - j)) % INNER) / INNER]
    forward = []
    backward = []
    for t in theta:
        forward.append(np.concatenate([np.cos(t), -np.sin(t)], axis=1))
        forward.append(np.concatenate([np.sin(t), np.cos(t)], axis=1))
        backward.append(np.concatenate([np.cos(t).T, np.sin(t).T], axis=1))
        backward.append(np.concatenate([-np.sin(t).T, np.cos(t).T], axis=1))
    fwd = np.concatenate(
        [np.concatenate([forward[0], forward[1]], axis=0), np.concatenate([forward[2], forward[3]], axis=0)], axis=1
    )
    inv = np.concatenate(backward, axis=0)
    sign = np.where(np.arange(INNER) % 2 == 0, 1.0, -1.0)
    t0 = theta[0]
    first = np.concatenate([np.cos(t0), -np.sin(t0)], axis=1)
    first[:, HALF] = sign
    first_inv = np.concatenate([2 * np.cos(t0).T, -2 * np.sin(t0).T], axis=0)
    first_inv[0, :] = 1.0
    first_inv[HALF, :] = sign
    t16 = 2 * np.pi * ((b * (16 + 32 * j)) % SIDE) / SIDE
    mid = np.concatenate([np.cos(t16), -np.sin(t16)], axis=1)
    mid_inv = np.concatenate([2 * np.cos(t16).T, -2 * np.sin(t16).T], axis=0)
    k1 = np.arange(16)[:, None]
    tw = 2 * np.pi * (k1 * np.arange(INNER)[None, :]) / SIDE
    twiddle = np.stack([np.cos(tw), np.sin(tw)]).astype(np.float32)
    return fwd, inv, first, first_inv, mid, mid_inv, twiddle


def column_tables():
    k1 = np.arange(OUTER)[:, None, None]
    k2 = np.arange(INNER)[None, :, None]
    r = np.arange(INNER)[None, None, :]
    theta = 2 * np.pi * (((k1 + OUTER * k2) * r) % SIDE) / SIDE
    fwd = np.concatenate([np.cos(theta), -np.sin(theta)], axis=1)
    theta = theta.transpose(0, 2, 1)
    inv = np.concatenate([np.cos(theta), np.sin(theta)], axis=1)
    return fwd, inv


def split(value):
    high = value.astype(BF16)
    return high, (value - high.astype(F32)).astype(BF16)


def mm(left, right):
    return lax.dot_general(left, right, (((1,), (0,)), ((), ())), preferred_element_type=F32)


def mm_nt(left, right):
    return lax.dot_general(left, right, (((1,), (1,)), ((), ())), preferred_element_type=F32)


def split_into(value, count):
    parts = []
    for i in range(count):
        parts.append(value.astype(BF16))
        if i + 1 < count:
            value = value - parts[-1].astype(F32)
    return parts


def data_by_table(value, tables):
    count = len(tables)
    parts = split_into(value, count)
    total = None
    for order in reversed(range(count)):
        for i in range(order + 1):
            term = mm(parts[i], tables[order - i])
            total = term if total is None else total + term
    return total


def table_by_data(tables, value):
    parts = split_into(value, len(tables))
    left = jnp.concatenate(tables[0:2], axis=1)
    right = jnp.concatenate(parts[0:2], axis=1)
    r = mm(left, jnp.concatenate([right, right], axis=0))
    total = r[:, INNER : 2 * INNER] + r[:, 0:INNER]
    if len(tables) == 3:
        left = jnp.concatenate([tables[0], tables[2]], axis=1)
        total = total + mm(left, jnp.concatenate([parts[2], parts[0]], axis=0))
    return total


def every(ref):
    return [ref[i] for i in range(ref.shape[0])]


def c_mul(value, factor):
    re, im = value
    c, s = factor.real, factor.imag
    if im is None:
        return (re * c, re * s)
    return (re * c - im * s, re * s + im * c)


def real_forward(xs):
    n = len(xs)
    if n == 2:
        return [(xs[0] + xs[1], None), (xs[0] - xs[1], None)]
    even, odd = real_forward(xs[0::2]), real_forward(xs[1::2])
    m = n // 2
    out = [None] * (m + 1)
    for k in range(m // 2 + 1):
        if k == 0:
            out[0] = (even[0][0] + odd[0][0], None)
            out[m] = (even[0][0] - odd[0][0], None)
        elif 2 * k == m:
            out[k] = (even[k][0], -odd[k][0])
        else:
            tr, ti = c_mul(odd[k], complex(math.cos(2 * math.pi * k / n), -math.sin(2 * math.pi * k / n)))
            er, ei = even[k]
            out[k] = (er + tr, ei + ti)
            out[m - k] = (er - tr, ti - ei)
    return out


def real_backward(spec):
    n = 2 * (len(spec) - 1)
    if n == 2:
        return [spec[0][0] + spec[1][0], spec[0][0] - spec[1][0]]
    m = n // 2
    even, odd = [], []
    for k in range(m // 2 + 1):
        if k == 0:
            even.append((spec[0][0] + spec[m][0], None))
            odd.append((spec[0][0] - spec[m][0], None))
        elif 2 * k == m:
            even.append((2.0 * spec[k][0], None))
            odd.append((-2.0 * spec[k][1], None))
        else:
            ar, ai = spec[k]
            br, bi = spec[m - k]
            even.append((ar + br, ai - bi))
            odd.append(c_mul((ar - br, ai + bi), complex(math.cos(2 * math.pi * k / n), math.sin(2 * math.pi * k / n))))
    xe, xo = real_backward(even), real_backward(odd)
    out = [None] * n
    out[0::2] = xe
    out[1::2] = xo
    return out


def packed_fft(xs, sign, flip):
    n = len(xs)
    if n == 1:
        return xs
    even, odd = packed_fft(xs[0::2], sign, flip), packed_fft(xs[1::2], sign, flip)
    out = [None] * n
    for k in range(n // 2):
        t = odd[k]
        if k:
            turned = pltpu.roll(t, HALF, 1) * flip
            c, s = math.cos(2 * math.pi * k / n), sign * math.sin(2 * math.pi * k / n)
            t = (-s) * turned if 4 * k == n else c * t - s * turned
        out[k] = even[k] + t
        out[k + n // 2] = even[k] - t
    return out


def flip_lanes(rows):
    lane = lax.broadcasted_iota(jnp.int32, (rows, INNER), 1)
    return jnp.where(lane < HALF, 1.0, -1.0).astype(F32)


def put_message(ref, d, value, fine):
    lane = lax.broadcasted_iota(jnp.int32, (INNER, INNER), 1)
    high = value.astype(BF16)
    ref[d, 0:INNER, :] = high
    rest = value - high.astype(F32)
    if fine:
        third = rest - rest.astype(BF16).astype(F32)
        rest = jnp.where((lane & (HALF - 1)) == 7, pltpu.roll(third, 7, 1), rest)
    rest = jnp.where(lane < 8, rest, pltpu.roll(rest, 72, 1))
    rest = jnp.where(lane < 16, rest, 0.0)
    total = rest[0:16]
    for g in range(1, 8):
        total = total + pltpu.roll(rest[16 * g : 16 * g + 16], 16 * g, 1)
    ref[d, INNER : INNER + TAIL, :] = total.astype(BF16)


def get_message(ref, d, fine):
    lane = lax.broadcasted_iota(jnp.int32, (INNER, INNER), 1)
    packed = ref[d, INNER : INNER + TAIL, :].astype(F32)
    rest = jnp.concatenate([packed] + [pltpu.roll(packed, INNER - 16 * g, 1) for g in range(1, 8)], axis=0)
    rest = jnp.where(lane < 8, rest, pltpu.roll(rest, 56, 1))
    column = lane & (HALF - 1)
    if fine:
        third = jnp.where(column == 0, pltpu.roll(rest, INNER - 7, 1), 0.0)
        rest = jnp.where(column < 7, rest, 0.0) + third
    else:
        rest = jnp.where(column < 8, rest, 0.0)
    return ref[d, 0:INNER, :].astype(F32) + rest


def row_forward_kernel(tiled, fine, x_ref, tw_ref, f_ref, a_ref, m_ref, out_ref, y_scr, e_scr):
    def slab(g, carry):
        if tiled:
            xs = [x_ref[pl.ds(pl.multiple_of(g * 256 + a * 8, 8), 8), :] for a in range(OUTER)]
        else:
            xs = [x_ref[pl.ds(pl.multiple_of(g * 8, 8), 8), a * INNER : (a + 1) * INNER] for a in range(OUTER)]
        ys = real_forward(xs)
        rows = pl.ds(pl.multiple_of(g * 8, 8), 8)
        e_scr[0, rows, :] = ys[0][0]
        e_scr[1, rows, :] = ys[16][0]
        for k in range(1, 16):
            c = tw_ref[0, k : k + 1, :]
            s = tw_ref[1, k : k + 1, :]
            re, im = ys[k]
            base = pl.ds(pl.multiple_of((k - 1) * INNER + g * 8, 8), 8)
            y_scr[base, 0:INNER] = re * c + im * s
            y_scr[base, INNER : 2 * INNER] = im * c - re * s
        return carry

    lax.fori_loop(0, 16, slab, 0, unroll=2)
    put_message(out_ref, 0, data_by_table(e_scr[0], every(a_ref)), fine)
    put_message(out_ref, 1, data_by_table(e_scr[1], every(m_ref)), fine)

    def group(q, carry):
        v = data_by_table(y_scr[pl.ds(pl.multiple_of(q * 384, 8), 384), :], every(f_ref))
        for i in range(3):
            rows = v[i * INNER : (i + 1) * INNER]
            put_message(out_ref, 2 + 2 * (3 * q + i), rows[:, 0:INNER], fine)
            put_message(out_ref, 3 + 2 * (3 * q + i), rows[:, INNER : 2 * INNER], fine)
        return carry

    lax.fori_loop(0, 5, group, 0)


def row_backward_kernel(final, *refs):
    if final:
        in_ref, base_ref, tw_ref, f_ref, a_ref, m_ref, out_ref, z_scr, e_scr = refs
    else:
        in_ref, tw_ref, f_ref, a_ref, m_ref, out_ref, z_scr, e_scr = refs
    e_scr[0] = data_by_table(get_message(in_ref, 0, False), every(a_ref))
    e_scr[1] = data_by_table(get_message(in_ref, 1, False), every(m_ref))

    def group(q, carry):
        parts = []
        for i in range(3):
            k = 3 * q + i
            parts.append(jnp.concatenate([get_message(in_ref, 2 + 2 * k + h, False) for h in range(2)], axis=1))
        v = jnp.concatenate(parts, axis=0)
        z_scr[pl.ds(pl.multiple_of(q * 384, 8), 384), :] = data_by_table(v, every(f_ref))
        return carry

    lax.fori_loop(0, 5, group, 0)

    def slab(g, carry):
        rows = pl.ds(pl.multiple_of(g * 8, 8), 8)
        spec = [(e_scr[0, rows, :], None)]
        for k in range(1, 16):
            c = tw_ref[0, k : k + 1, :]
            s = tw_ref[1, k : k + 1, :]
            base = pl.ds(pl.multiple_of((k - 1) * INNER + g * 8, 8), 8)
            re = z_scr[base, 0:INNER]
            im = z_scr[base, INNER : 2 * INNER]
            spec.append((re * c - im * s, im * c + re * s))
        spec.append((e_scr[1, rows, :], None))
        xs = real_backward(spec)
        for a in range(OUTER):
            if final:
                cols = slice(a * INNER, (a + 1) * INNER)
                out_ref[rows, cols] = base_ref[rows, cols] + xs[a]
            else:
                out_ref[pl.ds(pl.multiple_of(g * 256 + a * 8, 8), 8), :] = xs[a]
        return carry

    lax.fori_loop(0, 16, slab, 0, unroll=2)


def take_all(in_ref, scr, fine):
    def step(s, carry):
        scr[s] = get_message(in_ref, s, fine)
        return carry

    lax.fori_loop(0, OUTER, step, 0, unroll=4)


def give_all(scr, out_ref):
    def step(s, carry):
        put_message(out_ref, s, scr[s], False)
        return carry

    lax.fori_loop(0, OUTER, step, 0, unroll=4)


def column_first_step(in_ref, y_scr, sign):
    flip = flip_lanes(8)

    def slab(g, carry):
        rows = pl.ds(pl.multiple_of(g * 8, 8), 8)
        ys = packed_fft([in_ref[s, rows, :] for s in range(OUTER)], sign, flip)
        for k in range(OUTER):
            y_scr[k, rows, :] = ys[k]
        return carry

    lax.fori_loop(0, 16, slab, 0, unroll=2)


def apply_packed(e_ref, k1, value, flip):
    r = table_by_data([e_ref[i, k1] for i in range(e_ref.shape[0])], value)
    return r[0:INNER] - pltpu.roll(r[INNER : 2 * INNER], HALF, 1) * flip


MESH = pl.DeviceIdType.MESH


def greet_peers(me, barrier, extra=()):
    def greet(i, carry):
        pl.semaphore_signal(barrier, inc=1, device_id={"strip": lax.rem(me + i, PEERS)}, device_id_type=MESH)
        return carry

    lax.fori_loop(1, PEERS, greet, 0)
    for device in extra:
        pl.semaphore_signal(barrier, inc=1, device_id=device, device_id_type=MESH)
    pl.semaphore_wait(barrier, PEERS - 1 + len(extra))


class Exchange:
    def __init__(self, me, in_ref, out_ref, send_sem, recv_sem, own_sem):
        self.me, self.in_ref, self.out_ref = me, in_ref, out_ref
        self.send_sem, self.recv_sem = send_sem, recv_sem
        self.own = pltpu.make_async_copy(in_ref.at[me], out_ref.at[me], own_sem)

    def copy(self, peer, send, source):
        return pltpu.make_async_remote_copy(
            src_ref=self.in_ref.at[peer],
            dst_ref=self.out_ref.at[source],
            send_sem=self.send_sem.at[send],
            recv_sem=self.recv_sem.at[source],
            device_id={"strip": peer},
            device_id_type=MESH,
        )

    def peer(self, i):
        return lax.rem(self.me + 1 + i, PEERS)

    def source(self, i):
        return lax.rem(self.me + PEERS - 1 - i, PEERS)

    def send(self, i):
        self.copy(self.peer(i), i, self.me).start()

    def wait_source(self, i):
        self.copy(self.peer(i), i, self.source(i)).wait_recv()

    def wait_sends(self):
        def step(i, carry):
            self.copy(self.peer(i), i, self.me).wait_send()
            return carry

        lax.fori_loop(0, PEERS - 1, step, 0)

    def start(self, first=0, last=PEERS - 1):
        def step(i, carry):
            self.copy(self.peer(i), i, self.me).start()
            return carry

        lax.fori_loop(first, last, step, 0)
        if first == 0:
            self.own.start()

    def wait(self):
        def step(i, carry):
            self.wait_source(i)
            return carry

        self.own.wait()
        lax.fori_loop(0, PEERS - 1, step, 0)
        self.wait_sends()


def exchange_sems():
    return [pltpu.SemaphoreType.DMA((PEERS,)), pltpu.SemaphoreType.DMA((PEERS,)), pltpu.SemaphoreType.DMA]


def edge_lanes():
    lane = lax.broadcasted_iota(jnp.int32, (INNER, INNER), 1)
    return jnp.logical_or(lane == 0, lane == HALF), lane < HALF


def edge_gather(ref):
    mask, _ = edge_lanes()

    def step(k1, acc):
        return acc + pltpu.roll(jnp.where(mask, ref[k1], 0.0), k1, 1)

    return lax.fori_loop(0, OUTER, step, jnp.zeros((INNER, INNER), F32), unroll=4)


def edge_split(spec, amp):
    i = lax.broadcasted_iota(jnp.int32, (INNER, INNER), 0)
    j = lax.broadcasted_iota(jnp.int32, (INNER, INNER), 1)
    one = jnp.ones((INNER, INNER), F32)
    none = jnp.zeros((INNER, INNER), F32)
    rows = jnp.where(i + j == INNER - 1, one, none).astype(BF16)
    rows0 = jnp.where(((i + j) & (INNER - 1)) == 0, one, none).astype(BF16)
    sign = jnp.where(j < HALF, one, -one)
    col = j & (HALF - 1)
    same = (i < HALF) == (j < HALF)
    lanes = jnp.where(
        jnp.logical_and(same, jnp.logical_and(col > 0, col + (i & (HALF - 1)) == OUTER)), sign, none
    ).astype(BF16)
    lanes0 = jnp.where(jnp.logical_and(i == j, col == 0), sign, none).astype(BF16)

    def move(left, value, right):
        value = sum(mm(left, p) for p in reversed(split_into(value, 3)))
        return sum(mm(p, right) for p in reversed(split_into(value, 3)))

    rev = move(rows, spec, lanes) + move(rows0, spec, lanes0)
    swapped = pltpu.roll(amp, HALF, 1)
    _, left = edge_lanes()
    a0 = jnp.where(left, amp, swapped)
    a2 = jnp.where(left, swapped, amp)
    return 0.5 * (spec + rev), 0.5 * (spec - rev), a0, a2


def turn(c, s, value, flip):
    return c * value + s * (pltpu.roll(value, HALF, 1) * flip)


EARLY = 8
MIDDLE = 18


def first_kernel(
    scale, rate, wind, prior, x_ref, tw, f_ref, a_ref, m_ref, fi_ref, ai_ref, mi_ref, ef, ei, slot_ref, prec_ref,
    sent_ref, ids_ref,
    own_ref, here_ref, amp_ref, resid_ref, par, here_ids_ref, prev_ref, next_ref, *scratch,
):
    y_scr, z_scr, msg_scr, land_scr, back_scr, tab_ref, row_scr, row_edge = scratch[0:8]
    up_ref, down_ref, tiles_scr, g_scr, phase_scr, landed, p_scr, table_scr, res_scr = scratch[8:17]
    sid_scr, sid_sem, side_sems = scratch[17:20]
    sems = scratch[20:]
    me = lax.axis_index("strip")
    slot_at = lax.axis_index("tm")
    above, below = lax.rem(slot_at + 1, 4), lax.rem(slot_at + 3, 4)
    greet_peers(me, pltpu.get_barrier_semaphore(), ({"tm": above}, {"tm": below}))
    ids = Exchange(me, ids_ref, here_ids_ref, *sems[0:3])
    weights = Exchange(me, sent_ref, here_ref, *sems[3:6])
    pencils = Exchange(me, msg_scr, land_scr, *sems[6:9])
    back = Exchange(me, msg_scr, back_scr, *sems[9:12])
    phases = Exchange(me, phase_scr, landed, *sems[12:15])
    residuals = Exchange(me, res_scr, resid_ref, *sems[15:18])
    ids.start()
    weights.start(0, EARLY)
    row_forward_kernel(False, True, x_ref, tw, f_ref, a_ref, m_ref, msg_scr, row_scr, row_edge)
    pencils.start()
    weights.start(EARLY, MIDDLE)
    tables_kernel(scale, rate, wind, prior, tab_ref, amp_ref, par)
    pencils.wait()
    take_all(land_scr, z_scr, True)
    column_first_step(z_scr, y_scr, -1.0)
    flip = flip_lanes(INNER)

    def step(k1, carry):
        value = apply_packed(ef, k1, y_scr[k1], flip)
        amp = amp_ref[k1]
        once = value * amp
        twice = once * amp
        y_scr[k1] = value
        z_scr[k1] = par[0] * once
        own_ref[k1] = par[3] * twice
        for n, ref, gain in ((0, up_ref, par[1]), (1, down_ref, par[2])):
            cb = tab_ref[2 * n]
            sb = tab_ref[2 * n + 1]
            ca = tab_ref[8, pl.ds(64 * n + k1, 1), :] * gain
            sa = tab_ref[8, pl.ds(64 * n + 32 + k1, 1), :] * gain
            ref[k1] = turn(cb * ca - sb * sa, sb * ca + cb * sa, twice, flip).astype(BF16)
        return carry

    lax.fori_loop(0, OUTER, step, 0, unroll=8)

    @pl.when(me == 0)
    def _():
        u0, u2, a0, a2 = edge_split(edge_gather(y_scr), edge_gather(amp_ref))
        mask, _ = edge_lanes()
        e0 = a0 * u0
        e2 = a2 * u2
        fixed = [par[0] * (e0 + e2)]
        e0 = a0 * e0
        e2 = a2 * e2
        fixed.append(par[3] * (e0 + e2))
        fixed.append(par[1] * turn(tab_ref[4], tab_ref[5], e0 + par[4] * e2, flip))
        fixed.append(par[2] * turn(tab_ref[6], tab_ref[7], e0 + par[5] * e2, flip))

        def put(k1, carry):
            back = lax.rem(INNER - k1, INNER)
            for ref, value in zip((z_scr, own_ref, up_ref, down_ref), fixed):
                value = jnp.where(mask, pltpu.roll(value, back, 1), ref[k1].astype(F32))
                ref[k1] = value.astype(ref.dtype)
            return carry

        lax.fori_loop(0, OUTER, put, 0, unroll=4)

    def inverse(k1, carry):
        z_scr[k1] = apply_packed(ei, k1, z_scr[k1], flip)
        return carry

    lax.fori_loop(0, OUTER, inverse, 0, unroll=8)
    column_first_step(z_scr, y_scr, 1.0)
    give_all(y_scr, msg_scr)
    back.start()
    weights.start(MIDDLE, PEERS - 1)
    ids.wait()
    fetch = pltpu.make_async_copy(here_ids_ref, sid_scr, sid_sem)
    fetch.start()
    back.wait()
    row_backward_kernel(False, back_scr, tw, fi_ref, ai_ref, mi_ref, tiles_scr, row_scr, row_edge)
    fetch.wait()
    ones = jnp.ones((2 * INNER, INNER), BF16)
    row = lax.broadcasted_iota(jnp.int32, (INNER, INNER), 0)
    lane = lax.broadcasted_iota(jnp.int32, (INNER, INNER), 1)
    place = lax.broadcasted_iota(jnp.int32, (1, INNER), 1)

    def gather_source(s):
        def some(q, carry):
            line = q // 8
            first = (q % 8) * 16
            picks = [sid_scr[s, line, first + j] for j in range(16)]
            rows = [tiles_scr[pl.ds(picks[j], 1), :] for j in range(16)]
            for j in range(16):
                g_scr[pl.ds(q * 16 + j, 1), :] = rows[j]
            return carry

        lax.fori_loop(0, SLOTS // 16, some, 0)
        count = sid_scr[s, 4, 0]
        sums = mm(jnp.concatenate(split(g_scr[...] * here_ref[s].astype(F32)), axis=1), ones)
        for q in range(4):
            got = jnp.where(row == lane, sums[q * INNER : (q + 1) * INNER], 0.0)
            got = jnp.sum(got, axis=0, keepdims=True)
            phase_scr[s, q : q + 1, :] = jnp.where(place + q * INNER < count, got, 0.0)

    weights.own.wait()
    gather_source(me)
    phases.own.start()

    def gather_next(i, carry):
        weights.wait_source(i)
        source = weights.source(i)
        gather_source(source)
        phases.copy(source, PEERS - 2 - i, me).start()
        return carry

    lax.fori_loop(0, PEERS - 1, gather_next, 0)
    weights.wait_sends()

    @pl.when(slot_at < 3)
    def _():
        for side in sides(side_sems, up_ref, prev_ref, above, 0):
            side.start()

    @pl.when(slot_at > 0)
    def _():
        for side in sides(side_sems, down_ref, next_ref, below, 1):
            side.start()

    phases.wait()
    for s in range(PEERS):
        table_scr[4 * s : 4 * s + 4, :] = landed[s]
    acc = weigh(slot_ref, prec_ref, table_scr[...], p_scr)
    for s in range(PEERS):
        res_scr[s] = acc[4 * s : 4 * s + 4]
    residuals.start()
    residuals.wait()

    @pl.when(slot_at < 3)
    def _():
        for side in sides(side_sems, up_ref, prev_ref, above, 0):
            side.wait_send()
        for side in sides(side_sems, down_ref, next_ref, below, 1):
            side.wait_recv()

    @pl.when(slot_at > 0)
    def _():
        for side in sides(side_sems, up_ref, prev_ref, above, 0):
            side.wait_recv()
        for side in sides(side_sems, down_ref, next_ref, below, 1):
            side.wait_send()


SIDE_PARTS = 4


def sides(sems, src, dst, device, n):
    copies = []
    for p in range(SIDE_PARTS):
        rows = pl.ds(p * (OUTER // SIDE_PARTS), OUTER // SIDE_PARTS)
        copies.append(
            pltpu.make_async_remote_copy(
                src_ref=src.at[rows],
                dst_ref=dst.at[rows],
                send_sem=sems.at[0, n, p],
                recv_sem=sems.at[1, n, p],
                device_id={"tm": device},
                device_id_type=MESH,
            )
        )
    return copies


def column_second_kernel(par, in_ref, amp_ref, own_ref, prev_ref, next_ref, ef, ei, back_ref, *scratch):
    y_scr, z_scr, msg_scr = scratch[0:3]
    me = lax.axis_index("strip")
    slot_at = lax.axis_index("tm")
    greet_peers(me, pltpu.get_barrier_semaphore())
    pencils = Exchange(me, in_ref, msg_scr, *scratch[3:6])
    pencils.start()
    pencils.wait()
    take_all(msg_scr, z_scr, False)
    column_first_step(z_scr, y_scr, -1.0)
    flip = flip_lanes(INNER)

    def step(k1, carry):
        value = apply_packed(ef, k1, y_scr[k1], flip)
        y_scr[k1] = value
        z_scr[k1] = par[0] * (value * amp_ref[k1]) + own_ref[k1]
        return carry

    lax.fori_loop(0, OUTER, step, 0, unroll=8)

    @pl.when(me == 0)
    def _():
        spec = edge_gather(y_scr)
        amp = edge_gather(amp_ref)
        u0, u2, a0, a2 = edge_split(spec, amp)
        mask, _ = edge_lanes()
        change = par[0] * (a0 * u0 + a2 * u2 - amp * spec)

        def put(k1, carry):
            back = lax.rem(INNER - k1, INNER)
            z_scr[k1] = z_scr[k1] + jnp.where(mask, pltpu.roll(change, back, 1), 0.0)
            return carry

        lax.fori_loop(0, OUTER, put, 0, unroll=4)

    def inverse(k1, carry):
        moved = jnp.where(slot_at > 0, prev_ref[k1].astype(F32), 0.0)
        moved = moved + jnp.where(slot_at < 3, next_ref[k1].astype(F32), 0.0)
        z_scr[k1] = apply_packed(ei, k1, z_scr[k1] - par[0] * moved, flip)
        return carry

    lax.fori_loop(0, OUTER, inverse, 0, unroll=8)
    column_first_step(z_scr, y_scr, 1.0)
    give_all(y_scr, msg_scr)
    back = Exchange(me, msg_scr, back_ref, *scratch[6:9])
    back.start()
    back.wait()


def route_kernel(t_ref, id_ref, slot_ref, tail_ref):
    row = lax.broadcasted_iota(jnp.int32, (INNER, 2 * INNER), 0)
    col = lax.broadcasted_iota(jnp.int32, (INNER, 2 * INNER), 1)
    tri = jnp.where(jnp.logical_or(row < col, col >= INNER), 1.0, 0.0).astype(BF16)
    peer = lax.broadcasted_iota(jnp.int32, (PEERS, INNER), 0)
    base = jnp.zeros((PEERS, INNER), F32)
    for i in range(0, POINT_ROWS, 8):
        hots = [jnp.where(peer == t_ref[i + j : i + j + 1, :], 1.0, 0.0) for j in range(8)]
        cum = mm(jnp.concatenate(hots, axis=0).astype(BF16), tri)
        for j in range(8):
            part = cum[j * PEERS : (j + 1) * PEERS]
            pos = jnp.sum(hots[j] * (part[:, 0:INNER] + base), axis=0, keepdims=True)
            base = base + part[:, INNER : 2 * INNER]
            slot_ref[i + j : i + j + 1, :] = t_ref[i + j : i + j + 1, :] * SLOTS + pos.astype(jnp.int32)
    batch = 4
    index = lax.broadcasted_iota(jnp.int32, (INNER, batch * INNER), 0)

    def wide(ref, i):
        return jnp.concatenate([ref[pl.ds(i * batch + j, 1), :] for j in range(batch)], axis=1)

    def put(i, acc):
        slot = wide(slot_ref, i)
        ids = wide(id_ref, i)
        r = lax.shift_right_logical(ids, 5)
        ids = lax.shift_right_logical(r, 3) * 256 + (ids & 31) * 8 + (r & 7)
        hot = jnp.where(index == (slot & 127), 1.0, 0.0).astype(BF16)
        line = index == lax.shift_right_logical(slot, 7)
        v = [
            jnp.where(line, d.astype(F32), 0.0).astype(BF16) for d in (lax.shift_right_logical(ids, 6), ids & 63)
        ]
        return acc + mm_nt(jnp.concatenate(v, axis=0), hot)

    acc = lax.fori_loop(0, POINT_ROWS // batch, put, jnp.zeros((2 * INNER, INNER), F32), unroll=2)
    ids = (acc[0:INNER] * 64.0 + acc[INNER : 2 * INNER]).astype(jnp.int32)
    count = base.astype(jnp.int32)
    tail_ref[...] = jnp.zeros_like(tail_ref)
    for s in range(PEERS):
        tail_ref[s, 0:4, :] = ids[4 * s : 4 * s + 4]
        tail_ref[s, 4:5, :] = count[s : s + 1]


def pack_kernel(slot_ref, w_ref, out_ref, w_scr, buf):
    def widen(i, carry):
        rows = pl.ds(pl.multiple_of(i * 64, 64), 64)
        w_scr[rows, :] = w_ref[rows, :].astype(F32)
        return carry

    lax.fori_loop(0, POINT_ROWS * INNER // 64, widen, 0, unroll=2)

    def some(q, carry):
        first = q * 32
        slots = [slot_ref[first + j] for j in range(32)]
        rows = [w_scr[pl.ds(first + j, 1), :] for j in range(32)]
        for j in range(32):
            buf[pl.ds(slots[j], 1), :] = rows[j]
        return carry

    lax.fori_loop(0, POINT_ROWS * INNER // 32, some, 0)

    def narrow(i, carry):
        rows = pl.ds(pl.multiple_of(i * INNER, INNER), INNER)
        out_ref[rows, :] = buf[rows, :].astype(BF16)
        return carry

    lax.fori_loop(0, PEERS * SLOTS // INNER, narrow, 0, unroll=2)


def weigh(slot_ref, prec_ref, phase, p_scr):
    high, low = split(phase)
    table = jnp.concatenate([high, low], axis=0)
    batch = 4
    index = lax.broadcasted_iota(jnp.int32, (INNER, batch * INNER), 0)

    def wide(ref, i):
        return jnp.concatenate([ref[pl.ds(i * batch + j, 1), :] for j in range(batch)], axis=1)

    def pick(i, carry):
        slot = wide(slot_ref, i)
        hot = jnp.where(index == (slot & 127), 1.0, 0.0).astype(BF16)
        v = mm(table, hot)
        v = v[0:INNER] + v[INNER : 2 * INNER]
        got = jnp.sum(jnp.where(index == lax.shift_right_logical(slot, 7), v, 0.0), axis=0, keepdims=True)
        for j in range(batch):
            p_scr[pl.ds(i * batch + j, 1), :] = got[:, j * INNER : (j + 1) * INNER]
        return carry

    lax.fori_loop(0, POINT_ROWS // batch, pick, 0, unroll=2)
    row = lax.broadcasted_iota(jnp.int32, (INNER, INNER), 0)
    lane = lax.broadcasted_iota(jnp.int32, (INNER, INNER), 1)
    same = jnp.where((row < HALF) == (lane < HALF), 1.0, 0.0).astype(BF16)
    prec = prec_ref[...]
    phase = p_scr[...]

    def total(value):
        return sum(mm(p, same) for p in reversed(split_into(value, 3)))

    p_scr[...] = prec * (phase - total(prec * phase) / total(prec))

    def put(i, acc):
        slot = wide(slot_ref, i)
        hot = jnp.where(index == (slot & 127), 1.0, 0.0).astype(BF16)
        v = jnp.where(index == lax.shift_right_logical(slot, 7), wide(p_scr, i), 0.0)
        vh, vl = split(v)
        return acc + mm_nt(jnp.concatenate([vh, vl], axis=0), hot)

    acc = lax.fori_loop(0, POINT_ROWS // batch, put, jnp.zeros((2 * INNER, INNER), F32), unroll=2)
    return acc[0:INNER] + acc[INNER : 2 * INNER]


COPIES = 8


def scatter_kernel(
    sid_ref, r_ref, w_ref, tw, f_ref, a_ref, m_ref, out_ref, rt_scr, u_scr, y_scr, e_scr, *accs
):
    def clear(i, carry):
        rows = pl.ds(pl.multiple_of(i * 64, 64), 64)
        for acc in accs:
            acc[rows, :] = jnp.zeros((64, INNER), F32)
        return carry

    lax.fori_loop(0, SIDE // 64, clear, 0)
    rt_scr[...] = r_ref[...].T
    lane = lax.broadcasted_iota(jnp.int32, (INNER, INNER), 1)
    row = lax.broadcasted_iota(jnp.int32, (INNER, INNER), 0)

    def scaled(s, carry):
        for q in range(4):
            col = jnp.sum(jnp.where(lane == s * 4 + q, rt_scr[...], 0.0), axis=1, keepdims=True)
            rows = pl.ds(pl.multiple_of(s * SLOTS + q * INNER, INNER), INNER)
            used = row + q * INNER < sid_ref[s * ID_STRIDE + SLOTS]
            u_scr[rows, :] = jnp.where(used, w_ref[rows, :].astype(F32) * col, 0.0)
        return carry

    lax.fori_loop(0, PEERS, scaled, 0, unroll=2)

    def source(s, carry):
        def some(q, inner):
            first = s * SLOTS + q * 16
            line = s * ID_STRIDE + q * 16
            ids = [sid_ref[line + j] for j in range(16)]
            us = [u_scr[pl.ds(first + j, 1), :] for j in range(16)]
            for h in range(0, 16, COPIES):
                sums = [accs[j][pl.ds(ids[h + j], 1), :] + us[h + j] for j in range(COPIES)]
                for j in range(COPIES):
                    accs[j][pl.ds(ids[h + j], 1), :] = sums[j]
            return inner

        return lax.fori_loop(0, lax.shift_right_logical(sid_ref[s * ID_STRIDE + SLOTS] + 15, 4), some, carry)

    lax.fori_loop(0, PEERS, source, 0)

    def add(i, carry):
        rows = pl.ds(pl.multiple_of(i * 64, 64), 64)
        total = accs[0][rows, :]
        for acc in accs[1:]:
            total = total + acc[rows, :]
        accs[0][rows, :] = total
        return carry

    lax.fori_loop(0, SIDE // 64, add, 0)
    row_forward_kernel(True, False, accs[0], tw, f_ref, a_ref, m_ref, out_ref, y_scr, e_scr)


def call(kernel, name, out_shapes, args, smem=0, scratch=(), any_args=(), any_outs=(), smem_outs=(), collective_id=None):
    spaces = [pltpu.SMEM if i < smem else pl.ANY if i in any_args else pltpu.VMEM for i in range(len(args))]
    outs = [pl.ANY if i in any_outs else pltpu.SMEM if i in smem_outs else pltpu.VMEM for i in range(len(out_shapes))]
    remote = dict(collective_id=collective_id, has_side_effects=True) if collective_id is not None else {}
    return pl.pallas_call(
        kernel,
        out_shape=out_shapes,
        in_specs=[pl.BlockSpec(memory_space=space) for space in spaces],
        out_specs=[pl.BlockSpec(memory_space=space) for space in outs],
        scratch_shapes=list(scratch),
        compiler_params=pltpu.CompilerParams(vmem_limit_bytes=VMEM_BYTES, **remote),
        cost_estimate=pl.CostEstimate(flops=1024, bytes_accessed=1024, transcendentals=0),
        name=name,
    )(*args)


def shape(dims, dtype=F32):
    return jax.ShapeDtypeStruct(dims, dtype)


PENCILS = (PEERS, INNER, INNER)
MESSAGES = (PEERS, INNER + TAIL, INNER)


def row_backward(pencils, base, tables):
    final = base is not None
    args = [pencils] + ([base] if final else []) + tables
    return call(
        lambda *refs: row_backward_kernel(final, *refs),
        "row_backward",
        [shape((INNER, SIDE) if final else (SIDE, INNER))],
        args,
        scratch=[pltpu.VMEM((15 * INNER, 2 * INNER), F32), pltpu.VMEM((2, INNER, INNER), F32)],
    )[0]


def tables_kernel(scale, rate, wind, prior, tab_ref, amp_ref, par_ref):
    strip = lax.axis_index("strip")
    live = (lax.axis_index("tm") < 3).astype(F32)
    k1 = (strip // 2).astype(F32)
    even = strip % 2 == 0
    row = lax.broadcasted_iota(jnp.int32, (INNER, INNER), 0)
    lane = lax.broadcasted_iota(jnp.int32, (INNER, INNER), 1)
    line = row.astype(F32)
    j = (lane & (HALF - 1)).astype(F32)
    cols = jnp.where(even, k1 + OUTER * j, k1 + OUTER * (INNER - 1.0 - j))
    cols = jnp.where(strip == 1, 16.0 + OUTER * j, cols)
    winds = ((wind[0, 0].astype(F32), wind[0, 1].astype(F32)), (prior[1], prior[2]))

    def cosine(turns):
        turns = turns - SIDE * jnp.floor(turns * (1.0 / SIDE))
        return jnp.cos(turns * (2.0 * math.pi / SIDE))

    small = jnp.zeros((INNER, INNER), F32)
    for kind in range(4):
        wind_row, wind_col = winds[kind // 2]
        quarter = (0.0, 3.0 * SIDE / 4, 0.0, SIDE / 4.0)[kind]
        base = OUTER * line * wind_row + quarter
        tab_ref[kind] = cosine(base + cols * wind_col)
        tab_ref[4 + kind] = cosine(base + j * wind_row)
        turns = (row & (OUTER - 1)).astype(F32) * wind_row + quarter
        small = jnp.where(lax.shift_right_logical(row, 5) == kind, turns, small)
    tab_ref[8] = cosine(small)

    fold = jnp.where(even, k1 + OUTER * j, OUTER - k1 + OUTER * j)
    fold = jnp.where(strip == 1, 16.0 + OUTER * j, fold)
    fold = jnp.where(jnp.logical_and(strip == 0, lane == HALF), SIDE / 2.0, fold)
    fold = fold * fold

    def step(k, carry):
        kr = line * OUTER + k.astype(F32)
        kr = jnp.minimum(kr, SIDE - kr)
        radius = (kr * kr + fold) / (KZERO * KZERO)
        amp_ref[k] = SIDE / (2.0 * KZERO) * jnp.exp((-11.0 / 12.0) * jnp.log(1.0 + radius))
        return carry

    lax.fori_loop(0, OUTER, step, 0, unroll=2)
    norm = scale[0] / (SIDE * SIDE)
    mine = rate[0] * live
    par_ref[0] = norm
    par_ref[1] = mine * scale[0]
    par_ref[2] = prior[0] * scale[0]
    par_ref[3] = (mine + prior[0]) * scale[0] * norm
    par_ref[4] = 1.0 - 2.0 * (wind[0, 1] & 1).astype(F32)
    par_ref[5] = 1.0 - 2.0 * (prior[2].astype(jnp.int32) & 1).astype(F32)
    par_ref[6] = 0.0
    par_ref[7] = 0.0


def const(*tables):
    return [jnp.asarray(t) for t in tables]


def local(
    screen_vec,
    prior_scale,
    flow_weight,
    wind,
    pierce_point_strip,
    pierce_block,
    pierce_weights,
    noise_prec,
):
    fwd, inv, first, first_inv, mid, mid_inv, twiddle = row_tables()
    row_fwd_tables = const(twiddle, pieces(fwd, 2), pieces(first, 2), pieces(mid, 2))
    row_fine_tables = const(twiddle, pieces(fwd, 3), pieces(first, 3), pieces(mid, 3))
    row_inv_tables = const(twiddle, pieces(inv, 2), pieces(first_inv, 2), pieces(mid_inv, 2))
    col_fwd, col_inv = column_tables()
    col_fine_tables = const(pieces(col_fwd, 3), pieces(col_inv, 2))
    col_tables = const(pieces(col_fwd, 2), pieces(col_inv, 2))

    x = screen_vec[0]
    weights = pierce_weights[0].reshape(POINT_ROWS * INNER, INNER)
    target = pierce_point_strip.reshape(POINT_ROWS, INNER)
    block = pierce_block.reshape(POINT_ROWS, INNER)
    prec = noise_prec.reshape(POINT_ROWS, INNER)

    mine = jnp.concatenate([flow_weight, wind[0].astype(F32)])
    prior = lax.ppermute(mine, "tm", [(i, i + 1) for i in range(lax.axis_size("tm") - 1)])
    slots, ids = call(
        route_kernel,
        "route",
        [shape((POINT_ROWS, INNER), jnp.int32), shape((PEERS, ID_ROWS, INNER), jnp.int32)],
        [target, block],
    )
    ids, prior, prec = lax.optimization_barrier((ids, prior, prec))
    sent = call(
        pack_kernel,
        "pack",
        [shape((PEERS * SLOTS, INNER), BF16)],
        [slots.reshape(-1), weights],
        smem=1,
        scratch=[pltpu.VMEM((POINT_ROWS * INNER, INNER), F32), pltpu.VMEM((PEERS * SLOTS, INNER), F32)],
    )[0]

    spectral = [pltpu.VMEM(PENCILS, F32), pltpu.VMEM(PENCILS, F32)]
    rows = [pltpu.VMEM((15 * INNER, 2 * INNER), F32), pltpu.VMEM((2, INNER, INNER), F32)]
    message = shape(MESSAGES, BF16)
    points = pltpu.VMEM((PEERS * SLOTS, INNER), F32)
    screen = pltpu.VMEM((SIDE, INNER), F32)
    small = (PEERS, 4, INNER)
    own, arrived, amp, resid, par, here_ids, from_prev, from_next = call(
        first_kernel,
        "first",
        [
            shape(PENCILS),
            shape((PEERS, SLOTS, INNER), BF16),
            shape(PENCILS),
            shape(small),
            shape((8,)),
            shape((PEERS, ID_ROWS, INNER), jnp.int32),
            shape(PENCILS, BF16),
            shape(PENCILS, BF16),
        ],
        [prior_scale, flow_weight, wind, prior, x]
        + row_fine_tables
        + row_inv_tables[1:]
        + col_fine_tables
        + [slots, prec, sent.reshape(PEERS, SLOTS, INNER), ids],
        smem=4,
        any_args=(16, 17),
        any_outs=(5, 6, 7),
        smem_outs=(4,),
        collective_id=3,
        scratch=spectral
        + [pltpu.VMEM(MESSAGES, BF16)] * 3
        + [pltpu.VMEM((9, INNER, INNER), F32)]
        + rows
        + [pltpu.VMEM(PENCILS, BF16)] * 2
        + [
            screen,
            pltpu.VMEM((SLOTS, INNER), F32),
            pltpu.VMEM(small, F32),
            pltpu.VMEM(small, F32),
            pltpu.VMEM((POINT_ROWS, INNER), F32),
            pltpu.VMEM((INNER, INNER), F32),
            pltpu.VMEM(small, F32),
            pltpu.SMEM((PEERS, ID_ROWS, INNER), jnp.int32),
            pltpu.SemaphoreType.DMA,
            pltpu.SemaphoreType.DMA((2, 2, SIDE_PARTS)),
        ]
        + exchange_sems() * 6,
    )
    here = arrived.reshape(PEERS * SLOTS, INNER)
    here_ids = here_ids.reshape(PEERS * ID_STRIDE)

    pencils = call(
        scatter_kernel,
        "scatter",
        [message],
        [here_ids, resid.reshape(INNER, INNER), here] + row_fwd_tables,
        smem=1,
        scratch=[pltpu.VMEM((INNER, INNER), F32), points] + rows + [screen] * COPIES,
    )[0]
    out_pencils = call(
        column_second_kernel,
        "column_second",
        [message],
        [par, pencils, amp, own, from_prev, from_next] + col_tables,
        smem=1,
        any_args=(1,),
        any_outs=(0,),
        collective_id=1,
        scratch=spectral + [pltpu.VMEM(MESSAGES, BF16)] + exchange_sems() + exchange_sems(),
    )[0]
    return row_backward(out_pencils, x, row_inv_tables)[None]


def solution(mesh):
    in_specs = (
        P("tm", "strip", None),
        P("tm"),
        P("tm"),
        P("tm", None),
        P("tm", "strip", None, None),
        P("tm", "strip", None),
        P("tm", "strip", None, None),
        P("tm", "strip", None),
    )
    out_specs = P("tm", "strip", None)
    return jax.shard_map(local, mesh=mesh, in_specs=in_specs, out_specs=out_specs, check_vma=False)
```

```python
import math

import jax
import jax.numpy as jnp
import ml_dtypes
import numpy as np
from jax import lax
from jax.experimental import pallas as pl
from jax.experimental.pallas import tpu as pltpu
from jax.sharding import PartitionSpec as P

KZERO = 2.0
SIDE = 4096
OUTER = 32
INNER = 128
HALF = 64
PEERS = 32
SLOTS = 512
POINT_ROWS = 64
TAIL = 16
ID_ROWS = 8
ID_STRIDE = ID_ROWS * 128
VMEM_BYTES = 56 * 1024 * 1024
F32 = jnp.float32
BF16 = jnp.bfloat16


def pieces(table, count):
    rest = np.asarray(table, np.float64)
    out = []
    for _ in range(count):
        out.append(rest.astype(np.float32).astype(ml_dtypes.bfloat16))
        rest = rest - out[-1].astype(np.float64)
    return np.stack(out)


def row_tables():
    b = np.arange(INNER)[:, None]
    j = np.arange(HALF)[None, :]
    theta = [2 * np.pi * ((b * j) % INNER) / INNER, 2 * np.pi * ((b * (INNER - 1 - j)) % INNER) / INNER]
    forward = []
    backward = []
    for t in theta:
        forward.append(np.concatenate([np.cos(t), -np.sin(t)], axis=1))
        forward.append(np.concatenate([np.sin(t), np.cos(t)], axis=1))
        backward.append(np.concatenate([np.cos(t).T, np.sin(t).T], axis=1))
        backward.append(np.concatenate([-np.sin(t).T, np.cos(t).T], axis=1))
    fwd = np.concatenate(
        [np.concatenate([forward[0], forward[1]], axis=0), np.concatenate([forward[2], forward[3]], axis=0)], axis=1
    )
    inv = np.concatenate(backward, axis=0)
    sign = np.where(np.arange(INNER) % 2 == 0, 1.0, -1.0)
    t0 = theta[0]
    first = np.concatenate([np.cos(t0), -np.sin(t0)], axis=1)
    first[:, HALF] = sign
    first_inv = np.concatenate([2 * np.cos(t0).T, -2 * np.sin(t0).T], axis=0)
    first_inv[0, :] = 1.0
    first_inv[HALF, :] = sign
    t16 = 2 * np.pi * ((b * (16 + 32 * j)) % SIDE) / SIDE
    mid = np.concatenate([np.cos(t16), -np.sin(t16)], axis=1)
    mid_inv = np.concatenate([2 * np.cos(t16).T, -2 * np.sin(t16).T], axis=0)
    k1 = np.arange(16)[:, None]
    tw = 2 * np.pi * (k1 * np.arange(INNER)[None, :]) / SIDE
    twiddle = np.stack([np.cos(tw), np.sin(tw)]).astype(np.float32)
    return fwd, inv, first, first_inv, mid, mid_inv, twiddle


def column_tables():
    k1 = np.arange(OUTER)[:, None, None]
    k2 = np.arange(INNER)[None, :, None]
    r = np.arange(INNER)[None, None, :]
    theta = 2 * np.pi * (((k1 + OUTER * k2) * r) % SIDE) / SIDE
    fwd = np.concatenate([np.cos(theta), -np.sin(theta)], axis=1)
    theta = theta.transpose(0, 2, 1)
    inv = np.concatenate([np.cos(theta), np.sin(theta)], axis=1)
    return fwd, inv


def split(value):
    high = value.astype(BF16)
    return high, (value - high.astype(F32)).astype(BF16)


def mm(left, right):
    return lax.dot_general(left, right, (((1,), (0,)), ((), ())), preferred_element_type=F32)


def mm_nt(left, right):
    return lax.dot_general(left, right, (((1,), (1,)), ((), ())), preferred_element_type=F32)


def split_into(value, count):
    parts = []
    for i in range(count):
        parts.append(value.astype(BF16))
        if i + 1 < count:
            value = value - parts[-1].astype(F32)
    return parts


def data_by_table(value, tables):
    count = len(tables)
    parts = split_into(value, count)
    total = None
    for order in reversed(range(count)):
        for i in range(order + 1):
            term = mm(parts[i], tables[order - i])
            total = term if total is None else total + term
    return total


def table_by_data(tables, value):
    parts = split_into(value, len(tables))
    left = jnp.concatenate(tables[0:2], axis=1)
    right = jnp.concatenate(parts[0:2], axis=1)
    r = mm(left, jnp.concatenate([right, right], axis=0))
    total = r[:, INNER : 2 * INNER] + r[:, 0:INNER]
    if len(tables) == 3:
        left = jnp.concatenate([tables[0], tables[2]], axis=1)
        total = total + mm(left, jnp.concatenate([parts[2], parts[0]], axis=0))
    return total


def every(ref):
    return [ref[i] for i in range(ref.shape[0])]


def c_mul(value, factor):
    re, im = value
    c, s = factor.real, factor.imag
    if im is None:
        return (re * c, re * s)
    return (re * c - im * s, re * s + im * c)


def real_forward(xs):
    n = len(xs)
    if n == 2:
        return [(xs[0] + xs[1], None), (xs[0] - xs[1], None)]
    even, odd = real_forward(xs[0::2]), real_forward(xs[1::2])
    m = n // 2
    out = [None] * (m + 1)
    for k in range(m // 2 + 1):
        if k == 0:
            out[0] = (even[0][0] + odd[0][0], None)
            out[m] = (even[0][0] - odd[0][0], None)
        elif 2 * k == m:
            out[k] = (even[k][0], -odd[k][0])
        else:
            tr, ti = c_mul(odd[k], complex(math.cos(2 * math.pi * k / n), -math.sin(2 * math.pi * k / n)))
            er, ei = even[k]
            out[k] = (er + tr, ei + ti)
            out[m - k] = (er - tr, ti - ei)
    return out


def real_backward(spec):
    n = 2 * (len(spec) - 1)
    if n == 2:
        return [spec[0][0] + spec[1][0], spec[0][0] - spec[1][0]]
    m = n // 2
    even, odd = [], []
    for k in range(m // 2 + 1):
        if k == 0:
            even.append((spec[0][0] + spec[m][0], None))
            odd.append((spec[0][0] - spec[m][0], None))
        elif 2 * k == m:
            even.append((2.0 * spec[k][0], None))
            odd.append((-2.0 * spec[k][1], None))
        else:
            ar, ai = spec[k]
            br, bi = spec[m - k]
            even.append((ar + br, ai - bi))
            odd.append(c_mul((ar - br, ai + bi), complex(math.cos(2 * math.pi * k / n), math.sin(2 * math.pi * k / n))))
    xe, xo = real_backward(even), real_backward(odd)
    out = [None] * n
    out[0::2] = xe
    out[1::2] = xo
    return out


def packed_fft(xs, sign, flip):
    n = len(xs)
    if n == 1:
        return xs
    even, odd = packed_fft(xs[0::2], sign, flip), packed_fft(xs[1::2], sign, flip)
    out = [None] * n
    for k in range(n // 2):
        t = odd[k]
        if k:
            turned = pltpu.roll(t, HALF, 1) * flip
            c, s = math.cos(2 * math.pi * k / n), sign * math.sin(2 * math.pi * k / n)
            t = (-s) * turned if 4 * k == n else c * t - s * turned
        out[k] = even[k] + t
        out[k + n // 2] = even[k] - t
    return out


def flip_lanes(rows):
    lane = lax.broadcasted_iota(jnp.int32, (rows, INNER), 1)
    return jnp.where(lane < HALF, 1.0, -1.0).astype(F32)


def put_message(ref, d, value, fine):
    lane = lax.broadcasted_iota(jnp.int32, (INNER, INNER), 1)
    high = value.astype(BF16)
    ref[d, 0:INNER, :] = high
    rest = value - high.astype(F32)
    if fine:
        third = rest - rest.astype(BF16).astype(F32)
        rest = jnp.where((lane & (HALF - 1)) == 7, pltpu.roll(third, 7, 1), rest)
    rest = jnp.where(lane < 8, rest, pltpu.roll(rest, 72, 1))
    rest = jnp.where(lane < 16, rest, 0.0)
    total = rest[0:16]
    for g in range(1, 8):
        total = total + pltpu.roll(rest[16 * g : 16 * g + 16], 16 * g, 1)
    ref[d, INNER : INNER + TAIL, :] = total.astype(BF16)


def get_message(ref, d, fine):
    lane = lax.broadcasted_iota(jnp.int32, (INNER, INNER), 1)
    packed = ref[d, INNER : INNER + TAIL, :].astype(F32)
    rest = jnp.concatenate([packed] + [pltpu.roll(packed, INNER - 16 * g, 1) for g in range(1, 8)], axis=0)
    rest = jnp.where(lane < 8, rest, pltpu.roll(rest, 56, 1))
    column = lane & (HALF - 1)
    if fine:
        third = jnp.where(column == 0, pltpu.roll(rest, INNER - 7, 1), 0.0)
        rest = jnp.where(column < 7, rest, 0.0) + third
    else:
        rest = jnp.where(column < 8, rest, 0.0)
    return ref[d, 0:INNER, :].astype(F32) + rest


def row_forward_kernel(tiled, fine, x_ref, tw_ref, f_ref, a_ref, m_ref, out_ref, y_scr, e_scr):
    def slab(g, carry):
        if tiled:
            xs = [x_ref[pl.ds(pl.multiple_of(g * 256 + a * 8, 8), 8), :] for a in range(OUTER)]
        else:
            xs = [x_ref[pl.ds(pl.multiple_of(g * 8, 8), 8), a * INNER : (a + 1) * INNER] for a in range(OUTER)]
        ys = real_forward(xs)
        rows = pl.ds(pl.multiple_of(g * 8, 8), 8)
        e_scr[0, rows, :] = ys[0][0]
        e_scr[1, rows, :] = ys[16][0]
        for k in range(1, 16):
            c = tw_ref[0, k : k + 1, :]
            s = tw_ref[1, k : k + 1, :]
            re, im = ys[k]
            base = pl.ds(pl.multiple_of((k - 1) * INNER + g * 8, 8), 8)
            y_scr[base, 0:INNER] = re * c + im * s
            y_scr[base, INNER : 2 * INNER] = im * c - re * s
        return carry

    lax.fori_loop(0, 16, slab, 0, unroll=2)
    put_message(out_ref, 0, data_by_table(e_scr[0], every(a_ref)), fine)
    put_message(out_ref, 1, data_by_table(e_scr[1], every(m_ref)), fine)

    def group(q, carry):
        v = data_by_table(y_scr[pl.ds(pl.multiple_of(q * 384, 8), 384), :], every(f_ref))
        for i in range(3):
            rows = v[i * INNER : (i + 1) * INNER]
            put_message(out_ref, 2 + 2 * (3 * q + i), rows[:, 0:INNER], fine)
            put_message(out_ref, 3 + 2 * (3 * q + i), rows[:, INNER : 2 * INNER], fine)
        return carry

    lax.fori_loop(0, 5, group, 0)


def row_backward_kernel(final, *refs):
    if final:
        in_ref, base_ref, tw_ref, f_ref, a_ref, m_ref, out_ref, z_scr, e_scr = refs
    else:
        in_ref, tw_ref, f_ref, a_ref, m_ref, out_ref, z_scr, e_scr = refs
    e_scr[0] = data_by_table(get_message(in_ref, 0, False), every(a_ref))
    e_scr[1] = data_by_table(get_message(in_ref, 1, False), every(m_ref))

    def group(q, carry):
        parts = []
        for i in range(3):
            k = 3 * q + i
            parts.append(jnp.concatenate([get_message(in_ref, 2 + 2 * k + h, False) for h in range(2)], axis=1))
        v = jnp.concatenate(parts, axis=0)
        z_scr[pl.ds(pl.multiple_of(q * 384, 8), 384), :] = data_by_table(v, every(f_ref))
        return carry

    lax.fori_loop(0, 5, group, 0)

    def slab(g, carry):
        rows = pl.ds(pl.multiple_of(g * 8, 8), 8)
        spec = [(e_scr[0, rows, :], None)]
        for k in range(1, 16):
            c = tw_ref[0, k : k + 1, :]
            s = tw_ref[1, k : k + 1, :]
            base = pl.ds(pl.multiple_of((k - 1) * INNER + g * 8, 8), 8)
            re = z_scr[base, 0:INNER]
            im = z_scr[base, INNER : 2 * INNER]
            spec.append((re * c - im * s, im * c + re * s))
        spec.append((e_scr[1, rows, :], None))
        xs = real_backward(spec)
        for a in range(OUTER):
            if final:
                cols = slice(a * INNER, (a + 1) * INNER)
                out_ref[rows, cols] = base_ref[rows, cols] + xs[a]
            else:
                out_ref[pl.ds(pl.multiple_of(g * 256 + a * 8, 8), 8), :] = xs[a]
        return carry

    lax.fori_loop(0, 16, slab, 0, unroll=2)


def take_all(exchange, scr, fine):
    exchange.own.wait()
    scr[exchange.me] = get_message(exchange.out_ref, exchange.me, fine)

    def step(i, carry):
        exchange.wait_source(i)
        source = exchange.source(i)
        scr[source] = get_message(exchange.out_ref, source, fine)
        return carry

    lax.fori_loop(0, PEERS - 1, step, 0)
    exchange.wait_sends()


def give_all(scr, exchange):
    def step(i, carry):
        peer = exchange.peer(i)
        put_message(exchange.in_ref, peer, scr[peer], False)
        exchange.send(i)
        return carry

    lax.fori_loop(0, PEERS - 1, step, 0)
    put_message(exchange.in_ref, exchange.me, scr[exchange.me], False)
    exchange.own.start()


def column_first_step(in_ref, y_scr, sign):
    flip = flip_lanes(8)

    def slab(g, carry):
        rows = pl.ds(pl.multiple_of(g * 8, 8), 8)
        ys = packed_fft([in_ref[s, rows, :] for s in range(OUTER)], sign, flip)
        for k in range(OUTER):
            y_scr[k, rows, :] = ys[k]
        return carry

    lax.fori_loop(0, 16, slab, 0, unroll=2)


def apply_packed(e_ref, k1, value, flip):
    r = table_by_data([e_ref[i, k1] for i in range(e_ref.shape[0])], value)
    return r[0:INNER] - pltpu.roll(r[INNER : 2 * INNER], HALF, 1) * flip


MESH = pl.DeviceIdType.MESH


def greet_peers(me, barrier, extra=()):
    def greet(i, carry):
        pl.semaphore_signal(barrier, inc=1, device_id={"strip": lax.rem(me + i, PEERS)}, device_id_type=MESH)
        return carry

    lax.fori_loop(1, PEERS, greet, 0)
    for device in extra:
        pl.semaphore_signal(barrier, inc=1, device_id=device, device_id_type=MESH)
    pl.semaphore_wait(barrier, PEERS - 1 + len(extra))


class Exchange:
    def __init__(self, me, in_ref, out_ref, send_sem, recv_sem, own_sem, flat=0):
        self.me, self.in_ref, self.out_ref, self.flat = me, in_ref, out_ref, flat
        self.send_sem, self.recv_sem = send_sem, recv_sem
        self.own = pltpu.make_async_copy(self.part(in_ref, me), self.part(out_ref, me), own_sem)

    def part(self, ref, i):
        return ref.at[pl.ds(pl.multiple_of(i * self.flat, self.flat), self.flat)] if self.flat else ref.at[i]

    def copy(self, peer, send, source):
        return pltpu.make_async_remote_copy(
            src_ref=self.part(self.in_ref, peer),
            dst_ref=self.part(self.out_ref, source),
            send_sem=self.send_sem.at[send],
            recv_sem=self.recv_sem.at[source],
            device_id={"strip": peer},
            device_id_type=MESH,
        )

    def peer(self, i):
        return lax.rem(self.me + 1 + i, PEERS)

    def source(self, i):
        return lax.rem(self.me + PEERS - 1 - i, PEERS)

    def send(self, i):
        self.copy(self.peer(i), i, self.me).start()

    def wait_source(self, i):
        self.copy(self.peer(i), i, self.source(i)).wait_recv()

    def wait_sends(self):
        def step(i, carry):
            self.copy(self.peer(i), i, self.me).wait_send()
            return carry

        lax.fori_loop(0, PEERS - 1, step, 0)

    def start(self, first=0, last=PEERS - 1):
        def step(i, carry):
            self.copy(self.peer(i), i, self.me).start()
            return carry

        lax.fori_loop(first, last, step, 0)
        if first == 0:
            self.own.start()

    def wait(self):
        def step(i, carry):
            self.wait_source(i)
            return carry

        self.own.wait()
        lax.fori_loop(0, PEERS - 1, step, 0)
        self.wait_sends()


class Moves:
    def __init__(self, pairs, sems):
        self.copies = [pltpu.make_async_copy(src, dst, sems.at[i]) for i, (src, dst) in enumerate(pairs)]

    def start(self):
        for copy in self.copies:
            copy.start()

    def wait(self):
        for copy in self.copies:
            copy.wait()


def exchange_sems():
    return [pltpu.SemaphoreType.DMA((PEERS,)), pltpu.SemaphoreType.DMA((PEERS,)), pltpu.SemaphoreType.DMA]


def edge_lanes():
    lane = lax.broadcasted_iota(jnp.int32, (INNER, INNER), 1)
    return jnp.logical_or(lane == 0, lane == HALF), lane < HALF


def edge_gather(ref):
    mask, _ = edge_lanes()

    def step(k1, acc):
        return acc + pltpu.roll(jnp.where(mask, ref[k1], 0.0), k1, 1)

    return lax.fori_loop(0, OUTER, step, jnp.zeros((INNER, INNER), F32), unroll=4)


def edge_split(spec, amp):
    i = lax.broadcasted_iota(jnp.int32, (INNER, INNER), 0)
    j = lax.broadcasted_iota(jnp.int32, (INNER, INNER), 1)
    one = jnp.ones((INNER, INNER), F32)
    none = jnp.zeros((INNER, INNER), F32)
    rows = jnp.where(i + j == INNER - 1, one, none).astype(BF16)
    rows0 = jnp.where(((i + j) & (INNER - 1)) == 0, one, none).astype(BF16)
    sign = jnp.where(j < HALF, one, -one)
    col = j & (HALF - 1)
    same = (i < HALF) == (j < HALF)
    lanes = jnp.where(
        jnp.logical_and(same, jnp.logical_and(col > 0, col + (i & (HALF - 1)) == OUTER)), sign, none
    ).astype(BF16)
    lanes0 = jnp.where(jnp.logical_and(i == j, col == 0), sign, none).astype(BF16)

    def move(left, value, right):
        value = sum(mm(left, p) for p in reversed(split_into(value, 3)))
        return sum(mm(p, right) for p in reversed(split_into(value, 3)))

    rev = move(rows, spec, lanes) + move(rows0, spec, lanes0)
    swapped = pltpu.roll(amp, HALF, 1)
    _, left = edge_lanes()
    a0 = jnp.where(left, amp, swapped)
    a2 = jnp.where(left, swapped, amp)
    return 0.5 * (spec + rev), 0.5 * (spec - rev), a0, a2


def turn(c, s, value, flip):
    return c * value + s * (pltpu.roll(value, HALF, 1) * flip)


EARLY = 8
MIDDLE = 18


def first_kernel(
    scale, rate, wind, prior, x_ref, tw, f_ref, a_ref, m_ref, fi_ref, ai_ref, mi_ref, slot_ref, prec_ref,
    ef_any, ei_any, sent_ref, ids_ref,
    resid_ref, par, own_any, here_any, amp_any, here_ids_ref, prev_ref, next_ref, *scratch,
):
    y_scr, z_scr, msg_scr, land_scr, back_scr, tab_ref, row_scr, row_edge = scratch[0:8]
    up_ref, down_ref, tiles_scr, g_scr, phase_scr, landed, p_scr, table_scr, res_scr = scratch[8:17]
    sid_scr, sid_sem, side_sems = scratch[17:20]
    ef, ei, own_ref, amp_ref, here_ref, in_sems, out_sems, here_sems = scratch[20:28]
    sems = scratch[28:]
    tables = Moves([(ef_any, ef), (ei_any, ei)], in_sems)
    tables.start()
    results = Moves([(own_ref, own_any), (amp_ref, amp_any)], out_sems)
    weights_out = Moves([(here_ref, here_any)], here_sems)
    me = lax.axis_index("strip")
    slot_at = lax.axis_index("tm")
    above, below = lax.rem(slot_at + 1, 4), lax.rem(slot_at + 3, 4)
    greet_peers(me, pltpu.get_barrier_semaphore(), ({"tm": above}, {"tm": below}))
    ids = Exchange(me, ids_ref, here_ids_ref, *sems[0:3], flat=ID_STRIDE)
    weights = Exchange(me, sent_ref, here_ref, *sems[3:6])
    pencils = Exchange(me, msg_scr, land_scr, *sems[6:9])
    back = Exchange(me, msg_scr, back_scr, *sems[9:12])
    phases = Exchange(me, phase_scr, landed, *sems[12:15])
    residuals = Exchange(me, res_scr, resid_ref, *sems[15:18])
    ids.start()
    weights.start(0, EARLY)
    row_forward_kernel(False, True, x_ref, tw, f_ref, a_ref, m_ref, msg_scr, row_scr, row_edge)
    pencils.start()
    weights.start(EARLY, MIDDLE)
    tables_kernel(scale, rate, wind, prior, tab_ref, amp_ref, par)
    take_all(pencils, z_scr, True)
    tables.wait()
    column_first_step(z_scr, y_scr, -1.0)
    flip = flip_lanes(INNER)

    def step(k1, carry):
        value = apply_packed(ef, k1, y_scr[k1], flip)
        amp = amp_ref[k1]
        once = value * amp
        twice = once * amp
        y_scr[k1] = value
        z_scr[k1] = par[0] * once
        own_ref[k1] = par[3] * twice
        for n, ref, gain in ((0, up_ref, par[1]), (1, down_ref, par[2])):
            cb = tab_ref[2 * n]
            sb = tab_ref[2 * n + 1]
            ca = tab_ref[8, pl.ds(64 * n + k1, 1), :] * gain
            sa = tab_ref[8, pl.ds(64 * n + 32 + k1, 1), :] * gain
            ref[k1] = turn(cb * ca - sb * sa, sb * ca + cb * sa, twice, flip).astype(BF16)
        return carry

    lax.fori_loop(0, OUTER, step, 0, unroll=8)

    @pl.when(me == 0)
    def _():
        u0, u2, a0, a2 = edge_split(edge_gather(y_scr), edge_gather(amp_ref))
        mask, _ = edge_lanes()
        e0 = a0 * u0
        e2 = a2 * u2
        fixed = [par[0] * (e0 + e2)]
        e0 = a0 * e0
        e2 = a2 * e2
        fixed.append(par[3] * (e0 + e2))
        fixed.append(par[1] * turn(tab_ref[4], tab_ref[5], e0 + par[4] * e2, flip))
        fixed.append(par[2] * turn(tab_ref[6], tab_ref[7], e0 + par[5] * e2, flip))

        def put(k1, carry):
            back = lax.rem(INNER - k1, INNER)
            for ref, value in zip((z_scr, own_ref, up_ref, down_ref), fixed):
                value = jnp.where(mask, pltpu.roll(value, back, 1), ref[k1].astype(F32))
                ref[k1] = value.astype(ref.dtype)
            return carry

        lax.fori_loop(0, OUTER, put, 0, unroll=4)

    def inverse(k1, carry):
        z_scr[k1] = apply_packed(ei, k1, z_scr[k1], flip)
        return carry

    lax.fori_loop(0, OUTER, inverse, 0, unroll=8)
    column_first_step(z_scr, y_scr, 1.0)
    give_all(y_scr, back)
    weights.start(MIDDLE, PEERS - 1)
    results.start()
    ids.wait()
    fetch = pltpu.make_async_copy(here_ids_ref, sid_scr, sid_sem)
    fetch.start()
    back.wait()
    row_backward_kernel(False, back_scr, tw, fi_ref, ai_ref, mi_ref, tiles_scr, row_scr, row_edge)
    fetch.wait()
    ones = jnp.ones((2 * INNER, INNER), BF16)
    row = lax.broadcasted_iota(jnp.int32, (INNER, INNER), 0)
    lane = lax.broadcasted_iota(jnp.int32, (INNER, INNER), 1)
    place = lax.broadcasted_iota(jnp.int32, (1, INNER), 1)

    def gather_source(s):
        def some(q, carry):
            first = s * ID_STRIDE + q * 16
            picks = [sid_scr[first + j] for j in range(16)]
            rows = [tiles_scr[pl.ds(picks[j], 1), :] for j in range(16)]
            for j in range(16):
                g_scr[pl.ds(q * 16 + j, 1), :] = rows[j]
            return carry

        lax.fori_loop(0, SLOTS // 16, some, 0)
        count = sid_scr[s * ID_STRIDE + SLOTS]
        sums = mm(jnp.concatenate(split(g_scr[...] * here_ref[s].astype(F32)), axis=1), ones)
        for q in range(4):
            got = jnp.where(row == lane, sums[q * INNER : (q + 1) * INNER], 0.0)
            got = jnp.sum(got, axis=0, keepdims=True)
            phase_scr[s, q : q + 1, :] = jnp.where(place + q * INNER < count, got, 0.0)

    weights.own.wait()
    gather_source(me)
    phases.own.start()

    def gather_next(i, carry):
        weights.wait_source(i)
        source = weights.source(i)
        gather_source(source)
        phases.copy(source, PEERS - 2 - i, me).start()
        return carry

    lax.fori_loop(0, PEERS - 1, gather_next, 0)
    weights.wait_sends()
    weights_out.start()

    @pl.when(slot_at < 3)
    def _():
        for side in sides(side_sems, up_ref, prev_ref, above, 0):
            side.start()

    @pl.when(slot_at > 0)
    def _():
        for side in sides(side_sems, down_ref, next_ref, below, 1):
            side.start()

    phases.wait()
    for s in range(PEERS):
        table_scr[4 * s : 4 * s + 4, :] = landed[s]
    acc = weigh(slot_ref, prec_ref, table_scr[...], p_scr)
    for s in range(PEERS):
        res_scr[s] = acc[4 * s : 4 * s + 4]
    residuals.start()
    results.wait()
    weights_out.wait()
    residuals.wait()

    @pl.when(slot_at < 3)
    def _():
        for side in sides(side_sems, up_ref, prev_ref, above, 0):
            side.wait_send()
        for side in sides(side_sems, down_ref, next_ref, below, 1):
            side.wait_recv()

    @pl.when(slot_at > 0)
    def _():
        for side in sides(side_sems, up_ref, prev_ref, above, 0):
            side.wait_recv()
        for side in sides(side_sems, down_ref, next_ref, below, 1):
            side.wait_send()


SIDE_PARTS = 4


def sides(sems, src, dst, device, n):
    copies = []
    for p in range(SIDE_PARTS):
        rows = pl.ds(p * (OUTER // SIDE_PARTS), OUTER // SIDE_PARTS)
        copies.append(
            pltpu.make_async_remote_copy(
                src_ref=src.at[rows],
                dst_ref=dst.at[rows],
                send_sem=sems.at[0, n, p],
                recv_sem=sems.at[1, n, p],
                device_id={"tm": device},
                device_id_type=MESH,
            )
        )
    return copies


def column_second_kernel(par, in_ref, amp_any, own_any, prev_any, next_any, ef_any, ei_any, back_ref, *scratch):
    y_scr, z_scr, msg_scr, out_scr = scratch[0:4]
    amp_ref, own_ref, prev_ref, next_ref, ef, ei, in_sems = scratch[10:17]
    inputs = Moves(
        [(amp_any, amp_ref), (own_any, own_ref), (prev_any, prev_ref), (next_any, next_ref), (ef_any, ef), (ei_any, ei)],
        in_sems,
    )
    inputs.start()
    me = lax.axis_index("strip")
    slot_at = lax.axis_index("tm")
    greet_peers(me, pltpu.get_barrier_semaphore())
    pencils = Exchange(me, in_ref, msg_scr, *scratch[4:7])
    pencils.start()
    take_all(pencils, z_scr, False)
    inputs.wait()
    column_first_step(z_scr, y_scr, -1.0)
    flip = flip_lanes(INNER)

    def step(k1, carry):
        value = apply_packed(ef, k1, y_scr[k1], flip)
        y_scr[k1] = value
        z_scr[k1] = par[0] * (value * amp_ref[k1]) + own_ref[k1]
        return carry

    lax.fori_loop(0, OUTER, step, 0, unroll=8)

    @pl.when(me == 0)
    def _():
        spec = edge_gather(y_scr)
        amp = edge_gather(amp_ref)
        u0, u2, a0, a2 = edge_split(spec, amp)
        mask, _ = edge_lanes()
        change = par[0] * (a0 * u0 + a2 * u2 - amp * spec)

        def put(k1, carry):
            back = lax.rem(INNER - k1, INNER)
            z_scr[k1] = z_scr[k1] + jnp.where(mask, pltpu.roll(change, back, 1), 0.0)
            return carry

        lax.fori_loop(0, OUTER, put, 0, unroll=4)

    def inverse(k1, carry):
        moved = jnp.where(slot_at > 0, prev_ref[k1].astype(F32), 0.0)
        moved = moved + jnp.where(slot_at < 3, next_ref[k1].astype(F32), 0.0)
        z_scr[k1] = apply_packed(ei, k1, z_scr[k1] - par[0] * moved, flip)
        return carry

    lax.fori_loop(0, OUTER, inverse, 0, unroll=8)
    column_first_step(z_scr, y_scr, 1.0)
    back = Exchange(me, out_scr, back_ref, *scratch[7:10])
    give_all(y_scr, back)
    back.wait()


def route_kernel(t_ref, id_ref, slot_ref, tail_ref):
    row = lax.broadcasted_iota(jnp.int32, (INNER, 2 * INNER), 0)
    col = lax.broadcasted_iota(jnp.int32, (INNER, 2 * INNER), 1)
    tri = jnp.where(jnp.logical_or(row < col, col >= INNER), 1.0, 0.0).astype(BF16)
    peer = lax.broadcasted_iota(jnp.int32, (PEERS, INNER), 0)
    base = jnp.zeros((PEERS, INNER), F32)
    for i in range(0, POINT_ROWS, 8):
        hots = [jnp.where(peer == t_ref[i + j : i + j + 1, :], 1.0, 0.0) for j in range(8)]
        cum = mm(jnp.concatenate(hots, axis=0).astype(BF16), tri)
        for j in range(8):
            part = cum[j * PEERS : (j + 1) * PEERS]
            pos = jnp.sum(hots[j] * (part[:, 0:INNER] + base), axis=0, keepdims=True)
            base = base + part[:, INNER : 2 * INNER]
            slot_ref[i + j : i + j + 1, :] = t_ref[i + j : i + j + 1, :] * SLOTS + pos.astype(jnp.int32)
    batch = 4
    index = lax.broadcasted_iota(jnp.int32, (INNER, batch * INNER), 0)

    def wide(ref, i):
        return jnp.concatenate([ref[pl.ds(i * batch + j, 1), :] for j in range(batch)], axis=1)

    def put(i, acc):
        slot = wide(slot_ref, i)
        ids = wide(id_ref, i)
        r = lax.shift_right_logical(ids, 5)
        ids = lax.shift_right_logical(r, 3) * 256 + (ids & 31) * 8 + (r & 7)
        hot = jnp.where(index == (slot & 127), 1.0, 0.0).astype(BF16)
        line = index == lax.shift_right_logical(slot, 7)
        v = [
            jnp.where(line, d.astype(F32), 0.0).astype(BF16) for d in (lax.shift_right_logical(ids, 6), ids & 63)
        ]
        return acc + mm_nt(jnp.concatenate(v, axis=0), hot)

    acc = lax.fori_loop(0, POINT_ROWS // batch, put, jnp.zeros((2 * INNER, INNER), F32), unroll=2)
    ids = (acc[0:INNER] * 64.0 + acc[INNER : 2 * INNER]).astype(jnp.int32)
    count = base.astype(jnp.int32)
    tail_ref[...] = jnp.zeros_like(tail_ref)
    for s in range(PEERS):
        tail_ref[s, 0:4, :] = ids[4 * s : 4 * s + 4]
        tail_ref[s, 4:5, :] = count[s : s + 1]


def pack_kernel(slot_ref, w_ref, out_ref, w_scr, buf):
    def widen(i, carry):
        rows = pl.ds(pl.multiple_of(i * 64, 64), 64)
        w_scr[rows, :] = w_ref[rows, :].astype(F32)
        return carry

    lax.fori_loop(0, POINT_ROWS * INNER // 64, widen, 0, unroll=2)

    def some(q, carry):
        first = q * 32
        slots = [slot_ref[first + j] for j in range(32)]
        rows = [w_scr[pl.ds(first + j, 1), :] for j in range(32)]
        for j in range(32):
            buf[pl.ds(slots[j], 1), :] = rows[j]
        return carry

    lax.fori_loop(0, POINT_ROWS * INNER // 32, some, 0)

    def narrow(i, carry):
        rows = pl.ds(pl.multiple_of(i * INNER, INNER), INNER)
        out_ref[rows, :] = buf[rows, :].astype(BF16)
        return carry

    lax.fori_loop(0, PEERS * SLOTS // INNER, narrow, 0, unroll=2)


def weigh(slot_ref, prec_ref, phase, p_scr):
    high, low = split(phase)
    table = jnp.concatenate([high, low], axis=0)
    batch = 4
    index = lax.broadcasted_iota(jnp.int32, (INNER, batch * INNER), 0)

    def wide(ref, i):
        return jnp.concatenate([ref[pl.ds(i * batch + j, 1), :] for j in range(batch)], axis=1)

    def pick(i, carry):
        slot = wide(slot_ref, i)
        hot = jnp.where(index == (slot & 127), 1.0, 0.0).astype(BF16)
        v = mm(table, hot)
        v = v[0:INNER] + v[INNER : 2 * INNER]
        got = jnp.sum(jnp.where(index == lax.shift_right_logical(slot, 7), v, 0.0), axis=0, keepdims=True)
        for j in range(batch):
            p_scr[pl.ds(i * batch + j, 1), :] = got[:, j * INNER : (j + 1) * INNER]
        return carry

    lax.fori_loop(0, POINT_ROWS // batch, pick, 0, unroll=2)
    row = lax.broadcasted_iota(jnp.int32, (INNER, INNER), 0)
    lane = lax.broadcasted_iota(jnp.int32, (INNER, INNER), 1)
    same = jnp.where((row < HALF) == (lane < HALF), 1.0, 0.0).astype(BF16)
    prec = prec_ref[...]
    phase = p_scr[...]

    def total(value):
        return sum(mm(p, same) for p in reversed(split_into(value, 3)))

    p_scr[...] = prec * (phase - total(prec * phase) / total(prec))

    def put(i, acc):
        slot = wide(slot_ref, i)
        hot = jnp.where(index == (slot & 127), 1.0, 0.0).astype(BF16)
        v = jnp.where(index == lax.shift_right_logical(slot, 7), wide(p_scr, i), 0.0)
        vh, vl = split(v)
        return acc + mm_nt(jnp.concatenate([vh, vl], axis=0), hot)

    acc = lax.fori_loop(0, POINT_ROWS // batch, put, jnp.zeros((2 * INNER, INNER), F32), unroll=2)
    return acc[0:INNER] + acc[INNER : 2 * INNER]


COPIES = 8


def scatter_kernel(
    sid_ref, r_ref, w_ref, tw, f_ref, a_ref, m_ref, out_ref, rt_scr, u_scr, y_scr, e_scr, *accs
):
    def clear(i, carry):
        rows = pl.ds(pl.multiple_of(i * 64, 64), 64)
        for acc in accs:
            acc[rows, :] = jnp.zeros((64, INNER), F32)
        return carry

    lax.fori_loop(0, SIDE // 64, clear, 0)
    rt_scr[...] = r_ref[...].T
    lane = lax.broadcasted_iota(jnp.int32, (INNER, INNER), 1)
    row = lax.broadcasted_iota(jnp.int32, (INNER, INNER), 0)

    def scaled(s, carry):
        for q in range(4):
            col = jnp.sum(jnp.where(lane == s * 4 + q, rt_scr[...], 0.0), axis=1, keepdims=True)
            rows = pl.ds(pl.multiple_of(s * SLOTS + q * INNER, INNER), INNER)
            used = row + q * INNER < sid_ref[s * ID_STRIDE + SLOTS]
            u_scr[rows, :] = jnp.where(used, w_ref[rows, :].astype(F32) * col, 0.0)
        return carry

    lax.fori_loop(0, PEERS, scaled, 0, unroll=2)

    def source(s, carry):
        def some(q, inner):
            first = s * SLOTS + q * 16
            line = s * ID_STRIDE + q * 16
            ids = [sid_ref[line + j] for j in range(16)]
            us = [u_scr[pl.ds(first + j, 1), :] for j in range(16)]
            for h in range(0, 16, COPIES):
                sums = [accs[j][pl.ds(ids[h + j], 1), :] + us[h + j] for j in range(COPIES)]
                for j in range(COPIES):
                    accs[j][pl.ds(ids[h + j], 1), :] = sums[j]
            return inner

        return lax.fori_loop(0, lax.shift_right_logical(sid_ref[s * ID_STRIDE + SLOTS] + 15, 4), some, carry)

    lax.fori_loop(0, PEERS, source, 0)

    def add(i, carry):
        rows = pl.ds(pl.multiple_of(i * 64, 64), 64)
        total = accs[0][rows, :]
        for acc in accs[1:]:
            total = total + acc[rows, :]
        accs[0][rows, :] = total
        return carry

    lax.fori_loop(0, SIDE // 64, add, 0)
    row_forward_kernel(True, False, accs[0], tw, f_ref, a_ref, m_ref, out_ref, y_scr, e_scr)


def call(kernel, name, out_shapes, args, smem=0, scratch=(), any_args=(), any_outs=(), smem_outs=(), collective_id=None):
    spaces = [pltpu.SMEM if i < smem else pl.ANY if i in any_args else pltpu.VMEM for i in range(len(args))]
    outs = [pl.ANY if i in any_outs else pltpu.SMEM if i in smem_outs else pltpu.VMEM for i in range(len(out_shapes))]
    remote = dict(collective_id=collective_id, has_side_effects=True) if collective_id is not None else {}
    return pl.pallas_call(
        kernel,
        out_shape=out_shapes,
        in_specs=[pl.BlockSpec(memory_space=space) for space in spaces],
        out_specs=[pl.BlockSpec(memory_space=space) for space in outs],
        scratch_shapes=list(scratch),
        compiler_params=pltpu.CompilerParams(vmem_limit_bytes=VMEM_BYTES, **remote),
        cost_estimate=pl.CostEstimate(flops=1024, bytes_accessed=1024, transcendentals=0),
        name=name,
    )(*args)


def shape(dims, dtype=F32):
    return jax.ShapeDtypeStruct(dims, dtype)


PENCILS = (PEERS, INNER, INNER)
MESSAGES = (PEERS, INNER + TAIL, INNER)


def row_backward(pencils, base, tables):
    final = base is not None
    args = [pencils] + ([base] if final else []) + tables
    return call(
        lambda *refs: row_backward_kernel(final, *refs),
        "row_backward",
        [shape((INNER, SIDE) if final else (SIDE, INNER))],
        args,
        scratch=[pltpu.VMEM((15 * INNER, 2 * INNER), F32), pltpu.VMEM((2, INNER, INNER), F32)],
    )[0]


def tables_kernel(scale, rate, wind, prior, tab_ref, amp_ref, par_ref):
    strip = lax.axis_index("strip")
    live = (lax.axis_index("tm") < 3).astype(F32)
    k1 = (strip // 2).astype(F32)
    even = strip % 2 == 0
    row = lax.broadcasted_iota(jnp.int32, (INNER, INNER), 0)
    lane = lax.broadcasted_iota(jnp.int32, (INNER, INNER), 1)
    line = row.astype(F32)
    j = (lane & (HALF - 1)).astype(F32)
    cols = jnp.where(even, k1 + OUTER * j, k1 + OUTER * (INNER - 1.0 - j))
    cols = jnp.where(strip == 1, 16.0 + OUTER * j, cols)
    winds = ((wind[0, 0].astype(F32), wind[0, 1].astype(F32)), (prior[1], prior[2]))

    def cosine(turns):
        turns = turns - SIDE * jnp.floor(turns * (1.0 / SIDE))
        return jnp.cos(turns * (2.0 * math.pi / SIDE))

    small = jnp.zeros((INNER, INNER), F32)
    for kind in range(4):
        wind_row, wind_col = winds[kind // 2]
        quarter = (0.0, 3.0 * SIDE / 4, 0.0, SIDE / 4.0)[kind]
        base = OUTER * line * wind_row + quarter
        tab_ref[kind] = cosine(base + cols * wind_col)
        tab_ref[4 + kind] = cosine(base + j * wind_row)
        turns = (row & (OUTER - 1)).astype(F32) * wind_row + quarter
        small = jnp.where(lax.shift_right_logical(row, 5) == kind, turns, small)
    tab_ref[8] = cosine(small)

    fold = jnp.where(even, k1 + OUTER * j, OUTER - k1 + OUTER * j)
    fold = jnp.where(strip == 1, 16.0 + OUTER * j, fold)
    fold = jnp.where(jnp.logical_and(strip == 0, lane == HALF), SIDE / 2.0, fold)
    fold = fold * fold

    def step(k, carry):
        kr = line * OUTER + k.astype(F32)
        kr = jnp.minimum(kr, SIDE - kr)
        radius = (kr * kr + fold) / (KZERO * KZERO)
        amp_ref[k] = SIDE / (2.0 * KZERO) * jnp.exp((-11.0 / 12.0) * jnp.log(1.0 + radius))
        return carry

    lax.fori_loop(0, OUTER, step, 0, unroll=2)
    norm = scale[0] / (SIDE * SIDE)
    mine = rate[0] * live
    par_ref[0] = norm
    par_ref[1] = mine * scale[0]
    par_ref[2] = prior[0] * scale[0]
    par_ref[3] = (mine + prior[0]) * scale[0] * norm
    par_ref[4] = 1.0 - 2.0 * (wind[0, 1] & 1).astype(F32)
    par_ref[5] = 1.0 - 2.0 * (prior[2].astype(jnp.int32) & 1).astype(F32)
    par_ref[6] = 0.0
    par_ref[7] = 0.0


def const(*tables):
    return [jnp.asarray(t) for t in tables]


def local(
    screen_vec,
    prior_scale,
    flow_weight,
    wind,
    pierce_point_strip,
    pierce_block,
    pierce_weights,
    noise_prec,
):
    fwd, inv, first, first_inv, mid, mid_inv, twiddle = row_tables()
    row_fwd_tables = const(twiddle, pieces(fwd, 2), pieces(first, 2), pieces(mid, 2))
    row_fine_tables = const(twiddle, pieces(fwd, 3), pieces(first, 3), pieces(mid, 3))
    row_inv_tables = const(twiddle, pieces(inv, 2), pieces(first_inv, 2), pieces(mid_inv, 2))
    col_fwd, col_inv = column_tables()
    col_fine_tables = const(pieces(col_fwd, 3), pieces(col_inv, 2))
    col_tables = const(pieces(col_fwd, 2), pieces(col_inv, 2))

    x = screen_vec[0]
    weights = pierce_weights[0].reshape(POINT_ROWS * INNER, INNER)
    target = pierce_point_strip.reshape(POINT_ROWS, INNER)
    block = pierce_block.reshape(POINT_ROWS, INNER)
    prec = noise_prec.reshape(POINT_ROWS, INNER)

    mine = jnp.concatenate([flow_weight, wind[0].astype(F32)])
    prior = lax.ppermute(mine, "tm", [(i, i + 1) for i in range(lax.axis_size("tm") - 1)])
    slots, ids = call(
        route_kernel,
        "route",
        [shape((POINT_ROWS, INNER), jnp.int32), shape((PEERS, ID_ROWS, INNER), jnp.int32)],
        [target, block],
    )
    ids, prior, prec = lax.optimization_barrier((ids, prior, prec))
    sent = call(
        pack_kernel,
        "pack",
        [shape((PEERS * SLOTS, INNER), BF16)],
        [slots.reshape(-1), weights],
        smem=1,
        scratch=[pltpu.VMEM((POINT_ROWS * INNER, INNER), F32), pltpu.VMEM((PEERS * SLOTS, INNER), F32)],
    )[0]

    spectral = [pltpu.VMEM(PENCILS, F32), pltpu.VMEM(PENCILS, F32)]
    rows = [pltpu.VMEM((15 * INNER, 2 * INNER), F32), pltpu.VMEM((2, INNER, INNER), F32)]
    message = shape(MESSAGES, BF16)
    points = pltpu.VMEM((PEERS * SLOTS, INNER), F32)
    screen = pltpu.VMEM((SIDE, INNER), F32)
    small = (PEERS, 4, INNER)
    resid, par, own, arrived, amp, here_ids, from_prev, from_next = call(
        first_kernel,
        "first",
        [
            shape(small),
            shape((8,)),
            shape(PENCILS),
            shape((PEERS, SLOTS, INNER), BF16),
            shape(PENCILS),
            shape((PEERS * ID_STRIDE,), jnp.int32),
            shape(PENCILS, BF16),
            shape(PENCILS, BF16),
        ],
        [prior_scale, flow_weight, wind, prior, x]
        + row_fine_tables
        + row_inv_tables[1:]
        + [slots, prec]
        + col_fine_tables
        + [sent.reshape(PEERS, SLOTS, INNER), ids.reshape(-1)],
        smem=4,
        any_args=(14, 15, 16, 17),
        any_outs=(2, 3, 4, 5, 6, 7),
        smem_outs=(1,),
        collective_id=3,
        scratch=spectral
        + [pltpu.VMEM(MESSAGES, BF16)] * 3
        + [pltpu.VMEM((9, INNER, INNER), F32)]
        + rows
        + [pltpu.VMEM(PENCILS, BF16)] * 2
        + [
            screen,
            pltpu.VMEM((SLOTS, INNER), F32),
            pltpu.VMEM(small, F32),
            pltpu.VMEM(small, F32),
            pltpu.VMEM((POINT_ROWS, INNER), F32),
            pltpu.VMEM((INNER, INNER), F32),
            pltpu.VMEM(small, F32),
            pltpu.SMEM((PEERS * ID_STRIDE,), jnp.int32),
            pltpu.SemaphoreType.DMA,
            pltpu.SemaphoreType.DMA((2, 2, SIDE_PARTS)),
            pltpu.VMEM(col_fine_tables[0].shape, BF16),
            pltpu.VMEM(col_fine_tables[1].shape, BF16),
            pltpu.VMEM(PENCILS, F32),
            pltpu.VMEM(PENCILS, F32),
            pltpu.VMEM((PEERS, SLOTS, INNER), BF16),
            pltpu.SemaphoreType.DMA((2,)),
            pltpu.SemaphoreType.DMA((2,)),
            pltpu.SemaphoreType.DMA((1,)),
        ]
        + exchange_sems() * 6,
    )
    here = arrived.reshape(PEERS * SLOTS, INNER)

    pencils = call(
        scatter_kernel,
        "scatter",
        [message],
        [here_ids, resid.reshape(INNER, INNER), here] + row_fwd_tables,
        smem=1,
        scratch=[pltpu.VMEM((INNER, INNER), F32), points] + rows + [screen] * COPIES,
    )[0]
    out_pencils = call(
        column_second_kernel,
        "column_second",
        [message],
        [par, pencils, amp, own, from_prev, from_next] + col_tables,
        smem=1,
        any_args=range(1, 8),
        any_outs=(0,),
        collective_id=1,
        scratch=spectral
        + [pltpu.VMEM(MESSAGES, BF16)] * 2
        + exchange_sems()
        + exchange_sems()
        + spectral
        + [pltpu.VMEM(PENCILS, BF16)] * 2
        + [pltpu.VMEM(t.shape, BF16) for t in col_tables]
        + [pltpu.SemaphoreType.DMA((6,))],
    )[0]
    return row_backward(out_pencils, x, row_inv_tables)[None]


def solution(mesh):
    in_specs = (
        P("tm", "strip", None),
        P("tm"),
        P("tm"),
        P("tm", None),
        P("tm", "strip", None, None),
        P("tm", "strip", None),
        P("tm", "strip", None, None),
        P("tm", "strip", None),
    )
    out_specs = P("tm", "strip", None)
    return jax.shard_map(local, mesh=mesh, in_specs=in_specs, out_specs=out_specs, check_vma=False)
```

```python
import math

import jax
import jax.numpy as jnp
import ml_dtypes
import numpy as np
from jax import lax
from jax.experimental import pallas as pl
from jax.experimental.pallas import tpu as pltpu
from jax.sharding import PartitionSpec as P

KZERO = 2.0
SIDE = 4096
OUTER = 32
INNER = 128
HALF = 64
PEERS = 32
SLOTS = 512
POINT_ROWS = 64
TAIL = 16
ID_ROWS = 8
ID_STRIDE = ID_ROWS * 128
VMEM_BYTES = 56 * 1024 * 1024
F32 = jnp.float32
BF16 = jnp.bfloat16


def pieces(table, count):
    rest = np.asarray(table, np.float64)
    out = []
    for _ in range(count):
        out.append(rest.astype(np.float32).astype(ml_dtypes.bfloat16))
        rest = rest - out[-1].astype(np.float64)
    return np.stack(out)


def row_tables():
    b = np.arange(INNER)[:, None]
    j = np.arange(HALF)[None, :]
    theta = [2 * np.pi * ((b * j) % INNER) / INNER, 2 * np.pi * ((b * (INNER - 1 - j)) % INNER) / INNER]
    forward = []
    backward = []
    for t in theta:
        forward.append(np.concatenate([np.cos(t), -np.sin(t)], axis=1))
        forward.append(np.concatenate([np.sin(t), np.cos(t)], axis=1))
        backward.append(np.concatenate([np.cos(t).T, np.sin(t).T], axis=1))
        backward.append(np.concatenate([-np.sin(t).T, np.cos(t).T], axis=1))
    fwd = np.concatenate(
        [np.concatenate([forward[0], forward[1]], axis=0), np.concatenate([forward[2], forward[3]], axis=0)], axis=1
    )
    inv = np.concatenate(backward, axis=0)
    sign = np.where(np.arange(INNER) % 2 == 0, 1.0, -1.0)
    t0 = theta[0]
    first = np.concatenate([np.cos(t0), -np.sin(t0)], axis=1)
    first[:, HALF] = sign
    first_inv = np.concatenate([2 * np.cos(t0).T, -2 * np.sin(t0).T], axis=0)
    first_inv[0, :] = 1.0
    first_inv[HALF, :] = sign
    t16 = 2 * np.pi * ((b * (16 + 32 * j)) % SIDE) / SIDE
    mid = np.concatenate([np.cos(t16), -np.sin(t16)], axis=1)
    mid_inv = np.concatenate([2 * np.cos(t16).T, -2 * np.sin(t16).T], axis=0)
    k1 = np.arange(16)[:, None]
    tw = 2 * np.pi * (k1 * np.arange(INNER)[None, :]) / SIDE
    twiddle = np.stack([np.cos(tw), np.sin(tw)]).astype(np.float32)
    return fwd, inv, first, first_inv, mid, mid_inv, twiddle


def column_tables():
    k1 = np.arange(OUTER)[:, None, None]
    k2 = np.arange(INNER)[None, :, None]
    r = np.arange(INNER)[None, None, :]
    theta = 2 * np.pi * (((k1 + OUTER * k2) * r) % SIDE) / SIDE
    fwd = np.concatenate([np.cos(theta), -np.sin(theta)], axis=1)
    theta = theta.transpose(0, 2, 1)
    inv = np.concatenate([np.cos(theta), np.sin(theta)], axis=1)
    return fwd, inv


def split(value):
    high = value.astype(BF16)
    return high, (value - high.astype(F32)).astype(BF16)


def mm(left, right):
    return lax.dot_general(left, right, (((1,), (0,)), ((), ())), preferred_element_type=F32)


def mm_nt(left, right):
    return lax.dot_general(left, right, (((1,), (1,)), ((), ())), preferred_element_type=F32)


def split_into(value, count):
    parts = []
    for i in range(count):
        parts.append(value.astype(BF16))
        if i + 1 < count:
            value = value - parts[-1].astype(F32)
    return parts


def data_by_table(value, tables):
    count = len(tables)
    parts = split_into(value, count)
    total = None
    for order in reversed(range(count)):
        for i in range(order + 1):
            term = mm(parts[i], tables[order - i])
            total = term if total is None else total + term
    return total


def table_by_data(tables, value):
    parts = split_into(value, len(tables))
    left = jnp.concatenate(tables[0:2], axis=1)
    right = jnp.concatenate(parts[0:2], axis=1)
    r = mm(left, jnp.concatenate([right, right], axis=0))
    total = r[:, INNER : 2 * INNER] + r[:, 0:INNER]
    if len(tables) == 3:
        left = jnp.concatenate([tables[0], tables[2]], axis=1)
        total = total + mm(left, jnp.concatenate([parts[2], parts[0]], axis=0))
    return total


def every(ref):
    return [ref[i] for i in range(ref.shape[0])]


def c_mul(value, factor):
    re, im = value
    c, s = factor.real, factor.imag
    if im is None:
        return (re * c, re * s)
    return (re * c - im * s, re * s + im * c)


def real_forward(xs):
    n = len(xs)
    if n == 2:
        return [(xs[0] + xs[1], None), (xs[0] - xs[1], None)]
    even, odd = real_forward(xs[0::2]), real_forward(xs[1::2])
    m = n // 2
    out = [None] * (m + 1)
    for k in range(m // 2 + 1):
        if k == 0:
            out[0] = (even[0][0] + odd[0][0], None)
            out[m] = (even[0][0] - odd[0][0], None)
        elif 2 * k == m:
            out[k] = (even[k][0], -odd[k][0])
        else:
            tr, ti = c_mul(odd[k], complex(math.cos(2 * math.pi * k / n), -math.sin(2 * math.pi * k / n)))
            er, ei = even[k]
            out[k] = (er + tr, ei + ti)
            out[m - k] = (er - tr, ti - ei)
    return out


def real_backward(spec):
    n = 2 * (len(spec) - 1)
    if n == 2:
        return [spec[0][0] + spec[1][0], spec[0][0] - spec[1][0]]
    m = n // 2
    even, odd = [], []
    for k in range(m // 2 + 1):
        if k == 0:
            even.append((spec[0][0] + spec[m][0], None))
            odd.append((spec[0][0] - spec[m][0], None))
        elif 2 * k == m:
            even.append((2.0 * spec[k][0], None))
            odd.append((-2.0 * spec[k][1], None))
        else:
            ar, ai = spec[k]
            br, bi = spec[m - k]
            even.append((ar + br, ai - bi))
            odd.append(c_mul((ar - br, ai + bi), complex(math.cos(2 * math.pi * k / n), math.sin(2 * math.pi * k / n))))
    xe, xo = real_backward(even), real_backward(odd)
    out = [None] * n
    out[0::2] = xe
    out[1::2] = xo
    return out


def packed_fft(xs, sign, flip):
    n = len(xs)
    if n == 1:
        return xs
    even, odd = packed_fft(xs[0::2], sign, flip), packed_fft(xs[1::2], sign, flip)
    out = [None] * n
    for k in range(n // 2):
        t = odd[k]
        if k:
            turned = pltpu.roll(t, HALF, 1) * flip
            c, s = math.cos(2 * math.pi * k / n), sign * math.sin(2 * math.pi * k / n)
            t = (-s) * turned if 4 * k == n else c * t - s * turned
        out[k] = even[k] + t
        out[k + n // 2] = even[k] - t
    return out


def flip_lanes(rows):
    lane = lax.broadcasted_iota(jnp.int32, (rows, INNER), 1)
    return jnp.where(lane < HALF, 1.0, -1.0).astype(F32)


def put_message(ref, d, value, fine):
    lane = lax.broadcasted_iota(jnp.int32, (INNER, INNER), 1)
    high = value.astype(BF16)
    ref[d, 0:INNER, :] = high
    rest = value - high.astype(F32)
    if fine:
        third = rest - rest.astype(BF16).astype(F32)
        rest = jnp.where((lane & (HALF - 1)) == 7, pltpu.roll(third, 7, 1), rest)
    rest = jnp.where(lane < 8, rest, pltpu.roll(rest, 72, 1))
    rest = jnp.where(lane < 16, rest, 0.0)
    total = rest[0:16]
    for g in range(1, 8):
        total = total + pltpu.roll(rest[16 * g : 16 * g + 16], 16 * g, 1)
    ref[d, INNER : INNER + TAIL, :] = total.astype(BF16)


def get_message(ref, d, fine):
    lane = lax.broadcasted_iota(jnp.int32, (INNER, INNER), 1)
    packed = ref[d, INNER : INNER + TAIL, :].astype(F32)
    rest = jnp.concatenate([packed] + [pltpu.roll(packed, INNER - 16 * g, 1) for g in range(1, 8)], axis=0)
    rest = jnp.where(lane < 8, rest, pltpu.roll(rest, 56, 1))
    column = lane & (HALF - 1)
    if fine:
        third = jnp.where(column == 0, pltpu.roll(rest, INNER - 7, 1), 0.0)
        rest = jnp.where(column < 7, rest, 0.0) + third
    else:
        rest = jnp.where(column < 8, rest, 0.0)
    return ref[d, 0:INNER, :].astype(F32) + rest


def row_forward_kernel(tiled, fine, x_ref, tw_ref, f_ref, a_ref, m_ref, out_ref, y_scr, e_scr):
    def slab(g, carry):
        if tiled:
            xs = [x_ref[pl.ds(pl.multiple_of(g * 256 + a * 8, 8), 8), :] for a in range(OUTER)]
        else:
            xs = [x_ref[pl.ds(pl.multiple_of(g * 8, 8), 8), a * INNER : (a + 1) * INNER] for a in range(OUTER)]
        ys = real_forward(xs)
        rows = pl.ds(pl.multiple_of(g * 8, 8), 8)
        e_scr[0, rows, :] = ys[0][0]
        e_scr[1, rows, :] = ys[16][0]
        for k in range(1, 16):
            c = tw_ref[0, k : k + 1, :]
            s = tw_ref[1, k : k + 1, :]
            re, im = ys[k]
            base = pl.ds(pl.multiple_of((k - 1) * INNER + g * 8, 8), 8)
            y_scr[base, 0:INNER] = re * c + im * s
            y_scr[base, INNER : 2 * INNER] = im * c - re * s
        return carry

    lax.fori_loop(0, 16, slab, 0, unroll=2)
    put_message(out_ref, 0, data_by_table(e_scr[0], every(a_ref)), fine)
    put_message(out_ref, 1, data_by_table(e_scr[1], every(m_ref)), fine)

    def group(q, carry):
        v = data_by_table(y_scr[pl.ds(pl.multiple_of(q * 384, 8), 384), :], every(f_ref))
        for i in range(3):
            rows = v[i * INNER : (i + 1) * INNER]
            put_message(out_ref, 2 + 2 * (3 * q + i), rows[:, 0:INNER], fine)
            put_message(out_ref, 3 + 2 * (3 * q + i), rows[:, INNER : 2 * INNER], fine)
        return carry

    lax.fori_loop(0, 5, group, 0)


def row_backward_kernel(final, *refs):
    if final:
        in_ref, base_ref, tw_ref, f_ref, a_ref, m_ref, out_ref, z_scr, e_scr = refs
    else:
        in_ref, tw_ref, f_ref, a_ref, m_ref, out_ref, z_scr, e_scr = refs
    e_scr[0] = data_by_table(get_message(in_ref, 0, False), every(a_ref))
    e_scr[1] = data_by_table(get_message(in_ref, 1, False), every(m_ref))

    def group(q, carry):
        parts = []
        for i in range(3):
            k = 3 * q + i
            parts.append(jnp.concatenate([get_message(in_ref, 2 + 2 * k + h, False) for h in range(2)], axis=1))
        v = jnp.concatenate(parts, axis=0)
        z_scr[pl.ds(pl.multiple_of(q * 384, 8), 384), :] = data_by_table(v, every(f_ref))
        return carry

    lax.fori_loop(0, 5, group, 0)

    def slab(g, carry):
        rows = pl.ds(pl.multiple_of(g * 8, 8), 8)
        spec = [(e_scr[0, rows, :], None)]
        for k in range(1, 16):
            c = tw_ref[0, k : k + 1, :]
            s = tw_ref[1, k : k + 1, :]
            base = pl.ds(pl.multiple_of((k - 1) * INNER + g * 8, 8), 8)
            re = z_scr[base, 0:INNER]
            im = z_scr[base, INNER : 2 * INNER]
            spec.append((re * c - im * s, im * c + re * s))
        spec.append((e_scr[1, rows, :], None))
        xs = real_backward(spec)
        for a in range(OUTER):
            if final:
                cols = slice(a * INNER, (a + 1) * INNER)
                out_ref[rows, cols] = base_ref[rows, cols] + xs[a]
            else:
                out_ref[pl.ds(pl.multiple_of(g * 256 + a * 8, 8), 8), :] = xs[a]
        return carry

    lax.fori_loop(0, 16, slab, 0, unroll=2)


def take_all(exchange, scr, fine):
    exchange.own.wait()
    scr[exchange.me] = get_message(exchange.out_ref, exchange.me, fine)

    def step(i, carry):
        exchange.wait_source(i)
        source = exchange.source(i)
        scr[source] = get_message(exchange.out_ref, source, fine)
        return carry

    lax.fori_loop(0, PEERS - 1, step, 0)
    exchange.wait_sends()


def give_all(scr, exchange):
    def step(i, carry):
        peer = exchange.peer(i)
        put_message(exchange.in_ref, peer, scr[peer], False)
        exchange.send(i)
        return carry

    lax.fori_loop(0, PEERS - 1, step, 0)
    put_message(exchange.in_ref, exchange.me, scr[exchange.me], False)
    exchange.own.start()


def column_first_step(in_ref, y_scr, sign):
    flip = flip_lanes(8)

    def slab(g, carry):
        rows = pl.ds(pl.multiple_of(g * 8, 8), 8)
        ys = packed_fft([in_ref[s, rows, :] for s in range(OUTER)], sign, flip)
        for k in range(OUTER):
            y_scr[k, rows, :] = ys[k]
        return carry

    lax.fori_loop(0, 16, slab, 0, unroll=2)


def apply_packed(e_ref, k1, value, flip):
    r = table_by_data([e_ref[i, k1] for i in range(e_ref.shape[0])], value)
    return r[0:INNER] - pltpu.roll(r[INNER : 2 * INNER], HALF, 1) * flip


MESH = pl.DeviceIdType.MESH


def greet_peers(me, barrier, extra=()):
    def greet(i, carry):
        pl.semaphore_signal(barrier, inc=1, device_id={"strip": lax.rem(me + i, PEERS)}, device_id_type=MESH)
        return carry

    lax.fori_loop(1, PEERS, greet, 0)
    for device in extra:
        pl.semaphore_signal(barrier, inc=1, device_id=device, device_id_type=MESH)
    pl.semaphore_wait(barrier, PEERS - 1 + len(extra))


class Exchange:
    def __init__(self, me, in_ref, out_ref, send_sem, recv_sem, own_sem, flat=0):
        self.me, self.in_ref, self.out_ref, self.flat = me, in_ref, out_ref, flat
        self.send_sem, self.recv_sem = send_sem, recv_sem
        self.own = pltpu.make_async_copy(self.part(in_ref, me), self.part(out_ref, me), own_sem)

    def part(self, ref, i):
        return ref.at[pl.ds(pl.multiple_of(i * self.flat, self.flat), self.flat)] if self.flat else ref.at[i]

    def copy(self, peer, send, source):
        return pltpu.make_async_remote_copy(
            src_ref=self.part(self.in_ref, peer),
            dst_ref=self.part(self.out_ref, source),
            send_sem=self.send_sem.at[send],
            recv_sem=self.recv_sem.at[source],
            device_id={"strip": peer},
            device_id_type=MESH,
        )

    def peer(self, i):
        return lax.rem(self.me + 1 + i, PEERS)

    def source(self, i):
        return lax.rem(self.me + PEERS - 1 - i, PEERS)

    def send(self, i):
        self.copy(self.peer(i), i, self.me).start()

    def wait_source(self, i):
        self.copy(self.peer(i), i, self.source(i)).wait_recv()

    def wait_sends(self):
        def step(i, carry):
            self.copy(self.peer(i), i, self.me).wait_send()
            return carry

        lax.fori_loop(0, PEERS - 1, step, 0)

    def start(self, first=0, last=PEERS - 1):
        def step(i, carry):
            self.copy(self.peer(i), i, self.me).start()
            return carry

        lax.fori_loop(first, last, step, 0)
        if first == 0:
            self.own.start()

    def wait(self):
        def step(i, carry):
            self.wait_source(i)
            return carry

        self.own.wait()
        lax.fori_loop(0, PEERS - 1, step, 0)
        self.wait_sends()


class Moves:
    def __init__(self, pairs, sems):
        self.copies = [pltpu.make_async_copy(src, dst, sems.at[i]) for i, (src, dst) in enumerate(pairs)]

    def start(self):
        for copy in self.copies:
            copy.start()

    def wait(self):
        for copy in self.copies:
            copy.wait()


def exchange_sems():
    return [pltpu.SemaphoreType.DMA((PEERS,)), pltpu.SemaphoreType.DMA((PEERS,)), pltpu.SemaphoreType.DMA]


def edge_lanes():
    lane = lax.broadcasted_iota(jnp.int32, (INNER, INNER), 1)
    return jnp.logical_or(lane == 0, lane == HALF), lane < HALF


def edge_gather(ref):
    mask, _ = edge_lanes()

    def step(k1, acc):
        return acc + pltpu.roll(jnp.where(mask, ref[k1], 0.0), k1, 1)

    return lax.fori_loop(0, OUTER, step, jnp.zeros((INNER, INNER), F32), unroll=4)


def edge_split(spec, amp):
    i = lax.broadcasted_iota(jnp.int32, (INNER, INNER), 0)
    j = lax.broadcasted_iota(jnp.int32, (INNER, INNER), 1)
    one = jnp.ones((INNER, INNER), F32)
    none = jnp.zeros((INNER, INNER), F32)
    rows = jnp.where(i + j == INNER - 1, one, none).astype(BF16)
    rows0 = jnp.where(((i + j) & (INNER - 1)) == 0, one, none).astype(BF16)
    sign = jnp.where(j < HALF, one, -one)
    col = j & (HALF - 1)
    same = (i < HALF) == (j < HALF)
    lanes = jnp.where(
        jnp.logical_and(same, jnp.logical_and(col > 0, col + (i & (HALF - 1)) == OUTER)), sign, none
    ).astype(BF16)
    lanes0 = jnp.where(jnp.logical_and(i == j, col == 0), sign, none).astype(BF16)

    def move(left, value, right):
        value = sum(mm(left, p) for p in reversed(split_into(value, 3)))
        return sum(mm(p, right) for p in reversed(split_into(value, 3)))

    rev = move(rows, spec, lanes) + move(rows0, spec, lanes0)
    swapped = pltpu.roll(amp, HALF, 1)
    _, left = edge_lanes()
    a0 = jnp.where(left, amp, swapped)
    a2 = jnp.where(left, swapped, amp)
    return 0.5 * (spec + rev), 0.5 * (spec - rev), a0, a2


def turn(c, s, value, flip):
    return c * value + s * (pltpu.roll(value, HALF, 1) * flip)


EARLY = 4
MIDDLE = 16


def first_kernel(
    scale, rate, wind, prior, x_ref, tw, f_ref, a_ref, m_ref, fi_ref, ai_ref, mi_ref, slot_ref, prec_ref,
    ef_any, ei_any, sent_ref, ids_ref,
    resid_ref, par, own_any, here_any, amp_any, here_ids_ref, prev_ref, next_ref, *scratch,
):
    y_scr, z_scr, msg_scr, land_scr, back_scr, tab_ref, row_scr, row_edge = scratch[0:8]
    up_ref, down_ref, tiles_scr, g_scr, phase_scr, landed, p_scr, table_scr, res_scr = scratch[8:17]
    sid_scr, sid_sem, side_sems = scratch[17:20]
    ef, ei, own_ref, amp_ref, here_ref, in_sems, out_sems, here_sems = scratch[20:28]
    sems = scratch[28:]
    tables = Moves([(ef_any, ef), (ei_any, ei)], in_sems)
    tables.start()
    results = Moves([(own_ref, own_any), (amp_ref, amp_any)], out_sems)
    weights_out = Moves([(here_ref, here_any)], here_sems)
    me = lax.axis_index("strip")
    slot_at = lax.axis_index("tm")
    above, below = lax.rem(slot_at + 1, 4), lax.rem(slot_at + 3, 4)
    greet_peers(me, pltpu.get_barrier_semaphore(), ({"tm": above}, {"tm": below}))
    ids = Exchange(me, ids_ref, here_ids_ref, *sems[0:3], flat=ID_STRIDE)
    weights = Exchange(me, sent_ref, here_ref, *sems[3:6])
    pencils = Exchange(me, msg_scr, land_scr, *sems[6:9])
    back = Exchange(me, msg_scr, back_scr, *sems[9:12])
    phases = Exchange(me, phase_scr, landed, *sems[12:15])
    residuals = Exchange(me, res_scr, resid_ref, *sems[15:18])
    ids.start()
    weights.start(0, EARLY)
    row_forward_kernel(False, True, x_ref, tw, f_ref, a_ref, m_ref, msg_scr, row_scr, row_edge)
    pencils.start()
    tables_kernel(scale, rate, wind, prior, tab_ref, amp_ref, par)
    take_all(pencils, z_scr, True)
    weights.start(EARLY, MIDDLE)
    tables.wait()
    column_first_step(z_scr, y_scr, -1.0)
    flip = flip_lanes(INNER)

    def step(k1, carry):
        value = apply_packed(ef, k1, y_scr[k1], flip)
        amp = amp_ref[k1]
        once = value * amp
        twice = once * amp
        y_scr[k1] = value
        z_scr[k1] = par[0] * once
        own_ref[k1] = par[3] * twice
        for n, ref, gain in ((0, up_ref, par[1]), (1, down_ref, par[2])):
            cb = tab_ref[2 * n]
            sb = tab_ref[2 * n + 1]
            ca = tab_ref[8, pl.ds(64 * n + k1, 1), :] * gain
            sa = tab_ref[8, pl.ds(64 * n + 32 + k1, 1), :] * gain
            ref[k1] = turn(cb * ca - sb * sa, sb * ca + cb * sa, twice, flip).astype(BF16)
        return carry

    lax.fori_loop(0, OUTER, step, 0, unroll=8)

    @pl.when(me == 0)
    def _():
        u0, u2, a0, a2 = edge_split(edge_gather(y_scr), edge_gather(amp_ref))
        mask, _ = edge_lanes()
        e0 = a0 * u0
        e2 = a2 * u2
        fixed = [par[0] * (e0 + e2)]
        e0 = a0 * e0
        e2 = a2 * e2
        fixed.append(par[3] * (e0 + e2))
        fixed.append(par[1] * turn(tab_ref[4], tab_ref[5], e0 + par[4] * e2, flip))
        fixed.append(par[2] * turn(tab_ref[6], tab_ref[7], e0 + par[5] * e2, flip))

        def put(k1, carry):
            back = lax.rem(INNER - k1, INNER)
            for ref, value in zip((z_scr, own_ref, up_ref, down_ref), fixed):
                value = jnp.where(mask, pltpu.roll(value, back, 1), ref[k1].astype(F32))
                ref[k1] = value.astype(ref.dtype)
            return carry

        lax.fori_loop(0, OUTER, put, 0, unroll=4)

    def inverse(k1, carry):
        z_scr[k1] = apply_packed(ei, k1, z_scr[k1], flip)
        return carry

    lax.fori_loop(0, OUTER, inverse, 0, unroll=8)
    column_first_step(z_scr, y_scr, 1.0)
    give_all(y_scr, back)
    results.start()
    ids.wait()
    fetch = pltpu.make_async_copy(here_ids_ref, sid_scr, sid_sem)
    fetch.start()
    back.wait()
    weights.start(MIDDLE, PEERS - 1)
    row_backward_kernel(False, back_scr, tw, fi_ref, ai_ref, mi_ref, tiles_scr, row_scr, row_edge)
    fetch.wait()
    ones = jnp.ones((2 * INNER, INNER), BF16)
    row = lax.broadcasted_iota(jnp.int32, (INNER, INNER), 0)
    lane = lax.broadcasted_iota(jnp.int32, (INNER, INNER), 1)
    place = lax.broadcasted_iota(jnp.int32, (1, INNER), 1)

    def gather_source(s):
        def some(q, carry):
            first = s * ID_STRIDE + q * 16
            picks = [sid_scr[first + j] for j in range(16)]
            rows = [tiles_scr[pl.ds(picks[j], 1), :] for j in range(16)]
            for j in range(16):
                g_scr[pl.ds(q * 16 + j, 1), :] = rows[j]
            return carry

        lax.fori_loop(0, SLOTS // 16, some, 0)
        count = sid_scr[s * ID_STRIDE + SLOTS]
        sums = mm(jnp.concatenate(split(g_scr[...] * here_ref[s].astype(F32)), axis=1), ones)
        for q in range(4):
            got = jnp.where(row == lane, sums[q * INNER : (q + 1) * INNER], 0.0)
            got = jnp.sum(got, axis=0, keepdims=True)
            phase_scr[s, q : q + 1, :] = jnp.where(place + q * INNER < count, got, 0.0)

    weights.own.wait()
    gather_source(me)
    phases.own.start()

    def gather_next(i, carry):
        weights.wait_source(i)
        source = weights.source(i)
        gather_source(source)
        phases.copy(source, PEERS - 2 - i, me).start()
        return carry

    lax.fori_loop(0, PEERS - 1, gather_next, 0)
    weights.wait_sends()
    weights_out.start()

    @pl.when(slot_at < 3)
    def _():
        for side in sides(side_sems, up_ref, prev_ref, above, 0):
            side.start()

    @pl.when(slot_at > 0)
    def _():
        for side in sides(side_sems, down_ref, next_ref, below, 1):
            side.start()

    phases.wait()
    for s in range(PEERS):
        table_scr[4 * s : 4 * s + 4, :] = landed[s]
    acc = weigh(slot_ref, prec_ref, table_scr[...], p_scr)
    for s in range(PEERS):
        res_scr[s] = acc[4 * s : 4 * s + 4]
    residuals.start()
    results.wait()
    weights_out.wait()
    residuals.wait()

    @pl.when(slot_at < 3)
    def _():
        for side in sides(side_sems, up_ref, prev_ref, above, 0):
            side.wait_send()
        for side in sides(side_sems, down_ref, next_ref, below, 1):
            side.wait_recv()

    @pl.when(slot_at > 0)
    def _():
        for side in sides(side_sems, up_ref, prev_ref, above, 0):
            side.wait_recv()
        for side in sides(side_sems, down_ref, next_ref, below, 1):
            side.wait_send()


SIDE_PARTS = 4


def sides(sems, src, dst, device, n):
    copies = []
    for p in range(SIDE_PARTS):
        rows = pl.ds(p * (OUTER // SIDE_PARTS), OUTER // SIDE_PARTS)
        copies.append(
            pltpu.make_async_remote_copy(
                src_ref=src.at[rows],
                dst_ref=dst.at[rows],
                send_sem=sems.at[0, n, p],
                recv_sem=sems.at[1, n, p],
                device_id={"tm": device},
                device_id_type=MESH,
            )
        )
    return copies


def column_second_kernel(par, in_ref, amp_any, own_any, prev_any, next_any, ef_any, ei_any, back_ref, *scratch):
    y_scr, z_scr, msg_scr, out_scr = scratch[0:4]
    amp_ref, own_ref, prev_ref, next_ref, ef, ei, in_sems = scratch[10:17]
    inputs = Moves(
        [(amp_any, amp_ref), (own_any, own_ref), (prev_any, prev_ref), (next_any, next_ref), (ef_any, ef), (ei_any, ei)],
        in_sems,
    )
    inputs.start()
    me = lax.axis_index("strip")
    slot_at = lax.axis_index("tm")
    greet_peers(me, pltpu.get_barrier_semaphore())
    pencils = Exchange(me, in_ref, msg_scr, *scratch[4:7])
    pencils.start()
    take_all(pencils, z_scr, False)
    inputs.wait()
    column_first_step(z_scr, y_scr, -1.0)
    flip = flip_lanes(INNER)

    def step(k1, carry):
        value = apply_packed(ef, k1, y_scr[k1], flip)
        y_scr[k1] = value
        z_scr[k1] = par[0] * (value * amp_ref[k1]) + own_ref[k1]
        return carry

    lax.fori_loop(0, OUTER, step, 0, unroll=8)

    @pl.when(me == 0)
    def _():
        spec = edge_gather(y_scr)
        amp = edge_gather(amp_ref)
        u0, u2, a0, a2 = edge_split(spec, amp)
        mask, _ = edge_lanes()
        change = par[0] * (a0 * u0 + a2 * u2 - amp * spec)

        def put(k1, carry):
            back = lax.rem(INNER - k1, INNER)
            z_scr[k1] = z_scr[k1] + jnp.where(mask, pltpu.roll(change, back, 1), 0.0)
            return carry

        lax.fori_loop(0, OUTER, put, 0, unroll=4)

    def inverse(k1, carry):
        moved = jnp.where(slot_at > 0, prev_ref[k1].astype(F32), 0.0)
        moved = moved + jnp.where(slot_at < 3, next_ref[k1].astype(F32), 0.0)
        z_scr[k1] = apply_packed(ei, k1, z_scr[k1] - par[0] * moved, flip)
        return carry

    lax.fori_loop(0, OUTER, inverse, 0, unroll=8)
    column_first_step(z_scr, y_scr, 1.0)
    back = Exchange(me, out_scr, back_ref, *scratch[7:10])
    give_all(y_scr, back)
    back.wait()


def side_by_side(ref):
    return jnp.concatenate([ref[0:POINT_ROWS, :], ref[POINT_ROWS : 2 * POINT_ROWS, :]], axis=1)


def route_kernel(t_any, id_any, slot_ref, tail_ref, t_ref, id_ref):
    t_ref[...] = side_by_side(t_any)
    id_ref[...] = side_by_side(id_any)
    row = lax.broadcasted_iota(jnp.int32, (INNER, 2 * INNER), 0)
    col = lax.broadcasted_iota(jnp.int32, (INNER, 2 * INNER), 1)
    tri = jnp.where(jnp.logical_or(row < col, col >= INNER), 1.0, 0.0).astype(BF16)
    peer = lax.broadcasted_iota(jnp.int32, (PEERS, INNER), 0)
    base = jnp.zeros((PEERS, INNER), F32)
    for i in range(0, POINT_ROWS, 8):
        hots = [jnp.where(peer == t_ref[i + j : i + j + 1, :], 1.0, 0.0) for j in range(8)]
        cum = mm(jnp.concatenate(hots, axis=0).astype(BF16), tri)
        for j in range(8):
            part = cum[j * PEERS : (j + 1) * PEERS]
            pos = jnp.sum(hots[j] * (part[:, 0:INNER] + base), axis=0, keepdims=True)
            base = base + part[:, INNER : 2 * INNER]
            slot_ref[i + j : i + j + 1, :] = t_ref[i + j : i + j + 1, :] * SLOTS + pos.astype(jnp.int32)
    batch = 4
    index = lax.broadcasted_iota(jnp.int32, (INNER, batch * INNER), 0)

    def wide(ref, i):
        return jnp.concatenate([ref[pl.ds(i * batch + j, 1), :] for j in range(batch)], axis=1)

    def put(i, acc):
        slot = wide(slot_ref, i)
        ids = wide(id_ref, i)
        r = lax.shift_right_logical(ids, 5)
        ids = lax.shift_right_logical(r, 3) * 256 + (ids & 31) * 8 + (r & 7)
        hot = jnp.where(index == (slot & 127), 1.0, 0.0).astype(BF16)
        line = index == lax.shift_right_logical(slot, 7)
        v = [
            jnp.where(line, d.astype(F32), 0.0).astype(BF16) for d in (lax.shift_right_logical(ids, 6), ids & 63)
        ]
        return acc + mm_nt(jnp.concatenate(v, axis=0), hot)

    acc = lax.fori_loop(0, POINT_ROWS // batch, put, jnp.zeros((2 * INNER, INNER), F32), unroll=2)
    ids = (acc[0:INNER] * 64.0 + acc[INNER : 2 * INNER]).astype(jnp.int32)
    count = base.astype(jnp.int32)
    tail_ref[...] = jnp.zeros_like(tail_ref)
    for s in range(PEERS):
        tail_ref[s, 0:4, :] = ids[4 * s : 4 * s + 4]
        tail_ref[s, 4:5, :] = count[s : s + 1]


def pack_kernel(slot_ref, w_ref, out_ref, w_scr, buf):
    def widen(i, carry):
        rows = pl.ds(pl.multiple_of(i * 64, 64), 64)
        w_scr[rows, :] = w_ref[rows, :].astype(F32)
        return carry

    lax.fori_loop(0, POINT_ROWS * INNER // 64, widen, 0, unroll=2)

    def some(q, carry):
        first = q * 32
        slots = [slot_ref[first + j] for j in range(32)]
        line = (q // 4 + (q % 4) // 2 * POINT_ROWS) * HALF + (q % 2) * 32
        rows = [w_scr[pl.ds(line + j, 1), :] for j in range(32)]
        for j in range(32):
            buf[pl.ds(slots[j], 1), :] = rows[j]
        return carry

    lax.fori_loop(0, POINT_ROWS * INNER // 32, some, 0)

    def narrow(i, carry):
        rows = pl.ds(pl.multiple_of(i * INNER, INNER), INNER)
        out_ref[rows, :] = buf[rows, :].astype(BF16)
        return carry

    lax.fori_loop(0, PEERS * SLOTS // INNER, narrow, 0, unroll=2)


def weigh(slot_ref, prec_ref, phase, p_scr):
    high, low = split(phase)
    table = jnp.concatenate([high, low], axis=0)
    batch = 4
    index = lax.broadcasted_iota(jnp.int32, (INNER, batch * INNER), 0)

    def wide(ref, i):
        return jnp.concatenate([ref[pl.ds(i * batch + j, 1), :] for j in range(batch)], axis=1)

    def pick(i, carry):
        slot = wide(slot_ref, i)
        hot = jnp.where(index == (slot & 127), 1.0, 0.0).astype(BF16)
        v = mm(table, hot)
        v = v[0:INNER] + v[INNER : 2 * INNER]
        got = jnp.sum(jnp.where(index == lax.shift_right_logical(slot, 7), v, 0.0), axis=0, keepdims=True)
        for j in range(batch):
            p_scr[pl.ds(i * batch + j, 1), :] = got[:, j * INNER : (j + 1) * INNER]
        return carry

    lax.fori_loop(0, POINT_ROWS // batch, pick, 0, unroll=2)
    row = lax.broadcasted_iota(jnp.int32, (INNER, INNER), 0)
    lane = lax.broadcasted_iota(jnp.int32, (INNER, INNER), 1)
    same = jnp.where((row < HALF) == (lane < HALF), 1.0, 0.0).astype(BF16)
    prec = side_by_side(prec_ref)
    phase = p_scr[...]

    def total(value):
        return sum(mm(p, same) for p in reversed(split_into(value, 3)))

    p_scr[...] = prec * (phase - total(prec * phase) / total(prec))

    def put(i, acc):
        slot = wide(slot_ref, i)
        hot = jnp.where(index == (slot & 127), 1.0, 0.0).astype(BF16)
        v = jnp.where(index == lax.shift_right_logical(slot, 7), wide(p_scr, i), 0.0)
        vh, vl = split(v)
        return acc + mm_nt(jnp.concatenate([vh, vl], axis=0), hot)

    acc = lax.fori_loop(0, POINT_ROWS // batch, put, jnp.zeros((2 * INNER, INNER), F32), unroll=2)
    return acc[0:INNER] + acc[INNER : 2 * INNER]


COPIES = 8


def scatter_kernel(
    sid_ref, r_ref, w_ref, tw, f_ref, a_ref, m_ref, out_ref, rt_scr, u_scr, y_scr, e_scr, *accs
):
    def clear(i, carry):
        rows = pl.ds(pl.multiple_of(i * 64, 64), 64)
        for acc in accs:
            acc[rows, :] = jnp.zeros((64, INNER), F32)
        return carry

    lax.fori_loop(0, SIDE // 64, clear, 0)
    rt_scr[...] = r_ref[...].T
    lane = lax.broadcasted_iota(jnp.int32, (INNER, INNER), 1)
    row = lax.broadcasted_iota(jnp.int32, (INNER, INNER), 0)

    def scaled(s, carry):
        for q in range(4):
            col = jnp.sum(jnp.where(lane == s * 4 + q, rt_scr[...], 0.0), axis=1, keepdims=True)
            rows = pl.ds(pl.multiple_of(s * SLOTS + q * INNER, INNER), INNER)
            used = row + q * INNER < sid_ref[s * ID_STRIDE + SLOTS]
            u_scr[rows, :] = jnp.where(used, w_ref[rows, :].astype(F32) * col, 0.0)
        return carry

    lax.fori_loop(0, PEERS, scaled, 0, unroll=2)

    def source(s, carry):
        def some(q, inner):
            first = s * SLOTS + q * 16
            line = s * ID_STRIDE + q * 16
            ids = [sid_ref[line + j] for j in range(16)]
            us = [u_scr[pl.ds(first + j, 1), :] for j in range(16)]
            for h in range(0, 16, COPIES):
                sums = [accs[j][pl.ds(ids[h + j], 1), :] + us[h + j] for j in range(COPIES)]
                for j in range(COPIES):
                    accs[j][pl.ds(ids[h + j], 1), :] = sums[j]
            return inner

        return lax.fori_loop(0, lax.shift_right_logical(sid_ref[s * ID_STRIDE + SLOTS] + 15, 4), some, carry)

    lax.fori_loop(0, PEERS, source, 0)

    def add(i, carry):
        rows = pl.ds(pl.multiple_of(i * 64, 64), 64)
        total = accs[0][rows, :]
        for acc in accs[1:]:
            total = total + acc[rows, :]
        accs[0][rows, :] = total
        return carry

    lax.fori_loop(0, SIDE // 64, add, 0)
    row_forward_kernel(True, False, accs[0], tw, f_ref, a_ref, m_ref, out_ref, y_scr, e_scr)


def call(kernel, name, out_shapes, args, smem=0, scratch=(), any_args=(), any_outs=(), smem_outs=(), collective_id=None):
    spaces = [pltpu.SMEM if i < smem else pl.ANY if i in any_args else pltpu.VMEM for i in range(len(args))]
    outs = [pl.ANY if i in any_outs else pltpu.SMEM if i in smem_outs else pltpu.VMEM for i in range(len(out_shapes))]
    remote = dict(collective_id=collective_id, has_side_effects=True) if collective_id is not None else {}
    return pl.pallas_call(
        kernel,
        out_shape=out_shapes,
        in_specs=[pl.BlockSpec(memory_space=space) for space in spaces],
        out_specs=[pl.BlockSpec(memory_space=space) for space in outs],
        scratch_shapes=list(scratch),
        compiler_params=pltpu.CompilerParams(vmem_limit_bytes=VMEM_BYTES, **remote),
        cost_estimate=pl.CostEstimate(flops=1024, bytes_accessed=1024, transcendentals=0),
        name=name,
    )(*args)


def shape(dims, dtype=F32):
    return jax.ShapeDtypeStruct(dims, dtype)


PENCILS = (PEERS, INNER, INNER)
MESSAGES = (PEERS, INNER + TAIL, INNER)


def row_backward(pencils, base, tables):
    final = base is not None
    args = [pencils] + ([base] if final else []) + tables
    return call(
        lambda *refs: row_backward_kernel(final, *refs),
        "row_backward",
        [shape((INNER, SIDE) if final else (SIDE, INNER))],
        args,
        scratch=[pltpu.VMEM((15 * INNER, 2 * INNER), F32), pltpu.VMEM((2, INNER, INNER), F32)],
    )[0]


def tables_kernel(scale, rate, wind, prior, tab_ref, amp_ref, par_ref):
    strip = lax.axis_index("strip")
    live = (lax.axis_index("tm") < 3).astype(F32)
    k1 = (strip // 2).astype(F32)
    even = strip % 2 == 0
    row = lax.broadcasted_iota(jnp.int32, (INNER, INNER), 0)
    lane = lax.broadcasted_iota(jnp.int32, (INNER, INNER), 1)
    line = row.astype(F32)
    j = (lane & (HALF - 1)).astype(F32)
    cols = jnp.where(even, k1 + OUTER * j, k1 + OUTER * (INNER - 1.0 - j))
    cols = jnp.where(strip == 1, 16.0 + OUTER * j, cols)
    winds = ((wind[0, 0].astype(F32), wind[0, 1].astype(F32)), (prior[1], prior[2]))

    def cosine(turns):
        turns = turns - SIDE * jnp.floor(turns * (1.0 / SIDE))
        return jnp.cos(turns * (2.0 * math.pi / SIDE))

    small = jnp.zeros((INNER, INNER), F32)
    for kind in range(4):
        wind_row, wind_col = winds[kind // 2]
        quarter = (0.0, 3.0 * SIDE / 4, 0.0, SIDE / 4.0)[kind]
        base = OUTER * line * wind_row + quarter
        tab_ref[kind] = cosine(base + cols * wind_col)
        tab_ref[4 + kind] = cosine(base + j * wind_row)
        turns = (row & (OUTER - 1)).astype(F32) * wind_row + quarter
        small = jnp.where(lax.shift_right_logical(row, 5) == kind, turns, small)
    tab_ref[8] = cosine(small)

    fold = jnp.where(even, k1 + OUTER * j, OUTER - k1 + OUTER * j)
    fold = jnp.where(strip == 1, 16.0 + OUTER * j, fold)
    fold = jnp.where(jnp.logical_and(strip == 0, lane == HALF), SIDE / 2.0, fold)
    fold = fold * fold

    def step(k, carry):
        kr = line * OUTER + k.astype(F32)
        kr = jnp.minimum(kr, SIDE - kr)
        radius = (kr * kr + fold) / (KZERO * KZERO)
        amp_ref[k] = SIDE / (2.0 * KZERO) * jnp.exp((-11.0 / 12.0) * jnp.log(1.0 + radius))
        return carry

    lax.fori_loop(0, OUTER, step, 0, unroll=2)
    norm = scale[0] / (SIDE * SIDE)
    mine = rate[0] * live
    par_ref[0] = norm
    par_ref[1] = mine * scale[0]
    par_ref[2] = prior[0] * scale[0]
    par_ref[3] = (mine + prior[0]) * scale[0] * norm
    par_ref[4] = 1.0 - 2.0 * (wind[0, 1] & 1).astype(F32)
    par_ref[5] = 1.0 - 2.0 * (prior[2].astype(jnp.int32) & 1).astype(F32)
    par_ref[6] = 0.0
    par_ref[7] = 0.0


def const(*tables):
    return [jnp.asarray(t) for t in tables]


def local(
    screen_vec,
    prior_scale,
    flow_weight,
    wind,
    pierce_point_strip,
    pierce_block,
    pierce_weights,
    noise_prec,
):
    fwd, inv, first, first_inv, mid, mid_inv, twiddle = row_tables()
    row_fwd_tables = const(twiddle, pieces(fwd, 2), pieces(first, 2), pieces(mid, 2))
    row_fine_tables = const(twiddle, pieces(fwd, 3), pieces(first, 3), pieces(mid, 3))
    row_inv_tables = const(twiddle, pieces(inv, 2), pieces(first_inv, 2), pieces(mid_inv, 2))
    col_fwd, col_inv = column_tables()
    col_fine_tables = const(pieces(col_fwd, 3), pieces(col_inv, 2))
    col_tables = const(pieces(col_fwd, 2), pieces(col_inv, 2))

    x = screen_vec[0]
    weights = pierce_weights[0].reshape(POINT_ROWS * INNER, INNER)
    target = pierce_point_strip.reshape(INNER, HALF)
    block = pierce_block.reshape(INNER, HALF)
    prec = noise_prec.reshape(INNER, HALF)

    mine = jnp.concatenate([flow_weight, wind[0].astype(F32)])
    prior = lax.ppermute(mine, "tm", [(i, i + 1) for i in range(lax.axis_size("tm") - 1)])
    slots, ids = call(
        route_kernel,
        "route",
        [shape((POINT_ROWS, INNER), jnp.int32), shape((PEERS, ID_ROWS, INNER), jnp.int32)],
        [target, block],
        scratch=[pltpu.VMEM((POINT_ROWS, INNER), jnp.int32)] * 2,
    )
    ids, prior, prec = lax.optimization_barrier((ids, prior, prec))
    sent = call(
        pack_kernel,
        "pack",
        [shape((PEERS * SLOTS, INNER), BF16)],
        [slots.reshape(-1), weights],
        smem=1,
        scratch=[pltpu.VMEM((POINT_ROWS * INNER, INNER), F32), pltpu.VMEM((PEERS * SLOTS, INNER), F32)],
    )[0]

    spectral = [pltpu.VMEM(PENCILS, F32), pltpu.VMEM(PENCILS, F32)]
    rows = [pltpu.VMEM((15 * INNER, 2 * INNER), F32), pltpu.VMEM((2, INNER, INNER), F32)]
    message = shape(MESSAGES, BF16)
    points = pltpu.VMEM((PEERS * SLOTS, INNER), F32)
    screen = pltpu.VMEM((SIDE, INNER), F32)
    small = (PEERS, 4, INNER)
    resid, par, own, arrived, amp, here_ids, from_prev, from_next = call(
        first_kernel,
        "first",
        [
            shape(small),
            shape((8,)),
            shape(PENCILS),
            shape((PEERS, SLOTS, INNER), BF16),
            shape(PENCILS),
            shape((PEERS * ID_STRIDE,), jnp.int32),
            shape(PENCILS, BF16),
            shape(PENCILS, BF16),
        ],
        [prior_scale, flow_weight, wind, prior, x]
        + row_fine_tables
        + row_inv_tables[1:]
        + [slots, prec]
        + col_fine_tables
        + [sent.reshape(PEERS, SLOTS, INNER), ids.reshape(-1)],
        smem=4,
        any_args=(14, 15, 16, 17),
        any_outs=(2, 3, 4, 5, 6, 7),
        smem_outs=(1,),
        collective_id=3,
        scratch=spectral
        + [pltpu.VMEM(MESSAGES, BF16)] * 3
        + [pltpu.VMEM((9, INNER, INNER), F32)]
        + rows
        + [pltpu.VMEM(PENCILS, BF16)] * 2
        + [
            screen,
            pltpu.VMEM((SLOTS, INNER), F32),
            pltpu.VMEM(small, F32),
            pltpu.VMEM(small, F32),
            pltpu.VMEM((POINT_ROWS, INNER), F32),
            pltpu.VMEM((INNER, INNER), F32),
            pltpu.VMEM(small, F32),
            pltpu.SMEM((PEERS * ID_STRIDE,), jnp.int32),
            pltpu.SemaphoreType.DMA,
            pltpu.SemaphoreType.DMA((2, 2, SIDE_PARTS)),
            pltpu.VMEM(col_fine_tables[0].shape, BF16),
            pltpu.VMEM(col_fine_tables[1].shape, BF16),
            pltpu.VMEM(PENCILS, F32),
            pltpu.VMEM(PENCILS, F32),
            pltpu.VMEM((PEERS, SLOTS, INNER), BF16),
            pltpu.SemaphoreType.DMA((2,)),
            pltpu.SemaphoreType.DMA((2,)),
            pltpu.SemaphoreType.DMA((1,)),
        ]
        + exchange_sems() * 6,
    )
    here = arrived.reshape(PEERS * SLOTS, INNER)

    pencils = call(
        scatter_kernel,
        "scatter",
        [message],
        [here_ids, resid.reshape(INNER, INNER), here] + row_fwd_tables,
        smem=1,
        scratch=[pltpu.VMEM((INNER, INNER), F32), points] + rows + [screen] * COPIES,
    )[0]
    out_pencils = call(
        column_second_kernel,
        "column_second",
        [message],
        [par, pencils, amp, own, from_prev, from_next] + col_tables,
        smem=1,
        any_args=range(1, 8),
        any_outs=(0,),
        collective_id=1,
        scratch=spectral
        + [pltpu.VMEM(MESSAGES, BF16)] * 2
        + exchange_sems()
        + exchange_sems()
        + spectral
        + [pltpu.VMEM(PENCILS, BF16)] * 2
        + [pltpu.VMEM(t.shape, BF16) for t in col_tables]
        + [pltpu.SemaphoreType.DMA((6,))],
    )[0]
    return row_backward(out_pencils, x, row_inv_tables)[None]


def solution(mesh):
    in_specs = (
        P("tm", "strip", None),
        P("tm"),
        P("tm"),
        P("tm", None),
        P("tm", "strip", None, None),
        P("tm", "strip", None),
        P("tm", "strip", None, None),
        P("tm", "strip", None),
    )
    out_specs = P("tm", "strip", None)
    return jax.shard_map(local, mesh=mesh, in_specs=in_specs, out_specs=out_specs, check_vma=False)
```

```python
import math

import jax
import jax.numpy as jnp
import ml_dtypes
import numpy as np
from jax import lax
from jax.experimental import pallas as pl
from jax.experimental.pallas import tpu as pltpu
from jax.sharding import PartitionSpec as P

KZERO = 2.0
SIDE = 4096
OUTER = 32
INNER = 128
HALF = 64
PEERS = 32
SLOTS = 512
POINT_ROWS = 64
TAIL = 16
ID_ROWS = 8
ID_STRIDE = ID_ROWS * 128
VMEM_BYTES = 56 * 1024 * 1024
F32 = jnp.float32
BF16 = jnp.bfloat16


def pieces(table, count):
    rest = np.asarray(table, np.float64)
    out = []
    for _ in range(count):
        out.append(rest.astype(np.float32).astype(ml_dtypes.bfloat16))
        rest = rest - out[-1].astype(np.float64)
    return np.stack(out)


def row_tables():
    b = np.arange(INNER)[:, None]
    j = np.arange(HALF)[None, :]
    theta = [2 * np.pi * ((b * j) % INNER) / INNER, 2 * np.pi * ((b * (INNER - 1 - j)) % INNER) / INNER]
    forward = []
    backward = []
    for t in theta:
        forward.append(np.concatenate([np.cos(t), -np.sin(t)], axis=1))
        forward.append(np.concatenate([np.sin(t), np.cos(t)], axis=1))
        backward.append(np.concatenate([np.cos(t).T, np.sin(t).T], axis=1))
        backward.append(np.concatenate([-np.sin(t).T, np.cos(t).T], axis=1))
    fwd = np.concatenate(
        [np.concatenate([forward[0], forward[1]], axis=0), np.concatenate([forward[2], forward[3]], axis=0)], axis=1
    )
    inv = np.concatenate(backward, axis=0)
    sign = np.where(np.arange(INNER) % 2 == 0, 1.0, -1.0)
    t0 = theta[0]
    first = np.concatenate([np.cos(t0), -np.sin(t0)], axis=1)
    first[:, HALF] = sign
    first_inv = np.concatenate([2 * np.cos(t0).T, -2 * np.sin(t0).T], axis=0)
    first_inv[0, :] = 1.0
    first_inv[HALF, :] = sign
    t16 = 2 * np.pi * ((b * (16 + 32 * j)) % SIDE) / SIDE
    mid = np.concatenate([np.cos(t16), -np.sin(t16)], axis=1)
    mid_inv = np.concatenate([2 * np.cos(t16).T, -2 * np.sin(t16).T], axis=0)
    k1 = np.arange(16)[:, None]
    tw = 2 * np.pi * (k1 * np.arange(INNER)[None, :]) / SIDE
    twiddle = np.stack([np.cos(tw), np.sin(tw)]).astype(np.float32)
    return fwd, inv, first, first_inv, mid, mid_inv, twiddle


def column_tables():
    k1 = np.arange(OUTER)[:, None, None]
    k2 = np.arange(INNER)[None, :, None]
    r = np.arange(INNER)[None, None, :]
    theta = 2 * np.pi * (((k1 + OUTER * k2) * r) % SIDE) / SIDE
    fwd = np.concatenate([np.cos(theta), -np.sin(theta)], axis=1)
    theta = theta.transpose(0, 2, 1)
    inv = np.concatenate([np.cos(theta), np.sin(theta)], axis=1)
    return fwd, inv


def split(value):
    high = value.astype(BF16)
    return high, (value - high.astype(F32)).astype(BF16)


def mm(left, right):
    return lax.dot_general(left, right, (((1,), (0,)), ((), ())), preferred_element_type=F32)


def mm_nt(left, right):
    return lax.dot_general(left, right, (((1,), (1,)), ((), ())), preferred_element_type=F32)


def split_into(value, count):
    parts = []
    for i in range(count):
        parts.append(value.astype(BF16))
        if i + 1 < count:
            value = value - parts[-1].astype(F32)
    return parts


def data_by_table(value, tables):
    count = len(tables)
    parts = split_into(value, count)
    total = None
    for order in reversed(range(count)):
        for i in range(order + 1):
            term = mm(parts[i], tables[order - i])
            total = term if total is None else total + term
    return total


def table_by_data(tables, value):
    parts = split_into(value, len(tables))
    left = jnp.concatenate(tables[0:2], axis=1)
    right = jnp.concatenate(parts[0:2], axis=1)
    r = mm(left, jnp.concatenate([right, right], axis=0))
    total = r[:, INNER : 2 * INNER] + r[:, 0:INNER]
    if len(tables) == 3:
        left = jnp.concatenate([tables[0], tables[2]], axis=1)
        total = total + mm(left, jnp.concatenate([parts[2], parts[0]], axis=0))
    return total


def every(ref):
    return [ref[i] for i in range(ref.shape[0])]


def c_mul(value, factor):
    re, im = value
    c, s = factor.real, factor.imag
    if im is None:
        return (re * c, re * s)
    return (re * c - im * s, re * s + im * c)


def real_forward(xs):
    n = len(xs)
    if n == 2:
        return [(xs[0] + xs[1], None), (xs[0] - xs[1], None)]
    even, odd = real_forward(xs[0::2]), real_forward(xs[1::2])
    m = n // 2
    out = [None] * (m + 1)
    for k in range(m // 2 + 1):
        if k == 0:
            out[0] = (even[0][0] + odd[0][0], None)
            out[m] = (even[0][0] - odd[0][0], None)
        elif 2 * k == m:
            out[k] = (even[k][0], -odd[k][0])
        else:
            tr, ti = c_mul(odd[k], complex(math.cos(2 * math.pi * k / n), -math.sin(2 * math.pi * k / n)))
            er, ei = even[k]
            out[k] = (er + tr, ei + ti)
            out[m - k] = (er - tr, ti - ei)
    return out


def real_backward(spec):
    n = 2 * (len(spec) - 1)
    if n == 2:
        return [spec[0][0] + spec[1][0], spec[0][0] - spec[1][0]]
    m = n // 2
    even, odd = [], []
    for k in range(m // 2 + 1):
        if k == 0:
            even.append((spec[0][0] + spec[m][0], None))
            odd.append((spec[0][0] - spec[m][0], None))
        elif 2 * k == m:
            even.append((2.0 * spec[k][0], None))
            odd.append((-2.0 * spec[k][1], None))
        else:
            ar, ai = spec[k]
            br, bi = spec[m - k]
            even.append((ar + br, ai - bi))
            odd.append(c_mul((ar - br, ai + bi), complex(math.cos(2 * math.pi * k / n), math.sin(2 * math.pi * k / n))))
    xe, xo = real_backward(even), real_backward(odd)
    out = [None] * n
    out[0::2] = xe
    out[1::2] = xo
    return out


def packed_fft(xs, sign, flip):
    n = len(xs)
    if n == 1:
        return xs
    even, odd = packed_fft(xs[0::2], sign, flip), packed_fft(xs[1::2], sign, flip)
    out = [None] * n
    for k in range(n // 2):
        t = odd[k]
        if k:
            turned = pltpu.roll(t, HALF, 1) * flip
            c, s = math.cos(2 * math.pi * k / n), sign * math.sin(2 * math.pi * k / n)
            t = (-s) * turned if 4 * k == n else c * t - s * turned
        out[k] = even[k] + t
        out[k + n // 2] = even[k] - t
    return out


def flip_lanes(rows):
    lane = lax.broadcasted_iota(jnp.int32, (rows, INNER), 1)
    return jnp.where(lane < HALF, 1.0, -1.0).astype(F32)


def put_message(ref, d, value, fine):
    lane = lax.broadcasted_iota(jnp.int32, (INNER, INNER), 1)
    high = value.astype(BF16)
    ref[d, 0:INNER, :] = high
    rest = value - high.astype(F32)
    if fine:
        third = rest - rest.astype(BF16).astype(F32)
        rest = jnp.where((lane & (HALF - 1)) == 7, pltpu.roll(third, 7, 1), rest)
    rest = jnp.where(lane < 8, rest, pltpu.roll(rest, 72, 1))
    rest = jnp.where(lane < 16, rest, 0.0)
    total = rest[0:16]
    for g in range(1, 8):
        total = total + pltpu.roll(rest[16 * g : 16 * g + 16], 16 * g, 1)
    ref[d, INNER : INNER + TAIL, :] = total.astype(BF16)


def get_message(ref, d, fine):
    lane = lax.broadcasted_iota(jnp.int32, (INNER, INNER), 1)
    packed = ref[d, INNER : INNER + TAIL, :].astype(F32)
    rest = jnp.concatenate([packed] + [pltpu.roll(packed, INNER - 16 * g, 1) for g in range(1, 8)], axis=0)
    rest = jnp.where(lane < 8, rest, pltpu.roll(rest, 56, 1))
    column = lane & (HALF - 1)
    if fine:
        third = jnp.where(column == 0, pltpu.roll(rest, INNER - 7, 1), 0.0)
        rest = jnp.where(column < 7, rest, 0.0) + third
    else:
        rest = jnp.where(column < 8, rest, 0.0)
    return ref[d, 0:INNER, :].astype(F32) + rest


def row_forward_kernel(tiled, fine, x_ref, tw_ref, f_ref, a_ref, m_ref, out_ref, y_scr, e_scr):
    def slab(g, carry):
        if tiled:
            xs = [x_ref[pl.ds(pl.multiple_of(g * 256 + a * 8, 8), 8), :] for a in range(OUTER)]
        else:
            xs = [x_ref[pl.ds(pl.multiple_of(g * 8, 8), 8), a * INNER : (a + 1) * INNER] for a in range(OUTER)]
        ys = real_forward(xs)
        rows = pl.ds(pl.multiple_of(g * 8, 8), 8)
        e_scr[0, rows, :] = ys[0][0]
        e_scr[1, rows, :] = ys[16][0]
        for k in range(1, 16):
            c = tw_ref[0, k : k + 1, :]
            s = tw_ref[1, k : k + 1, :]
            re, im = ys[k]
            base = pl.ds(pl.multiple_of((k - 1) * INNER + g * 8, 8), 8)
            y_scr[base, 0:INNER] = re * c + im * s
            y_scr[base, INNER : 2 * INNER] = im * c - re * s
        return carry

    lax.fori_loop(0, 16, slab, 0, unroll=2)
    put_message(out_ref, 0, data_by_table(e_scr[0], every(a_ref)), fine)
    put_message(out_ref, 1, data_by_table(e_scr[1], every(m_ref)), fine)

    def group(q, carry):
        v = data_by_table(y_scr[pl.ds(pl.multiple_of(q * 384, 8), 384), :], every(f_ref))
        for i in range(3):
            rows = v[i * INNER : (i + 1) * INNER]
            put_message(out_ref, 2 + 2 * (3 * q + i), rows[:, 0:INNER], fine)
            put_message(out_ref, 3 + 2 * (3 * q + i), rows[:, INNER : 2 * INNER], fine)
        return carry

    lax.fori_loop(0, 5, group, 0)


def row_backward_kernel(final, *refs):
    if final:
        in_ref, base_ref, tw_ref, f_ref, a_ref, m_ref, out_ref, z_scr, e_scr = refs
    else:
        in_ref, tw_ref, f_ref, a_ref, m_ref, out_ref, z_scr, e_scr = refs
    e_scr[0] = data_by_table(get_message(in_ref, 0, False), every(a_ref))
    e_scr[1] = data_by_table(get_message(in_ref, 1, False), every(m_ref))

    def group(q, carry):
        parts = []
        for i in range(3):
            k = 3 * q + i
            parts.append(jnp.concatenate([get_message(in_ref, 2 + 2 * k + h, False) for h in range(2)], axis=1))
        v = jnp.concatenate(parts, axis=0)
        z_scr[pl.ds(pl.multiple_of(q * 384, 8), 384), :] = data_by_table(v, every(f_ref))
        return carry

    lax.fori_loop(0, 5, group, 0)

    def slab(g, carry):
        rows = pl.ds(pl.multiple_of(g * 8, 8), 8)
        spec = [(e_scr[0, rows, :], None)]
        for k in range(1, 16):
            c = tw_ref[0, k : k + 1, :]
            s = tw_ref[1, k : k + 1, :]
            base = pl.ds(pl.multiple_of((k - 1) * INNER + g * 8, 8), 8)
            re = z_scr[base, 0:INNER]
            im = z_scr[base, INNER : 2 * INNER]
            spec.append((re * c - im * s, im * c + re * s))
        spec.append((e_scr[1, rows, :], None))
        xs = real_backward(spec)
        for a in range(OUTER):
            if final:
                cols = slice(a * INNER, (a + 1) * INNER)
                out_ref[rows, cols] = base_ref[rows, cols] + xs[a]
            else:
                out_ref[pl.ds(pl.multiple_of(g * 256 + a * 8, 8), 8), :] = xs[a]
        return carry

    lax.fori_loop(0, 16, slab, 0, unroll=2)


def take_all(exchange, scr, fine):
    exchange.own.wait()
    scr[exchange.me] = get_message(exchange.out_ref, exchange.me, fine)

    def step(i, carry):
        exchange.wait_source(i)
        source = exchange.source(i)
        scr[source] = get_message(exchange.out_ref, source, fine)
        return carry

    lax.fori_loop(0, PEERS - 1, step, 0)
    exchange.wait_sends()


def give_all(scr, exchange):
    def step(i, carry):
        peer = exchange.peer(i)
        put_message(exchange.in_ref, peer, scr[peer], False)
        exchange.send(i)
        return carry

    lax.fori_loop(0, PEERS - 1, step, 0)
    put_message(exchange.in_ref, exchange.me, scr[exchange.me], False)
    exchange.own.start()


def column_first_step(in_ref, y_scr, sign):
    flip = flip_lanes(8)

    def slab(g, carry):
        rows = pl.ds(pl.multiple_of(g * 8, 8), 8)
        ys = packed_fft([in_ref[s, rows, :] for s in range(OUTER)], sign, flip)
        for k in range(OUTER):
            y_scr[k, rows, :] = ys[k]
        return carry

    lax.fori_loop(0, 16, slab, 0, unroll=2)


def apply_packed(e_ref, k1, value, flip):
    r = table_by_data([e_ref[i, k1] for i in range(e_ref.shape[0])], value)
    return r[0:INNER] - pltpu.roll(r[INNER : 2 * INNER], HALF, 1) * flip


MESH = pl.DeviceIdType.MESH


def greet_peers(me, barrier, extra=()):
    def greet(i, carry):
        pl.semaphore_signal(barrier, inc=1, device_id={"strip": lax.rem(me + i, PEERS)}, device_id_type=MESH)
        return carry

    lax.fori_loop(1, PEERS, greet, 0)
    for device in extra:
        pl.semaphore_signal(barrier, inc=1, device_id=device, device_id_type=MESH)
    pl.semaphore_wait(barrier, PEERS - 1 + len(extra))


class Exchange:
    def __init__(self, me, in_ref, out_ref, send_sem, recv_sem, own_sem, flat=0):
        self.me, self.in_ref, self.out_ref, self.flat = me, in_ref, out_ref, flat
        self.send_sem, self.recv_sem = send_sem, recv_sem
        self.own = pltpu.make_async_copy(self.part(in_ref, me), self.part(out_ref, me), own_sem)

    def part(self, ref, i):
        return ref.at[pl.ds(pl.multiple_of(i * self.flat, self.flat), self.flat)] if self.flat else ref.at[i]

    def copy(self, peer, send, source):
        return pltpu.make_async_remote_copy(
            src_ref=self.part(self.in_ref, peer),
            dst_ref=self.part(self.out_ref, source),
            send_sem=self.send_sem.at[send],
            recv_sem=self.recv_sem.at[source],
            device_id={"strip": peer},
            device_id_type=MESH,
        )

    def peer(self, i):
        return lax.rem(self.me + 1 + i, PEERS)

    def source(self, i):
        return lax.rem(self.me + PEERS - 1 - i, PEERS)

    def send(self, i):
        self.copy(self.peer(i), i, self.me).start()

    def wait_source(self, i):
        self.copy(self.peer(i), i, self.source(i)).wait_recv()

    def wait_sends(self):
        def step(i, carry):
            self.copy(self.peer(i), i, self.me).wait_send()
            return carry

        lax.fori_loop(0, PEERS - 1, step, 0)

    def start(self, first=0, last=PEERS - 1):
        def step(i, carry):
            self.copy(self.peer(i), i, self.me).start()
            return carry

        lax.fori_loop(first, last, step, 0)
        if first == 0:
            self.own.start()

    def wait(self):
        def step(i, carry):
            self.wait_source(i)
            return carry

        self.own.wait()
        lax.fori_loop(0, PEERS - 1, step, 0)
        self.wait_sends()


class Moves:
    def __init__(self, pairs, sems):
        self.copies = [pltpu.make_async_copy(src, dst, sems.at[i]) for i, (src, dst) in enumerate(pairs)]

    def start(self):
        for copy in self.copies:
            copy.start()

    def wait(self):
        for copy in self.copies:
            copy.wait()


def exchange_sems():
    return [pltpu.SemaphoreType.DMA((PEERS,)), pltpu.SemaphoreType.DMA((PEERS,)), pltpu.SemaphoreType.DMA]


def edge_lanes():
    lane = lax.broadcasted_iota(jnp.int32, (INNER, INNER), 1)
    return jnp.logical_or(lane == 0, lane == HALF), lane < HALF


def edge_gather(ref):
    mask, _ = edge_lanes()

    def step(k1, acc):
        return acc + pltpu.roll(jnp.where(mask, ref[k1], 0.0), k1, 1)

    return lax.fori_loop(0, OUTER, step, jnp.zeros((INNER, INNER), F32), unroll=4)


def edge_split(spec, amp):
    i = lax.broadcasted_iota(jnp.int32, (INNER, INNER), 0)
    j = lax.broadcasted_iota(jnp.int32, (INNER, INNER), 1)
    one = jnp.ones((INNER, INNER), F32)
    none = jnp.zeros((INNER, INNER), F32)
    rows = jnp.where(i + j == INNER - 1, one, none).astype(BF16)
    rows0 = jnp.where(((i + j) & (INNER - 1)) == 0, one, none).astype(BF16)
    sign = jnp.where(j < HALF, one, -one)
    col = j & (HALF - 1)
    same = (i < HALF) == (j < HALF)
    lanes = jnp.where(
        jnp.logical_and(same, jnp.logical_and(col > 0, col + (i & (HALF - 1)) == OUTER)), sign, none
    ).astype(BF16)
    lanes0 = jnp.where(jnp.logical_and(i == j, col == 0), sign, none).astype(BF16)

    def move(left, value, right):
        value = sum(mm(left, p) for p in reversed(split_into(value, 3)))
        return sum(mm(p, right) for p in reversed(split_into(value, 3)))

    rev = move(rows, spec, lanes) + move(rows0, spec, lanes0)
    swapped = pltpu.roll(amp, HALF, 1)
    _, left = edge_lanes()
    a0 = jnp.where(left, amp, swapped)
    a2 = jnp.where(left, swapped, amp)
    return 0.5 * (spec + rev), 0.5 * (spec - rev), a0, a2


def turn(c, s, value, flip):
    return c * value + s * (pltpu.roll(value, HALF, 1) * flip)


EARLY = 4
MIDDLE = 16


def first_kernel(
    scale, rate, wind, prior, x_ref, tw, f_ref, a_ref, m_ref, fi_ref, ai_ref, mi_ref, slot_ref, prec_ref,
    ef_any, ei_any, sent_ref, ids_ref,
    resid_ref, par, own_any, here_any, amp_any, here_ids_ref, prev_ref, next_ref, *scratch,
):
    y_scr, z_scr, msg_scr, land_scr, back_scr, tab_ref, row_scr, row_edge = scratch[0:8]
    up_ref, down_ref, tiles_scr, g_scr, phase_scr, landed, p_scr, table_scr, res_scr = scratch[8:17]
    sid_scr, sid_sem, side_sems = scratch[17:20]
    ef, ei, own_ref, amp_ref, here_ref, in_sems, out_sems, here_sems = scratch[20:28]
    sems = scratch[28:]
    tables = Moves([(ef_any, ef), (ei_any, ei)], in_sems)
    tables.start()
    results = Moves([(own_ref, own_any), (amp_ref, amp_any)], out_sems)
    weights_out = Moves([(here_ref, here_any)], here_sems)
    me = lax.axis_index("strip")
    slot_at = lax.axis_index("tm")
    above, below = lax.rem(slot_at + 1, 4), lax.rem(slot_at + 3, 4)
    greet_peers(me, pltpu.get_barrier_semaphore(), ({"tm": above}, {"tm": below}))
    ids = Exchange(me, ids_ref, here_ids_ref, *sems[0:3], flat=ID_STRIDE)
    weights = Exchange(me, sent_ref, here_ref, *sems[3:6])
    pencils = Exchange(me, msg_scr, land_scr, *sems[6:9])
    back = Exchange(me, msg_scr, back_scr, *sems[9:12])
    phases = Exchange(me, phase_scr, landed, *sems[12:15])
    residuals = Exchange(me, res_scr, resid_ref, *sems[15:18])
    ids.start()
    weights.start(0, EARLY)
    row_forward_kernel(False, True, x_ref, tw, f_ref, a_ref, m_ref, msg_scr, row_scr, row_edge)
    pencils.start()
    tables_kernel(scale, rate, wind, prior, tab_ref, amp_ref, par)
    take_all(pencils, z_scr, True)
    weights.start(EARLY, MIDDLE)
    tables.wait()
    column_first_step(z_scr, y_scr, -1.0)
    flip = flip_lanes(INNER)

    def step(k1, carry):
        value = apply_packed(ef, k1, y_scr[k1], flip)
        amp = amp_ref[k1]
        once = value * amp
        twice = once * amp
        y_scr[k1] = value
        z_scr[k1] = par[0] * once
        own_ref[k1] = par[3] * twice
        for n, ref, gain in ((0, up_ref, par[1]), (1, down_ref, par[2])):
            cb = tab_ref[2 * n]
            sb = tab_ref[2 * n + 1]
            ca = tab_ref[8, pl.ds(64 * n + k1, 1), :] * gain
            sa = tab_ref[8, pl.ds(64 * n + 32 + k1, 1), :] * gain
            ref[k1] = turn(cb * ca - sb * sa, sb * ca + cb * sa, twice, flip).astype(BF16)
        return carry

    lax.fori_loop(0, OUTER, step, 0, unroll=8)

    @pl.when(me == 0)
    def _():
        u0, u2, a0, a2 = edge_split(edge_gather(y_scr), edge_gather(amp_ref))
        mask, _ = edge_lanes()
        e0 = a0 * u0
        e2 = a2 * u2
        fixed = [par[0] * (e0 + e2)]
        e0 = a0 * e0
        e2 = a2 * e2
        fixed.append(par[3] * (e0 + e2))
        fixed.append(par[1] * turn(tab_ref[4], tab_ref[5], e0 + par[4] * e2, flip))
        fixed.append(par[2] * turn(tab_ref[6], tab_ref[7], e0 + par[5] * e2, flip))

        def put(k1, carry):
            back = lax.rem(INNER - k1, INNER)
            for ref, value in zip((z_scr, own_ref, up_ref, down_ref), fixed):
                value = jnp.where(mask, pltpu.roll(value, back, 1), ref[k1].astype(F32))
                ref[k1] = value.astype(ref.dtype)
            return carry

        lax.fori_loop(0, OUTER, put, 0, unroll=4)

    def inverse(k1, carry):
        z_scr[k1] = apply_packed(ei, k1, z_scr[k1], flip)
        return carry

    lax.fori_loop(0, OUTER, inverse, 0, unroll=8)
    column_first_step(z_scr, y_scr, 1.0)
    give_all(y_scr, back)
    results.start()
    ids.wait()
    fetch = pltpu.make_async_copy(here_ids_ref, sid_scr, sid_sem)
    fetch.start()
    back.wait()
    weights.start(MIDDLE, PEERS - 1)
    row_backward_kernel(False, back_scr, tw, fi_ref, ai_ref, mi_ref, tiles_scr, row_scr, row_edge)
    fetch.wait()
    ones = jnp.ones((2 * INNER, INNER), BF16)
    row = lax.broadcasted_iota(jnp.int32, (INNER, INNER), 0)
    lane = lax.broadcasted_iota(jnp.int32, (INNER, INNER), 1)
    place = lax.broadcasted_iota(jnp.int32, (1, INNER), 1)

    def gather_source(s):
        def some(q, carry):
            first = s * ID_STRIDE + q * 32
            picks = [sid_scr[first + j] for j in range(32)]
            rows = [tiles_scr[pl.ds(picks[j], 1), :] for j in range(32)]
            for j in range(32):
                g_scr[pl.ds(q * 32 + j, 1), :] = rows[j]
            return carry

        lax.fori_loop(0, SLOTS // 32, some, 0)
        count = sid_scr[s * ID_STRIDE + SLOTS]
        sums = mm(jnp.concatenate(split(g_scr[...] * here_ref[s].astype(F32)), axis=1), ones)
        for q in range(4):
            got = jnp.where(row == lane, sums[q * INNER : (q + 1) * INNER], 0.0)
            got = jnp.sum(got, axis=0, keepdims=True)
            phase_scr[s, q : q + 1, :] = jnp.where(place + q * INNER < count, got, 0.0)

    weights.own.wait()
    gather_source(me)
    phases.own.start()

    def gather_next(i, carry):
        weights.wait_source(i)
        source = weights.source(i)
        gather_source(source)
        phases.copy(source, PEERS - 2 - i, me).start()
        return carry

    lax.fori_loop(0, PEERS - 1, gather_next, 0)
    weights.wait_sends()
    weights_out.start()

    @pl.when(slot_at < 3)
    def _():
        for side in sides(side_sems, up_ref, prev_ref, above, 0):
            side.start()

    @pl.when(slot_at > 0)
    def _():
        for side in sides(side_sems, down_ref, next_ref, below, 1):
            side.start()

    phases.wait()
    for s in range(PEERS):
        table_scr[4 * s : 4 * s + 4, :] = landed[s]
    acc = weigh(slot_ref, prec_ref, table_scr[...], p_scr)
    for s in range(PEERS):
        res_scr[s] = acc[4 * s : 4 * s + 4]
    residuals.start()
    results.wait()
    weights_out.wait()
    residuals.wait()

    @pl.when(slot_at < 3)
    def _():
        for side in sides(side_sems, up_ref, prev_ref, above, 0):
            side.wait_send()
        for side in sides(side_sems, down_ref, next_ref, below, 1):
            side.wait_recv()

    @pl.when(slot_at > 0)
    def _():
        for side in sides(side_sems, up_ref, prev_ref, above, 0):
            side.wait_recv()
        for side in sides(side_sems, down_ref, next_ref, below, 1):
            side.wait_send()


SIDE_PARTS = 4


def sides(sems, src, dst, device, n):
    copies = []
    for p in range(SIDE_PARTS):
        rows = pl.ds(p * (OUTER // SIDE_PARTS), OUTER // SIDE_PARTS)
        copies.append(
            pltpu.make_async_remote_copy(
                src_ref=src.at[rows],
                dst_ref=dst.at[rows],
                send_sem=sems.at[0, n, p],
                recv_sem=sems.at[1, n, p],
                device_id={"tm": device},
                device_id_type=MESH,
            )
        )
    return copies


def column_second_kernel(par, in_ref, amp_any, own_any, prev_any, next_any, ef_any, ei_any, back_ref, *scratch):
    y_scr, z_scr, msg_scr, out_scr = scratch[0:4]
    amp_ref, own_ref, prev_ref, next_ref, ef, ei, in_sems = scratch[10:17]
    inputs = Moves(
        [(amp_any, amp_ref), (own_any, own_ref), (prev_any, prev_ref), (next_any, next_ref), (ef_any, ef), (ei_any, ei)],
        in_sems,
    )
    inputs.start()
    me = lax.axis_index("strip")
    slot_at = lax.axis_index("tm")
    greet_peers(me, pltpu.get_barrier_semaphore())
    pencils = Exchange(me, in_ref, msg_scr, *scratch[4:7])
    pencils.start()
    take_all(pencils, z_scr, False)
    inputs.wait()
    column_first_step(z_scr, y_scr, -1.0)
    flip = flip_lanes(INNER)

    def step(k1, carry):
        value = apply_packed(ef, k1, y_scr[k1], flip)
        y_scr[k1] = value
        z_scr[k1] = par[0] * (value * amp_ref[k1]) + own_ref[k1]
        return carry

    lax.fori_loop(0, OUTER, step, 0, unroll=8)

    @pl.when(me == 0)
    def _():
        spec = edge_gather(y_scr)
        amp = edge_gather(amp_ref)
        u0, u2, a0, a2 = edge_split(spec, amp)
        mask, _ = edge_lanes()
        change = par[0] * (a0 * u0 + a2 * u2 - amp * spec)

        def put(k1, carry):
            back = lax.rem(INNER - k1, INNER)
            z_scr[k1] = z_scr[k1] + jnp.where(mask, pltpu.roll(change, back, 1), 0.0)
            return carry

        lax.fori_loop(0, OUTER, put, 0, unroll=4)

    def inverse(k1, carry):
        moved = jnp.where(slot_at > 0, prev_ref[k1].astype(F32), 0.0)
        moved = moved + jnp.where(slot_at < 3, next_ref[k1].astype(F32), 0.0)
        z_scr[k1] = apply_packed(ei, k1, z_scr[k1] - par[0] * moved, flip)
        return carry

    lax.fori_loop(0, OUTER, inverse, 0, unroll=8)
    column_first_step(z_scr, y_scr, 1.0)
    back = Exchange(me, out_scr, back_ref, *scratch[7:10])
    give_all(y_scr, back)
    back.wait()


def route_kernel(t_ref, id_ref, slot_ref, tail_ref):
    row = lax.broadcasted_iota(jnp.int32, (INNER, 2 * INNER), 0)
    col = lax.broadcasted_iota(jnp.int32, (INNER, 2 * INNER), 1)
    tri = jnp.where(jnp.logical_or(row < col, col >= INNER), 1.0, 0.0).astype(BF16)
    peer = lax.broadcasted_iota(jnp.int32, (PEERS, INNER), 0)
    base = jnp.zeros((PEERS, INNER), F32)
    for i in range(0, POINT_ROWS, 8):
        hots = [jnp.where(peer == t_ref[i + j : i + j + 1, :], 1.0, 0.0) for j in range(8)]
        cum = mm(jnp.concatenate(hots, axis=0).astype(BF16), tri)
        for j in range(8):
            part = cum[j * PEERS : (j + 1) * PEERS]
            pos = jnp.sum(hots[j] * (part[:, 0:INNER] + base), axis=0, keepdims=True)
            base = base + part[:, INNER : 2 * INNER]
            slot_ref[i + j : i + j + 1, :] = t_ref[i + j : i + j + 1, :] * SLOTS + pos.astype(jnp.int32)
    batch = 4
    index = lax.broadcasted_iota(jnp.int32, (INNER, batch * INNER), 0)

    def wide(ref, i):
        return jnp.concatenate([ref[pl.ds(i * batch + j, 1), :] for j in range(batch)], axis=1)

    def put(i, acc):
        slot = wide(slot_ref, i)
        ids = wide(id_ref, i)
        r = lax.shift_right_logical(ids, 5)
        ids = lax.shift_right_logical(r, 3) * 256 + (ids & 31) * 8 + (r & 7)
        hot = jnp.where(index == (slot & 127), 1.0, 0.0).astype(BF16)
        line = index == lax.shift_right_logical(slot, 7)
        v = [
            jnp.where(line, d.astype(F32), 0.0).astype(BF16) for d in (lax.shift_right_logical(ids, 6), ids & 63)
        ]
        return acc + mm_nt(jnp.concatenate(v, axis=0), hot)

    acc = lax.fori_loop(0, POINT_ROWS // batch, put, jnp.zeros((2 * INNER, INNER), F32), unroll=2)
    ids = (acc[0:INNER] * 64.0 + acc[INNER : 2 * INNER]).astype(jnp.int32)
    count = base.astype(jnp.int32)
    tail_ref[...] = jnp.zeros_like(tail_ref)
    for s in range(PEERS):
        tail_ref[s, 0:4, :] = ids[4 * s : 4 * s + 4]
        tail_ref[s, 4:5, :] = count[s : s + 1]


def pack_kernel(slot_ref, w_ref, out_ref, w_scr, buf):
    def widen(i, carry):
        rows = pl.ds(pl.multiple_of(i * 64, 64), 64)
        w_scr[rows, :] = w_ref[rows, :].astype(F32)
        return carry

    lax.fori_loop(0, POINT_ROWS * INNER // 64, widen, 0, unroll=2)

    def some(q, carry):
        antenna, direction = (q // 8) * 4, (q % 8) * 8
        first = direction * INNER + antenna
        line = pl.multiple_of(antenna * HALF + direction, 8)
        pairs = [(a, d) for a in range(4) for d in range(8)]
        slots = [slot_ref[first + d * INNER + a] for a, d in pairs]
        rows = [w_scr[pl.ds(line + a * HALF + d, 1), :] for a, d in pairs]
        for j in range(32):
            buf[pl.ds(slots[j], 1), :] = rows[j]
        return carry

    lax.fori_loop(0, POINT_ROWS * INNER // 32, some, 0)

    def narrow(i, carry):
        rows = pl.ds(pl.multiple_of(i * INNER, INNER), INNER)
        out_ref[rows, :] = buf[rows, :].astype(BF16)
        return carry

    lax.fori_loop(0, PEERS * SLOTS // INNER, narrow, 0, unroll=2)


def weigh(slot_ref, prec_ref, phase, p_scr):
    high, low = split(phase)
    table = jnp.concatenate([high, low], axis=0)
    batch = 4
    index = lax.broadcasted_iota(jnp.int32, (INNER, batch * INNER), 0)

    def wide(ref, i):
        return jnp.concatenate([ref[pl.ds(i * batch + j, 1), :] for j in range(batch)], axis=1)

    def pick(i, carry):
        slot = wide(slot_ref, i)
        hot = jnp.where(index == (slot & 127), 1.0, 0.0).astype(BF16)
        v = mm(table, hot)
        v = v[0:INNER] + v[INNER : 2 * INNER]
        got = jnp.sum(jnp.where(index == lax.shift_right_logical(slot, 7), v, 0.0), axis=0, keepdims=True)
        for j in range(batch):
            p_scr[pl.ds(i * batch + j, 1), :] = got[:, j * INNER : (j + 1) * INNER]
        return carry

    lax.fori_loop(0, POINT_ROWS // batch, pick, 0, unroll=4)
    prec = prec_ref[...]
    phase = p_scr[...]

    centre = jnp.sum(prec * phase, axis=0, keepdims=True) / jnp.sum(prec, axis=0, keepdims=True)
    p_scr[...] = prec * (phase - centre)

    def put(i, acc):
        slot = wide(slot_ref, i)
        hot = jnp.where(index == (slot & 127), 1.0, 0.0).astype(BF16)
        v = jnp.where(index == lax.shift_right_logical(slot, 7), wide(p_scr, i), 0.0)
        vh, vl = split(v)
        return acc + mm_nt(jnp.concatenate([vh, vl], axis=0), hot)

    acc = lax.fori_loop(0, POINT_ROWS // batch, put, jnp.zeros((2 * INNER, INNER), F32), unroll=4)
    return acc[0:INNER] + acc[INNER : 2 * INNER]


COPIES = 8


def scatter_kernel(
    sid_ref, r_ref, w_any, tw, f_ref, a_ref, m_ref, out_ref, rt_scr, u_scr, y_scr, e_scr, w_ref, w_sems, *accs
):
    fetch = Moves([(w_any, w_ref)], w_sems)
    fetch.start()
    def clear(i, carry):
        rows = pl.ds(pl.multiple_of(i * 64, 64), 64)
        for acc in accs:
            acc[rows, :] = jnp.zeros((64, INNER), F32)
        return carry

    lax.fori_loop(0, SIDE // 64, clear, 0)
    rt_scr[...] = r_ref[...].T
    fetch.wait()
    lane = lax.broadcasted_iota(jnp.int32, (INNER, INNER), 1)
    row = lax.broadcasted_iota(jnp.int32, (INNER, INNER), 0)

    def scaled(s, carry):
        for q in range(4):
            col = jnp.sum(jnp.where(lane == s * 4 + q, rt_scr[...], 0.0), axis=1, keepdims=True)
            rows = pl.ds(pl.multiple_of(s * SLOTS + q * INNER, INNER), INNER)
            used = row + q * INNER < sid_ref[s * ID_STRIDE + SLOTS]
            u_scr[rows, :] = jnp.where(used, w_ref[rows, :].astype(F32) * col, 0.0)
        return carry

    lax.fori_loop(0, PEERS, scaled, 0, unroll=2)

    def source(s, carry):
        def some(q, inner):
            first = s * SLOTS + q * 32
            line = s * ID_STRIDE + q * 32
            ids = [sid_ref[line + j] for j in range(32)]
            us = [u_scr[pl.ds(first + j, 1), :] for j in range(32)]
            for h in range(0, 32, COPIES):
                sums = [accs[j][pl.ds(ids[h + j], 1), :] + us[h + j] for j in range(COPIES)]
                for j in range(COPIES):
                    accs[j][pl.ds(ids[h + j], 1), :] = sums[j]
            return inner

        return lax.fori_loop(0, lax.shift_right_logical(sid_ref[s * ID_STRIDE + SLOTS] + 31, 5), some, carry)

    lax.fori_loop(0, PEERS, source, 0)

    def add(i, carry):
        rows = pl.ds(pl.multiple_of(i * 64, 64), 64)
        total = accs[0][rows, :]
        for acc in accs[1:]:
            total = total + acc[rows, :]
        accs[0][rows, :] = total
        return carry

    lax.fori_loop(0, SIDE // 64, add, 0)
    row_forward_kernel(True, False, accs[0], tw, f_ref, a_ref, m_ref, out_ref, y_scr, e_scr)


def call(kernel, name, out_shapes, args, smem=0, scratch=(), any_args=(), any_outs=(), smem_outs=(), collective_id=None):
    spaces = [pltpu.SMEM if i < smem else pl.ANY if i in any_args else pltpu.VMEM for i in range(len(args))]
    outs = [pl.ANY if i in any_outs else pltpu.SMEM if i in smem_outs else pltpu.VMEM for i in range(len(out_shapes))]
    remote = dict(collective_id=collective_id, has_side_effects=True) if collective_id is not None else {}
    return pl.pallas_call(
        kernel,
        out_shape=out_shapes,
        in_specs=[pl.BlockSpec(memory_space=space) for space in spaces],
        out_specs=[pl.BlockSpec(memory_space=space) for space in outs],
        scratch_shapes=list(scratch),
        compiler_params=pltpu.CompilerParams(vmem_limit_bytes=VMEM_BYTES, **remote),
        cost_estimate=pl.CostEstimate(flops=1024, bytes_accessed=1024, transcendentals=0),
        name=name,
    )(*args)


def shape(dims, dtype=F32):
    return jax.ShapeDtypeStruct(dims, dtype)


PENCILS = (PEERS, INNER, INNER)
MESSAGES = (PEERS, INNER + TAIL, INNER)


def row_backward(pencils, base, tables):
    final = base is not None
    args = [pencils] + ([base] if final else []) + tables
    return call(
        lambda *refs: row_backward_kernel(final, *refs),
        "row_backward",
        [shape((INNER, SIDE) if final else (SIDE, INNER))],
        args,
        scratch=[pltpu.VMEM((15 * INNER, 2 * INNER), F32), pltpu.VMEM((2, INNER, INNER), F32)],
    )[0]


def tables_kernel(scale, rate, wind, prior, tab_ref, amp_ref, par_ref):
    strip = lax.axis_index("strip")
    live = (lax.axis_index("tm") < 3).astype(F32)
    k1 = (strip // 2).astype(F32)
    even = strip % 2 == 0
    row = lax.broadcasted_iota(jnp.int32, (INNER, INNER), 0)
    lane = lax.broadcasted_iota(jnp.int32, (INNER, INNER), 1)
    line = row.astype(F32)
    j = (lane & (HALF - 1)).astype(F32)
    cols = jnp.where(even, k1 + OUTER * j, k1 + OUTER * (INNER - 1.0 - j))
    cols = jnp.where(strip == 1, 16.0 + OUTER * j, cols)
    winds = ((wind[0, 0].astype(F32), wind[0, 1].astype(F32)), (prior[1], prior[2]))

    def cosine(turns):
        turns = turns - SIDE * jnp.floor(turns * (1.0 / SIDE))
        return jnp.cos(turns * (2.0 * math.pi / SIDE))

    small = jnp.zeros((INNER, INNER), F32)
    for kind in range(4):
        wind_row, wind_col = winds[kind // 2]
        quarter = (0.0, 3.0 * SIDE / 4, 0.0, SIDE / 4.0)[kind]
        base = OUTER * line * wind_row + quarter
        tab_ref[kind] = cosine(base + cols * wind_col)
        tab_ref[4 + kind] = cosine(base + j * wind_row)
        turns = (row & (OUTER - 1)).astype(F32) * wind_row + quarter
        small = jnp.where(lax.shift_right_logical(row, 5) == kind, turns, small)
    tab_ref[8] = cosine(small)

    fold = jnp.where(even, k1 + OUTER * j, OUTER - k1 + OUTER * j)
    fold = jnp.where(strip == 1, 16.0 + OUTER * j, fold)
    fold = jnp.where(jnp.logical_and(strip == 0, lane == HALF), SIDE / 2.0, fold)
    fold = fold * fold

    def step(k, carry):
        kr = line * OUTER + k.astype(F32)
        kr = jnp.minimum(kr, SIDE - kr)
        radius = (kr * kr + fold) / (KZERO * KZERO)
        amp_ref[k] = SIDE / (2.0 * KZERO) * jnp.exp((-11.0 / 12.0) * jnp.log(1.0 + radius))
        return carry

    lax.fori_loop(0, OUTER, step, 0, unroll=2)
    norm = scale[0] / (SIDE * SIDE)
    mine = rate[0] * live
    par_ref[0] = norm
    par_ref[1] = mine * scale[0]
    par_ref[2] = prior[0] * scale[0]
    par_ref[3] = (mine + prior[0]) * scale[0] * norm
    par_ref[4] = 1.0 - 2.0 * (wind[0, 1] & 1).astype(F32)
    par_ref[5] = 1.0 - 2.0 * (prior[2].astype(jnp.int32) & 1).astype(F32)
    par_ref[6] = 0.0
    par_ref[7] = 0.0


def const(*tables):
    return [jnp.asarray(t) for t in tables]


def local(
    screen_vec,
    prior_scale,
    flow_weight,
    wind,
    pierce_point_strip,
    pierce_block,
    pierce_weights,
    noise_prec,
):
    fwd, inv, first, first_inv, mid, mid_inv, twiddle = row_tables()
    row_fwd_tables = const(twiddle, pieces(fwd, 2), pieces(first, 2), pieces(mid, 2))
    row_fine_tables = const(twiddle, pieces(fwd, 3), pieces(first, 3), pieces(mid, 3))
    row_inv_tables = const(twiddle, pieces(inv, 2), pieces(first_inv, 2), pieces(mid_inv, 2))
    col_fwd, col_inv = column_tables()
    col_fine_tables = const(pieces(col_fwd, 3), pieces(col_inv, 2))
    col_tables = const(pieces(col_fwd, 2), pieces(col_inv, 2))

    x = screen_vec[0]
    weights = pierce_weights[0].reshape(POINT_ROWS * INNER, INNER)
    target = pierce_point_strip.reshape(INNER, HALF).T
    block = pierce_block.reshape(INNER, HALF).T
    prec = noise_prec.reshape(INNER, HALF).T

    mine = jnp.concatenate([flow_weight, wind[0].astype(F32)])
    prior = lax.ppermute(mine, "tm", [(i, i + 1) for i in range(lax.axis_size("tm") - 1)])
    slots, ids = call(
        route_kernel,
        "route",
        [shape((POINT_ROWS, INNER), jnp.int32), shape((PEERS, ID_ROWS, INNER), jnp.int32)],
        [target, block],
    )
    ids, prior, prec = lax.optimization_barrier((ids, prior, prec))
    sent = call(
        pack_kernel,
        "pack",
        [shape((PEERS * SLOTS, INNER), BF16)],
        [slots.reshape(-1), weights],
        smem=1,
        scratch=[pltpu.VMEM((POINT_ROWS * INNER, INNER), F32), pltpu.VMEM((PEERS * SLOTS, INNER), F32)],
    )[0]

    spectral = [pltpu.VMEM(PENCILS, F32), pltpu.VMEM(PENCILS, F32)]
    rows = [pltpu.VMEM((15 * INNER, 2 * INNER), F32), pltpu.VMEM((2, INNER, INNER), F32)]
    message = shape(MESSAGES, BF16)
    points = pltpu.VMEM((PEERS * SLOTS, INNER), F32)
    screen = pltpu.VMEM((SIDE, INNER), F32)
    small = (PEERS, 4, INNER)
    resid, par, own, arrived, amp, here_ids, from_prev, from_next = call(
        first_kernel,
        "first",
        [
            shape(small),
            shape((8,)),
            shape(PENCILS),
            shape((PEERS, SLOTS, INNER), BF16),
            shape(PENCILS),
            shape((PEERS * ID_STRIDE,), jnp.int32),
            shape(PENCILS, BF16),
            shape(PENCILS, BF16),
        ],
        [prior_scale, flow_weight, wind, prior, x]
        + row_fine_tables
        + row_inv_tables[1:]
        + [slots, prec]
        + col_fine_tables
        + [sent.reshape(PEERS, SLOTS, INNER), ids.reshape(-1)],
        smem=4,
        any_args=(14, 15, 16, 17),
        any_outs=(2, 3, 4, 5, 6, 7),
        smem_outs=(1,),
        collective_id=3,
        scratch=spectral
        + [pltpu.VMEM(MESSAGES, BF16)] * 3
        + [pltpu.VMEM((9, INNER, INNER), F32)]
        + rows
        + [pltpu.VMEM(PENCILS, BF16)] * 2
        + [
            screen,
            pltpu.VMEM((SLOTS, INNER), F32),
            pltpu.VMEM(small, F32),
            pltpu.VMEM(small, F32),
            pltpu.VMEM((POINT_ROWS, INNER), F32),
            pltpu.VMEM((INNER, INNER), F32),
            pltpu.VMEM(small, F32),
            pltpu.SMEM((PEERS * ID_STRIDE,), jnp.int32),
            pltpu.SemaphoreType.DMA,
            pltpu.SemaphoreType.DMA((2, 2, SIDE_PARTS)),
            pltpu.VMEM(col_fine_tables[0].shape, BF16),
            pltpu.VMEM(col_fine_tables[1].shape, BF16),
            pltpu.VMEM(PENCILS, F32),
            pltpu.VMEM(PENCILS, F32),
            pltpu.VMEM((PEERS, SLOTS, INNER), BF16),
            pltpu.SemaphoreType.DMA((2,)),
            pltpu.SemaphoreType.DMA((2,)),
            pltpu.SemaphoreType.DMA((1,)),
        ]
        + exchange_sems() * 6,
    )
    here = arrived.reshape(PEERS * SLOTS, INNER)

    pencils = call(
        scatter_kernel,
        "scatter",
        [message],
        [here_ids, resid.reshape(INNER, INNER), here] + row_fwd_tables,
        smem=1,
        any_args=(2,),
        scratch=[pltpu.VMEM((INNER, INNER), F32), points]
        + rows
        + [pltpu.VMEM((PEERS * SLOTS, INNER), BF16), pltpu.SemaphoreType.DMA((1,))]
        + [screen] * COPIES,
    )[0]
    out_pencils = call(
        column_second_kernel,
        "column_second",
        [message],
        [par, pencils, amp, own, from_prev, from_next] + col_tables,
        smem=1,
        any_args=range(1, 8),
        any_outs=(0,),
        collective_id=1,
        scratch=spectral
        + [pltpu.VMEM(MESSAGES, BF16)] * 2
        + exchange_sems()
        + exchange_sems()
        + spectral
        + [pltpu.VMEM(PENCILS, BF16)] * 2
        + [pltpu.VMEM(t.shape, BF16) for t in col_tables]
        + [pltpu.SemaphoreType.DMA((6,))],
    )[0]
    return row_backward(out_pencils, x, row_inv_tables)[None]


def solution(mesh):
    in_specs = (
        P("tm", "strip", None),
        P("tm"),
        P("tm"),
        P("tm", None),
        P("tm", "strip", None, None),
        P("tm", "strip", None),
        P("tm", "strip", None, None),
        P("tm", "strip", None),
    )
    out_specs = P("tm", "strip", None)
    return jax.shard_map(local, mesh=mesh, in_specs=in_specs, out_specs=out_specs, check_vma=False)
```

```python
import math

import jax
import jax.numpy as jnp
import ml_dtypes
import numpy as np
from jax import lax
from jax.experimental import pallas as pl
from jax.experimental.pallas import tpu as pltpu
from jax.sharding import PartitionSpec as P

KZERO = 2.0
SIDE = 4096
OUTER = 32
INNER = 128
HALF = 64
PEERS = 32
SLOTS = 512
POINT_ROWS = 64
TAIL = 16
ID_ROWS = 8
ID_STRIDE = ID_ROWS * 128
VMEM_BYTES = 56 * 1024 * 1024
F32 = jnp.float32
BF16 = jnp.bfloat16


def pieces(table, count):
    rest = np.asarray(table, np.float64)
    out = []
    for _ in range(count):
        out.append(rest.astype(np.float32).astype(ml_dtypes.bfloat16))
        rest = rest - out[-1].astype(np.float64)
    return np.stack(out)


def row_tables():
    b = np.arange(INNER)[:, None]
    j = np.arange(HALF)[None, :]
    theta = [2 * np.pi * ((b * j) % INNER) / INNER, 2 * np.pi * ((b * (INNER - 1 - j)) % INNER) / INNER]
    forward = []
    backward = []
    for t in theta:
        forward.append(np.concatenate([np.cos(t), -np.sin(t)], axis=1))
        forward.append(np.concatenate([np.sin(t), np.cos(t)], axis=1))
        backward.append(np.concatenate([np.cos(t).T, np.sin(t).T], axis=1))
        backward.append(np.concatenate([-np.sin(t).T, np.cos(t).T], axis=1))
    fwd = np.concatenate(
        [np.concatenate([forward[0], forward[1]], axis=0), np.concatenate([forward[2], forward[3]], axis=0)], axis=1
    )
    inv = np.concatenate(backward, axis=0)
    sign = np.where(np.arange(INNER) % 2 == 0, 1.0, -1.0)
    t0 = theta[0]
    first = np.concatenate([np.cos(t0), -np.sin(t0)], axis=1)
    first[:, HALF] = sign
    first_inv = np.concatenate([2 * np.cos(t0).T, -2 * np.sin(t0).T], axis=0)
    first_inv[0, :] = 1.0
    first_inv[HALF, :] = sign
    t16 = 2 * np.pi * ((b * (16 + 32 * j)) % SIDE) / SIDE
    mid = np.concatenate([np.cos(t16), -np.sin(t16)], axis=1)
    mid_inv = np.concatenate([2 * np.cos(t16).T, -2 * np.sin(t16).T], axis=0)
    k1 = np.arange(16)[:, None]
    tw = 2 * np.pi * (k1 * np.arange(INNER)[None, :]) / SIDE
    twiddle = np.stack([np.cos(tw), np.sin(tw)]).astype(np.float32)
    return fwd, inv, first, first_inv, mid, mid_inv, twiddle


def column_tables():
    k1 = np.arange(OUTER)[:, None, None]
    k2 = np.arange(INNER)[None, :, None]
    r = np.arange(INNER)[None, None, :]
    theta = 2 * np.pi * (((k1 + OUTER * k2) * r) % SIDE) / SIDE
    fwd = np.concatenate([np.cos(theta), -np.sin(theta)], axis=1)
    theta = theta.transpose(0, 2, 1)
    inv = np.concatenate([np.cos(theta), np.sin(theta)], axis=1)
    return fwd, inv


def split(value):
    high = value.astype(BF16)
    return high, (value - high.astype(F32)).astype(BF16)


def mm(left, right):
    return lax.dot_general(left, right, (((1,), (0,)), ((), ())), preferred_element_type=F32)


def mm_nt(left, right):
    return lax.dot_general(left, right, (((1,), (1,)), ((), ())), preferred_element_type=F32)


def split_into(value, count):
    parts = []
    for i in range(count):
        parts.append(value.astype(BF16))
        if i + 1 < count:
            value = value - parts[-1].astype(F32)
    return parts


def data_by_table(value, tables):
    count = len(tables)
    parts = split_into(value, count)
    total = None
    for order in reversed(range(count)):
        for i in range(order + 1):
            term = mm(parts[i], tables[order - i])
            total = term if total is None else total + term
    return total


def table_by_data(tables, value):
    parts = split_into(value, len(tables))
    left = jnp.concatenate(tables[0:2], axis=1)
    right = jnp.concatenate(parts[0:2], axis=1)
    r = mm(left, jnp.concatenate([right, right], axis=0))
    total = r[:, INNER : 2 * INNER] + r[:, 0:INNER]
    if len(tables) == 3:
        left = jnp.concatenate([tables[0], tables[2]], axis=1)
        total = total + mm(left, jnp.concatenate([parts[2], parts[0]], axis=0))
    return total


def every(ref):
    return [ref[i] for i in range(ref.shape[0])]


def c_mul(value, factor):
    re, im = value
    c, s = factor.real, factor.imag
    if im is None:
        return (re * c, re * s)
    return (re * c - im * s, re * s + im * c)


def real_forward(xs):
    n = len(xs)
    if n == 2:
        return [(xs[0] + xs[1], None), (xs[0] - xs[1], None)]
    even, odd = real_forward(xs[0::2]), real_forward(xs[1::2])
    m = n // 2
    out = [None] * (m + 1)
    for k in range(m // 2 + 1):
        if k == 0:
            out[0] = (even[0][0] + odd[0][0], None)
            out[m] = (even[0][0] - odd[0][0], None)
        elif 2 * k == m:
            out[k] = (even[k][0], -odd[k][0])
        else:
            tr, ti = c_mul(odd[k], complex(math.cos(2 * math.pi * k / n), -math.sin(2 * math.pi * k / n)))
            er, ei = even[k]
            out[k] = (er + tr, ei + ti)
            out[m - k] = (er - tr, ti - ei)
    return out


def real_backward(spec):
    n = 2 * (len(spec) - 1)
    if n == 2:
        return [spec[0][0] + spec[1][0], spec[0][0] - spec[1][0]]
    m = n // 2
    even, odd = [], []
    for k in range(m // 2 + 1):
        if k == 0:
            even.append((spec[0][0] + spec[m][0], None))
            odd.append((spec[0][0] - spec[m][0], None))
        elif 2 * k == m:
            even.append((2.0 * spec[k][0], None))
            odd.append((-2.0 * spec[k][1], None))
        else:
            ar, ai = spec[k]
            br, bi = spec[m - k]
            even.append((ar + br, ai - bi))
            odd.append(c_mul((ar - br, ai + bi), complex(math.cos(2 * math.pi * k / n), math.sin(2 * math.pi * k / n))))
    xe, xo = real_backward(even), real_backward(odd)
    out = [None] * n
    out[0::2] = xe
    out[1::2] = xo
    return out


def packed_fft(xs, sign, flip):
    n = len(xs)
    if n == 1:
        return xs
    even, odd = packed_fft(xs[0::2], sign, flip), packed_fft(xs[1::2], sign, flip)
    out = [None] * n
    for k in range(n // 2):
        t = odd[k]
        if k:
            turned = pltpu.roll(t, HALF, 1) * flip
            c, s = math.cos(2 * math.pi * k / n), sign * math.sin(2 * math.pi * k / n)
            t = (-s) * turned if 4 * k == n else c * t - s * turned
        out[k] = even[k] + t
        out[k + n // 2] = even[k] - t
    return out


def flip_lanes(rows):
    lane = lax.broadcasted_iota(jnp.int32, (rows, INNER), 1)
    return jnp.where(lane < HALF, 1.0, -1.0).astype(F32)


def put_message(ref, d, value, fine):
    lane = lax.broadcasted_iota(jnp.int32, (INNER, INNER), 1)
    high = value.astype(BF16)
    ref[d, 0:INNER, :] = high
    rest = value - high.astype(F32)
    if fine:
        third = rest - rest.astype(BF16).astype(F32)
        rest = jnp.where((lane & (HALF - 1)) == 7, pltpu.roll(third, 7, 1), rest)
    rest = jnp.where(lane < 8, rest, pltpu.roll(rest, 72, 1))
    rest = jnp.where(lane < 16, rest, 0.0)
    total = rest[0:16]
    for g in range(1, 8):
        total = total + pltpu.roll(rest[16 * g : 16 * g + 16], 16 * g, 1)
    ref[d, INNER : INNER + TAIL, :] = total.astype(BF16)


def get_message(ref, d, fine):
    lane = lax.broadcasted_iota(jnp.int32, (INNER, INNER), 1)
    packed = ref[d, INNER : INNER + TAIL, :].astype(F32)
    rest = jnp.concatenate([packed] + [pltpu.roll(packed, INNER - 16 * g, 1) for g in range(1, 8)], axis=0)
    rest = jnp.where(lane < 8, rest, pltpu.roll(rest, 56, 1))
    column = lane & (HALF - 1)
    if fine:
        third = jnp.where(column == 0, pltpu.roll(rest, INNER - 7, 1), 0.0)
        rest = jnp.where(column < 7, rest, 0.0) + third
    else:
        rest = jnp.where(column < 8, rest, 0.0)
    return ref[d, 0:INNER, :].astype(F32) + rest


def row_forward_kernel(tiled, fine, x_ref, tw_ref, f_ref, a_ref, m_ref, out_ref, y_scr, e_scr):
    def slab(g, carry):
        if tiled:
            xs = [x_ref[pl.ds(pl.multiple_of(g * 256 + a * 8, 8), 8), :] for a in range(OUTER)]
        else:
            xs = [x_ref[pl.ds(pl.multiple_of(g * 8, 8), 8), a * INNER : (a + 1) * INNER] for a in range(OUTER)]
        ys = real_forward(xs)
        rows = pl.ds(pl.multiple_of(g * 8, 8), 8)
        e_scr[0, rows, :] = ys[0][0]
        e_scr[1, rows, :] = ys[16][0]
        for k in range(1, 16):
            c = tw_ref[0, k : k + 1, :]
            s = tw_ref[1, k : k + 1, :]
            re, im = ys[k]
            base = pl.ds(pl.multiple_of((k - 1) * INNER + g * 8, 8), 8)
            y_scr[base, 0:INNER] = re * c + im * s
            y_scr[base, INNER : 2 * INNER] = im * c - re * s
        return carry

    lax.fori_loop(0, 16, slab, 0, unroll=2)
    put_message(out_ref, 0, data_by_table(e_scr[0], every(a_ref)), fine)
    put_message(out_ref, 1, data_by_table(e_scr[1], every(m_ref)), fine)

    def group(q, carry):
        v = data_by_table(y_scr[pl.ds(pl.multiple_of(q * 384, 8), 384), :], every(f_ref))
        for i in range(3):
            rows = v[i * INNER : (i + 1) * INNER]
            put_message(out_ref, 2 + 2 * (3 * q + i), rows[:, 0:INNER], fine)
            put_message(out_ref, 3 + 2 * (3 * q + i), rows[:, INNER : 2 * INNER], fine)
        return carry

    lax.fori_loop(0, 5, group, 0)


def row_backward_kernel(final, *refs):
    if final:
        in_ref, base_ref, tw_ref, f_ref, a_ref, m_ref, out_ref, z_scr, e_scr = refs
    else:
        in_ref, tw_ref, f_ref, a_ref, m_ref, out_ref, z_scr, e_scr = refs
    e_scr[0] = data_by_table(get_message(in_ref, 0, False), every(a_ref))
    e_scr[1] = data_by_table(get_message(in_ref, 1, False), every(m_ref))

    def group(q, carry):
        parts = []
        for i in range(3):
            k = 3 * q + i
            parts.append(jnp.concatenate([get_message(in_ref, 2 + 2 * k + h, False) for h in range(2)], axis=1))
        v = jnp.concatenate(parts, axis=0)
        z_scr[pl.ds(pl.multiple_of(q * 384, 8), 384), :] = data_by_table(v, every(f_ref))
        return carry

    lax.fori_loop(0, 5, group, 0)

    def slab(g, carry):
        rows = pl.ds(pl.multiple_of(g * 8, 8), 8)
        spec = [(e_scr[0, rows, :], None)]
        for k in range(1, 16):
            c = tw_ref[0, k : k + 1, :]
            s = tw_ref[1, k : k + 1, :]
            base = pl.ds(pl.multiple_of((k - 1) * INNER + g * 8, 8), 8)
            re = z_scr[base, 0:INNER]
            im = z_scr[base, INNER : 2 * INNER]
            spec.append((re * c - im * s, im * c + re * s))
        spec.append((e_scr[1, rows, :], None))
        xs = real_backward(spec)
        for a in range(OUTER):
            if final:
                cols = slice(a * INNER, (a + 1) * INNER)
                out_ref[rows, cols] = base_ref[rows, cols] + xs[a]
            else:
                out_ref[pl.ds(pl.multiple_of(g * 256 + a * 8, 8), 8), :] = xs[a]
        return carry

    lax.fori_loop(0, 16, slab, 0, unroll=2)


def take_all(exchange, scr, fine):
    exchange.own.wait()
    scr[exchange.me] = get_message(exchange.out_ref, exchange.me, fine)

    def step(i, carry):
        exchange.wait_source(i)
        source = exchange.source(i)
        scr[source] = get_message(exchange.out_ref, source, fine)
        return carry

    lax.fori_loop(0, PEERS - 1, step, 0)
    exchange.wait_sends()


def give_all(scr, exchange):
    def step(i, carry):
        peer = exchange.peer(i)
        put_message(exchange.in_ref, peer, scr[peer], False)
        exchange.send(i)
        return carry

    lax.fori_loop(0, PEERS - 1, step, 0)
    put_message(exchange.in_ref, exchange.me, scr[exchange.me], False)
    exchange.own.start()


def column_first_step(in_ref, y_scr, sign):
    flip = flip_lanes(8)

    def slab(g, carry):
        rows = pl.ds(pl.multiple_of(g * 8, 8), 8)
        ys = packed_fft([in_ref[s, rows, :] for s in range(OUTER)], sign, flip)
        for k in range(OUTER):
            y_scr[k, rows, :] = ys[k]
        return carry

    lax.fori_loop(0, 16, slab, 0, unroll=2)


def apply_packed(e_ref, k1, value, flip):
    r = table_by_data([e_ref[i, k1] for i in range(e_ref.shape[0])], value)
    return r[0:INNER] - pltpu.roll(r[INNER : 2 * INNER], HALF, 1) * flip


MESH = pl.DeviceIdType.MESH


def greet_peers(me, barrier, extra=()):
    def greet(i, carry):
        pl.semaphore_signal(barrier, inc=1, device_id={"strip": lax.rem(me + i, PEERS)}, device_id_type=MESH)
        return carry

    lax.fori_loop(1, PEERS, greet, 0)
    for device in extra:
        pl.semaphore_signal(barrier, inc=1, device_id=device, device_id_type=MESH)
    pl.semaphore_wait(barrier, PEERS - 1 + len(extra))


STRIDE = 11
REPLY = 45


class Exchange:
    def __init__(self, me, in_ref, out_ref, send_sem, recv_sem, own_sem, flat=0):
        self.me, self.in_ref, self.out_ref, self.flat = me, in_ref, out_ref, flat
        self.send_sem, self.recv_sem = send_sem, recv_sem
        self.own = pltpu.make_async_copy(self.part(in_ref, me), self.part(out_ref, me), own_sem)

    def part(self, ref, i):
        return ref.at[pl.ds(pl.multiple_of(i * self.flat, self.flat), self.flat)] if self.flat else ref.at[i]

    def copy(self, peer, send, source):
        return pltpu.make_async_remote_copy(
            src_ref=self.part(self.in_ref, peer),
            dst_ref=self.part(self.out_ref, source),
            send_sem=self.send_sem.at[send],
            recv_sem=self.recv_sem.at[source],
            device_id={"strip": peer},
            device_id_type=MESH,
        )

    def peer(self, i):
        return lax.rem(self.me + 1 + lax.rem(i * STRIDE, PEERS - 1), PEERS)

    def source(self, i):
        return lax.rem(self.me + PEERS - 1 - lax.rem(i * STRIDE, PEERS - 1), PEERS)

    def reply(self, i):
        return lax.rem(REPLY - i, PEERS - 1)

    def send(self, i):
        self.copy(self.peer(i), i, self.me).start()

    def wait_source(self, i):
        self.copy(self.peer(i), i, self.source(i)).wait_recv()

    def wait_sends(self):
        def step(i, carry):
            self.copy(self.peer(i), i, self.me).wait_send()
            return carry

        lax.fori_loop(0, PEERS - 1, step, 0)

    def start(self, first=0, last=PEERS - 1):
        def step(i, carry):
            self.copy(self.peer(i), i, self.me).start()
            return carry

        lax.fori_loop(first, last, step, 0)
        if first == 0:
            self.own.start()

    def wait(self):
        def step(i, carry):
            self.wait_source(i)
            return carry

        self.own.wait()
        lax.fori_loop(0, PEERS - 1, step, 0)
        self.wait_sends()


class Moves:
    def __init__(self, pairs, sems):
        self.copies = [pltpu.make_async_copy(src, dst, sems.at[i]) for i, (src, dst) in enumerate(pairs)]

    def start(self):
        for copy in self.copies:
            copy.start()

    def wait(self):
        for copy in self.copies:
            copy.wait()


def exchange_sems():
    return [pltpu.SemaphoreType.DMA((PEERS,)), pltpu.SemaphoreType.DMA((PEERS,)), pltpu.SemaphoreType.DMA]


def edge_lanes():
    lane = lax.broadcasted_iota(jnp.int32, (INNER, INNER), 1)
    return jnp.logical_or(lane == 0, lane == HALF), lane < HALF


def edge_gather(ref):
    mask, _ = edge_lanes()

    def step(k1, acc):
        return acc + pltpu.roll(jnp.where(mask, ref[k1], 0.0), k1, 1)

    return lax.fori_loop(0, OUTER, step, jnp.zeros((INNER, INNER), F32), unroll=4)


def edge_split(spec, amp):
    i = lax.broadcasted_iota(jnp.int32, (INNER, INNER), 0)
    j = lax.broadcasted_iota(jnp.int32, (INNER, INNER), 1)
    one = jnp.ones((INNER, INNER), F32)
    none = jnp.zeros((INNER, INNER), F32)
    rows = jnp.where(i + j == INNER - 1, one, none).astype(BF16)
    rows0 = jnp.where(((i + j) & (INNER - 1)) == 0, one, none).astype(BF16)
    sign = jnp.where(j < HALF, one, -one)
    col = j & (HALF - 1)
    same = (i < HALF) == (j < HALF)
    lanes = jnp.where(
        jnp.logical_and(same, jnp.logical_and(col > 0, col + (i & (HALF - 1)) == OUTER)), sign, none
    ).astype(BF16)
    lanes0 = jnp.where(jnp.logical_and(i == j, col == 0), sign, none).astype(BF16)

    def move(left, value, right):
        value = sum(mm(left, p) for p in reversed(split_into(value, 3)))
        return sum(mm(p, right) for p in reversed(split_into(value, 3)))

    rev = move(rows, spec, lanes) + move(rows0, spec, lanes0)
    swapped = pltpu.roll(amp, HALF, 1)
    _, left = edge_lanes()
    a0 = jnp.where(left, amp, swapped)
    a2 = jnp.where(left, swapped, amp)
    return 0.5 * (spec + rev), 0.5 * (spec - rev), a0, a2


def turn(c, s, value, flip):
    return c * value + s * (pltpu.roll(value, HALF, 1) * flip)


EARLY = 4
MIDDLE = 16


def first_kernel(
    scale, rate, wind, prior, x_ref, tw, f_ref, a_ref, m_ref, fi_ref, ai_ref, mi_ref, slot_ref, prec_ref,
    ef_any, ei_any, sent_ref, ids_ref,
    resid_ref, par, own_any, here_any, amp_any, here_ids_ref, prev_ref, next_ref, *scratch,
):
    y_scr, z_scr, msg_scr, land_scr, back_scr, tab_ref, row_scr, row_edge = scratch[0:8]
    up_ref, down_ref, tiles_scr, g_scr, phase_scr, landed, p_scr, table_scr, res_scr = scratch[8:17]
    sid_scr, sid_sem, side_sems = scratch[17:20]
    ef, ei, own_ref, amp_ref, here_ref, in_sems, out_sems, here_sems = scratch[20:28]
    sems = scratch[28:]
    tables = Moves([(ef_any, ef), (ei_any, ei)], in_sems)
    tables.start()
    results = Moves([(own_ref, own_any), (amp_ref, amp_any)], out_sems)
    weights_out = Moves([(here_ref, here_any)], here_sems)
    me = lax.axis_index("strip")
    slot_at = lax.axis_index("tm")
    above, below = lax.rem(slot_at + 1, 4), lax.rem(slot_at + 3, 4)
    greet_peers(me, pltpu.get_barrier_semaphore(), ({"tm": above}, {"tm": below}))
    ids = Exchange(me, ids_ref, here_ids_ref, *sems[0:3], flat=ID_STRIDE)
    weights = Exchange(me, sent_ref, here_ref, *sems[3:6])
    pencils = Exchange(me, msg_scr, land_scr, *sems[6:9])
    back = Exchange(me, msg_scr, back_scr, *sems[9:12])
    phases = Exchange(me, phase_scr, landed, *sems[12:15])
    residuals = Exchange(me, res_scr, resid_ref, *sems[15:18])
    ids.start()
    weights.start(0, EARLY)
    row_forward_kernel(False, True, x_ref, tw, f_ref, a_ref, m_ref, msg_scr, row_scr, row_edge)
    pencils.start()
    tables_kernel(scale, rate, wind, prior, tab_ref, amp_ref, par)
    take_all(pencils, z_scr, True)
    weights.start(EARLY, MIDDLE)
    tables.wait()
    column_first_step(z_scr, y_scr, -1.0)
    flip = flip_lanes(INNER)

    def step(k1, carry):
        value = apply_packed(ef, k1, y_scr[k1], flip)
        amp = amp_ref[k1]
        once = value * amp
        twice = once * amp
        y_scr[k1] = value
        z_scr[k1] = par[0] * once
        own_ref[k1] = par[3] * twice
        for n, ref, gain in ((0, up_ref, par[1]), (1, down_ref, par[2])):
            cb = tab_ref[2 * n]
            sb = tab_ref[2 * n + 1]
            ca = tab_ref[8, pl.ds(64 * n + k1, 1), :] * gain
            sa = tab_ref[8, pl.ds(64 * n + 32 + k1, 1), :] * gain
            ref[k1] = turn(cb * ca - sb * sa, sb * ca + cb * sa, twice, flip).astype(BF16)
        return carry

    lax.fori_loop(0, OUTER, step, 0, unroll=8)

    @pl.when(me == 0)
    def _():
        u0, u2, a0, a2 = edge_split(edge_gather(y_scr), edge_gather(amp_ref))
        mask, _ = edge_lanes()
        e0 = a0 * u0
        e2 = a2 * u2
        fixed = [par[0] * (e0 + e2)]
        e0 = a0 * e0
        e2 = a2 * e2
        fixed.append(par[3] * (e0 + e2))
        fixed.append(par[1] * turn(tab_ref[4], tab_ref[5], e0 + par[4] * e2, flip))
        fixed.append(par[2] * turn(tab_ref[6], tab_ref[7], e0 + par[5] * e2, flip))

        def put(k1, carry):
            back = lax.rem(INNER - k1, INNER)
            for ref, value in zip((z_scr, own_ref, up_ref, down_ref), fixed):
                value = jnp.where(mask, pltpu.roll(value, back, 1), ref[k1].astype(F32))
                ref[k1] = value.astype(ref.dtype)
            return carry

        lax.fori_loop(0, OUTER, put, 0, unroll=4)

    def inverse(k1, carry):
        z_scr[k1] = apply_packed(ei, k1, z_scr[k1], flip)
        return carry

    lax.fori_loop(0, OUTER, inverse, 0, unroll=8)
    column_first_step(z_scr, y_scr, 1.0)
    give_all(y_scr, back)
    results.start()
    ids.wait()
    fetch = pltpu.make_async_copy(here_ids_ref, sid_scr, sid_sem)
    fetch.start()
    back.wait()
    weights.start(MIDDLE, PEERS - 1)
    row_backward_kernel(False, back_scr, tw, fi_ref, ai_ref, mi_ref, tiles_scr, row_scr, row_edge)
    fetch.wait()
    ones = jnp.ones((2 * INNER, INNER), BF16)
    row = lax.broadcasted_iota(jnp.int32, (INNER, INNER), 0)
    lane = lax.broadcasted_iota(jnp.int32, (INNER, INNER), 1)
    place = lax.broadcasted_iota(jnp.int32, (1, INNER), 1)

    def pick(s, place_at):
        def some(q, carry):
            first = s * ID_STRIDE + q * 32
            picks = [sid_scr[first + j] for j in range(32)]
            rows = [tiles_scr[pl.ds(picks[j], 1), :] for j in range(32)]
            for j in range(32):
                g_scr[pl.ds(place_at + q * 32 + j, 1), :] = rows[j]
            return carry

        lax.fori_loop(0, SLOTS // 32, some, 0)

    def gather_pair(pair):
        for n, s in enumerate(pair):
            pick(s, n * SLOTS)
        for n, s in enumerate(pair):
            count = sid_scr[s * ID_STRIDE + SLOTS]
            picked = g_scr[n * SLOTS : (n + 1) * SLOTS, :]
            sums = mm(jnp.concatenate(split(picked * here_ref[s].astype(F32)), axis=1), ones)
            for q in range(4):
                got = jnp.where(row == lane, sums[q * INNER : (q + 1) * INNER], 0.0)
                got = jnp.sum(got, axis=0, keepdims=True)
                phase_scr[s, q : q + 1, :] = jnp.where(place + q * INNER < count, got, 0.0)

    def gather_next(h, carry):
        steps = (2 * h, 2 * h + 1)
        for i in steps:
            weights.wait_source(i)
        gather_pair([weights.source(i) for i in steps])
        for i in steps:
            phases.copy(weights.source(i), phases.reply(i), me).start()
        return carry

    lax.fori_loop(0, PEERS // 2 - 1, gather_next, 0)
    weights.own.wait()
    weights.wait_source(PEERS - 2)
    last = weights.source(PEERS - 2)
    gather_pair([last, me])
    phases.copy(last, phases.reply(PEERS - 2), me).start()
    phases.own.start()
    weights.wait_sends()
    weights_out.start()

    @pl.when(slot_at < 3)
    def _():
        for side in sides(side_sems, up_ref, prev_ref, above, 0):
            side.start()

    @pl.when(slot_at > 0)
    def _():
        for side in sides(side_sems, down_ref, next_ref, below, 1):
            side.start()

    phases.wait()
    for s in range(PEERS):
        table_scr[4 * s : 4 * s + 4, :] = landed[s]
    acc = weigh(slot_ref, prec_ref, table_scr[...], p_scr)
    for s in range(PEERS):
        res_scr[s] = acc[4 * s : 4 * s + 4]
    residuals.start()
    results.wait()
    weights_out.wait()
    residuals.wait()

    @pl.when(slot_at < 3)
    def _():
        for side in sides(side_sems, up_ref, prev_ref, above, 0):
            side.wait_send()
        for side in sides(side_sems, down_ref, next_ref, below, 1):
            side.wait_recv()

    @pl.when(slot_at > 0)
    def _():
        for side in sides(side_sems, up_ref, prev_ref, above, 0):
            side.wait_recv()
        for side in sides(side_sems, down_ref, next_ref, below, 1):
            side.wait_send()


SIDE_PARTS = 4


def sides(sems, src, dst, device, n):
    copies = []
    for p in range(SIDE_PARTS):
        rows = pl.ds(p * (OUTER // SIDE_PARTS), OUTER // SIDE_PARTS)
        copies.append(
            pltpu.make_async_remote_copy(
                src_ref=src.at[rows],
                dst_ref=dst.at[rows],
                send_sem=sems.at[0, n, p],
                recv_sem=sems.at[1, n, p],
                device_id={"tm": device},
                device_id_type=MESH,
            )
        )
    return copies


def column_second_kernel(par, in_ref, amp_any, own_any, prev_any, next_any, ef_any, ei_any, back_ref, *scratch):
    y_scr, z_scr, msg_scr, out_scr = scratch[0:4]
    amp_ref, own_ref, prev_ref, next_ref, ef, ei, in_sems = scratch[10:17]
    inputs = Moves(
        [(amp_any, amp_ref), (own_any, own_ref), (prev_any, prev_ref), (next_any, next_ref), (ef_any, ef), (ei_any, ei)],
        in_sems,
    )
    inputs.start()
    me = lax.axis_index("strip")
    slot_at = lax.axis_index("tm")
    greet_peers(me, pltpu.get_barrier_semaphore())
    pencils = Exchange(me, in_ref, msg_scr, *scratch[4:7])
    pencils.start()
    take_all(pencils, z_scr, False)
    inputs.wait()
    column_first_step(z_scr, y_scr, -1.0)
    flip = flip_lanes(INNER)

    def step(k1, carry):
        value = apply_packed(ef, k1, y_scr[k1], flip)
        y_scr[k1] = value
        z_scr[k1] = par[0] * (value * amp_ref[k1]) + own_ref[k1]
        return carry

    lax.fori_loop(0, OUTER, step, 0, unroll=8)

    @pl.when(me == 0)
    def _():
        spec = edge_gather(y_scr)
        amp = edge_gather(amp_ref)
        u0, u2, a0, a2 = edge_split(spec, amp)
        mask, _ = edge_lanes()
        change = par[0] * (a0 * u0 + a2 * u2 - amp * spec)

        def put(k1, carry):
            back = lax.rem(INNER - k1, INNER)
            z_scr[k1] = z_scr[k1] + jnp.where(mask, pltpu.roll(change, back, 1), 0.0)
            return carry

        lax.fori_loop(0, OUTER, put, 0, unroll=4)

    def inverse(k1, carry):
        moved = jnp.where(slot_at > 0, prev_ref[k1].astype(F32), 0.0)
        moved = moved + jnp.where(slot_at < 3, next_ref[k1].astype(F32), 0.0)
        z_scr[k1] = apply_packed(ei, k1, z_scr[k1] - par[0] * moved, flip)
        return carry

    lax.fori_loop(0, OUTER, inverse, 0, unroll=8)
    column_first_step(z_scr, y_scr, 1.0)
    back = Exchange(me, out_scr, back_ref, *scratch[7:10])
    give_all(y_scr, back)
    back.wait()


def route_kernel(t_ref, id_ref, slot_ref, tail_ref):
    row = lax.broadcasted_iota(jnp.int32, (INNER, 2 * INNER), 0)
    col = lax.broadcasted_iota(jnp.int32, (INNER, 2 * INNER), 1)
    tri = jnp.where(jnp.logical_or(row < col, col >= INNER), 1.0, 0.0).astype(BF16)
    peer = lax.broadcasted_iota(jnp.int32, (PEERS, INNER), 0)
    base = jnp.zeros((PEERS, INNER), F32)
    for i in range(0, POINT_ROWS, 8):
        hots = [jnp.where(peer == t_ref[i + j : i + j + 1, :], 1.0, 0.0) for j in range(8)]
        cum = mm(jnp.concatenate(hots, axis=0).astype(BF16), tri)
        for j in range(8):
            part = cum[j * PEERS : (j + 1) * PEERS]
            pos = jnp.sum(hots[j] * (part[:, 0:INNER] + base), axis=0, keepdims=True)
            base = base + part[:, INNER : 2 * INNER]
            slot_ref[i + j : i + j + 1, :] = t_ref[i + j : i + j + 1, :] * SLOTS + pos.astype(jnp.int32)
    batch = 4
    index = lax.broadcasted_iota(jnp.int32, (INNER, batch * INNER), 0)

    def wide(ref, i):
        return jnp.concatenate([ref[pl.ds(i * batch + j, 1), :] for j in range(batch)], axis=1)

    def put(i, acc):
        slot = wide(slot_ref, i)
        ids = wide(id_ref, i)
        r = lax.shift_right_logical(ids, 5)
        ids = lax.shift_right_logical(r, 3) * 256 + (ids & 31) * 8 + (r & 7)
        hot = jnp.where(index == (slot & 127), 1.0, 0.0).astype(BF16)
        line = index == lax.shift_right_logical(slot, 7)
        v = [
            jnp.where(line, d.astype(F32), 0.0).astype(BF16) for d in (lax.shift_right_logical(ids, 6), ids & 63)
        ]
        return acc + mm_nt(jnp.concatenate(v, axis=0), hot)

    acc = lax.fori_loop(0, POINT_ROWS // batch, put, jnp.zeros((2 * INNER, INNER), F32), unroll=2)
    ids = (acc[0:INNER] * 64.0 + acc[INNER : 2 * INNER]).astype(jnp.int32)
    count = base.astype(jnp.int32)
    tail_ref[...] = jnp.zeros_like(tail_ref)
    for s in range(PEERS):
        tail_ref[s, 0:4, :] = ids[4 * s : 4 * s + 4]
        tail_ref[s, 4:5, :] = count[s : s + 1]


def pack_kernel(slot_ref, w_ref, out_ref, w_scr, buf):
    def widen(i, carry):
        rows = pl.ds(pl.multiple_of(i * 64, 64), 64)
        w_scr[rows, :] = w_ref[rows, :].astype(F32)
        return carry

    lax.fori_loop(0, POINT_ROWS * INNER // 64, widen, 0, unroll=2)

    def some(q, carry):
        antenna, direction = (q // 8) * 4, (q % 8) * 8
        first = direction * INNER + antenna
        line = pl.multiple_of(antenna * HALF + direction, 8)
        pairs = [(a, d) for a in range(4) for d in range(8)]
        slots = [slot_ref[first + d * INNER + a] for a, d in pairs]
        rows = [w_scr[pl.ds(line + a * HALF + d, 1), :] for a, d in pairs]
        for j in range(32):
            buf[pl.ds(slots[j], 1), :] = rows[j]
        return carry

    lax.fori_loop(0, POINT_ROWS * INNER // 32, some, 0)

    def narrow(i, carry):
        rows = pl.ds(pl.multiple_of(i * INNER, INNER), INNER)
        out_ref[rows, :] = buf[rows, :].astype(BF16)
        return carry

    lax.fori_loop(0, PEERS * SLOTS // INNER, narrow, 0, unroll=2)


def weigh(slot_ref, prec_ref, phase, p_scr):
    high, low = split(phase)
    table = jnp.concatenate([high, low], axis=0)
    batch = 4
    index = lax.broadcasted_iota(jnp.int32, (INNER, batch * INNER), 0)

    def wide(ref, i):
        return jnp.concatenate([ref[pl.ds(i * batch + j, 1), :] for j in range(batch)], axis=1)

    def pick(i, carry):
        slot = wide(slot_ref, i)
        hot = jnp.where(index == (slot & 127), 1.0, 0.0).astype(BF16)
        v = mm(table, hot)
        v = v[0:INNER] + v[INNER : 2 * INNER]
        got = jnp.sum(jnp.where(index == lax.shift_right_logical(slot, 7), v, 0.0), axis=0, keepdims=True)
        for j in range(batch):
            p_scr[pl.ds(i * batch + j, 1), :] = got[:, j * INNER : (j + 1) * INNER]
        return carry

    lax.fori_loop(0, POINT_ROWS // batch, pick, 0, unroll=4)
    prec = prec_ref[...]
    phase = p_scr[...]

    centre = jnp.sum(prec * phase, axis=0, keepdims=True) / jnp.sum(prec, axis=0, keepdims=True)
    p_scr[...] = prec * (phase - centre)

    def put(i, acc):
        slot = wide(slot_ref, i)
        hot = jnp.where(index == (slot & 127), 1.0, 0.0).astype(BF16)
        v = jnp.where(index == lax.shift_right_logical(slot, 7), wide(p_scr, i), 0.0)
        vh, vl = split(v)
        return acc + mm_nt(jnp.concatenate([vh, vl], axis=0), hot)

    acc = lax.fori_loop(0, POINT_ROWS // batch, put, jnp.zeros((2 * INNER, INNER), F32), unroll=4)
    return acc[0:INNER] + acc[INNER : 2 * INNER]


COPIES = 8


def scatter_kernel(
    sid_ref, r_ref, w_any, tw, f_ref, a_ref, m_ref, out_ref, rt_scr, u_scr, y_scr, e_scr, w_ref, w_sems, *accs
):
    fetch = Moves([(w_any, w_ref)], w_sems)
    fetch.start()
    def clear(i, carry):
        rows = pl.ds(pl.multiple_of(i * 64, 64), 64)
        for acc in accs:
            acc[rows, :] = jnp.zeros((64, INNER), F32)
        return carry

    lax.fori_loop(0, SIDE // 64, clear, 0)
    rt_scr[...] = r_ref[...].T
    fetch.wait()
    lane = lax.broadcasted_iota(jnp.int32, (INNER, INNER), 1)
    row = lax.broadcasted_iota(jnp.int32, (INNER, INNER), 0)

    def scaled(s, carry):
        for q in range(4):
            col = jnp.sum(jnp.where(lane == s * 4 + q, rt_scr[...], 0.0), axis=1, keepdims=True)
            rows = pl.ds(pl.multiple_of(s * SLOTS + q * INNER, INNER), INNER)
            used = row + q * INNER < sid_ref[s * ID_STRIDE + SLOTS]
            u_scr[rows, :] = jnp.where(used, w_ref[rows, :].astype(F32) * col, 0.0)
        return carry

    lax.fori_loop(0, PEERS, scaled, 0, unroll=2)

    def source(s, carry):
        def some(q, inner):
            first = s * SLOTS + q * 32
            line = s * ID_STRIDE + q * 32
            ids = [sid_ref[line + j] for j in range(32)]
            us = [u_scr[pl.ds(first + j, 1), :] for j in range(32)]
            for h in range(0, 32, COPIES):
                sums = [accs[j][pl.ds(ids[h + j], 1), :] + us[h + j] for j in range(COPIES)]
                for j in range(COPIES):
                    accs[j][pl.ds(ids[h + j], 1), :] = sums[j]
            return inner

        return lax.fori_loop(0, lax.shift_right_logical(sid_ref[s * ID_STRIDE + SLOTS] + 31, 5), some, carry)

    lax.fori_loop(0, PEERS, source, 0)

    def add(i, carry):
        rows = pl.ds(pl.multiple_of(i * 64, 64), 64)
        total = accs[0][rows, :]
        for acc in accs[1:]:
            total = total + acc[rows, :]
        accs[0][rows, :] = total
        return carry

    lax.fori_loop(0, SIDE // 64, add, 0)
    row_forward_kernel(True, False, accs[0], tw, f_ref, a_ref, m_ref, out_ref, y_scr, e_scr)


def call(kernel, name, out_shapes, args, smem=0, scratch=(), any_args=(), any_outs=(), smem_outs=(), collective_id=None):
    spaces = [pltpu.SMEM if i < smem else pl.ANY if i in any_args else pltpu.VMEM for i in range(len(args))]
    outs = [pl.ANY if i in any_outs else pltpu.SMEM if i in smem_outs else pltpu.VMEM for i in range(len(out_shapes))]
    remote = dict(collective_id=collective_id, has_side_effects=True) if collective_id is not None else {}
    return pl.pallas_call(
        kernel,
        out_shape=out_shapes,
        in_specs=[pl.BlockSpec(memory_space=space) for space in spaces],
        out_specs=[pl.BlockSpec(memory_space=space) for space in outs],
        scratch_shapes=list(scratch),
        compiler_params=pltpu.CompilerParams(vmem_limit_bytes=VMEM_BYTES, **remote),
        cost_estimate=pl.CostEstimate(flops=1024, bytes_accessed=1024, transcendentals=0),
        name=name,
    )(*args)


def shape(dims, dtype=F32):
    return jax.ShapeDtypeStruct(dims, dtype)


PENCILS = (PEERS, INNER, INNER)
MESSAGES = (PEERS, INNER + TAIL, INNER)


def row_backward(pencils, base, tables):
    final = base is not None
    args = [pencils] + ([base] if final else []) + tables
    return call(
        lambda *refs: row_backward_kernel(final, *refs),
        "row_backward",
        [shape((INNER, SIDE) if final else (SIDE, INNER))],
        args,
        scratch=[pltpu.VMEM((15 * INNER, 2 * INNER), F32), pltpu.VMEM((2, INNER, INNER), F32)],
    )[0]


def tables_kernel(scale, rate, wind, prior, tab_ref, amp_ref, par_ref):
    strip = lax.axis_index("strip")
    live = (lax.axis_index("tm") < 3).astype(F32)
    k1 = (strip // 2).astype(F32)
    even = strip % 2 == 0
    row = lax.broadcasted_iota(jnp.int32, (INNER, INNER), 0)
    lane = lax.broadcasted_iota(jnp.int32, (INNER, INNER), 1)
    line = row.astype(F32)
    j = (lane & (HALF - 1)).astype(F32)
    cols = jnp.where(even, k1 + OUTER * j, k1 + OUTER * (INNER - 1.0 - j))
    cols = jnp.where(strip == 1, 16.0 + OUTER * j, cols)
    winds = ((wind[0, 0].astype(F32), wind[0, 1].astype(F32)), (prior[1], prior[2]))

    def cosine(turns):
        turns = turns - SIDE * jnp.floor(turns * (1.0 / SIDE))
        return jnp.cos(turns * (2.0 * math.pi / SIDE))

    small = jnp.zeros((INNER, INNER), F32)
    for kind in range(4):
        wind_row, wind_col = winds[kind // 2]
        quarter = (0.0, 3.0 * SIDE / 4, 0.0, SIDE / 4.0)[kind]
        base = OUTER * line * wind_row + quarter
        tab_ref[kind] = cosine(base + cols * wind_col)
        tab_ref[4 + kind] = cosine(base + j * wind_row)
        turns = (row & (OUTER - 1)).astype(F32) * wind_row + quarter
        small = jnp.where(lax.shift_right_logical(row, 5) == kind, turns, small)
    tab_ref[8] = cosine(small)

    fold = jnp.where(even, k1 + OUTER * j, OUTER - k1 + OUTER * j)
    fold = jnp.where(strip == 1, 16.0 + OUTER * j, fold)
    fold = jnp.where(jnp.logical_and(strip == 0, lane == HALF), SIDE / 2.0, fold)
    fold = fold * fold

    def step(k, carry):
        kr = line * OUTER + k.astype(F32)
        kr = jnp.minimum(kr, SIDE - kr)
        radius = (kr * kr + fold) / (KZERO * KZERO)
        amp_ref[k] = SIDE / (2.0 * KZERO) * jnp.exp((-11.0 / 12.0) * jnp.log(1.0 + radius))
        return carry

    lax.fori_loop(0, OUTER, step, 0, unroll=2)
    norm = scale[0] / (SIDE * SIDE)
    mine = rate[0] * live
    par_ref[0] = norm
    par_ref[1] = mine * scale[0]
    par_ref[2] = prior[0] * scale[0]
    par_ref[3] = (mine + prior[0]) * scale[0] * norm
    par_ref[4] = 1.0 - 2.0 * (wind[0, 1] & 1).astype(F32)
    par_ref[5] = 1.0 - 2.0 * (prior[2].astype(jnp.int32) & 1).astype(F32)
    par_ref[6] = 0.0
    par_ref[7] = 0.0


def const(*tables):
    return [jnp.asarray(t) for t in tables]


def local(
    screen_vec,
    prior_scale,
    flow_weight,
    wind,
    pierce_point_strip,
    pierce_block,
    pierce_weights,
    noise_prec,
):
    fwd, inv, first, first_inv, mid, mid_inv, twiddle = row_tables()
    row_fwd_tables = const(twiddle, pieces(fwd, 2), pieces(first, 2), pieces(mid, 2))
    row_fine_tables = const(twiddle, pieces(fwd, 3), pieces(first, 3), pieces(mid, 3))
    row_inv_tables = const(twiddle, pieces(inv, 2), pieces(first_inv, 2), pieces(mid_inv, 2))
    col_fwd, col_inv = column_tables()
    col_fine_tables = const(pieces(col_fwd, 3), pieces(col_inv, 2))
    col_tables = const(pieces(col_fwd, 2), pieces(col_inv, 2))

    x = screen_vec[0]
    weights = pierce_weights[0].reshape(POINT_ROWS * INNER, INNER)
    target = pierce_point_strip.reshape(INNER, HALF).T
    block = pierce_block.reshape(INNER, HALF).T
    prec = noise_prec.reshape(INNER, HALF).T

    mine = jnp.concatenate([flow_weight, wind[0].astype(F32)])
    prior = lax.ppermute(mine, "tm", [(i, i + 1) for i in range(lax.axis_size("tm") - 1)])
    slots, ids = call(
        route_kernel,
        "route",
        [shape((POINT_ROWS, INNER), jnp.int32), shape((PEERS, ID_ROWS, INNER), jnp.int32)],
        [target, block],
    )
    ids, prior, prec = lax.optimization_barrier((ids, prior, prec))
    sent = call(
        pack_kernel,
        "pack",
        [shape((PEERS * SLOTS, INNER), BF16)],
        [slots.reshape(-1), weights],
        smem=1,
        scratch=[pltpu.VMEM((POINT_ROWS * INNER, INNER), F32), pltpu.VMEM((PEERS * SLOTS, INNER), F32)],
    )[0]

    spectral = [pltpu.VMEM(PENCILS, F32), pltpu.VMEM(PENCILS, F32)]
    rows = [pltpu.VMEM((15 * INNER, 2 * INNER), F32), pltpu.VMEM((2, INNER, INNER), F32)]
    message = shape(MESSAGES, BF16)
    points = pltpu.VMEM((PEERS * SLOTS, INNER), F32)
    screen = pltpu.VMEM((SIDE, INNER), F32)
    small = (PEERS, 4, INNER)
    resid, par, own, arrived, amp, here_ids, from_prev, from_next = call(
        first_kernel,
        "first",
        [
            shape(small),
            shape((8,)),
            shape(PENCILS),
            shape((PEERS, SLOTS, INNER), BF16),
            shape(PENCILS),
            shape((PEERS * ID_STRIDE,), jnp.int32),
            shape(PENCILS, BF16),
            shape(PENCILS, BF16),
        ],
        [prior_scale, flow_weight, wind, prior, x]
        + row_fine_tables
        + row_inv_tables[1:]
        + [slots, prec]
        + col_fine_tables
        + [sent.reshape(PEERS, SLOTS, INNER), ids.reshape(-1)],
        smem=4,
        any_args=(14, 15, 16, 17),
        any_outs=(2, 3, 4, 5, 6, 7),
        smem_outs=(1,),
        collective_id=3,
        scratch=spectral
        + [pltpu.VMEM(MESSAGES, BF16)] * 3
        + [pltpu.VMEM((9, INNER, INNER), F32)]
        + rows
        + [pltpu.VMEM(PENCILS, BF16)] * 2
        + [
            screen,
            pltpu.VMEM((2 * SLOTS, INNER), F32),
            pltpu.VMEM(small, F32),
            pltpu.VMEM(small, F32),
            pltpu.VMEM((POINT_ROWS, INNER), F32),
            pltpu.VMEM((INNER, INNER), F32),
            pltpu.VMEM(small, F32),
            pltpu.SMEM((PEERS * ID_STRIDE,), jnp.int32),
            pltpu.SemaphoreType.DMA,
            pltpu.SemaphoreType.DMA((2, 2, SIDE_PARTS)),
            pltpu.VMEM(col_fine_tables[0].shape, BF16),
            pltpu.VMEM(col_fine_tables[1].shape, BF16),
            pltpu.VMEM(PENCILS, F32),
            pltpu.VMEM(PENCILS, F32),
            pltpu.VMEM((PEERS, SLOTS, INNER), BF16),
            pltpu.SemaphoreType.DMA((2,)),
            pltpu.SemaphoreType.DMA((2,)),
            pltpu.SemaphoreType.DMA((1,)),
        ]
        + exchange_sems() * 6,
    )
    here = arrived.reshape(PEERS * SLOTS, INNER)

    pencils = call(
        scatter_kernel,
        "scatter",
        [message],
        [here_ids, resid.reshape(INNER, INNER), here] + row_fwd_tables,
        smem=1,
        any_args=(2,),
        scratch=[pltpu.VMEM((INNER, INNER), F32), points]
        + rows
        + [pltpu.VMEM((PEERS * SLOTS, INNER), BF16), pltpu.SemaphoreType.DMA((1,))]
        + [screen] * COPIES,
    )[0]
    out_pencils = call(
        column_second_kernel,
        "column_second",
        [message],
        [par, pencils, amp, own, from_prev, from_next] + col_tables,
        smem=1,
        any_args=range(1, 8),
        any_outs=(0,),
        collective_id=1,
        scratch=spectral
        + [pltpu.VMEM(MESSAGES, BF16)] * 2
        + exchange_sems()
        + exchange_sems()
        + spectral
        + [pltpu.VMEM(PENCILS, BF16)] * 2
        + [pltpu.VMEM(t.shape, BF16) for t in col_tables]
        + [pltpu.SemaphoreType.DMA((6,))],
    )[0]
    return row_backward(out_pencils, x, row_inv_tables)[None]


def solution(mesh):
    in_specs = (
        P("tm", "strip", None),
        P("tm"),
        P("tm"),
        P("tm", None),
        P("tm", "strip", None, None),
        P("tm", "strip", None),
        P("tm", "strip", None, None),
        P("tm", "strip", None),
    )
    out_specs = P("tm", "strip", None)
    return jax.shard_map(local, mesh=mesh, in_specs=in_specs, out_specs=out_specs, check_vma=False)
```

```python
import math

import jax
import jax.numpy as jnp
import ml_dtypes
import numpy as np
from jax import lax
from jax.experimental import pallas as pl
from jax.experimental.pallas import tpu as pltpu
from jax.sharding import PartitionSpec as P

KZERO = 2.0
SIDE = 4096
OUTER = 32
INNER = 128
HALF = 64
PEERS = 32
SLOTS = 512
POINT_ROWS = 64
TAIL = 16
ID_ROWS = 8
ID_STRIDE = ID_ROWS * 128
VMEM_BYTES = 56 * 1024 * 1024
F32 = jnp.float32
BF16 = jnp.bfloat16


def pieces(table, count):
    rest = np.asarray(table, np.float64)
    out = []
    for _ in range(count):
        out.append(rest.astype(np.float32).astype(ml_dtypes.bfloat16))
        rest = rest - out[-1].astype(np.float64)
    return np.stack(out)


def row_tables():
    b = np.arange(INNER)[:, None]
    j = np.arange(HALF)[None, :]
    theta = [2 * np.pi * ((b * j) % INNER) / INNER, 2 * np.pi * ((b * (INNER - 1 - j)) % INNER) / INNER]
    forward = []
    backward = []
    for t in theta:
        forward.append(np.concatenate([np.cos(t), -np.sin(t)], axis=1))
        forward.append(np.concatenate([np.sin(t), np.cos(t)], axis=1))
        backward.append(np.concatenate([np.cos(t).T, np.sin(t).T], axis=1))
        backward.append(np.concatenate([-np.sin(t).T, np.cos(t).T], axis=1))
    fwd = np.concatenate(
        [np.concatenate([forward[0], forward[1]], axis=0), np.concatenate([forward[2], forward[3]], axis=0)], axis=1
    )
    inv = np.concatenate(backward, axis=0)
    sign = np.where(np.arange(INNER) % 2 == 0, 1.0, -1.0)
    t0 = theta[0]
    first = np.concatenate([np.cos(t0), -np.sin(t0)], axis=1)
    first[:, HALF] = sign
    first_inv = np.concatenate([2 * np.cos(t0).T, -2 * np.sin(t0).T], axis=0)
    first_inv[0, :] = 1.0
    first_inv[HALF, :] = sign
    t16 = 2 * np.pi * ((b * (16 + 32 * j)) % SIDE) / SIDE
    mid = np.concatenate([np.cos(t16), -np.sin(t16)], axis=1)
    mid_inv = np.concatenate([2 * np.cos(t16).T, -2 * np.sin(t16).T], axis=0)
    k1 = np.arange(16)[:, None]
    tw = 2 * np.pi * (k1 * np.arange(INNER)[None, :]) / SIDE
    twiddle = np.stack([np.cos(tw), np.sin(tw)]).astype(np.float32)
    return fwd, inv, first, first_inv, mid, mid_inv, twiddle


def column_tables():
    k1 = np.arange(OUTER)[:, None, None]
    k2 = np.arange(INNER)[None, :, None]
    r = np.arange(INNER)[None, None, :]
    theta = 2 * np.pi * (((k1 + OUTER * k2) * r) % SIDE) / SIDE
    fwd = np.concatenate([np.cos(theta), -np.sin(theta)], axis=1)
    theta = theta.transpose(0, 2, 1)
    inv = np.concatenate([np.cos(theta), np.sin(theta)], axis=1)
    return fwd, inv


def split(value):
    high = value.astype(BF16)
    return high, (value - high.astype(F32)).astype(BF16)


def mm(left, right):
    return lax.dot_general(left, right, (((1,), (0,)), ((), ())), preferred_element_type=F32)


def mm_nt(left, right):
    return lax.dot_general(left, right, (((1,), (1,)), ((), ())), preferred_element_type=F32)


def split_into(value, count):
    parts = []
    for i in range(count):
        parts.append(value.astype(BF16))
        if i + 1 < count:
            value = value - parts[-1].astype(F32)
    return parts


def data_by_table(value, tables):
    count = len(tables)
    parts = split_into(value, count)
    total = None
    for order in reversed(range(count)):
        for i in range(order + 1):
            term = mm(parts[i], tables[order - i])
            total = term if total is None else total + term
    return total


def table_by_data(tables, value):
    parts = split_into(value, len(tables))
    left = jnp.concatenate(tables[0:2], axis=1)
    right = jnp.concatenate(parts[0:2], axis=1)
    r = mm(left, jnp.concatenate([right, right], axis=0))
    total = r[:, INNER : 2 * INNER] + r[:, 0:INNER]
    if len(tables) == 3:
        left = jnp.concatenate([tables[0], tables[2]], axis=1)
        total = total + mm(left, jnp.concatenate([parts[2], parts[0]], axis=0))
    return total


def every(ref):
    return [ref[i] for i in range(ref.shape[0])]


def c_mul(value, factor):
    re, im = value
    c, s = factor.real, factor.imag
    if im is None:
        return (re * c, re * s)
    return (re * c - im * s, re * s + im * c)


def real_forward(xs):
    n = len(xs)
    if n == 2:
        return [(xs[0] + xs[1], None), (xs[0] - xs[1], None)]
    even, odd = real_forward(xs[0::2]), real_forward(xs[1::2])
    m = n // 2
    out = [None] * (m + 1)
    for k in range(m // 2 + 1):
        if k == 0:
            out[0] = (even[0][0] + odd[0][0], None)
            out[m] = (even[0][0] - odd[0][0], None)
        elif 2 * k == m:
            out[k] = (even[k][0], -odd[k][0])
        else:
            tr, ti = c_mul(odd[k], complex(math.cos(2 * math.pi * k / n), -math.sin(2 * math.pi * k / n)))
            er, ei = even[k]
            out[k] = (er + tr, ei + ti)
            out[m - k] = (er - tr, ti - ei)
    return out


def real_backward(spec):
    n = 2 * (len(spec) - 1)
    if n == 2:
        return [spec[0][0] + spec[1][0], spec[0][0] - spec[1][0]]
    m = n // 2
    even, odd = [], []
    for k in range(m // 2 + 1):
        if k == 0:
            even.append((spec[0][0] + spec[m][0], None))
            odd.append((spec[0][0] - spec[m][0], None))
        elif 2 * k == m:
            even.append((2.0 * spec[k][0], None))
            odd.append((-2.0 * spec[k][1], None))
        else:
            ar, ai = spec[k]
            br, bi = spec[m - k]
            even.append((ar + br, ai - bi))
            odd.append(c_mul((ar - br, ai + bi), complex(math.cos(2 * math.pi * k / n), math.sin(2 * math.pi * k / n))))
    xe, xo = real_backward(even), real_backward(odd)
    out = [None] * n
    out[0::2] = xe
    out[1::2] = xo
    return out


def packed_fft(xs, sign, flip):
    n = len(xs)
    if n == 1:
        return xs
    even, odd = packed_fft(xs[0::2], sign, flip), packed_fft(xs[1::2], sign, flip)
    out = [None] * n
    for k in range(n // 2):
        t = odd[k]
        if k:
            turned = pltpu.roll(t, HALF, 1) * flip
            c, s = math.cos(2 * math.pi * k / n), sign * math.sin(2 * math.pi * k / n)
            t = (-s) * turned if 4 * k == n else c * t - s * turned
        out[k] = even[k] + t
        out[k + n // 2] = even[k] - t
    return out


def flip_lanes(rows):
    lane = lax.broadcasted_iota(jnp.int32, (rows, INNER), 1)
    return jnp.where(lane < HALF, 1.0, -1.0).astype(F32)


def put_message(ref, d, value, fine):
    lane = lax.broadcasted_iota(jnp.int32, (INNER, INNER), 1)
    high = value.astype(BF16)
    ref[d, 0:INNER, :] = high
    rest = value - high.astype(F32)
    if fine:
        third = rest - rest.astype(BF16).astype(F32)
        rest = jnp.where((lane & (HALF - 1)) == 7, pltpu.roll(third, 7, 1), rest)
    rest = jnp.where(lane < 8, rest, pltpu.roll(rest, 72, 1))
    rest = jnp.where(lane < 16, rest, 0.0)
    total = rest[0:16]
    for g in range(1, 8):
        total = total + pltpu.roll(rest[16 * g : 16 * g + 16], 16 * g, 1)
    ref[d, INNER : INNER + TAIL, :] = total.astype(BF16)


def get_message(ref, d, fine):
    lane = lax.broadcasted_iota(jnp.int32, (INNER, INNER), 1)
    packed = ref[d, INNER : INNER + TAIL, :].astype(F32)
    rest = jnp.concatenate([packed] + [pltpu.roll(packed, INNER - 16 * g, 1) for g in range(1, 8)], axis=0)
    rest = jnp.where(lane < 8, rest, pltpu.roll(rest, 56, 1))
    column = lane & (HALF - 1)
    if fine:
        third = jnp.where(column == 0, pltpu.roll(rest, INNER - 7, 1), 0.0)
        rest = jnp.where(column < 7, rest, 0.0) + third
    else:
        rest = jnp.where(column < 8, rest, 0.0)
    return ref[d, 0:INNER, :].astype(F32) + rest


def row_forward_kernel(tiled, fine, x_ref, tw_ref, f_ref, a_ref, m_ref, out_ref, y_scr, e_scr):
    def slab(g, carry):
        if tiled:
            xs = [x_ref[pl.ds(pl.multiple_of(g * 256 + a * 8, 8), 8), :] for a in range(OUTER)]
        else:
            xs = [x_ref[pl.ds(pl.multiple_of(g * 8, 8), 8), a * INNER : (a + 1) * INNER] for a in range(OUTER)]
        ys = real_forward(xs)
        rows = pl.ds(pl.multiple_of(g * 8, 8), 8)
        e_scr[0, rows, :] = ys[0][0]
        e_scr[1, rows, :] = ys[16][0]
        for k in range(1, 16):
            c = tw_ref[0, k : k + 1, :]
            s = tw_ref[1, k : k + 1, :]
            re, im = ys[k]
            base = pl.ds(pl.multiple_of((k - 1) * INNER + g * 8, 8), 8)
            y_scr[base, 0:INNER] = re * c + im * s
            y_scr[base, INNER : 2 * INNER] = im * c - re * s
        return carry

    lax.fori_loop(0, 16, slab, 0, unroll=2)
    put_message(out_ref, 0, data_by_table(e_scr[0], every(a_ref)), fine)
    put_message(out_ref, 1, data_by_table(e_scr[1], every(m_ref)), fine)

    def group(q, carry):
        v = data_by_table(y_scr[pl.ds(pl.multiple_of(q * 384, 8), 384), :], every(f_ref))
        for i in range(3):
            rows = v[i * INNER : (i + 1) * INNER]
            put_message(out_ref, 2 + 2 * (3 * q + i), rows[:, 0:INNER], fine)
            put_message(out_ref, 3 + 2 * (3 * q + i), rows[:, INNER : 2 * INNER], fine)
        return carry

    lax.fori_loop(0, 5, group, 0)


def row_backward_kernel(final, *refs):
    if final:
        in_ref, base_ref, tw_ref, f_ref, a_ref, m_ref, out_ref, z_scr, e_scr = refs
    else:
        in_ref, tw_ref, f_ref, a_ref, m_ref, out_ref, z_scr, e_scr = refs
    e_scr[0] = data_by_table(get_message(in_ref, 0, False), every(a_ref))
    e_scr[1] = data_by_table(get_message(in_ref, 1, False), every(m_ref))

    def group(q, carry):
        parts = []
        for i in range(3):
            k = 3 * q + i
            parts.append(jnp.concatenate([get_message(in_ref, 2 + 2 * k + h, False) for h in range(2)], axis=1))
        v = jnp.concatenate(parts, axis=0)
        z_scr[pl.ds(pl.multiple_of(q * 384, 8), 384), :] = data_by_table(v, every(f_ref))
        return carry

    lax.fori_loop(0, 5, group, 0)

    def slab(g, carry):
        rows = pl.ds(pl.multiple_of(g * 8, 8), 8)
        spec = [(e_scr[0, rows, :], None)]
        for k in range(1, 16):
            c = tw_ref[0, k : k + 1, :]
            s = tw_ref[1, k : k + 1, :]
            base = pl.ds(pl.multiple_of((k - 1) * INNER + g * 8, 8), 8)
            re = z_scr[base, 0:INNER]
            im = z_scr[base, INNER : 2 * INNER]
            spec.append((re * c - im * s, im * c + re * s))
        spec.append((e_scr[1, rows, :], None))
        xs = real_backward(spec)
        for a in range(OUTER):
            if final:
                cols = slice(a * INNER, (a + 1) * INNER)
                out_ref[rows, cols] = base_ref[rows, cols] + xs[a]
            else:
                out_ref[pl.ds(pl.multiple_of(g * 256 + a * 8, 8), 8), :] = xs[a]
        return carry

    lax.fori_loop(0, 16, slab, 0, unroll=2)


def take_all(exchange, scr, fine):
    def unpack(pair):
        values = [get_message(exchange.out_ref, source, fine) for source in pair]
        for source, value in zip(pair, values):
            scr[source] = value

    def step(h, carry):
        steps = (2 * h, 2 * h + 1)
        for i in steps:
            exchange.wait_source(i)
        unpack([exchange.source(i) for i in steps])
        return carry

    lax.fori_loop(0, PEERS // 2 - 1, step, 0)
    exchange.own.wait()
    exchange.wait_source(PEERS - 2)
    unpack([exchange.source(PEERS - 2), exchange.me])
    exchange.wait_sends()


def give_all(scr, exchange):
    def pack(pair):
        for peer in pair:
            put_message(exchange.in_ref, peer, scr[peer], False)

    def step(h, carry):
        steps = (2 * h, 2 * h + 1)
        pack([exchange.peer(i) for i in steps])
        for i in steps:
            exchange.send(i)
        return carry

    lax.fori_loop(0, PEERS // 2 - 1, step, 0)
    pack([exchange.peer(PEERS - 2), exchange.me])
    exchange.send(PEERS - 2)
    exchange.own.start()


def column_first_step(in_ref, y_scr, sign):
    flip = flip_lanes(8)

    def slab(g, carry):
        rows = pl.ds(pl.multiple_of(g * 8, 8), 8)
        ys = packed_fft([in_ref[s, rows, :] for s in range(OUTER)], sign, flip)
        for k in range(OUTER):
            y_scr[k, rows, :] = ys[k]
        return carry

    lax.fori_loop(0, 16, slab, 0, unroll=2)


def apply_packed(e_ref, k1, value, flip):
    r = table_by_data([e_ref[i, k1] for i in range(e_ref.shape[0])], value)
    return r[0:INNER] - pltpu.roll(r[INNER : 2 * INNER], HALF, 1) * flip


MESH = pl.DeviceIdType.MESH


def greet_peers(me, barrier, extra=()):
    def greet(i, carry):
        pl.semaphore_signal(barrier, inc=1, device_id={"strip": lax.rem(me + i, PEERS)}, device_id_type=MESH)
        return carry

    lax.fori_loop(1, PEERS, greet, 0)
    for device in extra:
        pl.semaphore_signal(barrier, inc=1, device_id=device, device_id_type=MESH)
    pl.semaphore_wait(barrier, PEERS - 1 + len(extra))


STRIDE = 11
REPLY = 45


class Exchange:
    def __init__(self, me, in_ref, out_ref, send_sem, recv_sem, own_sem, flat=0):
        self.me, self.in_ref, self.out_ref, self.flat = me, in_ref, out_ref, flat
        self.send_sem, self.recv_sem = send_sem, recv_sem
        self.own = pltpu.make_async_copy(self.part(in_ref, me), self.part(out_ref, me), own_sem)

    def part(self, ref, i):
        return ref.at[pl.ds(pl.multiple_of(i * self.flat, self.flat), self.flat)] if self.flat else ref.at[i]

    def copy(self, peer, send, source):
        return pltpu.make_async_remote_copy(
            src_ref=self.part(self.in_ref, peer),
            dst_ref=self.part(self.out_ref, source),
            send_sem=self.send_sem.at[send],
            recv_sem=self.recv_sem.at[source],
            device_id={"strip": peer},
            device_id_type=MESH,
        )

    def peer(self, i):
        return lax.rem(self.me + 1 + lax.rem(i * STRIDE, PEERS - 1), PEERS)

    def source(self, i):
        return lax.rem(self.me + PEERS - 1 - lax.rem(i * STRIDE, PEERS - 1), PEERS)

    def reply(self, i):
        return lax.rem(REPLY - i, PEERS - 1)

    def send(self, i):
        self.copy(self.peer(i), i, self.me).start()

    def wait_source(self, i):
        self.copy(self.peer(i), i, self.source(i)).wait_recv()

    def wait_sends(self):
        def step(i, carry):
            self.copy(self.peer(i), i, self.me).wait_send()
            return carry

        lax.fori_loop(0, PEERS - 1, step, 0)

    def start(self, first=0, last=PEERS - 1):
        def step(i, carry):
            self.copy(self.peer(i), i, self.me).start()
            return carry

        lax.fori_loop(first, last, step, 0)
        if first == 0:
            self.own.start()

    def wait(self):
        def step(i, carry):
            self.wait_source(i)
            return carry

        self.own.wait()
        lax.fori_loop(0, PEERS - 1, step, 0)
        self.wait_sends()


class Moves:
    def __init__(self, pairs, sems):
        self.copies = [pltpu.make_async_copy(src, dst, sems.at[i]) for i, (src, dst) in enumerate(pairs)]

    def start(self):
        for copy in self.copies:
            copy.start()

    def wait(self):
        for copy in self.copies:
            copy.wait()


def exchange_sems():
    return [pltpu.SemaphoreType.DMA((PEERS,)), pltpu.SemaphoreType.DMA((PEERS,)), pltpu.SemaphoreType.DMA]


def edge_lanes():
    lane = lax.broadcasted_iota(jnp.int32, (INNER, INNER), 1)
    return jnp.logical_or(lane == 0, lane == HALF), lane < HALF


def edge_gather(ref):
    mask, _ = edge_lanes()

    def step(k1, acc):
        return acc + pltpu.roll(jnp.where(mask, ref[k1], 0.0), k1, 1)

    return lax.fori_loop(0, OUTER, step, jnp.zeros((INNER, INNER), F32), unroll=4)


def edge_split(spec, amp):
    i = lax.broadcasted_iota(jnp.int32, (INNER, INNER), 0)
    j = lax.broadcasted_iota(jnp.int32, (INNER, INNER), 1)
    one = jnp.ones((INNER, INNER), F32)
    none = jnp.zeros((INNER, INNER), F32)
    rows = jnp.where(i + j == INNER - 1, one, none).astype(BF16)
    rows0 = jnp.where(((i + j) & (INNER - 1)) == 0, one, none).astype(BF16)
    sign = jnp.where(j < HALF, one, -one)
    col = j & (HALF - 1)
    same = (i < HALF) == (j < HALF)
    lanes = jnp.where(
        jnp.logical_and(same, jnp.logical_and(col > 0, col + (i & (HALF - 1)) == OUTER)), sign, none
    ).astype(BF16)
    lanes0 = jnp.where(jnp.logical_and(i == j, col == 0), sign, none).astype(BF16)

    def move(left, value, right):
        value = sum(mm(left, p) for p in reversed(split_into(value, 3)))
        return sum(mm(p, right) for p in reversed(split_into(value, 3)))

    rev = move(rows, spec, lanes) + move(rows0, spec, lanes0)
    swapped = pltpu.roll(amp, HALF, 1)
    _, left = edge_lanes()
    a0 = jnp.where(left, amp, swapped)
    a2 = jnp.where(left, swapped, amp)
    return 0.5 * (spec + rev), 0.5 * (spec - rev), a0, a2


def turn(c, s, value, flip):
    return c * value + s * (pltpu.roll(value, HALF, 1) * flip)


EARLY = 4
MIDDLE = 18


def first_kernel(
    scale, rate, wind, prior, x_ref, tw, f_ref, a_ref, m_ref, fi_ref, ai_ref, mi_ref, slot_ref, prec_ref,
    ef_any, ei_any, sent_ref, ids_ref,
    resid_ref, par, own_any, here_any, amp_any, here_ids_ref, prev_ref, next_ref, *scratch,
):
    y_scr, z_scr, msg_scr, land_scr, back_scr, tab_ref, row_scr, row_edge = scratch[0:8]
    up_ref, down_ref, tiles_scr, g_scr, phase_scr, landed, p_scr, table_scr, res_scr = scratch[8:17]
    sid_scr, sid_sem, side_sems = scratch[17:20]
    ef, ei, own_ref, amp_ref, here_ref, in_sems, out_sems, here_sems = scratch[20:28]
    fix_scr = scratch[28]
    sems = scratch[29:]
    tables = Moves([(ef_any, ef), (ei_any, ei)], in_sems)
    tables.start()
    results = Moves([(own_ref, own_any), (amp_ref, amp_any)], out_sems)
    weights_out = Moves([(here_ref, here_any)], here_sems)
    me = lax.axis_index("strip")
    slot_at = lax.axis_index("tm")
    above, below = lax.rem(slot_at + 1, 4), lax.rem(slot_at + 3, 4)
    greet_peers(me, pltpu.get_barrier_semaphore(), ({"tm": above}, {"tm": below}))
    ids = Exchange(me, ids_ref, here_ids_ref, *sems[0:3], flat=ID_STRIDE)
    weights = Exchange(me, sent_ref, here_ref, *sems[3:6])
    pencils = Exchange(me, msg_scr, land_scr, *sems[6:9])
    back = Exchange(me, msg_scr, back_scr, *sems[9:12])
    phases = Exchange(me, phase_scr, landed, *sems[12:15])
    residuals = Exchange(me, res_scr, resid_ref, *sems[15:18])
    ids.start()
    weights.start(0, EARLY)
    row_forward_kernel(False, True, x_ref, tw, f_ref, a_ref, m_ref, msg_scr, row_scr, row_edge)
    pencils.start()
    tables_kernel(scale, rate, wind, prior, tab_ref, amp_ref, par)
    take_all(pencils, z_scr, True)
    weights.start(EARLY, MIDDLE)
    tables.wait()
    column_first_step(z_scr, y_scr, -1.0)
    flip = flip_lanes(INNER)

    def step(k1, carry):
        value = apply_packed(ef, k1, y_scr[k1], flip)
        amp = amp_ref[k1]
        once = value * amp
        twice = once * amp
        y_scr[k1] = value
        z_scr[k1] = par[0] * once
        own_ref[k1] = par[3] * twice
        for n, ref, gain in ((0, up_ref, par[1]), (1, down_ref, par[2])):
            cb = tab_ref[2 * n]
            sb = tab_ref[2 * n + 1]
            ca = tab_ref[8, pl.ds(64 * n + k1, 1), :] * gain
            sa = tab_ref[8, pl.ds(64 * n + 32 + k1, 1), :] * gain
            ref[k1] = turn(cb * ca - sb * sa, sb * ca + cb * sa, twice, flip).astype(BF16)
        return carry

    lax.fori_loop(0, OUTER, step, 0, unroll=8)

    @pl.when(me == 0)
    def _():
        u0, u2, a0, a2 = edge_split(edge_gather(y_scr), edge_gather(amp_ref))
        mask, _ = edge_lanes()
        e0 = a0 * u0
        e2 = a2 * u2
        change = par[0] * (e0 + e2)
        e0 = a0 * e0
        e2 = a2 * e2
        fix_scr[0] = par[3] * (e0 + e2)
        fix_scr[1] = par[1] * turn(tab_ref[4], tab_ref[5], e0 + par[4] * e2, flip)
        fix_scr[2] = par[2] * turn(tab_ref[6], tab_ref[7], e0 + par[5] * e2, flip)

        def put(k1, carry):
            back = lax.rem(INNER - k1, INNER)
            z_scr[k1] = jnp.where(mask, pltpu.roll(change, back, 1), z_scr[k1])
            return carry

        lax.fori_loop(0, OUTER, put, 0, unroll=4)

    def inverse(k1, carry):
        z_scr[k1] = apply_packed(ei, k1, z_scr[k1], flip)
        return carry

    lax.fori_loop(0, OUTER, inverse, 0, unroll=8)
    column_first_step(z_scr, y_scr, 1.0)
    give_all(y_scr, back)

    @pl.when(me == 0)
    def _():
        mask, _ = edge_lanes()

        def put(k1, carry):
            place_at = lax.rem(INNER - k1, INNER)
            for n, ref in enumerate((own_ref, up_ref, down_ref)):
                value = jnp.where(mask, pltpu.roll(fix_scr[n], place_at, 1), ref[k1].astype(F32))
                ref[k1] = value.astype(ref.dtype)
            return carry

        lax.fori_loop(0, OUTER, put, 0, unroll=2)

    results.start()
    ids.wait()
    fetch = pltpu.make_async_copy(here_ids_ref, sid_scr, sid_sem)
    fetch.start()
    back.wait()
    weights.start(MIDDLE, PEERS - 1)
    row_backward_kernel(False, back_scr, tw, fi_ref, ai_ref, mi_ref, tiles_scr, row_scr, row_edge)
    fetch.wait()
    ones = jnp.ones((2 * INNER, INNER), BF16)
    row = lax.broadcasted_iota(jnp.int32, (INNER, INNER), 0)
    lane = lax.broadcasted_iota(jnp.int32, (INNER, INNER), 1)
    place = lax.broadcasted_iota(jnp.int32, (1, INNER), 1)

    def pick(s, place_at):
        def some(q, carry):
            first = s * ID_STRIDE + q * 32
            picks = [sid_scr[first + j] for j in range(32)]
            rows = [tiles_scr[pl.ds(picks[j], 1), :] for j in range(32)]
            for j in range(32):
                g_scr[pl.ds(place_at + q * 32 + j, 1), :] = rows[j]
            return carry

        lax.fori_loop(0, SLOTS // 32, some, 0)

    def gather_pair(pair):
        for n, s in enumerate(pair):
            pick(s, n * SLOTS)
        for n, s in enumerate(pair):
            count = sid_scr[s * ID_STRIDE + SLOTS]
            picked = g_scr[n * SLOTS : (n + 1) * SLOTS, :]
            sums = mm(jnp.concatenate(split(picked * here_ref[s].astype(F32)), axis=1), ones)
            for q in range(4):
                got = jnp.where(row == lane, sums[q * INNER : (q + 1) * INNER], 0.0)
                got = jnp.sum(got, axis=0, keepdims=True)
                phase_scr[s, q : q + 1, :] = jnp.where(place + q * INNER < count, got, 0.0)

    def gather_next(h, carry):
        steps = (2 * h, 2 * h + 1)
        for i in steps:
            weights.wait_source(i)
        gather_pair([weights.source(i) for i in steps])
        for i in steps:
            phases.copy(weights.source(i), phases.reply(i), me).start()
        return carry

    lax.fori_loop(0, PEERS // 2 - 1, gather_next, 0)
    weights.own.wait()
    weights.wait_source(PEERS - 2)
    last = weights.source(PEERS - 2)
    gather_pair([last, me])
    phases.copy(last, phases.reply(PEERS - 2), me).start()
    phases.own.start()
    weights.wait_sends()
    weights_out.start()

    @pl.when(slot_at < 3)
    def _():
        for side in sides(side_sems, up_ref, prev_ref, above, 0):
            side.start()

    @pl.when(slot_at > 0)
    def _():
        for side in sides(side_sems, down_ref, next_ref, below, 1):
            side.start()

    phases.wait()
    for s in range(PEERS):
        table_scr[4 * s : 4 * s + 4, :] = landed[s]
    acc = weigh(slot_ref, prec_ref, table_scr[...], p_scr)
    for s in range(PEERS):
        res_scr[s] = acc[4 * s : 4 * s + 4]
    residuals.start()
    results.wait()
    weights_out.wait()
    residuals.wait()

    @pl.when(slot_at < 3)
    def _():
        for side in sides(side_sems, up_ref, prev_ref, above, 0):
            side.wait_send()
        for side in sides(side_sems, down_ref, next_ref, below, 1):
            side.wait_recv()

    @pl.when(slot_at > 0)
    def _():
        for side in sides(side_sems, up_ref, prev_ref, above, 0):
            side.wait_recv()
        for side in sides(side_sems, down_ref, next_ref, below, 1):
            side.wait_send()


SIDE_PARTS = 4


def sides(sems, src, dst, device, n):
    copies = []
    for p in range(SIDE_PARTS):
        rows = pl.ds(p * (OUTER // SIDE_PARTS), OUTER // SIDE_PARTS)
        copies.append(
            pltpu.make_async_remote_copy(
                src_ref=src.at[rows],
                dst_ref=dst.at[rows],
                send_sem=sems.at[0, n, p],
                recv_sem=sems.at[1, n, p],
                device_id={"tm": device},
                device_id_type=MESH,
            )
        )
    return copies


def column_second_kernel(par, in_ref, amp_any, own_any, prev_any, next_any, ef_any, ei_any, back_ref, *scratch):
    y_scr, z_scr, msg_scr, out_scr = scratch[0:4]
    amp_ref, own_ref, prev_ref, next_ref, ef, ei, in_sems = scratch[10:17]
    inputs = Moves(
        [(amp_any, amp_ref), (own_any, own_ref), (prev_any, prev_ref), (next_any, next_ref), (ef_any, ef), (ei_any, ei)],
        in_sems,
    )
    inputs.start()
    me = lax.axis_index("strip")
    slot_at = lax.axis_index("tm")
    greet_peers(me, pltpu.get_barrier_semaphore())
    pencils = Exchange(me, in_ref, msg_scr, *scratch[4:7])
    pencils.start()
    take_all(pencils, z_scr, False)
    inputs.wait()
    column_first_step(z_scr, y_scr, -1.0)
    flip = flip_lanes(INNER)

    def step(k1, carry):
        value = apply_packed(ef, k1, y_scr[k1], flip)
        y_scr[k1] = value
        z_scr[k1] = par[0] * (value * amp_ref[k1]) + own_ref[k1]
        return carry

    lax.fori_loop(0, OUTER, step, 0, unroll=8)

    @pl.when(me == 0)
    def _():
        spec = edge_gather(y_scr)
        amp = edge_gather(amp_ref)
        u0, u2, a0, a2 = edge_split(spec, amp)
        mask, _ = edge_lanes()
        change = par[0] * (a0 * u0 + a2 * u2 - amp * spec)

        def put(k1, carry):
            back = lax.rem(INNER - k1, INNER)
            z_scr[k1] = z_scr[k1] + jnp.where(mask, pltpu.roll(change, back, 1), 0.0)
            return carry

        lax.fori_loop(0, OUTER, put, 0, unroll=4)

    def inverse(k1, carry):
        moved = jnp.where(slot_at > 0, prev_ref[k1].astype(F32), 0.0)
        moved = moved + jnp.where(slot_at < 3, next_ref[k1].astype(F32), 0.0)
        z_scr[k1] = apply_packed(ei, k1, z_scr[k1] - par[0] * moved, flip)
        return carry

    lax.fori_loop(0, OUTER, inverse, 0, unroll=8)
    column_first_step(z_scr, y_scr, 1.0)
    back = Exchange(me, out_scr, back_ref, *scratch[7:10])
    give_all(y_scr, back)
    back.wait()


def route_kernel(t_ref, id_ref, slot_ref, tail_ref):
    row = lax.broadcasted_iota(jnp.int32, (INNER, 2 * INNER), 0)
    col = lax.broadcasted_iota(jnp.int32, (INNER, 2 * INNER), 1)
    tri = jnp.where(jnp.logical_or(row < col, col >= INNER), 1.0, 0.0).astype(BF16)
    peer = lax.broadcasted_iota(jnp.int32, (PEERS, INNER), 0)
    base = jnp.zeros((PEERS, INNER), F32)
    for i in range(0, POINT_ROWS, 8):
        hots = [jnp.where(peer == t_ref[i + j : i + j + 1, :], 1.0, 0.0) for j in range(8)]
        cum = mm(jnp.concatenate(hots, axis=0).astype(BF16), tri)
        for j in range(8):
            part = cum[j * PEERS : (j + 1) * PEERS]
            pos = jnp.sum(hots[j] * (part[:, 0:INNER] + base), axis=0, keepdims=True)
            base = base + part[:, INNER : 2 * INNER]
            slot_ref[i + j : i + j + 1, :] = t_ref[i + j : i + j + 1, :] * SLOTS + pos.astype(jnp.int32)
    batch = 4
    index = lax.broadcasted_iota(jnp.int32, (INNER, batch * INNER), 0)

    def wide(ref, i):
        return jnp.concatenate([ref[pl.ds(i * batch + j, 1), :] for j in range(batch)], axis=1)

    def put(i, acc):
        slot = wide(slot_ref, i)
        ids = wide(id_ref, i)
        r = lax.shift_right_logical(ids, 5)
        ids = lax.shift_right_logical(r, 3) * 256 + (ids & 31) * 8 + (r & 7)
        hot = jnp.where(index == (slot & 127), 1.0, 0.0).astype(BF16)
        line = index == lax.shift_right_logical(slot, 7)
        v = [
            jnp.where(line, d.astype(F32), 0.0).astype(BF16) for d in (lax.shift_right_logical(ids, 6), ids & 63)
        ]
        return acc + mm_nt(jnp.concatenate(v, axis=0), hot)

    acc = lax.fori_loop(0, POINT_ROWS // batch, put, jnp.zeros((2 * INNER, INNER), F32), unroll=2)
    ids = (acc[0:INNER] * 64.0 + acc[INNER : 2 * INNER]).astype(jnp.int32)
    count = base.astype(jnp.int32)
    tail_ref[...] = jnp.zeros_like(tail_ref)
    for s in range(PEERS):
        tail_ref[s, 0:4, :] = ids[4 * s : 4 * s + 4]
        tail_ref[s, 4:5, :] = count[s : s + 1]


def pack_kernel(slot_ref, w_ref, out_ref, w_scr, buf):
    def widen(i, carry):
        rows = pl.ds(pl.multiple_of(i * 64, 64), 64)
        w_scr[rows, :] = w_ref[rows, :].astype(F32)
        return carry

    lax.fori_loop(0, POINT_ROWS * INNER // 64, widen, 0, unroll=2)

    def some(q, carry):
        antenna, direction = (q // 8) * 4, (q % 8) * 8
        first = direction * INNER + antenna
        line = pl.multiple_of(antenna * HALF + direction, 8)
        pairs = [(a, d) for a in range(4) for d in range(8)]
        slots = [slot_ref[first + d * INNER + a] for a, d in pairs]
        rows = [w_scr[pl.ds(line + a * HALF + d, 1), :] for a, d in pairs]
        for j in range(32):
            buf[pl.ds(slots[j], 1), :] = rows[j]
        return carry

    lax.fori_loop(0, POINT_ROWS * INNER // 32, some, 0)

    def narrow(i, carry):
        rows = pl.ds(pl.multiple_of(i * INNER, INNER), INNER)
        out_ref[rows, :] = buf[rows, :].astype(BF16)
        return carry

    lax.fori_loop(0, PEERS * SLOTS // INNER, narrow, 0, unroll=2)


def weigh(slot_ref, prec_ref, phase, p_scr):
    high, low = split(phase)
    table = jnp.concatenate([high, low], axis=0)
    batch = 4
    index = lax.broadcasted_iota(jnp.int32, (INNER, batch * INNER), 0)

    def wide(ref, i):
        return jnp.concatenate([ref[pl.ds(i * batch + j, 1), :] for j in range(batch)], axis=1)

    def pick(i, carry):
        slot = wide(slot_ref, i)
        hot = jnp.where(index == (slot & 127), 1.0, 0.0).astype(BF16)
        v = mm(table, hot)
        v = v[0:INNER] + v[INNER : 2 * INNER]
        got = jnp.sum(jnp.where(index == lax.shift_right_logical(slot, 7), v, 0.0), axis=0, keepdims=True)
        for j in range(batch):
            p_scr[pl.ds(i * batch + j, 1), :] = got[:, j * INNER : (j + 1) * INNER]
        return carry

    lax.fori_loop(0, POINT_ROWS // batch, pick, 0, unroll=4)
    prec = prec_ref[...]
    phase = p_scr[...]

    centre = jnp.sum(prec * phase, axis=0, keepdims=True) / jnp.sum(prec, axis=0, keepdims=True)
    p_scr[...] = prec * (phase - centre)

    def put(i, acc):
        slot = wide(slot_ref, i)
        hot = jnp.where(index == (slot & 127), 1.0, 0.0).astype(BF16)
        v = jnp.where(index == lax.shift_right_logical(slot, 7), wide(p_scr, i), 0.0)
        vh, vl = split(v)
        return acc + mm_nt(jnp.concatenate([vh, vl], axis=0), hot)

    acc = lax.fori_loop(0, POINT_ROWS // batch, put, jnp.zeros((2 * INNER, INNER), F32), unroll=4)
    return acc[0:INNER] + acc[INNER : 2 * INNER]


COPIES = 8


def scatter_kernel(
    sid_ref, r_ref, w_any, tw, f_ref, a_ref, m_ref, out_ref, rt_scr, u_scr, y_scr, e_scr, w_ref, w_sems, *accs
):
    fetch = Moves([(w_any, w_ref)], w_sems)
    fetch.start()
    def clear(i, carry):
        rows = pl.ds(pl.multiple_of(i * 64, 64), 64)
        for acc in accs:
            acc[rows, :] = jnp.zeros((64, INNER), F32)
        return carry

    lax.fori_loop(0, SIDE // 64, clear, 0)
    rt_scr[...] = r_ref[...].T
    fetch.wait()
    lane = lax.broadcasted_iota(jnp.int32, (INNER, INNER), 1)
    row = lax.broadcasted_iota(jnp.int32, (INNER, INNER), 0)

    def scaled(s, carry):
        for q in range(4):
            col = jnp.sum(jnp.where(lane == s * 4 + q, rt_scr[...], 0.0), axis=1, keepdims=True)
            rows = pl.ds(pl.multiple_of(s * SLOTS + q * INNER, INNER), INNER)
            used = row + q * INNER < sid_ref[s * ID_STRIDE + SLOTS]
            u_scr[rows, :] = jnp.where(used, w_ref[rows, :].astype(F32) * col, 0.0)
        return carry

    lax.fori_loop(0, PEERS, scaled, 0, unroll=4)

    def source(s, carry):
        def some(q, inner):
            first = s * SLOTS + q * 32
            line = s * ID_STRIDE + q * 32
            ids = [sid_ref[line + j] for j in range(32)]
            us = [u_scr[pl.ds(first + j, 1), :] for j in range(32)]
            for h in range(0, 32, COPIES):
                sums = [accs[j][pl.ds(ids[h + j], 1), :] + us[h + j] for j in range(COPIES)]
                for j in range(COPIES):
                    accs[j][pl.ds(ids[h + j], 1), :] = sums[j]
            return inner

        return lax.fori_loop(0, lax.shift_right_logical(sid_ref[s * ID_STRIDE + SLOTS] + 31, 5), some, carry)

    lax.fori_loop(0, PEERS, source, 0)

    def add(i, carry):
        rows = pl.ds(pl.multiple_of(i * 64, 64), 64)
        total = accs[0][rows, :]
        for acc in accs[1:]:
            total = total + acc[rows, :]
        accs[0][rows, :] = total
        return carry

    lax.fori_loop(0, SIDE // 64, add, 0)
    row_forward_kernel(True, False, accs[0], tw, f_ref, a_ref, m_ref, out_ref, y_scr, e_scr)


def call(kernel, name, out_shapes, args, smem=0, scratch=(), any_args=(), any_outs=(), smem_outs=(), collective_id=None):
    spaces = [pltpu.SMEM if i < smem else pl.ANY if i in any_args else pltpu.VMEM for i in range(len(args))]
    outs = [pl.ANY if i in any_outs else pltpu.SMEM if i in smem_outs else pltpu.VMEM for i in range(len(out_shapes))]
    remote = dict(collective_id=collective_id, has_side_effects=True) if collective_id is not None else {}
    return pl.pallas_call(
        kernel,
        out_shape=out_shapes,
        in_specs=[pl.BlockSpec(memory_space=space) for space in spaces],
        out_specs=[pl.BlockSpec(memory_space=space) for space in outs],
        scratch_shapes=list(scratch),
        compiler_params=pltpu.CompilerParams(vmem_limit_bytes=VMEM_BYTES, **remote),
        cost_estimate=pl.CostEstimate(flops=1024, bytes_accessed=1024, transcendentals=0),
        name=name,
    )(*args)


def shape(dims, dtype=F32):
    return jax.ShapeDtypeStruct(dims, dtype)


PENCILS = (PEERS, INNER, INNER)
MESSAGES = (PEERS, INNER + TAIL, INNER)


def row_backward(pencils, base, tables):
    final = base is not None
    args = [pencils] + ([base] if final else []) + tables
    return call(
        lambda *refs: row_backward_kernel(final, *refs),
        "row_backward",
        [shape((INNER, SIDE) if final else (SIDE, INNER))],
        args,
        scratch=[pltpu.VMEM((15 * INNER, 2 * INNER), F32), pltpu.VMEM((2, INNER, INNER), F32)],
    )[0]


def tables_kernel(scale, rate, wind, prior, tab_ref, amp_ref, par_ref):
    strip = lax.axis_index("strip")
    live = (lax.axis_index("tm") < 3).astype(F32)
    k1 = (strip // 2).astype(F32)
    even = strip % 2 == 0
    row = lax.broadcasted_iota(jnp.int32, (INNER, INNER), 0)
    lane = lax.broadcasted_iota(jnp.int32, (INNER, INNER), 1)
    line = row.astype(F32)
    j = (lane & (HALF - 1)).astype(F32)
    cols = jnp.where(even, k1 + OUTER * j, k1 + OUTER * (INNER - 1.0 - j))
    cols = jnp.where(strip == 1, 16.0 + OUTER * j, cols)
    winds = ((wind[0, 0].astype(F32), wind[0, 1].astype(F32)), (prior[1], prior[2]))

    def cosine(turns):
        turns = turns - SIDE * jnp.floor(turns * (1.0 / SIDE))
        return jnp.cos(turns * (2.0 * math.pi / SIDE))

    small = jnp.zeros((INNER, INNER), F32)
    for kind in range(4):
        wind_row, wind_col = winds[kind // 2]
        quarter = (0.0, 3.0 * SIDE / 4, 0.0, SIDE / 4.0)[kind]
        base = OUTER * line * wind_row + quarter
        tab_ref[kind] = cosine(base + cols * wind_col)
        tab_ref[4 + kind] = cosine(base + j * wind_row)
        turns = (row & (OUTER - 1)).astype(F32) * wind_row + quarter
        small = jnp.where(lax.shift_right_logical(row, 5) == kind, turns, small)
    tab_ref[8] = cosine(small)

    fold = jnp.where(even, k1 + OUTER * j, OUTER - k1 + OUTER * j)
    fold = jnp.where(strip == 1, 16.0 + OUTER * j, fold)
    fold = jnp.where(jnp.logical_and(strip == 0, lane == HALF), SIDE / 2.0, fold)
    fold = fold * fold

    def step(k, carry):
        kr = line * OUTER + k.astype(F32)
        kr = jnp.minimum(kr, SIDE - kr)
        radius = (kr * kr + fold) / (KZERO * KZERO)
        amp_ref[k] = SIDE / (2.0 * KZERO) * jnp.exp((-11.0 / 12.0) * jnp.log(1.0 + radius))
        return carry

    lax.fori_loop(0, OUTER, step, 0, unroll=2)
    norm = scale[0] / (SIDE * SIDE)
    mine = rate[0] * live
    par_ref[0] = norm
    par_ref[1] = mine * scale[0]
    par_ref[2] = prior[0] * scale[0]
    par_ref[3] = (mine + prior[0]) * scale[0] * norm
    par_ref[4] = 1.0 - 2.0 * (wind[0, 1] & 1).astype(F32)
    par_ref[5] = 1.0 - 2.0 * (prior[2].astype(jnp.int32) & 1).astype(F32)
    par_ref[6] = 0.0
    par_ref[7] = 0.0


def const(*tables):
    return [jnp.asarray(t) for t in tables]


def local(
    screen_vec,
    prior_scale,
    flow_weight,
    wind,
    pierce_point_strip,
    pierce_block,
    pierce_weights,
    noise_prec,
):
    fwd, inv, first, first_inv, mid, mid_inv, twiddle = row_tables()
    row_fwd_tables = const(twiddle, pieces(fwd, 2), pieces(first, 2), pieces(mid, 2))
    row_fine_tables = const(twiddle, pieces(fwd, 3), pieces(first, 3), pieces(mid, 3))
    row_inv_tables = const(twiddle, pieces(inv, 2), pieces(first_inv, 2), pieces(mid_inv, 2))
    col_fwd, col_inv = column_tables()
    col_fine_tables = const(pieces(col_fwd, 3), pieces(col_inv, 2))
    col_tables = const(pieces(col_fwd, 2), pieces(col_inv, 2))

    x = screen_vec[0]
    weights = pierce_weights[0].reshape(POINT_ROWS * INNER, INNER)
    target = pierce_point_strip.reshape(INNER, HALF).T
    block = pierce_block.reshape(INNER, HALF).T
    prec = noise_prec.reshape(INNER, HALF).T

    mine = jnp.concatenate([flow_weight, wind[0].astype(F32)])
    prior = lax.ppermute(mine, "tm", [(i, i + 1) for i in range(lax.axis_size("tm") - 1)])
    slots, ids = call(
        route_kernel,
        "route",
        [shape((POINT_ROWS, INNER), jnp.int32), shape((PEERS, ID_ROWS, INNER), jnp.int32)],
        [target, block],
    )
    ids, prior, prec = lax.optimization_barrier((ids, prior, prec))
    sent = call(
        pack_kernel,
        "pack",
        [shape((PEERS * SLOTS, INNER), BF16)],
        [slots.reshape(-1), weights],
        smem=1,
        scratch=[pltpu.VMEM((POINT_ROWS * INNER, INNER), F32), pltpu.VMEM((PEERS * SLOTS, INNER), F32)],
    )[0]

    spectral = [pltpu.VMEM(PENCILS, F32), pltpu.VMEM(PENCILS, F32)]
    rows = [pltpu.VMEM((15 * INNER, 2 * INNER), F32), pltpu.VMEM((2, INNER, INNER), F32)]
    message = shape(MESSAGES, BF16)
    points = pltpu.VMEM((PEERS * SLOTS, INNER), F32)
    screen = pltpu.VMEM((SIDE, INNER), F32)
    small = (PEERS, 4, INNER)
    resid, par, own, arrived, amp, here_ids, from_prev, from_next = call(
        first_kernel,
        "first",
        [
            shape(small),
            shape((8,)),
            shape(PENCILS),
            shape((PEERS, SLOTS, INNER), BF16),
            shape(PENCILS),
            shape((PEERS * ID_STRIDE,), jnp.int32),
            shape(PENCILS, BF16),
            shape(PENCILS, BF16),
        ],
        [prior_scale, flow_weight, wind, prior, x]
        + row_fine_tables
        + row_inv_tables[1:]
        + [slots, prec]
        + col_fine_tables
        + [sent.reshape(PEERS, SLOTS, INNER), ids.reshape(-1)],
        smem=4,
        any_args=(14, 15, 16, 17),
        any_outs=(2, 3, 4, 5, 6, 7),
        smem_outs=(1,),
        collective_id=3,
        scratch=spectral
        + [pltpu.VMEM(MESSAGES, BF16)] * 3
        + [pltpu.VMEM((9, INNER, INNER), F32)]
        + rows
        + [pltpu.VMEM(PENCILS, BF16)] * 2
        + [
            screen,
            pltpu.VMEM((2 * SLOTS, INNER), F32),
            pltpu.VMEM(small, F32),
            pltpu.VMEM(small, F32),
            pltpu.VMEM((POINT_ROWS, INNER), F32),
            pltpu.VMEM((INNER, INNER), F32),
            pltpu.VMEM(small, F32),
            pltpu.SMEM((PEERS * ID_STRIDE,), jnp.int32),
            pltpu.SemaphoreType.DMA,
            pltpu.SemaphoreType.DMA((2, 2, SIDE_PARTS)),
            pltpu.VMEM(col_fine_tables[0].shape, BF16),
            pltpu.VMEM(col_fine_tables[1].shape, BF16),
            pltpu.VMEM(PENCILS, F32),
            pltpu.VMEM(PENCILS, F32),
            pltpu.VMEM((PEERS, SLOTS, INNER), BF16),
            pltpu.SemaphoreType.DMA((2,)),
            pltpu.SemaphoreType.DMA((2,)),
            pltpu.SemaphoreType.DMA((1,)),
            pltpu.VMEM((3, INNER, INNER), F32),
        ]
        + exchange_sems() * 6,
    )
    here = arrived.reshape(PEERS * SLOTS, INNER)

    pencils = call(
        scatter_kernel,
        "scatter",
        [message],
        [here_ids, resid.reshape(INNER, INNER), here] + row_fwd_tables,
        smem=1,
        any_args=(2,),
        scratch=[pltpu.VMEM((INNER, INNER), F32), points]
        + rows
        + [pltpu.VMEM((PEERS * SLOTS, INNER), BF16), pltpu.SemaphoreType.DMA((1,))]
        + [screen] * COPIES,
    )[0]
    out_pencils = call(
        column_second_kernel,
        "column_second",
        [message],
        [par, pencils, amp, own, from_prev, from_next] + col_tables,
        smem=1,
        any_args=range(1, 8),
        any_outs=(0,),
        collective_id=1,
        scratch=spectral
        + [pltpu.VMEM(MESSAGES, BF16)] * 2
        + exchange_sems()
        + exchange_sems()
        + spectral
        + [pltpu.VMEM(PENCILS, BF16)] * 2
        + [pltpu.VMEM(t.shape, BF16) for t in col_tables]
        + [pltpu.SemaphoreType.DMA((6,))],
    )[0]
    return row_backward(out_pencils, x, row_inv_tables)[None]


def solution(mesh):
    in_specs = (
        P("tm", "strip", None),
        P("tm"),
        P("tm"),
        P("tm", None),
        P("tm", "strip", None, None),
        P("tm", "strip", None),
        P("tm", "strip", None, None),
        P("tm", "strip", None),
    )
    out_specs = P("tm", "strip", None)
    return jax.shard_map(local, mesh=mesh, in_specs=in_specs, out_specs=out_specs, check_vma=False)
```

```python
import math

import jax
import jax.numpy as jnp
import ml_dtypes
import numpy as np
from jax import lax
from jax.experimental import pallas as pl
from jax.experimental.pallas import tpu as pltpu
from jax.sharding import PartitionSpec as P

KZERO = 2.0
SIDE = 4096
OUTER = 32
INNER = 128
HALF = 64
PEERS = 32
SLOTS = 512
POINT_ROWS = 64
TAIL = 16
ID_ROWS = 8
ID_STRIDE = ID_ROWS * 128
VMEM_BYTES = 56 * 1024 * 1024
F32 = jnp.float32
BF16 = jnp.bfloat16


def pieces(table, count):
    rest = np.asarray(table, np.float64)
    out = []
    for _ in range(count):
        out.append(rest.astype(np.float32).astype(ml_dtypes.bfloat16))
        rest = rest - out[-1].astype(np.float64)
    return np.stack(out)


def row_tables():
    b = np.arange(INNER)[:, None]
    j = np.arange(HALF)[None, :]
    theta = [2 * np.pi * ((b * j) % INNER) / INNER, 2 * np.pi * ((b * (INNER - 1 - j)) % INNER) / INNER]
    forward = []
    backward = []
    for t in theta:
        forward.append(np.concatenate([np.cos(t), -np.sin(t)], axis=1))
        forward.append(np.concatenate([np.sin(t), np.cos(t)], axis=1))
        backward.append(np.concatenate([np.cos(t).T, np.sin(t).T], axis=1))
        backward.append(np.concatenate([-np.sin(t).T, np.cos(t).T], axis=1))
    fwd = np.concatenate(
        [np.concatenate([forward[0], forward[1]], axis=0), np.concatenate([forward[2], forward[3]], axis=0)], axis=1
    )
    inv = np.concatenate(backward, axis=0)
    sign = np.where(np.arange(INNER) % 2 == 0, 1.0, -1.0)
    t0 = theta[0]
    first = np.concatenate([np.cos(t0), -np.sin(t0)], axis=1)
    first[:, HALF] = sign
    first_inv = np.concatenate([2 * np.cos(t0).T, -2 * np.sin(t0).T], axis=0)
    first_inv[0, :] = 1.0
    first_inv[HALF, :] = sign
    t16 = 2 * np.pi * ((b * (16 + 32 * j)) % SIDE) / SIDE
    mid = np.concatenate([np.cos(t16), -np.sin(t16)], axis=1)
    mid_inv = np.concatenate([2 * np.cos(t16).T, -2 * np.sin(t16).T], axis=0)
    k1 = np.arange(16)[:, None]
    tw = 2 * np.pi * (k1 * np.arange(INNER)[None, :]) / SIDE
    twiddle = np.stack([np.cos(tw), np.sin(tw)]).astype(np.float32)
    return fwd, inv, first, first_inv, mid, mid_inv, twiddle


def column_tables():
    k1 = np.arange(OUTER)[:, None, None]
    k2 = np.arange(INNER)[None, :, None]
    r = np.arange(INNER)[None, None, :]
    theta = 2 * np.pi * (((k1 + OUTER * k2) * r) % SIDE) / SIDE
    fwd = np.concatenate([np.cos(theta), -np.sin(theta)], axis=1)
    theta = theta.transpose(0, 2, 1)
    inv = np.concatenate([np.cos(theta), np.sin(theta)], axis=1)
    return fwd, inv


def split(value):
    high = value.astype(BF16)
    return high, (value - high.astype(F32)).astype(BF16)


def mm(left, right):
    return lax.dot_general(left, right, (((1,), (0,)), ((), ())), preferred_element_type=F32)


def mm_nt(left, right):
    return lax.dot_general(left, right, (((1,), (1,)), ((), ())), preferred_element_type=F32)


def split_into(value, count):
    parts = []
    for i in range(count):
        parts.append(value.astype(BF16))
        if i + 1 < count:
            value = value - parts[-1].astype(F32)
    return parts


def data_by_table(value, tables):
    count = len(tables)
    parts = split_into(value, count)
    total = None
    for order in reversed(range(count)):
        for i in range(order + 1):
            term = mm(parts[i], tables[order - i])
            total = term if total is None else total + term
    return total


def table_by_data(tables, value):
    parts = split_into(value, len(tables))
    left = jnp.concatenate(tables[0:2], axis=1)
    right = jnp.concatenate(parts[0:2], axis=1)
    r = mm(left, jnp.concatenate([right, right], axis=0))
    total = r[:, INNER : 2 * INNER] + r[:, 0:INNER]
    if len(tables) == 3:
        left = jnp.concatenate([tables[0], tables[2]], axis=1)
        total = total + mm(left, jnp.concatenate([parts[2], parts[0]], axis=0))
    return total


def every(ref):
    return [ref[i] for i in range(ref.shape[0])]


def c_mul(value, factor):
    re, im = value
    c, s = factor.real, factor.imag
    if im is None:
        return (re * c, re * s)
    return (re * c - im * s, re * s + im * c)


def real_forward(xs):
    n = len(xs)
    if n == 2:
        return [(xs[0] + xs[1], None), (xs[0] - xs[1], None)]
    even, odd = real_forward(xs[0::2]), real_forward(xs[1::2])
    m = n // 2
    out = [None] * (m + 1)
    for k in range(m // 2 + 1):
        if k == 0:
            out[0] = (even[0][0] + odd[0][0], None)
            out[m] = (even[0][0] - odd[0][0], None)
        elif 2 * k == m:
            out[k] = (even[k][0], -odd[k][0])
        else:
            tr, ti = c_mul(odd[k], complex(math.cos(2 * math.pi * k / n), -math.sin(2 * math.pi * k / n)))
            er, ei = even[k]
            out[k] = (er + tr, ei + ti)
            out[m - k] = (er - tr, ti - ei)
    return out


def real_backward(spec):
    n = 2 * (len(spec) - 1)
    if n == 2:
        return [spec[0][0] + spec[1][0], spec[0][0] - spec[1][0]]
    m = n // 2
    even, odd = [], []
    for k in range(m // 2 + 1):
        if k == 0:
            even.append((spec[0][0] + spec[m][0], None))
            odd.append((spec[0][0] - spec[m][0], None))
        elif 2 * k == m:
            even.append((2.0 * spec[k][0], None))
            odd.append((-2.0 * spec[k][1], None))
        else:
            ar, ai = spec[k]
            br, bi = spec[m - k]
            even.append((ar + br, ai - bi))
            odd.append(c_mul((ar - br, ai + bi), complex(math.cos(2 * math.pi * k / n), math.sin(2 * math.pi * k / n))))
    xe, xo = real_backward(even), real_backward(odd)
    out = [None] * n
    out[0::2] = xe
    out[1::2] = xo
    return out


def packed_fft(xs, sign, flip):
    n = len(xs)
    if n == 1:
        return xs
    even, odd = packed_fft(xs[0::2], sign, flip), packed_fft(xs[1::2], sign, flip)
    out = [None] * n
    for k in range(n // 2):
        t = odd[k]
        if k:
            turned = pltpu.roll(t, HALF, 1) * flip
            c, s = math.cos(2 * math.pi * k / n), sign * math.sin(2 * math.pi * k / n)
            t = (-s) * turned if 4 * k == n else c * t - s * turned
        out[k] = even[k] + t
        out[k + n // 2] = even[k] - t
    return out


def flip_lanes(rows):
    lane = lax.broadcasted_iota(jnp.int32, (rows, INNER), 1)
    return jnp.where(lane < HALF, 1.0, -1.0).astype(F32)


def put_message(ref, d, value, fine):
    lane = lax.broadcasted_iota(jnp.int32, (INNER, INNER), 1)
    high = value.astype(BF16)
    ref[d, 0:INNER, :] = high
    rest = value - high.astype(F32)
    if fine:
        third = rest - rest.astype(BF16).astype(F32)
        rest = jnp.where((lane & (HALF - 1)) == 7, pltpu.roll(third, 7, 1), rest)
    rest = jnp.where(lane < 8, rest, pltpu.roll(rest, 72, 1))
    rest = jnp.where(lane < 16, rest, 0.0)
    total = rest[0:16]
    for g in range(1, 8):
        total = total + pltpu.roll(rest[16 * g : 16 * g + 16], 16 * g, 1)
    ref[d, INNER : INNER + TAIL, :] = total.astype(BF16)


def get_message(ref, d, fine):
    lane = lax.broadcasted_iota(jnp.int32, (INNER, INNER), 1)
    packed = ref[d, INNER : INNER + TAIL, :].astype(F32)
    rest = jnp.concatenate([packed] + [pltpu.roll(packed, INNER - 16 * g, 1) for g in range(1, 8)], axis=0)
    rest = jnp.where(lane < 8, rest, pltpu.roll(rest, 56, 1))
    column = lane & (HALF - 1)
    if fine:
        third = jnp.where(column == 0, pltpu.roll(rest, INNER - 7, 1), 0.0)
        rest = jnp.where(column < 7, rest, 0.0) + third
    else:
        rest = jnp.where(column < 8, rest, 0.0)
    return ref[d, 0:INNER, :].astype(F32) + rest


def row_forward_kernel(tiled, fine, x_ref, tw_ref, f_ref, a_ref, m_ref, out_ref, y_scr, e_scr):
    def slab(g, carry):
        if tiled:
            xs = [x_ref[pl.ds(pl.multiple_of(g * 256 + a * 8, 8), 8), :] for a in range(OUTER)]
        else:
            xs = [x_ref[pl.ds(pl.multiple_of(g * 8, 8), 8), a * INNER : (a + 1) * INNER] for a in range(OUTER)]
        ys = real_forward(xs)
        rows = pl.ds(pl.multiple_of(g * 8, 8), 8)
        e_scr[0, rows, :] = ys[0][0]
        e_scr[1, rows, :] = ys[16][0]
        for k in range(1, 16):
            c = tw_ref[0, k : k + 1, :]
            s = tw_ref[1, k : k + 1, :]
            re, im = ys[k]
            base = pl.ds(pl.multiple_of((k - 1) * INNER + g * 8, 8), 8)
            y_scr[base, 0:INNER] = re * c + im * s
            y_scr[base, INNER : 2 * INNER] = im * c - re * s
        return carry

    lax.fori_loop(0, 16, slab, 0, unroll=2)
    put_message(out_ref, 0, data_by_table(e_scr[0], every(a_ref)), fine)
    put_message(out_ref, 1, data_by_table(e_scr[1], every(m_ref)), fine)

    def group(q, carry):
        v = data_by_table(y_scr[pl.ds(pl.multiple_of(q * 384, 8), 384), :], every(f_ref))
        for i in range(3):
            rows = v[i * INNER : (i + 1) * INNER]
            put_message(out_ref, 2 + 2 * (3 * q + i), rows[:, 0:INNER], fine)
            put_message(out_ref, 3 + 2 * (3 * q + i), rows[:, INNER : 2 * INNER], fine)
        return carry

    lax.fori_loop(0, 5, group, 0)


def row_backward_kernel(final, *refs):
    if final:
        in_ref, base_ref, tw_ref, f_ref, a_ref, m_ref, out_ref, z_scr, e_scr = refs
    else:
        in_ref, tw_ref, f_ref, a_ref, m_ref, out_ref, z_scr, e_scr = refs
    e_scr[0] = data_by_table(get_message(in_ref, 0, False), every(a_ref))
    e_scr[1] = data_by_table(get_message(in_ref, 1, False), every(m_ref))

    def group(q, carry):
        parts = []
        for i in range(3):
            k = 3 * q + i
            parts.append(jnp.concatenate([get_message(in_ref, 2 + 2 * k + h, False) for h in range(2)], axis=1))
        v = jnp.concatenate(parts, axis=0)
        z_scr[pl.ds(pl.multiple_of(q * 384, 8), 384), :] = data_by_table(v, every(f_ref))
        return carry

    lax.fori_loop(0, 5, group, 0)

    def slab(g, carry):
        rows = pl.ds(pl.multiple_of(g * 8, 8), 8)
        spec = [(e_scr[0, rows, :], None)]
        for k in range(1, 16):
            c = tw_ref[0, k : k + 1, :]
            s = tw_ref[1, k : k + 1, :]
            base = pl.ds(pl.multiple_of((k - 1) * INNER + g * 8, 8), 8)
            re = z_scr[base, 0:INNER]
            im = z_scr[base, INNER : 2 * INNER]
            spec.append((re * c - im * s, im * c + re * s))
        spec.append((e_scr[1, rows, :], None))
        xs = real_backward(spec)
        for a in range(OUTER):
            if final:
                cols = slice(a * INNER, (a + 1) * INNER)
                out_ref[rows, cols] = base_ref[rows, cols] + xs[a]
            else:
                out_ref[pl.ds(pl.multiple_of(g * 256 + a * 8, 8), 8), :] = xs[a]
        return carry

    lax.fori_loop(0, 16, slab, 0, unroll=2)


def take_all(exchange, scr, fine):
    def unpack(pair):
        values = [get_message(exchange.out_ref, source, fine) for source in pair]
        for source, value in zip(pair, values):
            scr[source] = value

    def step(h, carry):
        steps = (2 * h, 2 * h + 1)
        for i in steps:
            exchange.wait_source(i)
        unpack([exchange.source(i) for i in steps])
        return carry

    lax.fori_loop(0, PEERS // 2 - 1, step, 0)
    exchange.own.wait()
    exchange.wait_source(PEERS - 2)
    unpack([exchange.source(PEERS - 2), exchange.me])
    exchange.wait_sends()


def give_all(scr, exchange):
    def pack(pair):
        for peer in pair:
            put_message(exchange.in_ref, peer, scr[peer], False)

    def step(h, carry):
        steps = (2 * h, 2 * h + 1)
        pack([exchange.peer(i) for i in steps])
        for i in steps:
            exchange.send(i)
        return carry

    lax.fori_loop(0, PEERS // 2 - 1, step, 0)
    pack([exchange.peer(PEERS - 2), exchange.me])
    exchange.send(PEERS - 2)
    exchange.own.start()


def column_first_step(in_ref, y_scr, sign):
    flip = flip_lanes(8)

    def slab(g, carry):
        rows = pl.ds(pl.multiple_of(g * 8, 8), 8)
        ys = packed_fft([in_ref[s, rows, :] for s in range(OUTER)], sign, flip)
        for k in range(OUTER):
            y_scr[k, rows, :] = ys[k]
        return carry

    lax.fori_loop(0, 16, slab, 0, unroll=2)


def apply_packed(e_ref, k1, value, flip):
    r = table_by_data([e_ref[i, k1] for i in range(e_ref.shape[0])], value)
    return r[0:INNER] - pltpu.roll(r[INNER : 2 * INNER], HALF, 1) * flip


MESH = pl.DeviceIdType.MESH


def greet_peers(me, barrier, extra=()):
    def greet(i, carry):
        pl.semaphore_signal(barrier, inc=1, device_id={"strip": lax.rem(me + i, PEERS)}, device_id_type=MESH)
        return carry

    lax.fori_loop(1, PEERS, greet, 0)
    for device in extra:
        pl.semaphore_signal(barrier, inc=1, device_id=device, device_id_type=MESH)
    pl.semaphore_wait(barrier, PEERS - 1 + len(extra))


STRIDE = 11
REPLY = 45


class Exchange:
    def __init__(self, me, in_ref, out_ref, send_sem, recv_sem, own_sem, flat=0):
        self.me, self.in_ref, self.out_ref, self.flat = me, in_ref, out_ref, flat
        self.send_sem, self.recv_sem = send_sem, recv_sem
        self.own = pltpu.make_async_copy(self.part(in_ref, me), self.part(out_ref, me), own_sem)

    def part(self, ref, i):
        return ref.at[pl.ds(pl.multiple_of(i * self.flat, self.flat), self.flat)] if self.flat else ref.at[i]

    def copy(self, peer, send, source):
        return pltpu.make_async_remote_copy(
            src_ref=self.part(self.in_ref, peer),
            dst_ref=self.part(self.out_ref, source),
            send_sem=self.send_sem.at[send],
            recv_sem=self.recv_sem.at[source],
            device_id={"strip": peer},
            device_id_type=MESH,
        )

    def peer(self, i):
        return lax.rem(self.me + 1 + lax.rem(i * STRIDE, PEERS - 1), PEERS)

    def source(self, i):
        return lax.rem(self.me + PEERS - 1 - lax.rem(i * STRIDE, PEERS - 1), PEERS)

    def reply(self, i):
        return lax.rem(REPLY - i, PEERS - 1)

    def send(self, i):
        self.copy(self.peer(i), i, self.me).start()

    def wait_source(self, i):
        self.copy(self.peer(i), i, self.source(i)).wait_recv()

    def wait_sends(self):
        def step(i, carry):
            self.copy(self.peer(i), i, self.me).wait_send()
            return carry

        lax.fori_loop(0, PEERS - 1, step, 0)

    def start(self, first=0, last=PEERS - 1):
        def step(i, carry):
            self.copy(self.peer(i), i, self.me).start()
            return carry

        lax.fori_loop(first, last, step, 0)
        if first == 0:
            self.own.start()

    def wait(self):
        def step(i, carry):
            self.wait_source(i)
            return carry

        self.own.wait()
        lax.fori_loop(0, PEERS - 1, step, 0)
        self.wait_sends()


class Moves:
    def __init__(self, pairs, sems):
        self.copies = [pltpu.make_async_copy(src, dst, sems.at[i]) for i, (src, dst) in enumerate(pairs)]

    def start(self):
        for copy in self.copies:
            copy.start()

    def wait(self):
        for copy in self.copies:
            copy.wait()


def exchange_sems():
    return [pltpu.SemaphoreType.DMA((PEERS,)), pltpu.SemaphoreType.DMA((PEERS,)), pltpu.SemaphoreType.DMA]


def edge_lanes():
    lane = lax.broadcasted_iota(jnp.int32, (INNER, INNER), 1)
    return jnp.logical_or(lane == 0, lane == HALF), lane < HALF


def edge_gather(ref):
    mask, _ = edge_lanes()

    def step(k1, acc):
        return acc + pltpu.roll(jnp.where(mask, ref[k1], 0.0), k1, 1)

    return lax.fori_loop(0, OUTER, step, jnp.zeros((INNER, INNER), F32), unroll=4)


def edge_split(spec, amp):
    i = lax.broadcasted_iota(jnp.int32, (INNER, INNER), 0)
    j = lax.broadcasted_iota(jnp.int32, (INNER, INNER), 1)
    one = jnp.ones((INNER, INNER), F32)
    none = jnp.zeros((INNER, INNER), F32)
    rows = jnp.where(i + j == INNER - 1, one, none).astype(BF16)
    rows0 = jnp.where(((i + j) & (INNER - 1)) == 0, one, none).astype(BF16)
    sign = jnp.where(j < HALF, one, -one)
    col = j & (HALF - 1)
    same = (i < HALF) == (j < HALF)
    lanes = jnp.where(
        jnp.logical_and(same, jnp.logical_and(col > 0, col + (i & (HALF - 1)) == OUTER)), sign, none
    ).astype(BF16)
    lanes0 = jnp.where(jnp.logical_and(i == j, col == 0), sign, none).astype(BF16)

    def move(left, value, right):
        value = sum(mm(left, p) for p in reversed(split_into(value, 3)))
        return sum(mm(p, right) for p in reversed(split_into(value, 3)))

    rev = move(rows, spec, lanes) + move(rows0, spec, lanes0)
    swapped = pltpu.roll(amp, HALF, 1)
    _, left = edge_lanes()
    a0 = jnp.where(left, amp, swapped)
    a2 = jnp.where(left, swapped, amp)
    return 0.5 * (spec + rev), 0.5 * (spec - rev), a0, a2


def turn(c, s, value, flip):
    return c * value + s * (pltpu.roll(value, HALF, 1) * flip)


EARLY = 4
MIDDLE = 21


def first_kernel(
    scale, rate, wind, prior, x_ref, tw, f_ref, a_ref, m_ref, fi_ref, ai_ref, mi_ref, slot_ref, prec_ref,
    ef_any, ei_any, sent_ref, ids_ref,
    resid_ref, par, own_any, here_any, amp_any, here_ids_ref, prev_ref, next_ref, *scratch,
):
    y_scr, z_scr, msg_scr, land_scr, back_scr, tab_ref, row_scr, row_edge = scratch[0:8]
    up_ref, down_ref, tiles_scr, g_scr, phase_scr, landed, p_scr, table_scr, res_scr = scratch[8:17]
    sid_scr, sid_sem, side_sems = scratch[17:20]
    ef, ei, own_ref, amp_ref, here_ref, in_sems, out_sems, here_sems = scratch[20:28]
    fix_scr = scratch[28]
    sems = scratch[29:]
    tables = Moves([(ef_any, ef), (ei_any, ei)], in_sems)
    tables.start()
    results = Moves([(own_ref, own_any), (amp_ref, amp_any)], out_sems)
    weights_out = Moves([(here_ref, here_any)], here_sems)
    me = lax.axis_index("strip")
    slot_at = lax.axis_index("tm")
    above, below = lax.rem(slot_at + 1, 4), lax.rem(slot_at + 3, 4)
    greet_peers(me, pltpu.get_barrier_semaphore(), ({"tm": above}, {"tm": below}))
    ids = Exchange(me, ids_ref, here_ids_ref, *sems[0:3], flat=ID_STRIDE)
    weights = Exchange(me, sent_ref, here_ref, *sems[3:6])
    pencils = Exchange(me, msg_scr, land_scr, *sems[6:9])
    back = Exchange(me, msg_scr, back_scr, *sems[9:12])
    phases = Exchange(me, phase_scr, landed, *sems[12:15])
    residuals = Exchange(me, res_scr, resid_ref, *sems[15:18])
    ids.start()
    weights.start(0, EARLY)
    row_forward_kernel(False, True, x_ref, tw, f_ref, a_ref, m_ref, msg_scr, row_scr, row_edge)
    pencils.start()
    tables_kernel(scale, rate, wind, prior, tab_ref, amp_ref, par)
    take_all(pencils, z_scr, True)
    weights.start(EARLY, MIDDLE)
    tables.wait()
    column_first_step(z_scr, y_scr, -1.0)
    flip = flip_lanes(INNER)

    def step(k1, carry):
        value = apply_packed(ef, k1, y_scr[k1], flip)
        amp = amp_ref[k1]
        once = value * amp
        twice = once * amp
        y_scr[k1] = value
        z_scr[k1] = par[0] * once
        own_ref[k1] = par[3] * twice
        for n, ref, gain in ((0, up_ref, par[1]), (1, down_ref, par[2])):
            cb = tab_ref[2 * n]
            sb = tab_ref[2 * n + 1]
            ca = tab_ref[8, pl.ds(64 * n + k1, 1), :] * gain
            sa = tab_ref[8, pl.ds(64 * n + 32 + k1, 1), :] * gain
            ref[k1] = turn(cb * ca - sb * sa, sb * ca + cb * sa, twice, flip).astype(BF16)
        return carry

    lax.fori_loop(0, OUTER, step, 0, unroll=8)

    @pl.when(me == 0)
    def _():
        u0, u2, a0, a2 = edge_split(edge_gather(y_scr), edge_gather(amp_ref))
        mask, _ = edge_lanes()
        e0 = a0 * u0
        e2 = a2 * u2
        change = par[0] * (e0 + e2)
        e0 = a0 * e0
        e2 = a2 * e2
        fix_scr[0] = par[3] * (e0 + e2)
        fix_scr[1] = par[1] * turn(tab_ref[4], tab_ref[5], e0 + par[4] * e2, flip)
        fix_scr[2] = par[2] * turn(tab_ref[6], tab_ref[7], e0 + par[5] * e2, flip)

        def put(k1, carry):
            back = lax.rem(INNER - k1, INNER)
            z_scr[k1] = jnp.where(mask, pltpu.roll(change, back, 1), z_scr[k1])
            return carry

        lax.fori_loop(0, OUTER, put, 0, unroll=4)

    def inverse(k1, carry):
        z_scr[k1] = apply_packed(ei, k1, z_scr[k1], flip)
        return carry

    lax.fori_loop(0, OUTER, inverse, 0, unroll=8)
    column_first_step(z_scr, y_scr, 1.0)
    give_all(y_scr, back)

    @pl.when(me == 0)
    def _():
        mask, _ = edge_lanes()

        def put(k1, carry):
            place_at = lax.rem(INNER - k1, INNER)
            for n, ref in enumerate((own_ref, up_ref, down_ref)):
                value = jnp.where(mask, pltpu.roll(fix_scr[n], place_at, 1), ref[k1].astype(F32))
                ref[k1] = value.astype(ref.dtype)
            return carry

        lax.fori_loop(0, OUTER, put, 0, unroll=2)

    results.start()
    ids.wait()
    fetch = pltpu.make_async_copy(here_ids_ref, sid_scr, sid_sem)
    fetch.start()
    back.wait()
    weights.start(MIDDLE, PEERS - 1)
    row_backward_kernel(False, back_scr, tw, fi_ref, ai_ref, mi_ref, tiles_scr, row_scr, row_edge)
    fetch.wait()
    ones = jnp.ones((2 * INNER, INNER), BF16)
    row = lax.broadcasted_iota(jnp.int32, (INNER, INNER), 0)
    lane = lax.broadcasted_iota(jnp.int32, (INNER, INNER), 1)
    place = lax.broadcasted_iota(jnp.int32, (1, INNER), 1)

    def pick(s, place_at):
        def some(q, carry):
            first = s * ID_STRIDE + q * 32
            picks = [sid_scr[first + j] for j in range(32)]
            rows = [tiles_scr[pl.ds(picks[j], 1), :] for j in range(32)]
            for j in range(32):
                g_scr[pl.ds(place_at + q * 32 + j, 1), :] = rows[j]
            return carry

        lax.fori_loop(0, SLOTS // 32, some, 0)

    def gather_pair(pair):
        for n, s in enumerate(pair):
            pick(s, n * SLOTS)
        for n, s in enumerate(pair):
            count = sid_scr[s * ID_STRIDE + SLOTS]
            picked = g_scr[n * SLOTS : (n + 1) * SLOTS, :]
            sums = mm(jnp.concatenate(split(picked * here_ref[s].astype(F32)), axis=1), ones)
            for q in range(4):
                got = jnp.where(row == lane, sums[q * INNER : (q + 1) * INNER], 0.0)
                got = jnp.sum(got, axis=0, keepdims=True)
                phase_scr[s, q : q + 1, :] = jnp.where(place + q * INNER < count, got, 0.0)

    def gather_next(h, carry):
        steps = (2 * h, 2 * h + 1)
        for i in steps:
            weights.wait_source(i)
        gather_pair([weights.source(i) for i in steps])
        for i in steps:
            phases.copy(weights.source(i), phases.reply(i), me).start()
        return carry

    lax.fori_loop(0, PEERS // 2 - 1, gather_next, 0)
    weights.own.wait()
    weights.wait_source(PEERS - 2)
    last = weights.source(PEERS - 2)
    gather_pair([last, me])
    phases.copy(last, phases.reply(PEERS - 2), me).start()
    phases.own.start()
    weights.wait_sends()
    weights_out.start()

    @pl.when(slot_at < 3)
    def _():
        for side in sides(side_sems, up_ref, prev_ref, above, 0):
            side.start()

    @pl.when(slot_at > 0)
    def _():
        for side in sides(side_sems, down_ref, next_ref, below, 1):
            side.start()

    phases.wait()
    for s in range(PEERS):
        table_scr[4 * s : 4 * s + 4, :] = landed[s]
    acc = weigh(slot_ref, prec_ref, table_scr[...], p_scr)
    for s in range(PEERS):
        res_scr[s] = acc[4 * s : 4 * s + 4]
    residuals.start()
    results.wait()
    weights_out.wait()
    residuals.wait()

    @pl.when(slot_at < 3)
    def _():
        for side in sides(side_sems, up_ref, prev_ref, above, 0):
            side.wait_send()
        for side in sides(side_sems, down_ref, next_ref, below, 1):
            side.wait_recv()

    @pl.when(slot_at > 0)
    def _():
        for side in sides(side_sems, up_ref, prev_ref, above, 0):
            side.wait_recv()
        for side in sides(side_sems, down_ref, next_ref, below, 1):
            side.wait_send()


SIDE_PARTS = 4


def sides(sems, src, dst, device, n):
    copies = []
    for p in range(SIDE_PARTS):
        rows = pl.ds(p * (OUTER // SIDE_PARTS), OUTER // SIDE_PARTS)
        copies.append(
            pltpu.make_async_remote_copy(
                src_ref=src.at[rows],
                dst_ref=dst.at[rows],
                send_sem=sems.at[0, n, p],
                recv_sem=sems.at[1, n, p],
                device_id={"tm": device},
                device_id_type=MESH,
            )
        )
    return copies


def column_second_kernel(par, in_ref, amp_any, own_any, prev_any, next_any, ef_any, ei_any, back_ref, *scratch):
    y_scr, z_scr, msg_scr, out_scr = scratch[0:4]
    amp_ref, own_ref, prev_ref, next_ref, ef, ei, in_sems = scratch[10:17]
    inputs = Moves(
        [(amp_any, amp_ref), (own_any, own_ref), (prev_any, prev_ref), (next_any, next_ref), (ef_any, ef), (ei_any, ei)],
        in_sems,
    )
    inputs.start()
    me = lax.axis_index("strip")
    slot_at = lax.axis_index("tm")
    greet_peers(me, pltpu.get_barrier_semaphore())
    pencils = Exchange(me, in_ref, msg_scr, *scratch[4:7])
    pencils.start()
    take_all(pencils, z_scr, False)
    inputs.wait()
    column_first_step(z_scr, y_scr, -1.0)
    flip = flip_lanes(INNER)

    def step(k1, carry):
        value = apply_packed(ef, k1, y_scr[k1], flip)
        y_scr[k1] = value
        z_scr[k1] = par[0] * (value * amp_ref[k1]) + own_ref[k1]
        return carry

    lax.fori_loop(0, OUTER, step, 0, unroll=8)

    @pl.when(me == 0)
    def _():
        spec = edge_gather(y_scr)
        amp = edge_gather(amp_ref)
        u0, u2, a0, a2 = edge_split(spec, amp)
        mask, _ = edge_lanes()
        change = par[0] * (a0 * u0 + a2 * u2 - amp * spec)

        def put(k1, carry):
            back = lax.rem(INNER - k1, INNER)
            z_scr[k1] = z_scr[k1] + jnp.where(mask, pltpu.roll(change, back, 1), 0.0)
            return carry

        lax.fori_loop(0, OUTER, put, 0, unroll=4)

    def inverse(k1, carry):
        moved = jnp.where(slot_at > 0, prev_ref[k1].astype(F32), 0.0)
        moved = moved + jnp.where(slot_at < 3, next_ref[k1].astype(F32), 0.0)
        z_scr[k1] = apply_packed(ei, k1, z_scr[k1] - par[0] * moved, flip)
        return carry

    lax.fori_loop(0, OUTER, inverse, 0, unroll=8)
    column_first_step(z_scr, y_scr, 1.0)
    back = Exchange(me, out_scr, back_ref, *scratch[7:10])
    give_all(y_scr, back)
    back.wait()


def route_kernel(t_ref, id_ref, slot_ref, tail_ref):
    row = lax.broadcasted_iota(jnp.int32, (INNER, 2 * INNER), 0)
    col = lax.broadcasted_iota(jnp.int32, (INNER, 2 * INNER), 1)
    tri = jnp.where(jnp.logical_or(row < col, col >= INNER), 1.0, 0.0).astype(BF16)
    peer = lax.broadcasted_iota(jnp.int32, (PEERS, INNER), 0)
    base = jnp.zeros((PEERS, INNER), F32)
    for i in range(0, POINT_ROWS, 8):
        hots = [jnp.where(peer == t_ref[i + j : i + j + 1, :], 1.0, 0.0) for j in range(8)]
        cum = mm(jnp.concatenate(hots, axis=0).astype(BF16), tri)
        for j in range(8):
            part = cum[j * PEERS : (j + 1) * PEERS]
            pos = jnp.sum(hots[j] * (part[:, 0:INNER] + base), axis=0, keepdims=True)
            base = base + part[:, INNER : 2 * INNER]
            slot_ref[i + j : i + j + 1, :] = t_ref[i + j : i + j + 1, :] * SLOTS + pos.astype(jnp.int32)
    batch = 4
    index = lax.broadcasted_iota(jnp.int32, (INNER, batch * INNER), 0)

    def wide(ref, i):
        return jnp.concatenate([ref[pl.ds(i * batch + j, 1), :] for j in range(batch)], axis=1)

    def put(i, acc):
        slot = wide(slot_ref, i)
        ids = wide(id_ref, i)
        r = lax.shift_right_logical(ids, 5)
        ids = lax.shift_right_logical(r, 3) * 256 + (ids & 31) * 8 + (r & 7)
        hot = jnp.where(index == (slot & 127), 1.0, 0.0).astype(BF16)
        line = index == lax.shift_right_logical(slot, 7)
        v = [
            jnp.where(line, d.astype(F32), 0.0).astype(BF16) for d in (lax.shift_right_logical(ids, 6), ids & 63)
        ]
        return acc + mm_nt(jnp.concatenate(v, axis=0), hot)

    acc = lax.fori_loop(0, POINT_ROWS // batch, put, jnp.zeros((2 * INNER, INNER), F32), unroll=2)
    ids = (acc[0:INNER] * 64.0 + acc[INNER : 2 * INNER]).astype(jnp.int32)
    count = base.astype(jnp.int32)
    tail_ref[...] = jnp.zeros_like(tail_ref)
    for s in range(PEERS):
        tail_ref[s, 0:4, :] = ids[4 * s : 4 * s + 4]
        tail_ref[s, 4:5, :] = count[s : s + 1]


def pack_kernel(slot_ref, w_ref, out_ref, w_scr, buf):
    def widen(i, carry):
        rows = pl.ds(pl.multiple_of(i * 64, 64), 64)
        w_scr[rows, :] = w_ref[rows, :].astype(F32)
        return carry

    lax.fori_loop(0, POINT_ROWS * INNER // 64, widen, 0, unroll=2)

    def some(q, carry):
        antenna, direction = (q // 8) * 4, (q % 8) * 8
        first = direction * INNER + antenna
        line = pl.multiple_of(antenna * HALF + direction, 8)
        pairs = [(a, d) for a in range(4) for d in range(8)]
        slots = [slot_ref[first + d * INNER + a] for a, d in pairs]
        rows = [w_scr[pl.ds(line + a * HALF + d, 1), :] for a, d in pairs]
        for j in range(32):
            buf[pl.ds(slots[j], 1), :] = rows[j]
        return carry

    lax.fori_loop(0, POINT_ROWS * INNER // 32, some, 0)

    def narrow(i, carry):
        rows = pl.ds(pl.multiple_of(i * INNER, INNER), INNER)
        out_ref[rows, :] = buf[rows, :].astype(BF16)
        return carry

    lax.fori_loop(0, PEERS * SLOTS // INNER, narrow, 0, unroll=2)


def weigh(slot_ref, prec_ref, phase, p_scr):
    high, low = split(phase)
    table = jnp.concatenate([high, low], axis=0)
    batch = 4
    index = lax.broadcasted_iota(jnp.int32, (INNER, batch * INNER), 0)

    def wide(ref, i):
        return jnp.concatenate([ref[pl.ds(i * batch + j, 1), :] for j in range(batch)], axis=1)

    def pick(i, carry):
        slot = wide(slot_ref, i)
        hot = jnp.where(index == (slot & 127), 1.0, 0.0).astype(BF16)
        v = mm(table, hot)
        v = v[0:INNER] + v[INNER : 2 * INNER]
        got = jnp.sum(jnp.where(index == lax.shift_right_logical(slot, 7), v, 0.0), axis=0, keepdims=True)
        for j in range(batch):
            p_scr[pl.ds(i * batch + j, 1), :] = got[:, j * INNER : (j + 1) * INNER]
        return carry

    lax.fori_loop(0, POINT_ROWS // batch, pick, 0, unroll=4)
    prec = prec_ref[...]
    phase = p_scr[...]

    centre = jnp.sum(prec * phase, axis=0, keepdims=True) / jnp.sum(prec, axis=0, keepdims=True)
    p_scr[...] = prec * (phase - centre)

    def put(i, acc):
        slot = wide(slot_ref, i)
        hot = jnp.where(index == (slot & 127), 1.0, 0.0).astype(BF16)
        v = jnp.where(index == lax.shift_right_logical(slot, 7), wide(p_scr, i), 0.0)
        vh, vl = split(v)
        return acc + mm_nt(jnp.concatenate([vh, vl], axis=0), hot)

    acc = lax.fori_loop(0, POINT_ROWS // batch, put, jnp.zeros((2 * INNER, INNER), F32), unroll=4)
    return acc[0:INNER] + acc[INNER : 2 * INNER]


COPIES = 8


def scatter_kernel(
    sid_ref, r_ref, w_any, tw, f_ref, a_ref, m_ref, out_ref, rt_scr, u_scr, y_scr, e_scr, w_ref, w_sems, *accs
):
    fetch = Moves([(w_any, w_ref)], w_sems)
    fetch.start()
    def clear(i, carry):
        rows = pl.ds(pl.multiple_of(i * 64, 64), 64)
        for acc in accs:
            acc[rows, :] = jnp.zeros((64, INNER), F32)
        return carry

    lax.fori_loop(0, SIDE // 64, clear, 0)
    rt_scr[...] = r_ref[...].T
    fetch.wait()
    lane = lax.broadcasted_iota(jnp.int32, (INNER, INNER), 1)
    row = lax.broadcasted_iota(jnp.int32, (INNER, INNER), 0)

    def scaled(s, carry):
        for q in range(4):
            col = jnp.sum(jnp.where(lane == s * 4 + q, rt_scr[...], 0.0), axis=1, keepdims=True)
            rows = pl.ds(pl.multiple_of(s * SLOTS + q * INNER, INNER), INNER)
            used = row + q * INNER < sid_ref[s * ID_STRIDE + SLOTS]
            u_scr[rows, :] = jnp.where(used, w_ref[rows, :].astype(F32) * col, 0.0)
        return carry

    lax.fori_loop(0, PEERS, scaled, 0, unroll=4)

    def source(s, carry):
        def some(q, inner):
            first = s * SLOTS + q * 32
            line = s * ID_STRIDE + q * 32
            ids = [sid_ref[line + j] for j in range(32)]
            us = [u_scr[pl.ds(first + j, 1), :] for j in range(32)]
            for h in range(0, 32, COPIES):
                sums = [accs[j][pl.ds(ids[h + j], 1), :] + us[h + j] for j in range(COPIES)]
                for j in range(COPIES):
                    accs[j][pl.ds(ids[h + j], 1), :] = sums[j]
            return inner

        return lax.fori_loop(0, lax.shift_right_logical(sid_ref[s * ID_STRIDE + SLOTS] + 31, 5), some, carry)

    lax.fori_loop(0, PEERS, source, 0)

    def add(i, carry):
        rows = pl.ds(pl.multiple_of(i * 64, 64), 64)
        total = accs[0][rows, :]
        for acc in accs[1:]:
            total = total + acc[rows, :]
        accs[0][rows, :] = total
        return carry

    lax.fori_loop(0, SIDE // 64, add, 0)
    row_forward_kernel(True, False, accs[0], tw, f_ref, a_ref, m_ref, out_ref, y_scr, e_scr)


def call(kernel, name, out_shapes, args, smem=0, scratch=(), any_args=(), any_outs=(), smem_outs=(), collective_id=None):
    spaces = [pltpu.SMEM if i < smem else pl.ANY if i in any_args else pltpu.VMEM for i in range(len(args))]
    outs = [pl.ANY if i in any_outs else pltpu.SMEM if i in smem_outs else pltpu.VMEM for i in range(len(out_shapes))]
    remote = dict(collective_id=collective_id, has_side_effects=True) if collective_id is not None else {}
    return pl.pallas_call(
        kernel,
        out_shape=out_shapes,
        in_specs=[pl.BlockSpec(memory_space=space) for space in spaces],
        out_specs=[pl.BlockSpec(memory_space=space) for space in outs],
        scratch_shapes=list(scratch),
        compiler_params=pltpu.CompilerParams(vmem_limit_bytes=VMEM_BYTES, **remote),
        cost_estimate=pl.CostEstimate(flops=1024, bytes_accessed=1024, transcendentals=0),
        name=name,
    )(*args)


def shape(dims, dtype=F32):
    return jax.ShapeDtypeStruct(dims, dtype)


PENCILS = (PEERS, INNER, INNER)
MESSAGES = (PEERS, INNER + TAIL, INNER)


def row_backward(pencils, base, tables):
    final = base is not None
    args = [pencils] + ([base] if final else []) + tables
    return call(
        lambda *refs: row_backward_kernel(final, *refs),
        "row_backward",
        [shape((INNER, SIDE) if final else (SIDE, INNER))],
        args,
        scratch=[pltpu.VMEM((15 * INNER, 2 * INNER), F32), pltpu.VMEM((2, INNER, INNER), F32)],
    )[0]


def tables_kernel(scale, rate, wind, prior, tab_ref, amp_ref, par_ref):
    strip = lax.axis_index("strip")
    live = (lax.axis_index("tm") < 3).astype(F32)
    k1 = (strip // 2).astype(F32)
    even = strip % 2 == 0
    row = lax.broadcasted_iota(jnp.int32, (INNER, INNER), 0)
    lane = lax.broadcasted_iota(jnp.int32, (INNER, INNER), 1)
    line = row.astype(F32)
    j = (lane & (HALF - 1)).astype(F32)
    cols = jnp.where(even, k1 + OUTER * j, k1 + OUTER * (INNER - 1.0 - j))
    cols = jnp.where(strip == 1, 16.0 + OUTER * j, cols)
    winds = ((wind[0, 0].astype(F32), wind[0, 1].astype(F32)), (prior[1], prior[2]))

    def cosine(turns):
        turns = turns - SIDE * jnp.floor(turns * (1.0 / SIDE))
        return jnp.cos(turns * (2.0 * math.pi / SIDE))

    small = jnp.zeros((INNER, INNER), F32)
    for kind in range(4):
        wind_row, wind_col = winds[kind // 2]
        quarter = (0.0, 3.0 * SIDE / 4, 0.0, SIDE / 4.0)[kind]
        base = OUTER * line * wind_row + quarter
        tab_ref[kind] = cosine(base + cols * wind_col)
        tab_ref[4 + kind] = cosine(base + j * wind_row)
        turns = (row & (OUTER - 1)).astype(F32) * wind_row + quarter
        small = jnp.where(lax.shift_right_logical(row, 5) == kind, turns, small)
    tab_ref[8] = cosine(small)

    fold = jnp.where(even, k1 + OUTER * j, OUTER - k1 + OUTER * j)
    fold = jnp.where(strip == 1, 16.0 + OUTER * j, fold)
    fold = jnp.where(jnp.logical_and(strip == 0, lane == HALF), SIDE / 2.0, fold)
    fold = fold * fold

    def step(k, carry):
        kr = line * OUTER + k.astype(F32)
        kr = jnp.minimum(kr, SIDE - kr)
        radius = (kr * kr + fold) / (KZERO * KZERO)
        amp_ref[k] = SIDE / (2.0 * KZERO) * jnp.exp((-11.0 / 12.0) * jnp.log(1.0 + radius))
        return carry

    lax.fori_loop(0, OUTER, step, 0, unroll=2)
    norm = scale[0] / (SIDE * SIDE)
    mine = rate[0] * live
    par_ref[0] = norm
    par_ref[1] = mine * scale[0]
    par_ref[2] = prior[0] * scale[0]
    par_ref[3] = (mine + prior[0]) * scale[0] * norm
    par_ref[4] = 1.0 - 2.0 * (wind[0, 1] & 1).astype(F32)
    par_ref[5] = 1.0 - 2.0 * (prior[2].astype(jnp.int32) & 1).astype(F32)
    par_ref[6] = 0.0
    par_ref[7] = 0.0


def const(*tables):
    return [jnp.asarray(t) for t in tables]


def local(
    screen_vec,
    prior_scale,
    flow_weight,
    wind,
    pierce_point_strip,
    pierce_block,
    pierce_weights,
    noise_prec,
):
    fwd, inv, first, first_inv, mid, mid_inv, twiddle = row_tables()
    row_fwd_tables = const(twiddle, pieces(fwd, 2), pieces(first, 2), pieces(mid, 2))
    row_fine_tables = const(twiddle, pieces(fwd, 3), pieces(first, 3), pieces(mid, 3))
    row_inv_tables = const(twiddle, pieces(inv, 2), pieces(first_inv, 2), pieces(mid_inv, 2))
    col_fwd, col_inv = column_tables()
    col_fine_tables = const(pieces(col_fwd, 3), pieces(col_inv, 2))
    col_tables = const(pieces(col_fwd, 2), pieces(col_inv, 2))

    x = screen_vec[0]
    weights = pierce_weights[0].reshape(POINT_ROWS * INNER, INNER)
    target = pierce_point_strip.reshape(INNER, HALF).T
    block = pierce_block.reshape(INNER, HALF).T
    prec = noise_prec.reshape(INNER, HALF).T

    mine = jnp.concatenate([flow_weight, wind[0].astype(F32)])
    prior = lax.ppermute(mine, "tm", [(i, i + 1) for i in range(lax.axis_size("tm") - 1)])
    slots, ids = call(
        route_kernel,
        "route",
        [shape((POINT_ROWS, INNER), jnp.int32), shape((PEERS, ID_ROWS, INNER), jnp.int32)],
        [target, block],
    )
    ids, prior, prec = lax.optimization_barrier((ids, prior, prec))
    sent = call(
        pack_kernel,
        "pack",
        [shape((PEERS * SLOTS, INNER), BF16)],
        [slots.reshape(-1), weights],
        smem=1,
        scratch=[pltpu.VMEM((POINT_ROWS * INNER, INNER), F32), pltpu.VMEM((PEERS * SLOTS, INNER), F32)],
    )[0]

    spectral = [pltpu.VMEM(PENCILS, F32), pltpu.VMEM(PENCILS, F32)]
    rows = [pltpu.VMEM((15 * INNER, 2 * INNER), F32), pltpu.VMEM((2, INNER, INNER), F32)]
    message = shape(MESSAGES, BF16)
    points = pltpu.VMEM((PEERS * SLOTS, INNER), F32)
    screen = pltpu.VMEM((SIDE, INNER), F32)
    small = (PEERS, 4, INNER)
    resid, par, own, arrived, amp, here_ids, from_prev, from_next = call(
        first_kernel,
        "first",
        [
            shape(small),
            shape((8,)),
            shape(PENCILS),
            shape((PEERS, SLOTS, INNER), BF16),
            shape(PENCILS),
            shape((PEERS * ID_STRIDE,), jnp.int32),
            shape(PENCILS, BF16),
            shape(PENCILS, BF16),
        ],
        [prior_scale, flow_weight, wind, prior, x]
        + row_fine_tables
        + row_inv_tables[1:]
        + [slots, prec]
        + col_fine_tables
        + [sent.reshape(PEERS, SLOTS, INNER), ids.reshape(-1)],
        smem=4,
        any_args=(14, 15, 16, 17),
        any_outs=(2, 3, 4, 5, 6, 7),
        smem_outs=(1,),
        collective_id=3,
        scratch=spectral
        + [pltpu.VMEM(MESSAGES, BF16)] * 3
        + [pltpu.VMEM((9, INNER, INNER), F32)]
        + rows
        + [pltpu.VMEM(PENCILS, BF16)] * 2
        + [
            screen,
            pltpu.VMEM((2 * SLOTS, INNER), F32),
            pltpu.VMEM(small, F32),
            pltpu.VMEM(small, F32),
            pltpu.VMEM((POINT_ROWS, INNER), F32),
            pltpu.VMEM((INNER, INNER), F32),
            pltpu.VMEM(small, F32),
            pltpu.SMEM((PEERS * ID_STRIDE,), jnp.int32),
            pltpu.SemaphoreType.DMA,
            pltpu.SemaphoreType.DMA((2, 2, SIDE_PARTS)),
            pltpu.VMEM(col_fine_tables[0].shape, BF16),
            pltpu.VMEM(col_fine_tables[1].shape, BF16),
            pltpu.VMEM(PENCILS, F32),
            pltpu.VMEM(PENCILS, F32),
            pltpu.VMEM((PEERS, SLOTS, INNER), BF16),
            pltpu.SemaphoreType.DMA((2,)),
            pltpu.SemaphoreType.DMA((2,)),
            pltpu.SemaphoreType.DMA((1,)),
            pltpu.VMEM((3, INNER, INNER), F32),
        ]
        + exchange_sems() * 6,
    )
    here = arrived.reshape(PEERS * SLOTS, INNER)

    pencils = call(
        scatter_kernel,
        "scatter",
        [message],
        [here_ids, resid.reshape(INNER, INNER), here] + row_fwd_tables,
        smem=1,
        any_args=(2,),
        scratch=[pltpu.VMEM((INNER, INNER), F32), points]
        + rows
        + [pltpu.VMEM((PEERS * SLOTS, INNER), BF16), pltpu.SemaphoreType.DMA((1,))]
        + [screen] * COPIES,
    )[0]
    out_pencils = call(
        column_second_kernel,
        "column_second",
        [message],
        [par, pencils, amp, own, from_prev, from_next] + col_tables,
        smem=1,
        any_args=range(1, 8),
        any_outs=(0,),
        collective_id=1,
        scratch=spectral
        + [pltpu.VMEM(MESSAGES, BF16)] * 2
        + exchange_sems()
        + exchange_sems()
        + spectral
        + [pltpu.VMEM(PENCILS, BF16)] * 2
        + [pltpu.VMEM(t.shape, BF16) for t in col_tables]
        + [pltpu.SemaphoreType.DMA((6,))],
    )[0]
    return row_backward(out_pencils, x, row_inv_tables)[None]


def solution(mesh):
    in_specs = (
        P("tm", "strip", None),
        P("tm"),
        P("tm"),
        P("tm", None),
        P("tm", "strip", None, None),
        P("tm", "strip", None),
        P("tm", "strip", None, None),
        P("tm", "strip", None),
    )
    out_specs = P("tm", "strip", None)
    return jax.shard_map(local, mesh=mesh, in_specs=in_specs, out_specs=out_specs, check_vma=False)
```
